32 devices in a mesh: dp: 4 (over y, x), rep: 8 (over z, core).
Axes of the slice: x: 2, y: 2, z: 4, core: 2. Of those that a mesh axis runs over, the one named last changes fastest.
Arguments:
- video: float32 [112, 65536], P(None, ('dp', 'rep')), may hold values from -6 to 6
- frame_counts: int32 [64], P(('dp', 'rep')), may hold values from 1 to 7, as said below
- momentum_index: int32 [1], replicated, may hold values from 1 to 9
- expand_weight: float32 [2, 640, 112], replicated, may hold values from -0.5 to 0.5
- wide_gains: float32 [4, 640], replicated, may hold values from 0.25 to 1.75
- wide_biases: float32 [4, 640], replicated, may hold values from -3 to 3
- narrow_gains: float32 [2, 112], replicated, may hold values from 0.25 to 1.75
- narrow_biases: float32 [2, 112], replicated, may hold values from -3 to 3
- depth_weight: float32 [2, 45, 640], replicated, may hold values from -0.875 to 0.875
- squeeze_weight: float32 [2, 160, 640], replicated, may hold values from -0.25 to 0.25
- squeeze_bias: float32 [2, 160], replicated, may hold values from -3 to 3
- excite_weight: float32 [2, 640, 160], replicated, may hold values from -0.5 to 0.5
- excite_bias: float32 [2, 640], replicated, may hold values from -3 to 3
- project_weight: float32 [2, 112, 640], replicated, may hold values from -0.25 to 0.25
- wide_means: float32 [4, 640], replicated, may hold values from -3 to 3
- wide_variances: float32 [4, 640], replicated, may hold values from 0.5 to 2
- narrow_means: float32 [2, 112], replicated, may hold values from -3 to 3
- narrow_variances: float32 [2, 112], replicated, may hold values from 0.5 to 2
- cotangent: float32 [112, 16384], P(None, ('dp', 'rep')), may hold values from -6 to 6
Outputs:
- activations: float32 [112, 16384], P(None, ('dp', 'rep'))
- video_grad: float32 [112, 65536], P(None, ('dp', 'rep'))
- expand_weight_grad: float32 [2, 640, 112], replicated
- wide_gains_grad: float32 [4, 640], replicated
- wide_biases_grad: float32 [4, 640], replicated
- narrow_gains_grad: float32 [2, 112], replicated
- narrow_biases_grad: float32 [2, 112], replicated
- depth_weight_grad: float32 [2, 45, 640], replicated
- squeeze_weight_grad: float32 [2, 160, 640], replicated
- squeeze_bias_grad: float32 [2, 160], replicated
- excite_weight_grad: float32 [2, 640, 160], replicated
- excite_bias_grad: float32 [2, 640], replicated
- project_weight_grad: float32 [2, 112, 640], replicated
- new_wide_means: float32 [4, 640], replicated
- new_wide_variances: float32 [4, 640], replicated
- new_narrow_means: float32 [2, 112], replicated
- new_narrow_variances: float32 [2, 112], replicated
The draws below stay inside these ranges and needn't reach their ends.
Inputs may be any that keep to these rules, and one draw needn't show every extreme that they name: `frame_counts`: each device's 2 entries give its clips' frame counts in order; they sum to at most 8, the slots after them are padding, and some device's entries sum to exactly 8.
All inputs are finite; a program needn't handle non-finite values.
Results may differ from the reference program's by a relative error of at most 0.0003.
Values sent between devices are 32-bit elements; how exact they have to be, the bound alone decides.
No kernel may reach another device: no remote copies, remote signals or barrier semaphores. Data moves between devices by JAX's collectives and lax.ppermute only.
A program may use at most 576 MiB of HBM per device.

```python
import math
from functools import partial
import jax
import jax.numpy as jnp
from jax import lax

CIN = 112
CEXP = 640
CSE = 160
SIDE = 16
FRAMES_DEV = 8
CLIPS_DEV = 2
CLIPS = 64
PIXELS = 65536
PIXELS_HALF = 16384
N_DP = 4
N_REP = 8


def draw_frame_counts(key, part):
    key = jax.random.fold_in(key, 7)
    device_count = CLIPS // CLIPS_DEV
    key_total, key_full, key_split = jax.random.split(key, 3)
    lowest = FRAMES_DEV - 2
    totals = jax.random.randint(key_total, (device_count,), lowest, FRAMES_DEV + 1)
    chosen = jax.random.randint(key_full, (), 0, device_count)
    is_full = jnp.arange(device_count) == chosen
    totals = jnp.where(is_full, FRAMES_DEV, totals)
    raw_split = jax.random.randint(key_split, (device_count,), 0, 1 << 20)
    first_len = raw_split % (totals - 5) + 5
    first_len = jnp.where(is_full, FRAMES_DEV - 1, first_len)
    return jnp.stack([first_len, totals - first_len], axis=1).reshape(-1).astype(jnp.int32)


def levels(rng, extent, shards, smallest, top_value):
    level, own = 1.0, jax.random.fold_in(rng, 6)
    for axis_at, parts in shards:
        heights = jnp.exp(jax.random.uniform(jax.random.fold_in(own, axis_at), (parts,), jnp.float32, smallest / len(shards), top_value / len(shards)))
        level = level * jnp.repeat(heights, extent[axis_at] // parts).reshape([-1 if axis == axis_at else 1 for axis in range(len(extent))])
    return level


def centred(rng, shape, spread, reach, pieces=(), kind=jnp.bfloat16):
    level = levels(rng, shape, pieces, -0.22, 0.18) if pieces else 1.0
    values = jax.random.normal(rng, shape, jnp.float32) * spread * level
    return jnp.minimum(jnp.maximum(values, -reach), reach).astype(kind)


def setup_inputs(seed: int = 0) -> dict:
    keys = jax.random.split(jax.random.key(seed), 20)
    return {
        "video": centred(keys[0], (CIN, PIXELS), 1.0, 6.0, ((1, 32),), jnp.float32),
        "frame_counts": draw_frame_counts(jax.random.fold_in(keys[19], 71), 0),
        "momentum_index": jax.random.randint(keys[2], (1,), 1, 10).astype(jnp.int32),
        "expand_weight": centred(keys[3], (2, CEXP, CIN), CIN ** -0.5, 0.5, (), jnp.float32),
        "wide_gains": jnp.clip(1.0 + 0.15 * jax.random.normal(keys[4], (4, CEXP), jnp.float32), 0.25, 1.75),
        "wide_biases": centred(keys[5], (4, CEXP), 0.5, 3.0, (), jnp.float32),
        "narrow_gains": jnp.clip(1.0 + 0.15 * jax.random.normal(keys[6], (2, CIN), jnp.float32), 0.25, 1.75),
        "narrow_biases": centred(keys[7], (2, CIN), 0.5, 3.0, (), jnp.float32),
        "depth_weight": centred(keys[8], (2, 45, CEXP), 45 ** -0.5, 0.875, (), jnp.float32),
        "squeeze_weight": centred(keys[9], (2, CSE, CEXP), CEXP ** -0.5, 0.25, (), jnp.float32),
        "squeeze_bias": centred(keys[10], (2, CSE), 0.5, 3.0, (), jnp.float32),
        "excite_weight": centred(keys[11], (2, CEXP, CSE), CSE ** -0.5, 0.5, (), jnp.float32),
        "excite_bias": centred(keys[12], (2, CEXP), 0.5, 3.0, (), jnp.float32),
        "project_weight": centred(keys[13], (2, CIN, CEXP), CEXP ** -0.5, 0.25, (), jnp.float32),
        "wide_means": centred(keys[14], (4, CEXP), 0.5, 3.0, (), jnp.float32),
        "wide_variances": jnp.clip(jnp.exp(jax.random.uniform(keys[15], (4, CEXP), jnp.float32, math.log(0.5), math.log(2.0))), 0.5, 2.0),
        "narrow_means": centred(keys[16], (2, CIN), 0.5, 3.0, (), jnp.float32),
        "narrow_variances": jnp.clip(jnp.exp(jax.random.uniform(keys[17], (2, CIN), jnp.float32, math.log(0.5), math.log(2.0))), 0.5, 2.0),
        "cotangent": centred(keys[18], (CIN, PIXELS_HALF), 1.0, 6.0, ((1, 32),), jnp.float32),
    }


@jax.custom_vjp
def low(v):
    return lax.optimization_barrier(v.astype(jnp.bfloat16)).astype(jnp.float32)

@jax.custom_vjp
def low_back(v):
    return v

def low_keep(v):
    return (low(v), None)

def low_pass(kept, grad):
    return (grad,)

def back_keep(v):
    return (v, None)

def back_low(kept, grad):
    return (low(grad),)
low.defvjp(low_keep, low_pass)
low_back.defvjp(back_keep, back_low)
EPSILON = 1e-05
HIGHEST = lax.Precision.HIGHEST

def silu(values):
    return values * jax.nn.sigmoid(values)

def layout_tables(counts_row, frames, frame_side):
    clip_total = counts_row.shape[0]
    clip_ends = jnp.cumsum(counts_row).astype(jnp.int32)
    slots = jnp.arange(frames, dtype=jnp.int32)
    clip_of = lax.optimization_barrier(jnp.sum((slots[:, None] >= clip_ends[None, :]).astype(jnp.int32), axis=1))
    begins = jnp.concatenate([jnp.zeros((1,), jnp.int32), clip_ends])
    choose = (clip_of[:, None] == jnp.arange(clip_total + 1, dtype=jnp.int32)[None, :]).astype(jnp.int32)
    starts = lax.optimization_barrier(jnp.sum(choose * begins[None, :], axis=1)).astype(jnp.int32)
    places = slots - starts
    live_frame = (clip_of < clip_total).astype(jnp.float32)
    same_clip = ((clip_of[:, None] == clip_of[None, :]) & (slots[:, None] <= slots[None, :])).astype(jnp.float32)
    cumulative = live_frame[:, None] * live_frame[None, :] * same_clip / (places[None, :].astype(jnp.float32) + 1.0)
    time_lags = jnp.arange(5, dtype=jnp.int32)
    steps_side = jnp.arange(3, dtype=jnp.int32) - 1
    coords = jnp.arange(frame_side, dtype=jnp.int32)
    lag_ok = (places[None, :] >= time_lags[:, None]).astype(jnp.float32)
    moved = coords[None, :] + steps_side[:, None]
    line_ok = ((moved >= 0) & (moved < frame_side)).astype(jnp.float32)
    tap_masks = lag_ok[:, None, None, :, None, None] * line_ok[None, :, None, None, :, None] * line_ok[None, None, :, None, None, :]
    tap_masks = tap_masks.reshape(45, frames * frame_side * frame_side)
    live_full = jnp.repeat(live_frame, frame_side * frame_side)
    live_half = jnp.repeat(live_frame, frame_side * frame_side // 4)
    return (live_full, live_half, tap_masks, cumulative)

def tap_offsets(frame_side):
    return [-time_lag * frame_side * frame_side + row_step * frame_side + col_step for time_lag in range(5) for row_step in (-1, 0, 1) for col_step in (-1, 0, 1)]

def depthwise_apply(values, tap_weights, tap_masks, frame_side):
    margin = 4 * frame_side * frame_side + frame_side + 1
    padded = jnp.pad(values, ((0, 0), (margin, margin)))
    pixel_count = values.shape[1]
    result = jnp.zeros_like(values)
    for tap_index, flat_step in enumerate(tap_offsets(frame_side)):
        shifted = lax.slice_in_dim(padded, margin + flat_step, margin + flat_step + pixel_count, axis=1)
        result = result + tap_weights[tap_index][:, None] * tap_masks[tap_index][None, :] * shifted
    return result

def halve(values, frame_side):
    channels = values.shape[0]
    half_side = frame_side // 2
    grid = values.reshape(channels, -1, half_side, 2, half_side, 2)
    return grid[:, :, :, 0, :, 0].reshape(channels, -1)

def normalize(values, stat_pair, gain, bias):
    average, variance = stat_pair
    return gain[:, None] * (values - average[:, None]) * lax.rsqrt(variance + EPSILON)[:, None] + bias[:, None]

def moments(values, live_mask):
    return (lax.optimization_barrier(jnp.sum(values * live_mask[None, :], axis=1)), lax.optimization_barrier(jnp.sum(values * values * live_mask[None, :], axis=1)))

def chain_to(inputs, layout, weights, stats, level, strided, frame_side):
    live_full, live_half, tap_masks, cumulative = layout
    expand_w, depth_w, down_w, down_b, up_w, up_b, proj_w, wide_g, wide_b = weights
    live_out = live_half if strided else live_full
    expanded = jnp.dot(expand_w, inputs, precision=HIGHEST)
    if level == 1:
        return expanded
    first_act = silu(normalize(expanded, stats[0], wide_g[0], wide_b[0])) * live_full[None, :]
    depth_out = depthwise_apply(first_act, depth_w, tap_masks, frame_side)
    if strided:
        depth_out = halve(depth_out, frame_side)
    if level == 2:
        return depth_out
    second_act = silu(normalize(depth_out, stats[1], wide_g[1], wide_b[1])) * live_out[None, :]
    channels = second_act.shape[0]
    frames = cumulative.shape[0]
    grouped = second_act.reshape(channels, frames, -1)
    running = jnp.dot(lax.optimization_barrier(jnp.mean(grouped, axis=2)), cumulative, precision=HIGHEST)
    squeezed = silu(jnp.dot(down_w, running, precision=HIGHEST) + down_b[:, None])
    gate_values = jax.nn.sigmoid(jnp.dot(up_w, squeezed, precision=HIGHEST) + up_b[:, None])
    excited = (grouped * gate_values[:, :, None]).reshape(channels, -1)
    return jnp.dot(proj_w, excited, precision=HIGHEST)

def moment_at(entry_item, weights, stats, level, strided, frame_side):
    block_input, live_full, live_half, tap_masks, cumulative = entry_item
    values = chain_to(block_input, (live_full, live_half, tap_masks, cumulative), weights, stats, level, strided, frame_side)
    live_mask = live_full if level == 1 or not strided else live_half
    return moments(values, live_mask)

def output_at(entry_item, weights, stats, narrow, strided, frame_side):
    block_input, live_full, live_half, tap_masks, cumulative = entry_item
    values = chain_to(block_input, (live_full, live_half, tap_masks, cumulative), weights, stats, 3, strided, frame_side)
    normed = normalize(values, stats[2], narrow[0], narrow[1])
    live_out = live_half if strided else live_full
    if not strided:
        normed = normed + block_input
    return normed * live_out[None, :]

def run_block(inputs, layouts, weights, narrow, totals, strided, frame_side):
    live_fulls, live_halves, mask_sets, cumulatives = layouts
    entries = (inputs, live_fulls, live_halves, mask_sets, cumulatives)
    stats = ()
    for level in (1, 2, 3):
        step_fn = jax.checkpoint(partial(moment_at, level=level, strided=strided, frame_side=frame_side))
        summed, squares = lax.map(lambda entry_item, frozen=stats, step_fn=step_fn: step_fn(entry_item, weights, frozen), entries)
        pixel_total = totals[0] if level == 1 else totals[1]
        average = lax.optimization_barrier(jnp.sum(summed, axis=0)) / pixel_total
        variance = lax.optimization_barrier(jnp.sum(squares, axis=0)) / pixel_total - average * average
        stats = stats + ((average, variance),)
    final_fn = jax.checkpoint(partial(output_at, strided=strided, frame_side=frame_side))
    outputs = lax.map(lambda entry_item: final_fn(entry_item, weights, stats, narrow), entries)
    return (outputs, stats)

def reference(video, frame_counts, momentum_index, expand_weight, wide_gains, wide_biases, narrow_gains, narrow_biases, depth_weight, squeeze_weight, squeeze_bias, excite_weight, excite_bias, project_weight, wide_means, wide_variances, narrow_means, narrow_variances, cotangent):
    device_count = N_DP * N_REP
    layouts = jax.vmap(lambda counts_row: layout_tables(counts_row, FRAMES_DEV, SIDE))(frame_counts.reshape(device_count, CLIPS_DEV))
    full_total = jnp.sum(layouts[0])
    half_total = jnp.sum(layouts[1])

    def forward(video_in, expand_w, wide_g, wide_b, narrow_g, narrow_b, depth_w, down_w, down_b, up_w, up_b, proj_w):
        inputs = video_in.reshape(CIN, device_count, -1).transpose(1, 0, 2)
        weights_one = (expand_w[0], depth_w[0], down_w[0], down_b[0], up_w[0], up_b[0], proj_w[0], wide_g[0:2], wide_b[0:2])
        weights_two = (expand_w[1], depth_w[1], down_w[1], down_b[1], up_w[1], up_b[1], proj_w[1], wide_g[2:4], wide_b[2:4])
        hidden, stats_one = run_block(inputs, layouts, weights_one, (narrow_g[0], narrow_b[0]), (full_total, full_total), False, SIDE)
        output, stats_two = run_block(hidden, layouts, weights_two, (narrow_g[1], narrow_b[1]), (full_total, half_total), True, SIDE)
        return (output.transpose(1, 0, 2).reshape(CIN, -1), (stats_one, stats_two))
    activations, pullback, all_stats = jax.vjp(forward, video, expand_weight, wide_gains, wide_biases, narrow_gains, narrow_biases, depth_weight, squeeze_weight, squeeze_bias, excite_weight, excite_bias, project_weight, has_aux=True)
    grads = pullback(cotangent)
    momentum = momentum_index[0].astype(jnp.float32) / 10.0
    stats_one, stats_two = all_stats
    full_fix = full_total / (full_total - 1.0)
    half_fix = half_total / (half_total - 1.0)
    batch_wide_means = jnp.stack([stats_one[0][0], stats_one[1][0], stats_two[0][0], stats_two[1][0]])
    batch_wide_vars = jnp.stack([stats_one[0][1] * full_fix, stats_one[1][1] * full_fix, stats_two[0][1] * full_fix, stats_two[1][1] * half_fix])
    batch_narrow_means = jnp.stack([stats_one[2][0], stats_two[2][0]])
    batch_narrow_vars = jnp.stack([stats_one[2][1] * full_fix, stats_two[2][1] * half_fix])
    new_wide_means = (1.0 - momentum) * wide_means + momentum * batch_wide_means
    new_wide_variances = (1.0 - momentum) * wide_variances + momentum * batch_wide_vars
    new_narrow_means = (1.0 - momentum) * narrow_means + momentum * batch_narrow_means
    new_narrow_variances = (1.0 - momentum) * narrow_variances + momentum * batch_narrow_vars
    return (activations, grads[0], grads[1], grads[2], grads[3], grads[4], grads[5], grads[6], grads[7], grads[8], grads[9], grads[10], grads[11], new_wide_means, new_wide_variances, new_narrow_means, new_narrow_variances)
```

```python
import jax
import jax.numpy as jnp
from jax import lax
from jax.sharding import PartitionSpec as P

SIDE = 16


EPSILON = 1e-05
HIGHEST = lax.Precision.HIGHEST


def silu(values):
    return values * jax.nn.sigmoid(values)


def silu_slope(values):
    sigmoid = jax.nn.sigmoid(values)
    return sigmoid * (1.0 + values * (1.0 - sigmoid))


def layout_tables(counts_row, frames, frame_side):
    clip_total = counts_row.shape[0]
    clip_ends = jnp.cumsum(counts_row)
    slots = jnp.arange(frames, dtype=jnp.int32)
    clip_of = jnp.sum((slots[:, None] >= clip_ends[None, :]).astype(jnp.int32), axis=1)
    begins = jnp.concatenate([jnp.zeros((1,), jnp.int32), clip_ends])
    choose = (clip_of[:, None] == jnp.arange(clip_total + 1, dtype=jnp.int32)[None, :]).astype(
        jnp.int32
    )
    starts = jnp.sum(choose * begins[None, :], axis=1)
    places = slots - starts
    live_frame = (clip_of < clip_total).astype(jnp.float32)
    same_clip = (
        (clip_of[:, None] == clip_of[None, :]) & (slots[:, None] <= slots[None, :])
    ).astype(jnp.float32)
    cumulative = (
        live_frame[:, None]
        * live_frame[None, :]
        * same_clip
        / (places[None, :].astype(jnp.float32) + 1.0)
    )
    time_lags = jnp.arange(5, dtype=jnp.int32)
    steps_side = jnp.arange(3, dtype=jnp.int32) - 1
    coords = jnp.arange(frame_side, dtype=jnp.int32)
    lag_ok = (places[None, :] >= time_lags[:, None]).astype(jnp.float32)
    moved = coords[None, :] + steps_side[:, None]
    line_ok = ((moved >= 0) & (moved < frame_side)).astype(jnp.float32)
    tap_masks = (
        lag_ok[:, None, None, :, None, None]
        * line_ok[None, :, None, None, :, None]
        * line_ok[None, None, :, None, None, :]
    )
    tap_masks = tap_masks.reshape(45, frames * frame_side * frame_side)
    live_full = jnp.repeat(live_frame, frame_side * frame_side)
    live_half = jnp.repeat(live_frame, frame_side * frame_side // 4)
    return (live_full, live_half, tap_masks, cumulative)


def tap_offsets(frame_side):
    return [
        -time_lag * frame_side * frame_side + row_step * frame_side + col_step
        for time_lag in range(5)
        for row_step in (-1, 0, 1)
        for col_step in (-1, 0, 1)
    ]


def margin_of(frame_side):
    return 4 * frame_side * frame_side + frame_side + 1


def border(values, frame_side):
    margin = margin_of(frame_side)
    return jnp.pad(values, ((0, 0), (margin, margin)))


def window(padded, flat_step, pixel_count, frame_side):
    begin_at = margin_of(frame_side) + flat_step
    return lax.slice_in_dim(padded, begin_at, begin_at + pixel_count, axis=1)


def depthwise_apply(values, tap_weights, tap_masks, frame_side):
    padded = border(values, frame_side)
    pixel_count = values.shape[1]
    result = jnp.zeros_like(values)
    for tap_index, flat_step in enumerate(tap_offsets(frame_side)):
        result = result + tap_weights[tap_index][:, None] * tap_masks[tap_index][None, :] * window(
            padded, flat_step, pixel_count, frame_side
        )
    return result


def depthwise_backward(first_act, grad_out, tap_weights, tap_masks, frame_side):
    padded_act = border(first_act, frame_side)
    pixel_count = first_act.shape[1]
    grad_input = jnp.zeros_like(first_act)
    grad_list = []
    for tap_index, flat_step in enumerate(tap_offsets(frame_side)):
        masked_grad = grad_out * tap_masks[tap_index][None, :]
        grad_list.append(
            jnp.sum(masked_grad * window(padded_act, flat_step, pixel_count, frame_side), axis=1)
        )
        grad_input = grad_input + tap_weights[tap_index][:, None] * window(
            border(masked_grad, frame_side), -flat_step, pixel_count, frame_side
        )
    return (grad_input, jnp.stack(grad_list))


def halve(values, frame_side):
    channels = values.shape[0]
    half_side = frame_side // 2
    grid = values.reshape(channels, -1, half_side, 2, half_side, 2)
    return grid[:, :, :, 0, :, 0].reshape(channels, -1)


def widen(values, frame_side):
    channels = values.shape[0]
    half_side = frame_side // 2
    grid = values.reshape(channels, -1, half_side, 1, half_side, 1)
    grid = jnp.pad(grid, ((0, 0), (0, 0), (0, 0), (0, 1), (0, 0), (0, 1)))
    return grid.reshape(channels, -1)


def pair_exchange(row, radices):
    sizes = {name: lax.axis_size(name) for name in ("dp", "rep")}
    names = ("dp", "rep")
    total = sizes["dp"] * sizes["rep"]
    stride = 1
    for radix in radices:
        parts = [row]
        for step in range(1, radix):
            flip = step * stride
            parts.append(lax.ppermute(row, names, [(i, i ^ flip) for i in range(total)]))
        while len(parts) > 1:
            parts = [parts[i] + parts[i + 1] for i in range(0, len(parts), 2)]
        row = parts[0]
        stride = stride * radix
    return row


def global_sum(pieces, form):
    sizes = [piece.size for piece in pieces]
    flat = jnp.concatenate([piece.reshape(-1) for piece in pieces])
    count = flat.shape[0]
    padded = -(-count // 1024) * 1024
    row = jnp.pad(flat, (0, padded - count)).reshape(-1, 128)
    total = lax.axis_size("dp") * lax.axis_size("rep")
    if form == "gather":
        row = jnp.sum(lax.all_gather(row, ("dp", "rep")), axis=0)
    elif form == "halving":
        row = pair_exchange(row, [2] * (total.bit_length() - 1))
    elif form == "wide":
        row = pair_exchange(row, [lax.axis_size("rep"), lax.axis_size("dp")])
    elif form == "alltoall":
        wide = jnp.broadcast_to(row[None], (total,) + row.shape)
        row = jnp.sum(lax.all_to_all(wide, ("dp", "rep"), 0, 0, tiled=True), axis=0)
    elif form == "axes":
        row = lax.psum(lax.psum(row, "dp"), "rep")
    else:
        row = lax.psum(row, ("dp", "rep"))
    flat = row.reshape(-1)
    results = []
    begin = 0
    for size, piece in zip(sizes, pieces):
        results.append(flat[begin : begin + size].reshape(piece.shape))
        begin += size
    return results


def batch_norm_stats(values, live_mask, form):
    kept = values * live_mask[None, :]
    summed, squares, pixel_total = global_sum(
        [jnp.sum(kept, axis=1), jnp.sum(kept * values, axis=1), jnp.sum(live_mask)], form
    )
    average = summed / pixel_total
    variance = squares / pixel_total - average * average
    return (average, variance, pixel_total)


def normed_of(values, stat_triple):
    return (values - stat_triple[0][:, None]) * lax.rsqrt(stat_triple[1] + EPSILON)[:, None]


def norm_backward(grad_y, normed, gain, stat_triple, live_mask, form):
    summed_grad, summed_cross = global_sum(
        [jnp.sum(grad_y, axis=1), jnp.sum(grad_y * normed, axis=1)], form
    )
    pixel_total = stat_triple[2]
    factor = gain * lax.rsqrt(stat_triple[1] + EPSILON)
    grad_z = factor[:, None] * (
        grad_y
        - (summed_grad / pixel_total)[:, None]
        - normed * (summed_cross / pixel_total)[:, None]
    )
    return (grad_z * live_mask[None, :], summed_cross, summed_grad)


def block_forward(inputs, layout, params, strided, frame_side, forms):
    live_full, live_half, tap_masks, cumulative = layout
    expand_w, depth_w, down_w, down_b, up_w, up_b, proj_w, wide_g, wide_b, narrow_g, narrow_b = (
        params
    )
    live_out = live_half if strided else live_full
    expanded = jnp.dot(expand_w, inputs, precision=HIGHEST)
    stats_one = batch_norm_stats(expanded, live_full, forms[0])
    normed_one = normed_of(expanded, stats_one)
    first_act = silu(wide_g[0][:, None] * normed_one + wide_b[0][:, None]) * live_full[None, :]
    depth_out = depthwise_apply(first_act, depth_w, tap_masks, frame_side)
    if strided:
        depth_out = halve(depth_out, frame_side)
    stats_two = batch_norm_stats(depth_out, live_out, forms[1])
    normed_two = normed_of(depth_out, stats_two)
    second_act = silu(wide_g[1][:, None] * normed_two + wide_b[1][:, None]) * live_out[None, :]
    channels = second_act.shape[0]
    frames = cumulative.shape[0]
    grouped = second_act.reshape(channels, frames, -1)
    running = jnp.dot(jnp.mean(grouped, axis=2), cumulative, precision=HIGHEST)
    squeeze_pre = jnp.dot(down_w, running, precision=HIGHEST) + down_b[:, None]
    squeezed = silu(squeeze_pre)
    gate_values = jax.nn.sigmoid(jnp.dot(up_w, squeezed, precision=HIGHEST) + up_b[:, None])
    excited = (grouped * gate_values[:, :, None]).reshape(channels, -1)
    projected = jnp.dot(proj_w, excited, precision=HIGHEST)
    stats_three = batch_norm_stats(projected, live_out, forms[2])
    normed_three = normed_of(projected, stats_three)
    result = narrow_g[:, None] * normed_three + narrow_b[:, None]
    if not strided:
        result = result + inputs
    result = result * live_out[None, :]
    kept_values = (
        inputs,
        normed_one,
        first_act,
        normed_two,
        second_act,
        running,
        squeeze_pre,
        squeezed,
        gate_values,
        excited,
        normed_three,
    )
    return (result, kept_values, (stats_one, stats_two, stats_three))


def block_backward(grad_out, kept_values, stats, params, layout, strided, frame_side, forms):
    (
        inputs,
        normed_one,
        first_act,
        normed_two,
        second_act,
        running,
        squeeze_pre,
        squeezed,
        gate_values,
        excited,
        normed_three,
    ) = kept_values
    expand_w, depth_w, down_w, down_b, up_w, up_b, proj_w, wide_g, wide_b, narrow_g, narrow_b = (
        params
    )
    live_full, live_half, tap_masks, cumulative = layout
    live_out = live_half if strided else live_full
    grad_three_y = grad_out * live_out[None, :]
    grad_z3, gain_three, bias_three = norm_backward(
        grad_three_y, normed_three, narrow_g, stats[2], live_out, forms[0]
    )
    grad_project = jnp.dot(grad_z3, excited.T, precision=HIGHEST)
    grad_excited = jnp.dot(proj_w.T, grad_z3, precision=HIGHEST)
    channels, frames = gate_values.shape
    grouped_grad = grad_excited.reshape(channels, frames, -1)
    grouped_act = second_act.reshape(channels, frames, -1)
    per_frame = grouped_grad.shape[2]
    grad_gates = jnp.sum(grouped_grad * grouped_act, axis=2)
    grad_up_pre = grad_gates * gate_values * (1.0 - gate_values)
    grad_up_bias = jnp.sum(grad_up_pre, axis=1)
    grad_up = jnp.dot(grad_up_pre, squeezed.T, precision=HIGHEST)
    grad_squeezed = jnp.dot(up_w.T, grad_up_pre, precision=HIGHEST)
    grad_down_pre = grad_squeezed * silu_slope(squeeze_pre)
    grad_down_bias = jnp.sum(grad_down_pre, axis=1)
    grad_down = jnp.dot(grad_down_pre, running.T, precision=HIGHEST)
    grad_running = jnp.dot(down_w.T, grad_down_pre, precision=HIGHEST)
    grad_pooled = jnp.dot(grad_running, cumulative.T, precision=HIGHEST)
    grad_second = (
        grouped_grad * gate_values[:, :, None] + grad_pooled[:, :, None] / per_frame
    ).reshape(channels, -1)
    pre_two = wide_g[1][:, None] * normed_two + wide_b[1][:, None]
    grad_two_y = grad_second * live_out[None, :] * silu_slope(pre_two)
    grad_z2, gain_two, bias_two = norm_backward(
        grad_two_y, normed_two, wide_g[1], stats[1], live_out, forms[1]
    )
    if strided:
        grad_z2 = widen(grad_z2, frame_side)
    grad_first, grad_depth = depthwise_backward(first_act, grad_z2, depth_w, tap_masks, frame_side)
    pre_one = wide_g[0][:, None] * normed_one + wide_b[0][:, None]
    grad_one_y = grad_first * live_full[None, :] * silu_slope(pre_one)
    grad_z1, gain_one, bias_one = norm_backward(
        grad_one_y, normed_one, wide_g[0], stats[0], live_full, forms[2]
    )
    grad_expand = jnp.dot(grad_z1, inputs.T, precision=HIGHEST)
    grad_inputs = jnp.dot(expand_w.T, grad_z1, precision=HIGHEST)
    if not strided:
        grad_inputs = grad_inputs + grad_three_y
    norm_grads = (gain_one, bias_one, gain_two, bias_two, gain_three, bias_three)
    return (
        grad_inputs,
        grad_expand,
        grad_depth,
        grad_down,
        grad_down_bias,
        grad_up,
        grad_up_bias,
        grad_project,
        norm_grads,
    )


def local(
    video,
    frame_counts,
    momentum_index,
    expand_weight,
    wide_gains,
    wide_biases,
    narrow_gains,
    narrow_biases,
    depth_weight,
    squeeze_weight,
    squeeze_bias,
    excite_weight,
    excite_bias,
    project_weight,
    wide_means,
    wide_variances,
    narrow_means,
    narrow_variances,
    cotangent,
):
    frame_side = SIDE
    frames = video.shape[1] // (frame_side * frame_side)
    layout = layout_tables(frame_counts, frames, frame_side)
    params_one = (
        expand_weight[0],
        depth_weight[0],
        squeeze_weight[0],
        squeeze_bias[0],
        excite_weight[0],
        excite_bias[0],
        project_weight[0],
        wide_gains[0:2],
        wide_biases[0:2],
        narrow_gains[0],
        narrow_biases[0],
    )
    params_two = (
        expand_weight[1],
        depth_weight[1],
        squeeze_weight[1],
        squeeze_bias[1],
        excite_weight[1],
        excite_bias[1],
        project_weight[1],
        wide_gains[2:4],
        wide_biases[2:4],
        narrow_gains[1],
        narrow_biases[1],
    )
    hidden, kept_one, stats_one = block_forward(
        video, layout, params_one, False, frame_side, ("gather", "halving", "wide")
    )
    activations, kept_two, stats_two = block_forward(
        hidden, layout, params_two, True, frame_side, ("alltoall", "axes", "halving")
    )
    (
        grad_hidden,
        two_expand,
        two_depth,
        two_down,
        two_down_bias,
        two_up,
        two_up_bias,
        two_project,
        norms_two,
    ) = block_backward(
        cotangent, kept_two, stats_two, params_two, layout, True, frame_side, ("wide", "gather", "halving")
    )
    (
        video_grad,
        one_expand,
        one_depth,
        one_down,
        one_down_bias,
        one_up,
        one_up_bias,
        one_project,
        norms_one,
    ) = block_backward(
        grad_hidden, kept_one, stats_one, params_one, layout, False, frame_side, ("wide", "alltoall", "halving")
    )
    weight_grads = lax.psum(
        (
            jnp.stack([one_expand, two_expand]),
            jnp.stack([one_depth, two_depth]),
            jnp.stack([one_down, two_down]),
            jnp.stack([one_down_bias, two_down_bias]),
            jnp.stack([one_up, two_up]),
            jnp.stack([one_up_bias, two_up_bias]),
            jnp.stack([one_project, two_project]),
        ),
        ("dp", "rep"),
    )
    wide_gains_grad = jnp.stack([norms_one[0], norms_one[2], norms_two[0], norms_two[2]])
    wide_biases_grad = jnp.stack([norms_one[1], norms_one[3], norms_two[1], norms_two[3]])
    narrow_gains_grad = jnp.stack([norms_one[4], norms_two[4]])
    narrow_biases_grad = jnp.stack([norms_one[5], norms_two[5]])
    momentum = momentum_index[0].astype(jnp.float32) / 10.0

    def unbiased(stat_triple):
        return stat_triple[1] * stat_triple[2] / (stat_triple[2] - 1.0)

    batch_wide_means = jnp.stack(
        [stats_one[0][0], stats_one[1][0], stats_two[0][0], stats_two[1][0]]
    )
    batch_wide_vars = jnp.stack(
        [
            unbiased(stats_one[0]),
            unbiased(stats_one[1]),
            unbiased(stats_two[0]),
            unbiased(stats_two[1]),
        ]
    )
    batch_narrow_means = jnp.stack([stats_one[2][0], stats_two[2][0]])
    batch_narrow_vars = jnp.stack([unbiased(stats_one[2]), unbiased(stats_two[2])])
    new_wide_means = (1.0 - momentum) * wide_means + momentum * batch_wide_means
    new_wide_variances = (1.0 - momentum) * wide_variances + momentum * batch_wide_vars
    new_narrow_means = (1.0 - momentum) * narrow_means + momentum * batch_narrow_means
    new_narrow_variances = (1.0 - momentum) * narrow_variances + momentum * batch_narrow_vars
    return (
        activations,
        video_grad,
        weight_grads[0],
        wide_gains_grad,
        wide_biases_grad,
        narrow_gains_grad,
        narrow_biases_grad,
        weight_grads[1],
        weight_grads[2],
        weight_grads[3],
        weight_grads[4],
        weight_grads[5],
        weight_grads[6],
        new_wide_means,
        new_wide_variances,
        new_narrow_means,
        new_narrow_variances,
    )


def solution(mesh):
    placed = (
        P(None, ("dp", "rep")),
        P(("dp", "rep")),
        P(),
        P(),
        P(),
        P(),
        P(),
        P(),
        P(),
        P(),
        P(),
        P(),
        P(),
        P(),
        P(),
        P(),
        P(),
        P(),
        P(None, ("dp", "rep")),
    )
    return jax.shard_map(
        local,
        mesh=mesh,
        in_specs=placed,
        out_specs=(
            P(None, ("dp", "rep")),
            P(None, ("dp", "rep")),
            P(),
            P(),
            P(),
            P(),
            P(),
            P(),
            P(),
            P(),
            P(),
            P(),
            P(),
            P(),
            P(),
            P(),
            P(),
        ),
        check_vma=False,
    )
```

```python
import functools

import jax
import jax.numpy as jnp
from jax import lax
from jax.experimental import pallas as pl
from jax.experimental.pallas import tpu as pltpu
from jax.sharding import PartitionSpec as P

SIDE = 16
LANES = 128
LAGS = 5
FULL_ROWS = 2 * SIDE
HALF_ROWS = SIDE // 2
EPSILON = 1e-05
HIGHEST = lax.Precision.HIGHEST
F32 = jnp.float32
NN = (((1,), (0,)), ((), ()))
NT = (((1,), (1,)), ((), ()))
TN = (((0,), (0,)), ((), ()))
VMEM_BYTES = 52 * 1024 * 1024


def sigmoid(values):
    return 0.5 * jnp.tanh(0.5 * values) + 0.5


def silu_slope(values, sig):
    return sig * (1.0 + values * (1.0 - sig))


def exact_dot(left, right, dims=NN):
    return lax.dot_general(left, right, dims, precision=HIGHEST, preferred_element_type=F32)


def halves(values):
    high = values.astype(jnp.bfloat16)
    return (high, (values - high.astype(F32)).astype(jnp.bfloat16))


def split_dot(left, right, dims=NN):
    one = functools.partial(lax.dot_general, dimension_numbers=dims, preferred_element_type=F32)
    return one(left[0], right[0]) + (one(left[0], right[1]) + one(left[1], right[0]))


def product(left, right, dims=NN):
    return split_dot(halves(left), halves(right), dims)


def pad_rows(values):
    return jnp.concatenate([values, jnp.zeros((LANES - values.shape[0], values.shape[1]), values.dtype)], axis=0)


def column_order():
    q = lax.broadcasted_iota(jnp.int32, (LANES, LANES), 0)
    n = lax.broadcasted_iota(jnp.int32, (LANES, LANES), 1)
    source = (q // 16) * 16 + (q % 8) * 2 + (q // 8) % 2
    return (source == n).astype(jnp.bfloat16)


def thirds(values):
    high = values.astype(jnp.bfloat16)
    rest = values - high.astype(F32)
    middle = rest.astype(jnp.bfloat16)
    return (high, middle, (rest - middle.astype(F32)).astype(jnp.bfloat16))


def picked(order, values, dims, order_left):
    total = None
    for piece in thirds(values):
        args = (order, piece) if order_left else (piece, order)
        part = lax.dot_general(*args, dims, preferred_element_type=F32)
        total = part if total is None else total + part
    return total


def live_frames(counts_ref):
    total = counts_ref[0]
    for clip in range(1, counts_ref.shape[0]):
        total = total + counts_ref[clip]
    return total


def place_of(counts_ref, frame):
    begin = jnp.int32(0)
    end = jnp.int32(0)
    for clip in range(counts_ref.shape[0]):
        end = end + counts_ref[clip]
        begin = jnp.where(frame >= end, end, begin)
    return frame - begin


def running_matrix(counts_ref, frames):
    after = lax.broadcasted_iota(jnp.int32, (frames, frames), 0)
    before = lax.broadcasted_iota(jnp.int32, (frames, frames), 1)
    begin = jnp.int32(0)
    matrix = jnp.zeros((frames, frames), F32)
    for clip in range(counts_ref.shape[0]):
        end = begin + counts_ref[clip]
        inside = (before >= begin) & (before <= after) & (after < end)
        matrix = matrix + jnp.where(inside, 1.0 / (after - begin + 1).astype(F32), 0.0)
        begin = end
    return matrix


def columns_up(values):
    spot = lax.broadcasted_iota(jnp.int32, values.shape, 1)
    return jnp.where(spot == 7, 0.0, pltpu.roll(values, 7, axis=1))


def columns_down(values):
    spot = lax.broadcasted_iota(jnp.int32, values.shape, 1)
    return jnp.where(spot == 0, 0.0, pltpu.roll(values, 1, axis=1))


def tile_sum(values):
    return jnp.sum(jnp.sum(values, axis=0), axis=0, keepdims=True)


def rows8(*rows):
    lanes = rows[0].shape[1]
    spot = lax.broadcasted_iota(jnp.int32, (8, lanes), 0)
    block = jnp.zeros((8, lanes), F32)
    for index, row in enumerate(rows):
        block = jnp.where(spot == index, row, block)
    return block


def pick_row(block, index):
    spot = lax.broadcasted_iota(jnp.int32, block.shape, 0)
    return jnp.sum(jnp.where(spot == index, block, 0.0), axis=0, keepdims=True)


def outer(left, right):
    return exact_dot(rows8(left), rows8(right), TN)


def row_dot(row, matrix, dims=NN):
    return exact_dot(rows8(row), matrix, dims)[0:1]


def prepare_kernel(counts_ref, video_ref, cot_ref, x_ref, xt_ref, cot_out_ref, send_ref):
    order = column_order()
    total = live_frames(counts_ref)
    pixels = video_ref.shape[1]
    gram = jnp.zeros((LANES, LANES), F32)
    summed = jnp.zeros((1, LANES), F32)
    for part in range(pixels // LANES):
        live = jnp.where(part // 2 < total, 1.0, 0.0).astype(F32)
        block = pad_rows(video_ref[:, part * LANES : (part + 1) * LANES] * live)
        rows = picked(order, block, NT, True)
        columns = picked(order, block, NT, False)
        x_ref[part * LANES : (part + 1) * LANES, :] = rows
        xt_ref[:, part * LANES : (part + 1) * LANES] = columns
        gram = gram + exact_dot(columns, rows)
        summed = summed + jnp.sum(rows, axis=0, keepdims=True)
    send_ref[0:LANES, :] = gram
    count = jnp.full((1, LANES), 1.0, F32) * (total * (SIDE * SIDE)).astype(F32)
    send_ref[LANES : LANES + 8, :] = rows8(summed, count)
    spot = lax.broadcasted_iota(jnp.int32, (LANES, LANES), 1)
    for part in range(cot_ref.shape[1] // LANES):
        frame = (spot + part * LANES) // (HALF_ROWS * 8)
        block = pad_rows(cot_ref[:, part * LANES : (part + 1) * LANES])
        cot_out_ref[part * LANES : (part + 1) * LANES, :] = jnp.where(frame < total, block, 0.0).T


def narrow_stats(base_ref, third_ref):
    count = base_ref[LANES + 1 : LANES + 2, :]
    mean_x = base_ref[LANES : LANES + 1, :] / count
    mean_z = third_ref[2 * LANES : 2 * LANES + 1, :] / count
    cov_x = base_ref[0:LANES, :] / count - outer(mean_x, mean_x)
    cov_z = third_ref[0:LANES, :] / count - outer(mean_z, mean_z)
    cov_xz = third_ref[LANES : 2 * LANES, :] / count - outer(mean_x, mean_z)
    diagonal = lax.broadcasted_iota(jnp.int32, (LANES, LANES), 0) == lax.broadcasted_iota(
        jnp.int32, (LANES, LANES), 1
    )
    variance = jnp.sum(jnp.where(diagonal, cov_z, 0.0), axis=0, keepdims=True)
    return (count, mean_x, mean_z, cov_x, cov_z, cov_xz, diagonal, variance)


def expand_tile(block, live_total, x_ref, w_pair, scale, shift, e_ref, a_ref):
    frames = a_ref.shape[0]

    def frame(t, carry):
        rows = halves(x_ref[pl.ds(pl.multiple_of(t * 256, 256), 256), :])
        values = split_dot(rows, w_pair).reshape(FULL_ROWS, 8, LANES)
        e_ref[pl.ds(pl.multiple_of(t * FULL_ROWS, FULL_ROWS), FULL_ROWS)] = values
        write_first(t, live_total, values, scale, shift, a_ref, block)
        return carry

    lax.fori_loop(0, frames, frame, 0)


def write_first(t, live_total, values, scale, shift, a_ref, planes):
    live = jnp.where(t < live_total, 1.0, 0.0).astype(F32)
    pre = values * scale + shift
    first = (pre * sigmoid(pre) * live).reshape(SIDE, 2, 8, LANES)
    even = first[:, 0]
    odd = first[:, 1]
    a_ref[t, 0, 1 : SIDE + 1] = even
    a_ref[t, 1, 1 : SIDE + 1] = odd
    if planes >= 3:
        a_ref[t, 2, 1 : SIDE + 1] = columns_down(odd)
    if planes >= 4:
        a_ref[t, 3, 1 : SIDE + 1] = columns_up(even)


def clear_edges(ref):
    planes = ref.shape[1]
    edge = jnp.zeros((8, LANES), F32)
    for t in range(ref.shape[0]):
        for plane in range(planes):
            ref[t, plane, 0] = edge
            ref[t, plane, ref.shape[2] - 1] = edge


def spread_taps(taps_ref, w_ref):
    for tap in range(w_ref.shape[0]):
        w_ref[tap] = jnp.broadcast_to(taps_ref[0, tap : tap + 1, :], (8, LANES))


def conv_full(t, k, a_ref, w_ref, d_ref, fresh):
    weights = [w_ref[k * 9 + tap] for tap in range(9)]
    source = t - k
    rows = {}
    for i in range(SIDE):
        for need in (i, i + 1, i + 2):
            if need not in rows:
                rows[need] = [a_ref[source, plane, need] for plane in range(4)]
        even = None
        odd = None
        for r in range(3):
            a_even, a_odd, a_odd_down, a_even_up = rows[i + r]
            left, centre, right = weights[3 * r : 3 * r + 3]
            part_even = centre * a_even + right * a_odd + left * a_odd_down
            part_odd = centre * a_odd + left * a_even + right * a_even_up
            even = part_even if even is None else even + part_even
            odd = part_odd if odd is None else odd + part_odd
        rows.pop(i)
        at = t * FULL_ROWS + 2 * i
        if fresh:
            d_ref[at] = even
            d_ref[at + 1] = odd
        else:
            d_ref[at] = d_ref[at] + even
            d_ref[at + 1] = d_ref[at + 1] + odd


def conv_half(t, k, a_ref, w_ref, d_ref, fresh):
    weights = [w_ref[k * 9 + tap] for tap in range(9)]
    source = t - k
    carried = [a_ref[source, plane, 0] for plane in range(3)]
    for i in range(HALF_ROWS):
        rows = [carried]
        for need in (2 * i + 1, 2 * i + 2):
            rows.append([a_ref[source, plane, need] for plane in range(3)])
        carried = rows[2]
        total = None
        for r in range(3):
            a_even, a_odd, a_odd_down = rows[r]
            left, centre, right = weights[3 * r : 3 * r + 3]
            part = centre * a_even + right * a_odd + left * a_odd_down
            total = part if total is None else total + part
        at = t * HALF_ROWS + i
        d_ref[at] = total if fresh else d_ref[at] + total


def convolve(counts_ref, total, a_ref, w_ref, d_ref, conv, per_frame):
    frames = a_ref.shape[0]

    def frame(t, carry):
        conv(t, 0, a_ref, w_ref, d_ref, True)
        last = jnp.minimum(place_of(counts_ref, t), LAGS - 1)

        def lag(k, inner):
            conv(t, k, a_ref, w_ref, d_ref, False)
            return inner

        return lax.fori_loop(1, last + 1, lag, carry)

    lax.fori_loop(0, total, frame, 0)

    def dead(t, carry):
        d_ref[pl.ds(t * per_frame, per_frame)] = jnp.zeros((per_frame, 8, LANES), F32)
        return carry

    lax.fori_loop(total, frames, dead, 0)


def tile_moments(d_ref, per_frame, frames):
    def frame(t, carry):
        values = d_ref[pl.ds(t * per_frame, per_frame)]
        return (carry[0] + jnp.sum(values, axis=0), carry[1] + jnp.sum(values * values, axis=0))

    zero = jnp.zeros((8, LANES), F32)
    summed, squares = lax.fori_loop(0, frames, frame, (zero, zero))
    return rows8(jnp.sum(summed, axis=0, keepdims=True), jnp.sum(squares, axis=0, keepdims=True))


def wide_stats(mean_row, covariance, w):
    average = row_dot(mean_row, w)
    variance = jnp.sum(w * exact_dot(covariance, w), axis=0, keepdims=True)
    return (average, variance)


def expand_zero_kernel(
    counts_ref, base_ref, x_ref, w_ref, gain_ref, bias_ref, taps_ref,
    e_ref, d_ref, stat_ref, send_ref, cov_ref, a_ref, taps8_ref,
):
    @pl.when(pl.program_id(0) == 0)
    def start():
        count = base_ref[LANES + 1 : LANES + 2, :]
        mean_x = base_ref[LANES : LANES + 1, :] / count
        cov_ref[0:LANES, :] = base_ref[0:LANES, :] / count - outer(mean_x, mean_x)
        cov_ref[LANES : LANES + 8, :] = rows8(mean_x, count)
        clear_edges(a_ref)

    total = live_frames(counts_ref)
    w = pad_rows(w_ref[0])
    average, variance = wide_stats(cov_ref[LANES : LANES + 1, :], cov_ref[0:LANES, :], w)
    stat_ref[...] = rows8(average, variance)
    scale = gain_ref[0:1, :] * lax.rsqrt(variance + EPSILON)
    shift = bias_ref[0:1, :] - average * scale
    expand_tile(4, total, x_ref, halves(w), scale, shift, e_ref, a_ref)
    spread_taps(taps_ref, taps8_ref)
    convolve(counts_ref, total, a_ref, taps8_ref, d_ref, conv_full, FULL_ROWS)
    send_ref[...] = tile_moments(d_ref, FULL_ROWS, a_ref.shape[0])


def expand_one_kernel(
    counts_ref, base_ref, third_ref, x_ref, z_ref, ngain_ref, nbias_ref, w_ref, gain_ref, bias_ref, taps_ref,
    x1_ref, x1t_ref, e_ref, d_ref, stat_ref, send_ref, cov_ref, cross_ref, a_ref, taps8_ref,
):
    total = live_frames(counts_ref)
    frames = a_ref.shape[0]

    @pl.when(pl.program_id(0) == 0)
    def start():
        count, mean_x, mean_z, cov_x, cov_z, cov_xz, diagonal, variance = narrow_stats(base_ref, third_ref)
        root = lax.rsqrt(variance + EPSILON)
        factor = ngain_ref[0:1, :] * root
        shift = nbias_ref[0:1, :] - factor * mean_z
        scaled = cov_xz * factor
        mixed = exact_dot(jnp.where(diagonal, factor, 0.0), cov_z)
        cov_ref[0:LANES, :] = cov_x + scaled + scaled.T + mixed * factor
        cov_ref[LANES : LANES + 8, :] = rows8(mean_x + nbias_ref[0:1, :], count, mean_z, variance)
        cross_ref[...] = (cov_xz + mixed) * root * count

        def frame(t, carry):
            live = jnp.where(t < total, 1.0, 0.0).astype(F32)
            at = pl.ds(pl.multiple_of(t * 256, 256), 256)
            rows = (x_ref[at, :] + factor * z_ref[at, :] + shift) * live
            x1_ref[at, :] = rows
            x1t_ref[:, at] = rows.T
            return carry

        lax.fori_loop(0, frames, frame, 0)
        clear_edges(a_ref)

    w = pad_rows(w_ref[0])
    average, variance = wide_stats(cov_ref[LANES : LANES + 1, :], cov_ref[0:LANES, :], w)
    stat_ref[...] = rows8(average, variance)
    scale = gain_ref[2:3, :] * lax.rsqrt(variance + EPSILON)
    shift = bias_ref[2:3, :] - average * scale
    expand_tile(3, total, x1_ref, halves(w), scale, shift, e_ref, a_ref)
    spread_taps(taps_ref, taps8_ref)
    convolve(counts_ref, total, a_ref, taps8_ref, d_ref, conv_half, HALF_ROWS)
    send_ref[...] = tile_moments(d_ref, HALF_ROWS, frames)


def second_scale(sums_ref, count, gain, bias):
    average = sums_ref[0:1, :] / count
    variance = sums_ref[1:2, :] / count - average * average
    root = lax.rsqrt(variance + EPSILON)
    scale = gain * root
    return (average, root, scale, bias - average * scale)


def squeeze_forward_kernel(
    block, counts_ref, base_ref, sums_ref, d_ref, gain_ref, bias_ref, down_ref, downb_ref, up_ref, upb_ref, proj_ref,
    other_ref, z_ref, gates_ref, running_ref, pre_ref, send_ref, second_ref, pooled_ref,
):
    phase = pl.program_id(0)
    tile = pl.program_id(1)
    tiles = pl.num_programs(1)
    total = live_frames(counts_ref)
    per_frame = FULL_ROWS if block == 0 else HALF_ROWS
    pixels = per_frame * 8
    frames = second_ref.shape[1] // per_frame
    count = base_ref[LANES + 1 : LANES + 2, :] * (1.0 if block == 0 else 0.25)
    norm_row = 2 * block + 1

    @pl.when(phase == 0)
    def activate():
        _, _, scale, shift = second_scale(
            sums_ref, count, gain_ref[norm_row : norm_row + 1, :], bias_ref[norm_row : norm_row + 1, :]
        )

        def frame(t, carry):
            live = jnp.where(t < total, 1.0, 0.0).astype(F32)
            at = pl.ds(t * per_frame, per_frame)
            pre = d_ref[at] * scale + shift
            second = pre * sigmoid(pre) * live
            second_ref[tile, at] = second
            pooled_ref[tile, pl.ds(t, 1), :] = tile_sum(second) * (1.0 / pixels)
            return carry

        lax.fori_loop(0, frames, frame, 0)

    @pl.when((phase == 1) & (tile == 0))
    def gate():
        matrix = running_matrix(counts_ref, frames)
        pre = downb_ref[block : block + 1, :]
        for index in range(pooled_ref.shape[0]):
            lanes = slice(index * LANES, (index + 1) * LANES)
            running = exact_dot(matrix, pooled_ref[index])
            running_ref[:, lanes] = running
            pre = pre + exact_dot(running, down_ref[0, :, lanes], NT)
        pre_ref[...] = pre
        squeezed = pre * sigmoid(pre)
        for index in range(pooled_ref.shape[0]):
            lanes = slice(index * LANES, (index + 1) * LANES)
            gates_ref[:, lanes] = sigmoid(
                exact_dot(squeezed, up_ref[0, :, lanes]) + upb_ref[block : block + 1, lanes]
            )
        z_ref[...] = jnp.zeros_like(z_ref)

    @pl.when(phase == 1)
    def project():
        w_pair = halves(pad_rows(proj_ref[0]))
        lanes = pl.ds(pl.multiple_of(tile * LANES, LANES), LANES)

        def frame(t, carry):
            gate_row = pick_row(gates_ref[:, lanes], t)
            excited = second_ref[tile, pl.ds(t * per_frame, per_frame)].reshape(pixels, LANES) * gate_row
            at = pl.ds(pl.multiple_of(t * pixels, pixels), pixels)
            z_ref[at, :] = z_ref[at, :] + split_dot(halves(excited), w_pair, NT)
            return carry

        lax.fori_loop(0, frames, frame, 0)

    @pl.when((phase == 1) & (tile == tiles - 1))
    def finish():
        if block == 0:
            def frame(t, carry):
                z = z_ref[pl.ds(pl.multiple_of(t * pixels, pixels), pixels), :]
                gram = carry[0] + exact_dot(z.T, z)
                cross = carry[1] + exact_dot(other_ref[:, pl.ds(pl.multiple_of(t * pixels, pixels), pixels)], z)
                return (gram, cross, carry[2] + jnp.sum(z, axis=0, keepdims=True))

            zero = jnp.zeros((LANES, LANES), F32)
            gram, cross, summed = lax.fori_loop(0, frames, frame, (zero, zero, jnp.zeros((1, LANES), F32)))
            send_ref[0:LANES, :] = gram
            send_ref[LANES : 2 * LANES, :] = cross
            send_ref[2 * LANES : 2 * LANES + 8, :] = rows8(summed)
        else:
            z = z_ref[...]
            dy = other_ref[...]
            send_ref[...] = rows8(
                *(jnp.sum(v, axis=0, keepdims=True) for v in (z, z * z, dy, dy * z))
            )


def squeeze_backward_body(
    block, counts_ref, count, sums_ref, d_ref, gain_ref, bias_ref, down_ref, up_ref, proj_ref, gates_ref, running_ref,
    pre_ref, dy2_ref, send_ref, dproj_ref, ddown_ref, ddownb_ref, dup_ref, dupb_ref, dz3_ref, dz3t_ref, dexc_ref,
    dgate_ref, head,
):
    phase = pl.program_id(0)
    tile = pl.program_id(1)
    total = live_frames(counts_ref)
    per_frame = FULL_ROWS if block == 0 else HALF_ROWS
    pixels = per_frame * 8
    frames = dz3_ref.shape[0] // pixels
    norm_row = 2 * block + 1
    tiles = dexc_ref.shape[0]
    lanes = pl.ds(pl.multiple_of(tile * LANES, LANES), LANES)

    @pl.when((phase == 0) & (tile == 0))
    def start():
        head()

    average, root, scale, shift = second_scale(
        sums_ref, count, gain_ref[norm_row : norm_row + 1, :], bias_ref[norm_row : norm_row + 1, :]
    )

    @pl.when(phase == 0)
    def excite():
        w_pair = halves(pad_rows(proj_ref[0]))

        def frame(t, carry):
            live = jnp.where(t < total, 1.0, 0.0).astype(F32)
            at = pl.ds(t * per_frame, per_frame)
            flat = pl.ds(pl.multiple_of(t * pixels, pixels), pixels)
            pre = d_ref[at] * scale + shift
            second = pre * sigmoid(pre) * live
            dexc = split_dot(halves(dz3_ref[flat, :]), w_pair).reshape(per_frame, 8, LANES)
            dexc_ref[tile, at] = dexc
            dgate_ref[tile, pl.ds(t, 1), :] = tile_sum(dexc * second)
            excited = second.reshape(pixels, LANES) * pick_row(gates_ref[:, lanes], t)
            return carry + product(dz3t_ref[t], excited)

        dproj = lax.fori_loop(0, frames, frame, jnp.zeros((LANES, LANES), F32))
        dproj_ref[...] = dproj[0 : dproj_ref.shape[0]]

    @pl.when((phase == 1) & (tile == 0))
    def squeeze():
        pre = pre_ref[...]
        sig = sigmoid(pre)
        squeezed = pre * sig
        dsqueezed = jnp.zeros_like(pre)
        for index in range(tiles):
            at = slice(index * LANES, (index + 1) * LANES)
            gates = gates_ref[:, at]
            du = dgate_ref[index] * gates * (1.0 - gates)
            dupb_ref[:, at] = rows8(jnp.sum(du, axis=0, keepdims=True))
            dup_ref[:, at] = exact_dot(squeezed, du, TN)
            dsqueezed = dsqueezed + exact_dot(du, up_ref[0, :, at], NT)
        dpre = dsqueezed * silu_slope(pre, sig)
        ddownb_ref[...] = rows8(jnp.sum(dpre, axis=0, keepdims=True))
        matrix = running_matrix(counts_ref, frames)
        for index in range(tiles):
            at = slice(index * LANES, (index + 1) * LANES)
            ddown_ref[:, at] = exact_dot(dpre, running_ref[:, at], TN)
            drunning = exact_dot(dpre, down_ref[0, :, at])
            dgate_ref[index] = exact_dot(matrix, drunning, TN) * (1.0 / pixels)

    @pl.when(phase == 1)
    def slope():
        def frame(t, carry):
            live = jnp.where(t < total, 1.0, 0.0).astype(F32)
            at = pl.ds(t * per_frame, per_frame)
            depth = d_ref[at]
            pre = depth * scale + shift
            sig = sigmoid(pre)
            dsecond = dexc_ref[tile, at] * pick_row(gates_ref[:, lanes], t) + pick_row(dgate_ref[tile], t)
            dy = dsecond * silu_slope(pre, sig) * live
            dy2_ref[at] = dy
            normed = (depth - average) * root
            return (carry[0] + jnp.sum(dy, axis=0), carry[1] + jnp.sum(dy * normed, axis=0))

        zero = jnp.zeros((8, LANES), F32)
        summed, cross = lax.fori_loop(0, frames, frame, (zero, zero))
        send_ref[...] = rows8(jnp.sum(summed, axis=0, keepdims=True), jnp.sum(cross, axis=0, keepdims=True))


def squeeze_one_backward_kernel(
    counts_ref, base_ref, sums_ref, third_ref, z_ref, cot_ref, ngain_ref, nbias_ref, d_ref, gain_ref, bias_ref, down_ref,
    up_ref, proj_ref, gates_ref, running_ref, pre_ref, act_ref, dy2_ref, send_ref, dproj_ref, ddown_ref, ddownb_ref,
    dup_ref, dupb_ref, dz3_ref, dz3t_ref, dexc_ref, dgate_ref,
):
    count = base_ref[LANES + 1 : LANES + 2, :] * 0.25
    total = live_frames(counts_ref)
    frames = dz3t_ref.shape[0]
    pixels = HALF_ROWS * 8

    def head():
        mean = third_ref[0:1, :] / count
        variance = third_ref[1:2, :] / count - mean * mean
        root = lax.rsqrt(variance + EPSILON)
        gain = ngain_ref[1:2, :]
        bias_sum = third_ref[2:3, :]
        gain_sum = root * (third_ref[3:4, :] - mean * bias_sum)
        row = lax.broadcasted_iota(jnp.int32, z_ref.shape, 0) // pixels
        live = row < total
        normed = (z_ref[...] - mean) * root
        act = jnp.where(live, gain * normed + nbias_ref[1:2, :], 0.0)
        act_ref[...] = act.T[0 : act_ref.shape[0]]
        dz3 = gain * root * (cot_ref[...] - bias_sum / count - normed * (gain_sum / count))
        dz3 = jnp.where(live, dz3, 0.0)
        dz3_ref[...] = dz3
        dz3t = dz3.T
        for t in range(frames):
            dz3t_ref[t] = dz3t[:, t * pixels : (t + 1) * pixels]

    squeeze_backward_body(
        1, counts_ref, count, sums_ref, d_ref, gain_ref, bias_ref, down_ref, up_ref, proj_ref, gates_ref, running_ref,
        pre_ref, dy2_ref, send_ref, dproj_ref, ddown_ref, ddownb_ref, dup_ref, dupb_ref, dz3_ref, dz3t_ref, dexc_ref,
        dgate_ref, head,
    )


def input_factors(sums_ref, stat_ref, count, gain, w_ref):
    width = sums_ref.shape[1]
    matrix = jnp.zeros((LANES, LANES), F32)
    shift = jnp.zeros((1, LANES), F32)
    for index in range(w_ref.shape[2] // LANES):
        at = slice(index * LANES, (index + 1) * LANES)
        w = pad_rows(w_ref[0, :, at])
        root = lax.rsqrt(stat_ref[1:2, at] + EPSILON)
        factor = gain[:, at] * root
        matrix = matrix + exact_dot(w * (factor * root * sums_ref[1:2, at] / count), w, NT)
        shift = shift + row_dot(factor * sums_ref[0:1, at] / count, w, NT)
    return (matrix, shift)


def squeeze_zero_backward_kernel(
    counts_ref, base_ref, sums_ref, one_ref, stat_ref, cov_ref, cross_ref, dxpre_ref, x1_ref, z_ref, ngain_ref, w_ref,
    gains_ref, d_ref, gain_ref, bias_ref, down_ref, up_ref, proj_ref, gates_ref, running_ref, pre_ref,
    dx1_ref, nsum_ref, dy2_ref, send_ref, dproj_ref, ddown_ref, ddownb_ref, dup_ref, dupb_ref,
    dz3_ref, dz3t_ref, dexc_ref, dgate_ref,
):
    count = base_ref[LANES + 1 : LANES + 2, :]
    total = live_frames(counts_ref)
    frames = dz3t_ref.shape[0]
    width = gains_ref.shape[1]

    def head():
        matrix, shift = input_factors(one_ref, stat_ref, count, gains_ref[2:3, :], w_ref)
        mean = cov_ref[LANES + 2 : LANES + 3, :]
        root = lax.rsqrt(cov_ref[LANES + 3 : LANES + 4, :] + EPSILON)
        mean_x1 = cov_ref[LANES : LANES + 1, :]
        gain_sum = one_ref[2:3, 0:LANES] - jnp.sum(matrix * cross_ref[...], axis=0, keepdims=True)
        bias_sum = one_ref[3:4, 0:LANES] - count * shift
        nsum_ref[...] = rows8(gain_sum, bias_sum)
        factor = ngain_ref[0:1, :] * root
        pair = halves(matrix)

        def frame(t, carry):
            live = jnp.where(t < total, 1.0, 0.0).astype(F32)
            at = pl.ds(pl.multiple_of(t * 256, 256), 256)
            centred = x1_ref[at, :] - mean_x1
            dx1 = (dxpre_ref[at, :] - split_dot(halves(centred), pair) - shift) * live
            dx1_ref[at, :] = dx1
            normed = (z_ref[at, :] - mean) * root
            dz3 = factor * (dx1 - bias_sum / count - normed * (gain_sum / count)) * live
            dz3_ref[at, :] = dz3
            dz3t_ref[t] = dz3.T
            return carry

        lax.fori_loop(0, frames, frame, 0)

    squeeze_backward_body(
        0, counts_ref, count, sums_ref, d_ref, gain_ref, bias_ref, down_ref, up_ref, proj_ref, gates_ref, running_ref,
        pre_ref, dy2_ref, send_ref, dproj_ref, ddown_ref, ddownb_ref, dup_ref, dupb_ref, dz3_ref, dz3t_ref, dexc_ref,
        dgate_ref, head,
    )


def back_full(t, k, a_ref, w_ref, z_ref, f_ref, dw_ref, fresh):
    weights = [w_ref[k * 9 + tap] for tap in range(9)]
    target = t - k
    sums = [None] * 9
    a_rows = {}
    z_rows = {}
    for i in range(SIDE):
        for need in (i, i + 1, i + 2):
            if need not in a_rows:
                a_rows[need] = [a_ref[target, plane, need] for plane in range(2)]
                z_rows[need] = [z_ref[t, plane, need] for plane in range(4)]
        even = None
        odd = None
        z_even, z_odd, z_odd_down, z_even_up = z_rows[i + 1]
        for r in range(3):
            b_even, b_odd, b_odd_down, b_even_up = z_rows[i + 2 - r]
            left, centre, right = weights[3 * r : 3 * r + 3]
            part_even = centre * b_even + right * b_odd_down + left * b_odd
            part_odd = centre * b_odd + right * b_even + left * b_even_up
            even = part_even if even is None else even + part_even
            odd = part_odd if odd is None else odd + part_odd
            a_even, a_odd = a_rows[i + r]
            pieces = (
                z_even_up * a_odd + z_odd * a_even,
                z_even * a_even + z_odd * a_odd,
                z_even * a_odd + z_odd_down * a_even,
            )
            for c in range(3):
                at = 3 * r + c
                sums[at] = pieces[c] if sums[at] is None else sums[at] + pieces[c]
        a_rows.pop(i)
        z_rows.pop(i)
        at = target * FULL_ROWS + 2 * i
        if fresh:
            f_ref[at] = even
            f_ref[at + 1] = odd
        else:
            f_ref[at] = f_ref[at] + even
            f_ref[at + 1] = f_ref[at + 1] + odd
    for tap in range(9):
        dw_ref[k * 9 + tap] = dw_ref[k * 9 + tap] + sums[tap]


def back_half(t, k, a_ref, w_ref, z_ref, f_ref, dw_ref, fresh):
    weights = [w_ref[k * 9 + tap] for tap in range(9)]
    target = t - k
    sums = [None] * 9

    def put(row, parity, value):
        at = target * FULL_ROWS + 2 * row + parity
        f_ref[at] = value if fresh else f_ref[at] + value

    carried = [a_ref[target, plane, 0] for plane in range(2)]
    here = [z_ref[t, plane, 0] for plane in range(2)]
    for i in range(HALF_ROWS):
        below = [z_ref[t, plane, i + 1] for plane in range(2)]
        dz, dz_up = here
        rows = [carried]
        for need in (2 * i + 1, 2 * i + 2):
            rows.append([a_ref[target, plane, need] for plane in range(2)])
        carried = rows[2]
        put(2 * i, 0, weights[4] * dz)
        put(2 * i, 1, weights[5] * dz + weights[3] * dz_up)
        put(2 * i + 1, 0, weights[7] * dz + weights[1] * below[0])
        put(
            2 * i + 1,
            1,
            weights[8] * dz + weights[6] * dz_up + (weights[2] * below[0] + weights[0] * below[1]),
        )
        for r in range(3):
            a_even, a_odd = rows[r]
            pieces = (dz_up * a_odd, dz * a_even, dz * a_odd)
            for c in range(3):
                at = 3 * r + c
                sums[at] = pieces[c] if sums[at] is None else sums[at] + pieces[c]
        here = below
    for tap in range(9):
        dw_ref[k * 9 + tap] = dw_ref[k * 9 + tap] + sums[tap]


def depth_backward_kernel(
    block, counts_ref, base_ref, sums_ref, grads_ref, stat_ref, cov_ref, dy2_ref, d_ref, e_ref, x_ref, xt_ref, w_ref, gain_ref,
    bias_ref, taps_ref, z3_ref, dxpre_ref, send_ref, q_ref, dtaps_ref, extra_ref, a_ref, z_ref, f_ref, taps8_ref, dw_ref,
):
    tile = pl.program_id(0)
    tiles = pl.num_programs(0)
    total = live_frames(counts_ref)
    frames = a_ref.shape[0]
    norm_row = 2 * block
    full = base_ref[LANES + 1 : LANES + 2, :]
    half = block == 1
    count = full * 0.25 if half else full
    per_frame = HALF_ROWS if half else FULL_ROWS

    @pl.when(tile == 0)
    def start():
        clear_edges(a_ref)
        clear_edges(z_ref)
        dxpre_ref[...] = jnp.zeros_like(dxpre_ref)

    average, root, scale_two, _ = second_scale(
        sums_ref, count, gain_ref[norm_row + 1 : norm_row + 2, :], bias_ref[norm_row + 1 : norm_row + 2, :]
    )
    bias_part = grads_ref[0:1, :] / count
    gain_part = grads_ref[1:2, :] / count
    average_one = stat_ref[0:1, :]
    root_one = lax.rsqrt(stat_ref[1:2, :] + EPSILON)
    gain_one = gain_ref[norm_row : norm_row + 1, :]
    scale_one = gain_one * root_one
    shift_one = bias_ref[norm_row : norm_row + 1, :] - average_one * scale_one

    def fill(t, carry):
        at = pl.ds(t * per_frame, per_frame)
        normed = (d_ref[at] - average) * root
        dz = scale_two * (dy2_ref[at] - bias_part - normed * gain_part)
        if half:
            z_ref[t, 0, 0:HALF_ROWS] = dz
            z_ref[t, 1, 0:HALF_ROWS] = columns_up(dz)
        else:
            pair = dz.reshape(SIDE, 2, 8, LANES)
            z_ref[t, 0, 1 : SIDE + 1] = pair[:, 0]
            z_ref[t, 1, 1 : SIDE + 1] = pair[:, 1]
            z_ref[t, 2, 1 : SIDE + 1] = columns_down(pair[:, 1])
            z_ref[t, 3, 1 : SIDE + 1] = columns_up(pair[:, 0])
        values = e_ref[pl.ds(pl.multiple_of(t * FULL_ROWS, FULL_ROWS), FULL_ROWS)]
        write_first(t, total, values, scale_one, shift_one, a_ref, 2)
        return carry

    lax.fori_loop(0, total, fill, 0)
    spread_taps(taps_ref, taps8_ref)
    dw_ref[...] = jnp.zeros_like(dw_ref)
    back = back_half if half else back_full

    def frame(t, carry):
        back(t, 0, a_ref, taps8_ref, z_ref, f_ref, dw_ref, True)
        last = jnp.minimum(place_of(counts_ref, t), LAGS - 1)

        def lag(k, inner):
            back(t, k, a_ref, taps8_ref, z_ref, f_ref, dw_ref, False)
            return inner

        return lax.fori_loop(1, last + 1, lag, carry)

    lax.fori_loop(0, total, frame, 0)
    dtaps_ref[...] = jnp.sum(dw_ref[...], axis=1)
    w_pair = halves(pad_rows(w_ref[0]))

    def finish(t, carry):
        rows = pl.ds(pl.multiple_of(t * FULL_ROWS, FULL_ROWS), FULL_ROWS)
        flat = pl.ds(pl.multiple_of(t * 256, 256), 256)
        values = e_ref[rows]
        pre = values * scale_one + shift_one
        dy = f_ref[rows] * silu_slope(pre, sigmoid(pre))
        normed = (values - average_one) * root_one
        summed = carry[0] + jnp.sum(dy, axis=0)
        cross = carry[1] + jnp.sum(dy * normed, axis=0)
        dy = dy.reshape(256, LANES)
        gathered = carry[2] + product(xt_ref[:, flat], dy)
        dxpre_ref[flat, :] = dxpre_ref[flat, :] + split_dot(halves(dy * scale_one), w_pair, NT)
        return (summed, cross, gathered)

    zero = jnp.zeros((8, LANES), F32)
    summed, cross, gathered = lax.fori_loop(0, total, finish, (zero, zero, jnp.zeros((LANES, LANES), F32)))
    send_ref[...] = rows8(jnp.sum(summed, axis=0, keepdims=True), jnp.sum(cross, axis=0, keepdims=True))
    q_ref[...] = gathered

    if half:
        @pl.when(tile == tiles - 1)
        def tail():
            mean = cov_ref[LANES + 2 : LANES + 3, :]
            root_three = lax.rsqrt(cov_ref[LANES + 3 : LANES + 4, :] + EPSILON)

            def part(t, carry):
                flat = pl.ds(pl.multiple_of(t * 256, 256), 256)
                dx = dxpre_ref[flat, :]
                normed = (z3_ref[flat, :] - mean) * root_three
                return (
                    carry[0] + jnp.sum(dx * normed, axis=0, keepdims=True),
                    carry[1] + jnp.sum(dx, axis=0, keepdims=True),
                )

            none = jnp.zeros((1, LANES), F32)
            cross_three, summed_three = lax.fori_loop(0, total, part, (none, none))
            extra_ref[...] = rows8(jnp.zeros((1, LANES), F32), jnp.zeros((1, LANES), F32), cross_three, summed_three)


def finish_kernel(
    counts_ref, momentum_ref, base_ref, cov0_ref, cov1_ref, stat0_ref, stat1_ref, sums0_ref, sums1_ref, third_ref, grad0_ref,
    grad1_ref, one_ref, zero_ref, nsum_ref, q_ref, dxpre_ref, x_ref, dx1_ref, w_ref, gain_ref, means_ref, vars_ref,
    nmeans_ref, nvars_ref,
    video_ref, dw_ref, wgain_ref, wbias_ref, ngain_ref, nbias_ref, newm_ref, newv_ref, newnm_ref, newnv_ref,
):
    total = live_frames(counts_ref)
    full = base_ref[LANES + 1 : LANES + 2, :]
    half = full * 0.25
    gain = gain_ref[0:1, :]
    matrix, shift = input_factors(zero_ref, stat0_ref, full, gain, w_ref)
    pair = halves(matrix)
    mean_x = cov0_ref[LANES : LANES + 1, :]
    order = column_order()
    narrow = video_ref.shape[0]
    for part in range(x_ref.shape[0] // LANES):
        at = slice(part * LANES, (part + 1) * LANES)
        live = jnp.where(part // 2 < total, 1.0, 0.0).astype(F32)
        centred = x_ref[at, :] - mean_x
        dx = (dxpre_ref[at, :] - split_dot(halves(centred), pair) - shift) * live + dx1_ref[at, :]
        video_ref[:, at] = picked(order, dx.T, NN, False)[0:narrow]
    momentum = momentum_ref[0].astype(F32) / 10.0
    for block, (cov_ref, stat_ref, top_ref) in enumerate(((cov0_ref, stat0_ref, zero_ref), (cov1_ref, stat1_ref, one_ref))):
        mean_row = cov_ref[LANES : LANES + 1, :]
        for index in range(w_ref.shape[2] // LANES):
            at = slice(index * LANES, (index + 1) * LANES)
            w = pad_rows(w_ref[block, :, at])
            root = lax.rsqrt(stat_ref[1:2, at] + EPSILON)
            factor = gain_ref[2 * block : 2 * block + 1, at] * root
            value = q_ref[block, :, at] - outer(mean_row, top_ref[0:1, at])
            value = value - exact_dot(cov_ref[0:LANES, :], w) * (root * top_ref[1:2, at])
            dw_ref[block, :, at] = (value * factor)[0:narrow]
    wide_count = jnp.broadcast_to(full[:, 0:1], (1, gain_ref.shape[1]))
    half_count = wide_count * 0.25
    wide = ((stat0_ref, None, wide_count), (sums0_ref, 1, wide_count), (stat1_ref, None, wide_count), (sums1_ref, 1, half_count))
    wgain_ref[...] = rows8(zero_ref[1:2, :], grad0_ref[1:2, :], one_ref[1:2, 0 : gain_ref.shape[1]], grad1_ref[1:2, :])[0:4]
    wbias_ref[...] = rows8(zero_ref[0:1, :], grad0_ref[0:1, :], one_ref[0:1, 0 : gain_ref.shape[1]], grad1_ref[0:1, :])[0:4]
    means = []
    variances = []
    for ref, raw, count in wide:
        mean = ref[0:1, :]
        variance = ref[1:2, :]
        if raw is not None:
            mean = mean / count
            variance = variance / count - mean * mean
        means.append(mean)
        variances.append(variance * count / (count - 1.0))
    newm_ref[...] = (1.0 - momentum) * means_ref[...] + momentum * rows8(*means)[0:4]
    newv_ref[...] = (1.0 - momentum) * vars_ref[...] + momentum * rows8(*variances)[0:4]
    mean_zero = cov1_ref[LANES + 2 : LANES + 3, :]
    var_zero = cov1_ref[LANES + 3 : LANES + 4, :]
    mean_one = third_ref[0:1, :] / half
    var_one = third_ref[1:2, :] / half - mean_one * mean_one
    gain_one = lax.rsqrt(var_one + EPSILON) * (third_ref[3:4, :] - mean_one * third_ref[2:3, :])
    ngain_ref[...] = rows8(nsum_ref[0:1, :], gain_one)[0:2, 0:narrow]
    nbias_ref[...] = rows8(nsum_ref[1:2, :], third_ref[2:3, :])[0:2, 0:narrow]
    means = rows8(mean_zero, mean_one)[0:2, 0:narrow]
    variances = rows8(var_zero * full / (full - 1.0), var_one * half / (half - 1.0))[0:2, 0:narrow]
    newnm_ref[...] = (1.0 - momentum) * nmeans_ref[...] + momentum * means
    newnv_ref[...] = (1.0 - momentum) * nvars_ref[...] + momentum * variances


def exchange(row):
    total = lax.axis_size("dp") * lax.axis_size("rep")
    flip = 1
    while flip < total:
        row = row + lax.ppermute(row, ("dp", "rep"), [(i, i ^ flip) for i in range(total)])
        flip = flip * 2
    return row


def shape(*dims):
    return jax.ShapeDtypeStruct(dims, F32)


def whole(array):
    rank = len(array.shape)
    return pl.BlockSpec(array.shape, lambda *ids: (0,) * rank)


SCALARS = pl.BlockSpec(memory_space=pltpu.SMEM)


def call(kernel, grid, in_specs, out_specs, out_shape, scratch, args):
    return pl.pallas_call(
        kernel,
        grid=grid,
        in_specs=in_specs,
        out_specs=out_specs,
        out_shape=out_shape,
        scratch_shapes=scratch,
        compiler_params=pltpu.CompilerParams(vmem_limit_bytes=VMEM_BYTES),
    )(*args)


def local(
    video, frame_counts, momentum_index, expand_weight, wide_gains, wide_biases, narrow_gains, narrow_biases, depth_weight,
    squeeze_weight, squeeze_bias, excite_weight, excite_bias, project_weight, wide_means, wide_variances, narrow_means,
    narrow_variances, cotangent,
):
    cin, pixels = video.shape
    half_pixels = cotangent.shape[1]
    width = expand_weight.shape[1]
    squeeze = squeeze_weight.shape[1]
    frames = pixels // (SIDE * SIDE)
    tiles = width // LANES
    taps = depth_weight.shape[1]
    w_t = jnp.swapaxes(expand_weight, 1, 2)
    up_t = jnp.swapaxes(excite_weight, 1, 2)
    lanes_pad = ((0, 0), (0, LANES - cin))
    ngains = jnp.pad(narrow_gains, lanes_pad)
    nbiases = jnp.pad(narrow_biases, lanes_pad)
    full_rows = frames * FULL_ROWS
    half_rows = frames * HALF_ROWS

    def tile_rows(rows):
        return pl.BlockSpec((rows, LANES), lambda j: (0, j))

    def tile_cube(rows):
        return pl.BlockSpec((rows, 8, LANES), lambda j: (0, 0, j))

    def weight_tile(block, rows):
        return pl.BlockSpec((1, rows, LANES), lambda j, block=block: (block, 0, j))

    x, x_t, cot, base = call(
        prepare_kernel, (1,),
        [SCALARS, whole(video), whole(cotangent)],
        [pl.BlockSpec((pixels, LANES), lambda j: (0, 0)), pl.BlockSpec((LANES, pixels), lambda j: (0, 0)),
         pl.BlockSpec((half_pixels, LANES), lambda j: (0, 0)), pl.BlockSpec((LANES + 8, LANES), lambda j: (0, 0))],
        [shape(pixels, LANES), shape(LANES, pixels), shape(half_pixels, LANES), shape(LANES + 8, LANES)],
        [], (frame_counts, video, cotangent),
    )
    base = exchange(base)
    planes = [pltpu.VMEM((frames, 4, SIDE + 2, 8, LANES), F32), pltpu.VMEM((taps, 8, LANES), F32)]
    e_zero, d_zero, stat_zero, sums_zero, cov_zero = call(
        expand_zero_kernel, (tiles,),
        [SCALARS, whole(base), whole(x), weight_tile(0, cin), tile_rows(4), tile_rows(4), weight_tile(0, taps)],
        [tile_cube(full_rows), tile_cube(full_rows), tile_rows(8), tile_rows(8),
         pl.BlockSpec((LANES + 8, LANES), lambda j: (0, 0))],
        [shape(full_rows, 8, width), shape(full_rows, 8, width), shape(8, width), shape(8, width), shape(LANES + 8, LANES)],
        planes, (frame_counts, base, x, w_t, wide_gains, wide_biases, depth_weight),
    )
    sums_zero = exchange(sums_zero)

    def phase_rows(rows, both=True):
        if both:
            return pl.BlockSpec((rows, LANES), lambda p, j: (0, j))
        return pl.BlockSpec((rows, LANES), lambda p, j: (0, j * (1 - p) + (tiles - 1) * p))

    def late_rows(rows):
        return pl.BlockSpec((rows, LANES), lambda p, j: (0, j * p))

    def phase_cube(rows):
        return pl.BlockSpec((rows, 8, LANES), lambda p, j: (0, 0, j * (1 - p) + (tiles - 1) * p))

    def both_cube(rows):
        return pl.BlockSpec((rows, 8, LANES), lambda p, j: (0, 0, j))

    def late_cube(rows):
        return pl.BlockSpec((rows, 8, LANES), lambda p, j: (0, 0, j * p))

    def fixed(*dims):
        return pl.BlockSpec(dims, lambda *ids: (0,) * len(dims))

    def of_block(block, rows, lanes):
        return pl.BlockSpec((1, rows, lanes), lambda *ids: (block, 0, 0))

    def squeeze_forward(block, base, sums, depth, other):
        rows = full_rows if block == 0 else half_rows
        send = (2 * LANES + 8, LANES) if block == 0 else (8, LANES)
        return call(
            functools.partial(squeeze_forward_kernel, block), (2, tiles),
            [SCALARS, whole(base), phase_rows(8, False), phase_cube(rows), phase_rows(4, False), phase_rows(4, False),
             of_block(block, squeeze, width), whole(squeeze_bias), of_block(block, squeeze, width), whole(excite_bias),
             pl.BlockSpec((1, cin, LANES), lambda p, j: (block, 0, j * p)), whole(other)],
            [fixed(rows * 8, LANES), fixed(8, width), fixed(8, width), fixed(8, squeeze), fixed(*send)],
            [shape(rows * 8, LANES), shape(8, width), shape(8, width), shape(8, squeeze), shape(*send)],
            [pltpu.VMEM((tiles, rows, 8, LANES), F32), pltpu.VMEM((tiles, frames, LANES), F32)],
            (frame_counts, base, sums, depth, wide_gains, wide_biases, squeeze_weight, squeeze_bias, up_t, excite_bias,
             project_weight, other),
        )

    z_zero, gates_zero, running_zero, pre_zero, third_zero = squeeze_forward(0, base, sums_zero, d_zero, x_t)
    third_zero = exchange(third_zero)

    x1, x1_t, e_one, d_one, stat_one, sums_one, cov_one, cross = call(
        expand_one_kernel, (tiles,),
        [SCALARS, whole(base), whole(third_zero), whole(x), whole(z_zero), whole(ngains), whole(nbiases),
         weight_tile(1, cin), tile_rows(4), tile_rows(4), weight_tile(1, taps)],
        [fixed(pixels, LANES), fixed(LANES, pixels), tile_cube(full_rows), tile_cube(half_rows), tile_rows(8), tile_rows(8),
         fixed(LANES + 8, LANES), fixed(LANES, LANES)],
        [shape(pixels, LANES), shape(LANES, pixels), shape(full_rows, 8, width), shape(half_rows, 8, width), shape(8, width),
         shape(8, width), shape(LANES + 8, LANES), shape(LANES, LANES)],
        planes,
        (frame_counts, base, third_zero, x, z_zero, ngains, nbiases, w_t, wide_gains, wide_biases, depth_weight),
    )
    sums_one = exchange(sums_one)
    z_one, gates_one, running_one, pre_one, third_one = squeeze_forward(1, base, sums_one, d_one, cot)
    third_one = exchange(third_one)

    def backward_specs(block):
        rows = full_rows if block == 0 else half_rows
        ins = [both_cube(rows), phase_rows(4), phase_rows(4), of_block(block, squeeze, width), of_block(block, squeeze, width),
               pl.BlockSpec((1, cin, LANES), lambda p, j: (block, 0, j * (1 - p) + (tiles - 1) * p)),
               fixed(8, width), fixed(8, width), fixed(8, squeeze)]
        outs = [late_cube(rows), late_rows(8), phase_rows(cin, False), fixed(squeeze, width), fixed(8, squeeze),
                fixed(squeeze, width), fixed(8, width)]
        shapes = [shape(rows, 8, width), shape(8, width), shape(cin, width), shape(squeeze, width), shape(8, squeeze),
                  shape(squeeze, width), shape(8, width)]
        per_frame = rows * 8 // frames
        scratch = [pltpu.VMEM((rows * 8, LANES), F32), pltpu.VMEM((frames, LANES, per_frame), F32),
                   pltpu.VMEM((tiles, rows, 8, LANES), F32), pltpu.VMEM((tiles, frames, LANES), F32)]
        return (ins, outs, shapes, scratch)

    ins, outs, shapes, scratch = backward_specs(1)
    activations, dy2_one, grad_one, dproj_one, ddown_one, ddownb_one, dup_one, dupb_one = call(
        squeeze_one_backward_kernel, (2, tiles),
        [SCALARS, whole(base), phase_rows(8), whole(third_one), whole(z_one), whole(cot), whole(ngains), whole(nbiases)] + ins,
        [fixed(cin, half_pixels)] + outs, [shape(cin, half_pixels)] + shapes, scratch,
        (frame_counts, base, sums_one, third_one, z_one, cot, ngains, nbiases, d_one, wide_gains, wide_biases, squeeze_weight,
         up_t, project_weight, gates_one, running_one, pre_one),
    )
    grad_one = exchange(grad_one)

    def depth_backward(block, sums, grads, stat, cov, dy2, depth, expanded, inputs, inputs_t, z3):
        rows = full_rows if block == 0 else half_rows
        z_shape = (frames, 4, SIDE + 2, 8, LANES) if block == 0 else (frames, 2, HALF_ROWS + 1, 8, LANES)
        return call(
            functools.partial(depth_backward_kernel, block), (tiles,),
            [SCALARS, whole(base), tile_rows(8), tile_rows(8), tile_rows(8), whole(cov), tile_cube(rows), tile_cube(rows),
             tile_cube(full_rows), whole(inputs), whole(inputs_t), weight_tile(block, cin), tile_rows(4), tile_rows(4),
             weight_tile(block, taps), whole(z3)],
            [fixed(pixels, LANES), tile_rows(8), tile_rows(LANES), tile_rows(taps), fixed(8, LANES)],
            [shape(pixels, LANES), shape(8, width), shape(LANES, width), shape(taps, width), shape(8, LANES)],
            [pltpu.VMEM((frames, 2, SIDE + 2, 8, LANES), F32), pltpu.VMEM(z_shape, F32), pltpu.VMEM((full_rows, 8, LANES), F32),
             pltpu.VMEM((taps, 8, LANES), F32), pltpu.VMEM((taps, 8, LANES), F32)],
            (frame_counts, base, sums, grads, stat, cov, dy2, depth, expanded, inputs, inputs_t, w_t, wide_gains, wide_biases,
             depth_weight, z3),
        )

    dxpre_one, top_one, q_one, dtaps_one, extra = depth_backward(
        1, sums_one, grad_one, stat_one, cov_one, dy2_one, d_one, e_one, x1, x1_t, z_zero
    )
    top_one = exchange(jnp.concatenate([top_one + jnp.pad(extra, ((0, 0), (0, width - LANES)))], axis=1))
    ins, outs, shapes, scratch = backward_specs(0)
    dx1, nsum, dy2_zero, grad_zero, dproj_zero, ddown_zero, ddownb_zero, dup_zero, dupb_zero = call(
        squeeze_zero_backward_kernel, (2, tiles),
        [SCALARS, whole(base), phase_rows(8), whole(top_one), whole(stat_one), whole(cov_one), whole(cross), whole(dxpre_one),
         whole(x1), whole(z_zero), whole(ngains), of_block(1, cin, width), whole(wide_gains)] + ins,
        [fixed(pixels, LANES), fixed(8, LANES)] + outs, [shape(pixels, LANES), shape(8, LANES)] + shapes, scratch,
        (frame_counts, base, sums_zero, top_one, stat_one, cov_one, cross, dxpre_one, x1, z_zero, ngains, w_t, wide_gains,
         d_zero, wide_gains, wide_biases, squeeze_weight, up_t, project_weight, gates_zero, running_zero, pre_zero),
    )
    grad_zero = exchange(grad_zero)
    early = lax.psum(
        (jnp.stack([dproj_zero, dproj_one]), jnp.stack([ddown_zero, ddown_one]), jnp.stack([dup_zero, dup_one]),
         jnp.stack([ddownb_zero[0], ddownb_one[0]]), jnp.stack([dupb_zero[0], dupb_one[0]]), q_one, dtaps_one),
        ("dp", "rep"),
    )
    dproj, ddown, dup, ddownb, dupb, q_one, dtaps_one = early
    dxpre_zero, top_zero, q_zero, dtaps_zero, _ = depth_backward(
        0, sums_zero, grad_zero, stat_zero, cov_zero, dy2_zero, d_zero, e_zero, x, x_t, z_zero
    )
    late = exchange(jnp.concatenate([top_zero, q_zero, dtaps_zero], axis=0))
    top_zero = late[0:8]
    q_zero = late[8 : 8 + LANES]
    dtaps_zero = late[8 + LANES :]
    final_args = (
        frame_counts, momentum_index, base, cov_zero, cov_one, stat_zero, stat_one, sums_zero, sums_one, third_one, grad_zero,
        grad_one, top_one, top_zero, nsum, jnp.stack([q_zero, q_one]), dxpre_zero, x, dx1, w_t, wide_gains, wide_means,
        wide_variances, narrow_means, narrow_variances,
    )
    final_shapes = [
        shape(cin, pixels), shape(2, cin, width), shape(4, width), shape(4, width), shape(2, cin), shape(2, cin),
        shape(4, width), shape(4, width), shape(2, cin), shape(2, cin),
    ]
    video_grad, dw_t, wgain, wbias, ngain, nbias, newm, newv, newnm, newnv = call(
        finish_kernel, (1,), [SCALARS, SCALARS] + [whole(array) for array in final_args[2:]],
        [whole(item) for item in final_shapes], final_shapes, [], final_args,
    )
    return (
        activations, video_grad, jnp.swapaxes(dw_t, 1, 2), wgain, wbias, ngain, nbias, jnp.stack([dtaps_zero, dtaps_one]),
        ddown, ddownb, jnp.swapaxes(dup, 1, 2), dupb, dproj, newm, newv, newnm, newnv,
    )


def solution(mesh):
    split = P(None, ("dp", "rep"))
    placed = (split, P(("dp", "rep"))) + (P(),) * 16 + (split,)
    return jax.shard_map(
        local, mesh=mesh, in_specs=placed, out_specs=(split, split) + (P(),) * 15, check_vma=False
    )
```

```python
import functools

import jax
import jax.numpy as jnp
from jax import lax
from jax.experimental import pallas as pl
from jax.experimental.pallas import tpu as pltpu
from jax.sharding import PartitionSpec as P

SIDE = 16
LANES = 128
LAGS = 5
FULL_ROWS = 2 * SIDE
HALF_ROWS = SIDE // 2
EPSILON = 1e-05
HIGHEST = lax.Precision.HIGHEST
F32 = jnp.float32
NN = (((1,), (0,)), ((), ()))
NT = (((1,), (1,)), ((), ()))
TN = (((0,), (0,)), ((), ()))
VMEM_BYTES = 52 * 1024 * 1024


def half_tanh(half_values):
    return jnp.tanh(half_values)


def sigmoid(values):
    return 0.5 * jnp.tanh(0.5 * values) + 0.5


def silu_slope(half_values, tanh):
    return 0.5 * (1.0 + tanh + half_values * (1.0 - tanh * tanh))


def exact_dot(left, right, dims=NN):
    return lax.dot_general(left, right, dims, precision=HIGHEST, preferred_element_type=F32)


def halves(values):
    high = values.astype(jnp.bfloat16)
    return (high, (values - high.astype(F32)).astype(jnp.bfloat16))


def side_by_side(values):
    return jnp.concatenate(halves(values), axis=1)


def right_square(w):
    both = side_by_side(w)
    return jnp.concatenate([both, both], axis=0)


def right_square_t(w):
    high, low = halves(w)
    return jnp.concatenate(
        [jnp.concatenate([high, high], axis=1), jnp.concatenate([low, low], axis=1)], axis=0
    )


def plain_dot(left, right, dims=NN):
    return lax.dot_general(left, right, dims, preferred_element_type=F32)


def fold_right(values):
    lanes = values.shape[1] // 2
    return values[:, :lanes] + values[:, lanes:]


def fold_square(values):
    rows = values.shape[0] // 2
    return fold_right(values[:rows] + values[rows:])


def stacked(values):
    high = values.astype(jnp.bfloat16).astype(F32)
    return jnp.concatenate([high, values - high], axis=0).astype(jnp.bfloat16)


def skinny_dot(left, right, dims=NN):
    rows = left.shape[0]
    both = stacked(left)
    high, low = halves(right)
    values = plain_dot(both, high, dims) + plain_dot(both, low, dims)
    return values[:rows] + values[rows:]


def frame_outer(left, right):
    a_high = left.astype(jnp.bfloat16).astype(F32)
    b_high = right.astype(jnp.bfloat16).astype(F32)
    a_low = left - a_high
    b_low = right - b_high
    a = jnp.concatenate([a_high, a_high, a_low, a_low], axis=0).astype(jnp.bfloat16)
    b = jnp.concatenate([b_high, b_low, b_high, b_low], axis=0).astype(jnp.bfloat16)
    return plain_dot(a, b, TN)


def pad_rows(values):
    return jnp.concatenate([values, jnp.zeros((LANES - values.shape[0], values.shape[1]), values.dtype)], axis=0)


def column_order():
    q = lax.broadcasted_iota(jnp.int32, (LANES, LANES), 0)
    n = lax.broadcasted_iota(jnp.int32, (LANES, LANES), 1)
    source = (q // 16) * 16 + (q % 8) * 2 + (q // 8) % 2
    return (source == n).astype(jnp.bfloat16)


def live_frames(counts_ref):
    total = counts_ref[0]
    for clip in range(1, counts_ref.shape[0]):
        total = total + counts_ref[clip]
    return total


def place_of(counts_ref, frame):
    begin = jnp.int32(0)
    end = jnp.int32(0)
    for clip in range(counts_ref.shape[0]):
        end = end + counts_ref[clip]
        begin = jnp.where(frame >= end, end, begin)
    return frame - begin


def running_matrix(counts_ref, frames):
    after = lax.broadcasted_iota(jnp.int32, (frames, frames), 0)
    before = lax.broadcasted_iota(jnp.int32, (frames, frames), 1)
    begin = jnp.int32(0)
    matrix = jnp.zeros((frames, frames), F32)
    for clip in range(counts_ref.shape[0]):
        end = begin + counts_ref[clip]
        inside = (before >= begin) & (before <= after) & (after < end)
        matrix = matrix + jnp.where(inside, 1.0 / (after - begin + 1).astype(F32), 0.0)
        begin = end
    return matrix


def columns_up(values):
    spot = lax.broadcasted_iota(jnp.int32, values.shape, 1)
    return jnp.where(spot == 7, 0.0, pltpu.roll(values, 7, axis=1))


def columns_down(values):
    spot = lax.broadcasted_iota(jnp.int32, values.shape, 1)
    return jnp.where(spot == 0, 0.0, pltpu.roll(values, 1, axis=1))


def tile_sum(values):
    return jnp.sum(jnp.sum(values, axis=0), axis=0, keepdims=True)


def rows8(*rows):
    lanes = rows[0].shape[1]
    spot = lax.broadcasted_iota(jnp.int32, (8, lanes), 0)
    block = jnp.zeros((8, lanes), F32)
    for index, row in enumerate(rows):
        block = jnp.where(spot == index, row, block)
    return block


def pick_row(block, index):
    spot = lax.broadcasted_iota(jnp.int32, block.shape, 0)
    return jnp.sum(jnp.where(spot == index, block, 0.0), axis=0, keepdims=True)


def outer(left, right):
    return exact_dot(rows8(left), rows8(right), TN)


def row_dot(row, matrix, dims=NN):
    return exact_dot(rows8(row), matrix, dims)[0:1]


def clear_edges(ref):
    planes = ref.shape[1]
    edge = jnp.zeros((8, LANES), F32)
    for t in range(ref.shape[0]):
        for plane in range(planes):
            ref[t, plane, 0] = edge
            ref[t, plane, ref.shape[2] - 1] = edge


def spread_taps(taps_ref, w_ref):
    for tap in range(w_ref.shape[0]):
        w_ref[tap] = jnp.broadcast_to(taps_ref[0, tap : tap + 1, :], (8, LANES))


def conv_full(t, k, a_ref, w_ref, d_ref, fresh):
    weights = [w_ref[k * 9 + tap] for tap in range(9)]
    source = t - k
    rows = {}
    for i in range(SIDE):
        for need in (i, i + 1, i + 2):
            if need not in rows:
                rows[need] = [a_ref[source, plane, need] for plane in range(4)]
        even = None
        odd = None
        for r in range(3):
            a_even, a_odd, a_odd_down, a_even_up = rows[i + r]
            left, centre, right = weights[3 * r : 3 * r + 3]
            part_even = centre * a_even + right * a_odd + left * a_odd_down
            part_odd = centre * a_odd + left * a_even + right * a_even_up
            even = part_even if even is None else even + part_even
            odd = part_odd if odd is None else odd + part_odd
        rows.pop(i)
        at = t * FULL_ROWS + 2 * i
        if fresh:
            d_ref[at] = even
            d_ref[at + 1] = odd
        else:
            d_ref[at] = d_ref[at] + even
            d_ref[at + 1] = d_ref[at + 1] + odd


def conv_half(t, k, a_ref, w_ref, d_ref, fresh):
    weights = [w_ref[k * 9 + tap] for tap in range(9)]
    source = t - k
    carried = [a_ref[source, plane, 0] for plane in range(3)]
    for i in range(HALF_ROWS):
        rows = [carried]
        for need in (2 * i + 1, 2 * i + 2):
            rows.append([a_ref[source, plane, need] for plane in range(3)])
        carried = rows[2]
        total = None
        for r in range(3):
            a_even, a_odd, a_odd_down = rows[r]
            left, centre, right = weights[3 * r : 3 * r + 3]
            part = centre * a_even + right * a_odd + left * a_odd_down
            total = part if total is None else total + part
        at = t * HALF_ROWS + i
        d_ref[at] = total if fresh else d_ref[at] + total


def row_total(ref, lanes=None):
    values = ref[...] if lanes is None else ref[:, :, lanes]
    return jnp.sum(values, axis=0)


def send_all(send_ref, rows, lanes):
    count = rows.shape[0]

    def one(device, carry):
        send_ref[pl.ds(device, 1), 0:count, lanes] = rows[None]
        return carry

    lax.fori_loop(0, send_ref.shape[0], one, 0)


def stack_rows(*rows):
    return rows8(*rows)[0 : len(rows)]


def pick_thirds(order, values, dims, order_left):
    pieces = []
    rest = values
    for _ in range(3):
        piece = rest.astype(jnp.bfloat16)
        rest = rest - piece.astype(F32)
        args = (order, piece) if order_left else (piece, order)
        pieces.append(plain_dot(*args, dims))
    return pieces


def prepare_kernel(
    counts_ref, video_ref, cot_ref, w_ref, x_ref, rows_ref, columns_ref, cot_out_ref, gram_ref, send_ref
):
    order = column_order()
    total = live_frames(counts_ref)
    pixels = video_ref.shape[1]
    gram = jnp.zeros((2 * LANES, 2 * LANES), F32)
    summed = jnp.zeros((1, LANES), F32)
    for frame in range(pixels // 256):
        live = jnp.where(frame < total, 1.0, 0.0).astype(F32)
        for part in (2 * frame, 2 * frame + 1):
            at = slice(part * LANES, (part + 1) * LANES)
            block = pad_rows(video_ref[:, at] * live)
            high, middle, low = pick_thirds(order, block, NT, True)
            rows = high + middle + low
            x_ref[at, :] = rows
            rows_ref[at, :] = jnp.concatenate([high, middle], axis=1).astype(jnp.bfloat16)
            first, second, _ = pick_thirds(order, block, NT, False)
            columns_ref[:, at] = jnp.concatenate([first, second], axis=0).astype(jnp.bfloat16)
            summed = summed + jnp.sum(rows, axis=0, keepdims=True)
        at = slice(frame * 256, (frame + 1) * 256)
        gram = gram + plain_dot(columns_ref[:, at], rows_ref[at, :])
    gram = fold_square(gram)
    gram_ref[0:LANES, :] = gram
    gram_ref[LANES : LANES + 8, :] = rows8(summed)
    w = pad_rows(w_ref[0])
    width = w.shape[1]
    sums = stack_rows(row_dot(summed, w), jnp.sum(w * exact_dot(gram, w), axis=0, keepdims=True))
    count = jnp.full((2, LANES), 1.0, F32) * (total * (SIDE * SIDE)).astype(F32)
    send_all(send_ref, sums, slice(0, width))
    send_all(send_ref, count, slice(width, width + LANES))
    spot = lax.broadcasted_iota(jnp.int32, (LANES, LANES), 1)
    for part in range(cot_ref.shape[1] // LANES):
        at = slice(part * LANES, (part + 1) * LANES)
        frame = (spot + part * LANES) // (HALF_ROWS * 8)
        cot_out_ref[at, :] = jnp.where(frame < total, pad_rows(cot_ref[:, at]), 0.0).T


def moments_of(sums, count):
    average = sums[0:1] / count
    return (average, sums[1:2] / count - average * average)


def narrow_kernel(
    counts_ref, sums_ref, stat_ref, gram0_ref, x_ref, z_ref, ngain_ref, nbias_ref, w_ref,
    x1_ref, rows_ref, columns_ref, gram_ref, stat_out_ref, send_ref,
):
    total = live_frames(counts_ref)
    count = stat_ref[2:3, 0:LANES]
    average, variance = moments_of(row_total(sums_ref), count)
    factor = ngain_ref[0:1, :] * lax.rsqrt(variance + EPSILON)
    shift = nbias_ref[0:1, :] - factor * average
    stat_out_ref[...] = rows8(average, variance, count)
    frames = x_ref.shape[0] // 256

    def frame(t, carry):
        gram, cross, summed = carry
        at = pl.ds(pl.multiple_of(t * 256, 256), 256)
        z = z_ref[at, :]
        rows = x_ref[at, :] + factor * z + shift
        x1_ref[at, :] = rows
        both = side_by_side(rows)
        rows_ref[at, :] = both
        columns = jnp.concatenate(halves(rows.T), axis=0)
        columns_ref[:, at] = columns
        gram = gram + plain_dot(columns, both)
        cross = cross + plain_dot(columns, side_by_side(z))
        return (gram, cross, summed + jnp.sum(rows, axis=0, keepdims=True))

    zero = jnp.zeros((2 * LANES, 2 * LANES), F32)
    gram, cross, summed = lax.fori_loop(0, total, frame, (zero, zero, jnp.zeros((1, LANES), F32)))

    def dead(t, carry):
        at = pl.ds(pl.multiple_of(t * 256, 256), 256)
        x1_ref[at, :] = jnp.zeros((256, LANES), F32)
        rows_ref[at, :] = jnp.zeros((256, 2 * LANES), jnp.bfloat16)
        columns_ref[:, at] = jnp.zeros((2 * LANES, 256), jnp.bfloat16)
        return carry

    lax.fori_loop(total, frames, dead, 0)
    gram = fold_square(gram)
    gram_ref[0:LANES, :] = gram
    gram_ref[LANES : 2 * LANES, :] = fold_square(cross)
    gram_ref[2 * LANES : 3 * LANES, :] = gram0_ref[0:LANES, :]
    gram_ref[3 * LANES : 3 * LANES + 8, :] = rows8(summed, gram0_ref[LANES : LANES + 1, :])
    w = pad_rows(w_ref[0])
    sums = stack_rows(row_dot(summed, w), jnp.sum(w * exact_dot(gram, w), axis=0, keepdims=True))
    send_all(send_ref, sums, slice(0, w.shape[1]))


def write_first(t, values, scale, shift, a_ref, planes):
    half_pre = values * scale + shift
    first = (half_pre + half_pre * half_tanh(half_pre)).reshape(SIDE, 2, 8, LANES)
    even = first[:, 0]
    odd = first[:, 1]
    a_ref[t, 0, 1 : SIDE + 1] = even
    a_ref[t, 1, 1 : SIDE + 1] = odd
    if planes >= 3:
        a_ref[t, 2, 1 : SIDE + 1] = columns_down(odd)
    if planes >= 4:
        a_ref[t, 3, 1 : SIDE + 1] = columns_up(even)


def expand_kernel(
    block, counts_ref, sums_ref, count_ref, rows_ref, w_ref, gain_ref, bias_ref, taps_ref,
    e_ref, d_ref, stat_ref, send_ref, a_ref, taps8_ref,
):
    @pl.when(pl.program_id(0) == 0)
    def start():
        clear_edges(a_ref)

    total = live_frames(counts_ref)
    frames = a_ref.shape[0]
    count = count_ref[2:3, :] if block else row_total(count_ref)[0:1]
    average, variance = moments_of(row_total(sums_ref), count)
    stat_ref[...] = rows8(average, variance, count)
    norm_row = 2 * block
    scale = gain_ref[norm_row : norm_row + 1, :] * lax.rsqrt(variance + EPSILON)
    shift = 0.5 * (bias_ref[norm_row : norm_row + 1, :] - average * scale)
    scale = 0.5 * scale
    square = right_square(pad_rows(w_ref[0]))

    def expand(t, carry):
        at = pl.ds(pl.multiple_of(t * 256, 256), 256)
        values = fold_right(plain_dot(rows_ref[at, :], square)).reshape(FULL_ROWS, 8, LANES)
        e_ref[pl.ds(pl.multiple_of(t * FULL_ROWS, FULL_ROWS), FULL_ROWS)] = values
        write_first(t, values, scale, shift, a_ref, 3 if block else 4)
        return carry

    lax.fori_loop(0, total, expand, 0)
    spread_taps(taps_ref, taps8_ref)
    per_frame = HALF_ROWS if block else FULL_ROWS
    conv = conv_half if block else conv_full

    def frame(t, carry):
        conv(t, 0, a_ref, taps8_ref, d_ref, True)
        last = jnp.minimum(place_of(counts_ref, t), LAGS - 1)

        def lag(k, inner):
            conv(t, k, a_ref, taps8_ref, d_ref, False)
            return inner

        lax.fori_loop(1, last + 1, lag, 0)
        values = d_ref[pl.ds(t * per_frame, per_frame)]
        return (carry[0] + jnp.sum(values, axis=0), carry[1] + jnp.sum(values * values, axis=0))

    zero = jnp.zeros((8, LANES), F32)
    summed, squares = lax.fori_loop(0, total, frame, (zero, zero))

    def dead(t, carry):
        d_ref[pl.ds(t * per_frame, per_frame)] = jnp.zeros((per_frame, 8, LANES), F32)
        return carry

    lax.fori_loop(total, frames, dead, 0)
    sums = stack_rows(jnp.sum(summed, axis=0, keepdims=True), jnp.sum(squares, axis=0, keepdims=True))
    send_all(send_ref, sums, slice(0, LANES))


def chunk_plan(block, total, frames):
    return (4, frames // 4) if block else (1, total)


def squeeze_forward_kernel(
    block, counts_ref, sums_ref, stat_ref, d_ref, gain_ref, bias_ref, down_ref, downb_ref, up_ref, upb_ref, proj_ref,
    cot_ref, z_ref, gates_ref, running_ref, pre_ref, stat_out_ref, send_ref, second_ref, pooled_ref,
):
    phase = pl.program_id(0)
    tile = pl.program_id(1)
    tiles = pl.num_programs(1)
    total = live_frames(counts_ref)
    per_frame = HALF_ROWS if block else FULL_ROWS
    pixels = per_frame * 8
    frames = second_ref.shape[1] // per_frame
    group, chunks = chunk_plan(block, total, frames)
    norm_row = 2 * block + 1

    @pl.when(phase == 0)
    def activate():
        count = stat_ref[2:3, 0:LANES] * (0.25 if block else 1.0)
        average, variance = moments_of(row_total(sums_ref), count)
        stat_out_ref[...] = rows8(average, variance, count)
        scale = gain_ref[norm_row : norm_row + 1, :] * lax.rsqrt(variance + EPSILON)
        shift = 0.5 * (bias_ref[norm_row : norm_row + 1, :] - average * scale)
        scale = 0.5 * scale
        if not block:
            pooled_ref[tile] = jnp.zeros((frames, LANES), F32)

        def chunk(index, carry):
            for inner in range(group):
                t = index * group + inner
                at = pl.ds(t * per_frame, per_frame)
                half_pre = d_ref[at] * scale + shift
                second = half_pre + half_pre * half_tanh(half_pre)
                if group > 1:
                    second = second * jnp.where(t < total, 1.0, 0.0).astype(F32)
                second_ref[tile, at] = second
                pooled_ref[tile, pl.ds(t, 1), :] = tile_sum(second) * (1.0 / pixels)
            return carry

        lax.fori_loop(0, chunks, chunk, 0)

    @pl.when((phase == 1) & (tile == 0))
    def gate():
        matrix = running_matrix(counts_ref, frames)
        pooled = jnp.concatenate([pooled_ref[index] for index in range(pooled_ref.shape[0])], axis=1)
        running = exact_dot(matrix, pooled)
        running_ref[...] = running
        pre = skinny_dot(running, down_ref[0], NT) + downb_ref[block : block + 1, :]
        pre_ref[...] = pre
        gates_ref[...] = sigmoid(skinny_dot(pre * sigmoid(pre), up_ref[0]) + upb_ref[block : block + 1, :])
        z_ref[...] = jnp.zeros_like(z_ref)

    @pl.when(phase == 1)
    def project():
        square = right_square_t(pad_rows(proj_ref[0]))
        lanes = pl.ds(pl.multiple_of(tile * LANES, LANES), LANES)
        gates = gates_ref[:, lanes]

        def chunk(index, carry):
            parts = []
            for inner in range(group):
                t = index * group + inner
                second = second_ref[tile, pl.ds(t * per_frame, per_frame)].reshape(pixels, LANES)
                parts.append(second * pick_row(gates, t))
            excited = parts[0] if group == 1 else jnp.concatenate(parts, axis=0)
            at = pl.ds(pl.multiple_of(index * 256, 256), 256)
            z_ref[at, :] = z_ref[at, :] + fold_right(plain_dot(side_by_side(excited), square, NT))
            return carry

        lax.fori_loop(0, chunks, chunk, 0)

    @pl.when((phase == 1) & (tile == tiles - 1))
    def finish():
        def chunk(index, carry):
            at = pl.ds(pl.multiple_of(index * 256, 256), 256)
            z = z_ref[at, :].reshape(32, 8, LANES)
            values = [z, z * z]
            if block:
                dy = cot_ref[at, :].reshape(32, 8, LANES)
                values = values + [dy, dy * z]
            return tuple(old + jnp.sum(new, axis=0) for old, new in zip(carry, values))

        zero = jnp.zeros((8, LANES), F32)
        sums = lax.fori_loop(0, chunks, chunk, (zero,) * (4 if block else 2))
        rows = stack_rows(*(jnp.sum(value, axis=0, keepdims=True) for value in sums))
        send_all(send_ref, rows, slice(0, LANES))


def squeeze_backward_body(
    block, counts_ref, stat_ref, d_ref, gain_ref, bias_ref, down_ref, up_ref, proj_ref, gates_ref, running_ref,
    pre_ref, dy2_ref, send_ref, pack_ref, dz3_ref, dz3t_ref, excited_ref, dexc_ref, dgate_ref, head,
):
    phase = pl.program_id(0)
    tile = pl.program_id(1)
    total = live_frames(counts_ref)
    per_frame = HALF_ROWS if block else FULL_ROWS
    pixels = per_frame * 8
    frames = dz3_ref.shape[0] // pixels
    group, chunks = chunk_plan(block, total, frames)
    norm_row = 2 * block + 1
    tiles = dexc_ref.shape[0]
    narrow = proj_ref.shape[1]
    squeeze = down_ref.shape[1]
    lanes = pl.ds(pl.multiple_of(tile * LANES, LANES), LANES)

    @pl.when((phase == 0) & (tile == 0))
    def start():
        head()
        excited_ref[...] = jnp.zeros_like(excited_ref)
        dgate_ref[...] = jnp.zeros_like(dgate_ref)

    average = stat_ref[0:1, :]
    root = lax.rsqrt(stat_ref[1:2, :] + EPSILON)
    scale = gain_ref[norm_row : norm_row + 1, :] * root
    shift = 0.5 * (bias_ref[norm_row : norm_row + 1, :] - average * scale)
    scale = 0.5 * scale
    gates = gates_ref[:, lanes]

    @pl.when(phase == 0)
    def excite():
        square = right_square(pad_rows(proj_ref[0]))

        def chunk(index, carry):
            flat = pl.ds(pl.multiple_of(index * 256, 256), 256)
            dexc = fold_right(plain_dot(dz3_ref[flat, :], square)).reshape(32, 8, LANES)
            dexc_ref[tile, pl.ds(pl.multiple_of(index * 32, 32), 32)] = dexc
            parts = []
            for inner in range(group):
                t = index * group + inner
                half_pre = d_ref[pl.ds(t * per_frame, per_frame)] * scale + shift
                second = half_pre + half_pre * half_tanh(half_pre)
                if group > 1:
                    second = second * jnp.where(t < total, 1.0, 0.0).astype(F32)
                own = dexc[inner * per_frame : (inner + 1) * per_frame]
                dgate_ref[tile, pl.ds(t, 1), :] = tile_sum(own * second)
                parts.append(second.reshape(pixels, LANES) * pick_row(gates, t))
            excited = parts[0] if group == 1 else jnp.concatenate(parts, axis=0)
            excited_ref[flat, :] = side_by_side(excited)
            return carry

        lax.fori_loop(0, chunks, chunk, 0)
        dproj = fold_square(plain_dot(dz3t_ref[...], excited_ref[...]))
        pack_ref[0:narrow, lanes] = dproj[0:narrow]

    @pl.when((phase == 1) & (tile == 0))
    def squeeze_part():
        pre = pre_ref[...]
        half_pre = 0.5 * pre
        tanh = half_tanh(half_pre)
        squeezed = half_pre + half_pre * tanh
        all_gates = gates_ref[...]
        dgate = jnp.concatenate([dgate_ref[index] for index in range(tiles)], axis=1)
        du = dgate * all_gates * (1.0 - all_gates)
        dpre = skinny_dot(du, up_ref[0], NT) * silu_slope(half_pre, tanh)
        pack_ref[narrow : narrow + squeeze, :] = frame_outer(dpre, running_ref[...])
        pack_ref[narrow + squeeze : narrow + 2 * squeeze, :] = frame_outer(squeezed, du)
        dpre_row = jnp.sum(dpre, axis=0, keepdims=True)
        dpre_row = jnp.concatenate([dpre_row, jnp.zeros((1, du.shape[1] - squeeze), F32)], axis=1)
        pack_ref[narrow + 2 * squeeze : narrow + 2 * squeeze + 8, :] = rows8(
            jnp.sum(du, axis=0, keepdims=True), dpre_row
        )
        drunning = skinny_dot(dpre, down_ref[0])
        dpooled = exact_dot(running_matrix(counts_ref, frames), drunning, TN) * (1.0 / pixels)
        for index in range(tiles):
            dgate_ref[index] = dpooled[:, index * LANES : (index + 1) * LANES]

    @pl.when(phase == 1)
    def slope():
        def chunk(index, carry):
            summed, cross = carry
            for inner in range(group):
                t = index * group + inner
                at = pl.ds(t * per_frame, per_frame)
                depth = d_ref[at]
                half_pre = depth * scale + shift
                dsecond = dexc_ref[tile, at] * pick_row(gates, t) + pick_row(dgate_ref[tile], t)
                dy = dsecond * silu_slope(half_pre, half_tanh(half_pre))
                if group > 1:
                    dy = dy * jnp.where(t < total, 1.0, 0.0).astype(F32)
                dy2_ref[at] = dy
                summed = summed + jnp.sum(dy, axis=0)
                cross = cross + jnp.sum(dy * (depth - average), axis=0)
            return (summed, cross)

        zero = jnp.zeros((8, LANES), F32)
        summed, cross = lax.fori_loop(0, chunks, chunk, (zero, zero))
        rows = stack_rows(jnp.sum(summed, axis=0, keepdims=True), root * jnp.sum(cross, axis=0, keepdims=True))
        send_all(send_ref, rows, slice(0, LANES))


def squeeze_one_backward_kernel(
    counts_ref, third_ref, z_ref, cot_ref, ngain_ref, nbias_ref, stat_ref, d_ref, gain_ref, bias_ref, down_ref,
    up_ref, proj_ref, gates_ref, running_ref, pre_ref, act_ref, nsum_ref, dy2_ref, send_ref, pack_ref,
    dz3_ref, dz3t_ref, excited_ref, dexc_ref, dgate_ref,
):
    total = live_frames(counts_ref)
    pixels = HALF_ROWS * 8

    def head():
        count = stat_ref[2:3, :]
        sums = row_total(third_ref)
        mean, variance = moments_of(sums, count)
        root = lax.rsqrt(variance + EPSILON)
        gain = ngain_ref[1:2, :]
        bias_sum = sums[2:3, :]
        gain_sum = root * (sums[3:4, :] - mean * bias_sum)
        nsum_ref[...] = rows8(gain_sum, bias_sum, mean, variance)
        row = lax.broadcasted_iota(jnp.int32, z_ref.shape, 0) // pixels
        live = row < total
        normed = (z_ref[...] - mean) * root
        act = jnp.where(live, gain * normed + nbias_ref[1:2, :], 0.0)
        act_ref[...] = act.T[0 : act_ref.shape[0]]
        dz3 = gain * root * (cot_ref[...] - bias_sum / count - normed * (gain_sum / count))
        dz3 = jnp.where(live, dz3, 0.0)
        dz3_ref[...] = side_by_side(dz3)
        dz3t_ref[...] = jnp.concatenate(halves(dz3.T), axis=0)

    squeeze_backward_body(
        1, counts_ref, stat_ref, d_ref, gain_ref, bias_ref, down_ref, up_ref, proj_ref, gates_ref, running_ref,
        pre_ref, dy2_ref, send_ref, pack_ref, dz3_ref, dz3t_ref, excited_ref, dexc_ref, dgate_ref, head,
    )


def input_factors(sums, stat_ref, count, gain, w):
    root = lax.rsqrt(stat_ref[1:2, :] + EPSILON)
    factor = gain * root
    matrix = exact_dot(w * (factor * root * sums[1:2] / count), w, NT)
    return (matrix, row_dot(factor * sums[0:1] / count, w, NT))


def covariance(gram, summed, count):
    mean = summed / count
    return (mean, gram / count - outer(mean, mean))


def squeeze_zero_backward_kernel(
    counts_ref, top_ref, stat1_ref, gram_ref, nstat_ref, dxpre_ref, x1_ref, z_ref, ngain_ref, w_ref, gains_ref,
    stat_ref, d_ref, gain_ref, bias_ref, down_ref, up_ref, proj_ref, gates_ref, running_ref, pre_ref,
    dx1_ref, nsum_ref, dy2_ref, send_ref, pack_ref, dz3_ref, dz3t_ref, excited_ref, dexc_ref, dgate_ref,
):
    total = live_frames(counts_ref)
    width = gains_ref.shape[1]

    def head():
        count = stat_ref[2:3, :]
        wide_count = jnp.broadcast_to(count[:, 0:1], (1, width))
        sums = row_total(top_ref, slice(0, width))
        extra = row_total(top_ref, slice(width, width + LANES))
        matrix, shift = input_factors(sums, stat1_ref, wide_count, gains_ref[2:3, :], pad_rows(w_ref[0]))
        mean = nstat_ref[0:1, :]
        root = lax.rsqrt(nstat_ref[1:2, :] + EPSILON)
        mean_x1 = gram_ref[3 * LANES : 3 * LANES + 1, :] / count
        cross = (gram_ref[LANES : 2 * LANES, :] - count * outer(mean_x1, mean)) * root
        gain_sum = extra[0:1] - jnp.sum(matrix * cross, axis=0, keepdims=True)
        bias_sum = extra[1:2] - count * shift
        nsum_ref[...] = rows8(gain_sum, bias_sum, mean, nstat_ref[1:2, :])
        factor = ngain_ref[0:1, :] * root
        square = right_square(matrix)

        def frame(t, carry):
            at = pl.ds(pl.multiple_of(t * 256, 256), 256)
            centred = side_by_side(x1_ref[at, :] - mean_x1)
            dx1 = dxpre_ref[at, :] - fold_right(plain_dot(centred, square)) - shift
            dx1_ref[at, :] = dx1
            normed = (z_ref[at, :] - mean) * root
            dz3 = factor * (dx1 - bias_sum / count - normed * (gain_sum / count))
            dz3_ref[at, :] = side_by_side(dz3)
            dz3t_ref[:, at] = jnp.concatenate(halves(dz3.T), axis=0)
            return carry

        lax.fori_loop(0, total, frame, 0)

        def dead(t, carry):
            at = pl.ds(pl.multiple_of(t * 256, 256), 256)
            dx1_ref[at, :] = jnp.zeros((256, LANES), F32)
            dz3t_ref[:, at] = jnp.zeros((2 * LANES, 256), jnp.bfloat16)
            return carry

        lax.fori_loop(total, dz3_ref.shape[0] // 256, dead, 0)

    squeeze_backward_body(
        0, counts_ref, stat_ref, d_ref, gain_ref, bias_ref, down_ref, up_ref, proj_ref, gates_ref, running_ref,
        pre_ref, dy2_ref, send_ref, pack_ref, dz3_ref, dz3t_ref, excited_ref, dexc_ref, dgate_ref, head,
    )

def back_full(t, k, a_ref, w_ref, z_ref, f_ref, dw_ref, fresh):
    weights = [w_ref[k * 9 + tap] for tap in range(9)]
    target = t - k
    sums = [None] * 9
    a_rows = {}
    z_rows = {}
    for i in range(SIDE):
        for need in (i, i + 1, i + 2):
            if need not in a_rows:
                a_rows[need] = [a_ref[target, plane, need] for plane in range(2)]
                z_rows[need] = [z_ref[t, plane, need] for plane in range(4)]
        even = None
        odd = None
        z_even, z_odd, z_odd_down, z_even_up = z_rows[i + 1]
        for r in range(3):
            b_even, b_odd, b_odd_down, b_even_up = z_rows[i + 2 - r]
            left, centre, right = weights[3 * r : 3 * r + 3]
            part_even = centre * b_even + right * b_odd_down + left * b_odd
            part_odd = centre * b_odd + right * b_even + left * b_even_up
            even = part_even if even is None else even + part_even
            odd = part_odd if odd is None else odd + part_odd
            a_even, a_odd = a_rows[i + r]
            pieces = (
                z_even_up * a_odd + z_odd * a_even,
                z_even * a_even + z_odd * a_odd,
                z_even * a_odd + z_odd_down * a_even,
            )
            for c in range(3):
                at = 3 * r + c
                sums[at] = pieces[c] if sums[at] is None else sums[at] + pieces[c]
        a_rows.pop(i)
        z_rows.pop(i)
        at = target * FULL_ROWS + 2 * i
        if fresh:
            f_ref[at] = even
            f_ref[at + 1] = odd
        else:
            f_ref[at] = f_ref[at] + even
            f_ref[at + 1] = f_ref[at + 1] + odd
    for tap in range(9):
        dw_ref[k * 9 + tap] = dw_ref[k * 9 + tap] + sums[tap]


def back_half(t, k, a_ref, w_ref, z_ref, f_ref, dw_ref, fresh):
    weights = [w_ref[k * 9 + tap] for tap in range(9)]
    target = t - k
    sums = [None] * 9

    def put(row, parity, value):
        at = target * FULL_ROWS + 2 * row + parity
        f_ref[at] = value if fresh else f_ref[at] + value

    carried = [a_ref[target, plane, 0] for plane in range(2)]
    here = [z_ref[t, plane, 0] for plane in range(2)]
    for i in range(HALF_ROWS):
        below = [z_ref[t, plane, i + 1] for plane in range(2)]
        dz, dz_up = here
        rows = [carried]
        for need in (2 * i + 1, 2 * i + 2):
            rows.append([a_ref[target, plane, need] for plane in range(2)])
        carried = rows[2]
        put(2 * i, 0, weights[4] * dz)
        put(2 * i, 1, weights[5] * dz + weights[3] * dz_up)
        put(2 * i + 1, 0, weights[7] * dz + weights[1] * below[0])
        put(
            2 * i + 1,
            1,
            weights[8] * dz + weights[6] * dz_up + (weights[2] * below[0] + weights[0] * below[1]),
        )
        for r in range(3):
            a_even, a_odd = rows[r]
            pieces = (dz_up * a_odd, dz * a_even, dz * a_odd)
            for c in range(3):
                at = 3 * r + c
                sums[at] = pieces[c] if sums[at] is None else sums[at] + pieces[c]
        here = below
    for tap in range(9):
        dw_ref[k * 9 + tap] = dw_ref[k * 9 + tap] + sums[tap]


def depth_backward_kernel(
    block, counts_ref, grads_ref, stat2_ref, stat_ref, nstat_ref, dy2_ref, d_ref, e_ref, columns_ref, w_ref, gain_ref,
    bias_ref, taps_ref, z3_ref, dxpre_ref, send_ref, q_ref, grad_rows_ref, a_ref, z_ref, f_ref, taps8_ref, dw_ref, pair_ref,
):
    tile = pl.program_id(0)
    tiles = pl.num_programs(0)
    total = live_frames(counts_ref)
    frames = a_ref.shape[0]
    norm_row = 2 * block
    half = block == 1
    per_frame = HALF_ROWS if half else FULL_ROWS
    taps = dw_ref.shape[0]

    @pl.when(tile == 0)
    def start():
        clear_edges(a_ref)
        clear_edges(z_ref)
        dxpre_ref[...] = jnp.zeros_like(dxpre_ref)
        pair_ref[...] = jnp.zeros_like(pair_ref)

    count = stat2_ref[2:3, :]
    grads = row_total(grads_ref)
    grad_rows_ref[...] = rows8(grads[0:1], grads[1:2])
    average = stat2_ref[0:1, :]
    root = lax.rsqrt(stat2_ref[1:2, :] + EPSILON)
    scale_two = gain_ref[norm_row + 1 : norm_row + 2, :] * root
    slope = scale_two * root * grads[1:2] / count
    level = scale_two * grads[0:1] / count - slope * average
    average_one = stat_ref[0:1, :]
    root_one = lax.rsqrt(stat_ref[1:2, :] + EPSILON)
    scale_one = gain_ref[norm_row : norm_row + 1, :] * root_one
    shift_half = 0.5 * (bias_ref[norm_row : norm_row + 1, :] - average_one * scale_one)
    scale_half = 0.5 * scale_one

    def fill(t, carry):
        at = pl.ds(t * per_frame, per_frame)
        dz = scale_two * dy2_ref[at] - (slope * d_ref[at] + level)
        if half:
            z_ref[t, 0, 0:HALF_ROWS] = dz
            z_ref[t, 1, 0:HALF_ROWS] = columns_up(dz)
        else:
            pair = dz.reshape(SIDE, 2, 8, LANES)
            z_ref[t, 0, 1 : SIDE + 1] = pair[:, 0]
            z_ref[t, 1, 1 : SIDE + 1] = pair[:, 1]
            z_ref[t, 2, 1 : SIDE + 1] = columns_down(pair[:, 1])
            z_ref[t, 3, 1 : SIDE + 1] = columns_up(pair[:, 0])
        values = e_ref[pl.ds(pl.multiple_of(t * FULL_ROWS, FULL_ROWS), FULL_ROWS)]
        write_first(t, values, scale_half, shift_half, a_ref, 2)
        return carry

    lax.fori_loop(0, total, fill, 0)
    spread_taps(taps_ref, taps8_ref)
    dw_ref[...] = jnp.zeros_like(dw_ref)
    back = back_half if half else back_full

    def frame(t, carry):
        back(t, 0, a_ref, taps8_ref, z_ref, f_ref, dw_ref, True)
        last = jnp.minimum(place_of(counts_ref, t), LAGS - 1)

        def lag(k, inner):
            back(t, k, a_ref, taps8_ref, z_ref, f_ref, dw_ref, False)
            return inner

        return lax.fori_loop(1, last + 1, lag, carry)

    lax.fori_loop(0, total, frame, 0)
    square = right_square_t(pad_rows(w_ref[0]))

    def finish(t, carry):
        rows = pl.ds(pl.multiple_of(t * FULL_ROWS, FULL_ROWS), FULL_ROWS)
        flat = pl.ds(pl.multiple_of(t * 256, 256), 256)
        values = e_ref[rows]
        half_pre = values * scale_half + shift_half
        dy = f_ref[rows] * silu_slope(half_pre, half_tanh(half_pre))
        summed = carry[0] + jnp.sum(dy, axis=0)
        cross = carry[1] + jnp.sum(dy * (values - average_one), axis=0)
        dy = dy.reshape(256, LANES)
        pair_ref[flat, :] = side_by_side(dy)
        scaled = side_by_side(dy * scale_one)
        dxpre_ref[flat, :] = dxpre_ref[flat, :] + fold_right(plain_dot(scaled, square, NT))
        return (summed, cross)

    zero = jnp.zeros((8, LANES), F32)
    summed, cross = lax.fori_loop(0, total, finish, (zero, zero))
    rows = stack_rows(jnp.sum(summed, axis=0, keepdims=True), root_one * jnp.sum(cross, axis=0, keepdims=True))
    send_all(send_ref, rows, pl.ds(pl.multiple_of(tile * LANES, LANES), LANES))
    gathered = fold_square(plain_dot(columns_ref[...], pair_ref[...]))
    narrow = w_ref.shape[1]
    dtaps = jnp.sum(dw_ref[...], axis=1)
    unused = (-taps) % 8
    dtaps = jnp.concatenate([dtaps, jnp.zeros((unused, LANES), F32)], axis=0)
    q_ref[0 : narrow // 8] = gathered[0:narrow].reshape(narrow // 8, 8, LANES)
    q_ref[narrow // 8 :] = dtaps.reshape((taps + unused) // 8, 8, LANES)

    if half:
        @pl.when(tile == tiles - 1)
        def tail():
            mean = nstat_ref[0:1, :]
            root_three = lax.rsqrt(nstat_ref[1:2, :] + EPSILON)

            def part(t, carry):
                flat = pl.ds(pl.multiple_of(t * 256, 256), 256)
                dx = dxpre_ref[flat, :].reshape(32, 8, LANES)
                normed = ((z3_ref[flat, :] - mean) * root_three).reshape(32, 8, LANES)
                return (carry[0] + jnp.sum(dx * normed, axis=0), carry[1] + jnp.sum(dx, axis=0))

            cross_three, summed_three = lax.fori_loop(0, total, part, (zero, zero))
            rows = stack_rows(
                jnp.sum(cross_three, axis=0, keepdims=True), jnp.sum(summed_three, axis=0, keepdims=True)
            )
            width = send_ref.shape[2] - LANES
            send_all(send_ref, rows, slice(width, width + LANES))


def finish_kernel(
    counts_ref, momentum_ref, gram_ref, stat01_ref, stat02_ref, stat11_ref, stat12_ref, grad0_ref,
    grad1_ref, one_ref, zero_ref, nsum0_ref, nsum1_ref, dxpre_ref, x_ref, dx1_ref, w_ref, gain_ref, means_ref, vars_ref,
    nmeans_ref, nvars_ref,
    video_ref, less_ref, factor_ref, wgain_ref, wbias_ref, ngain_ref, nbias_ref, newm_ref, newv_ref, newnm_ref, newnv_ref,
):
    total = live_frames(counts_ref)
    full = stat01_ref[2:3, :]
    count = full[:, 0:LANES]
    width = full.shape[1]
    top_zero = row_total(zero_ref)
    top_one = row_total(one_ref, slice(0, width))
    w_zero = pad_rows(w_ref[0])
    matrix, shift = input_factors(top_zero, stat01_ref, full, gain_ref[0:1, :], w_zero)
    square = right_square(matrix)
    mean_x, cov_zero = covariance(
        gram_ref[2 * LANES : 3 * LANES, :], gram_ref[3 * LANES + 1 : 3 * LANES + 2, :], count
    )
    order = column_order()
    narrow = video_ref.shape[0]
    for frame in range(x_ref.shape[0] // 256):
        @pl.when(frame < total)
        def live(frame=frame):
            at = slice(frame * 256, (frame + 1) * 256)
            centred = side_by_side(x_ref[at, :] - mean_x)
            dx = dxpre_ref[at, :] - fold_right(plain_dot(centred, square)) - shift + dx1_ref[at, :]
            for part in range(2):
                own = dx[part * LANES : (part + 1) * LANES].T[0:narrow]
                pieces = pick_thirds(order, own, NN, False)
                start = frame * 256 + part * LANES
                video_ref[:, start : start + LANES] = pieces[0] + pieces[1] + pieces[2]

        @pl.when(frame >= total)
        def dead(frame=frame):
            video_ref[:, frame * 256 : (frame + 1) * 256] = jnp.zeros((narrow, 256), F32)
    mean_one, cov_one = covariance(gram_ref[0:LANES, :], gram_ref[3 * LANES : 3 * LANES + 1, :], count)
    plan = ((mean_x, cov_zero, stat01_ref, top_zero, w_zero), (mean_one, cov_one, stat11_ref, top_one, pad_rows(w_ref[1])))
    for block, (mean_row, cov, stat_ref, top, w) in enumerate(plan):
        root = lax.rsqrt(stat_ref[1:2, :] + EPSILON)
        factor = gain_ref[2 * block : 2 * block + 1, :] * root
        less = outer(mean_row, top[0:1]) + exact_dot(cov, w) * (root * top[1:2])
        less_ref[block] = (less * factor)[0:narrow]
        factor_ref[8 * block : 8 * block + 8, :] = rows8(factor)
    momentum = momentum_ref[0].astype(F32) / 10.0
    wgain_ref[...] = stack_rows(top_zero[1:2], grad0_ref[1:2, :], top_one[1:2], grad1_ref[1:2, :])
    wbias_ref[...] = stack_rows(top_zero[0:1], grad0_ref[0:1, :], top_one[0:1], grad1_ref[0:1, :])
    stats = (stat01_ref, stat02_ref, stat11_ref, stat12_ref)
    means = stack_rows(*(ref[0:1, :] for ref in stats))
    variances = stack_rows(*(ref[1:2, :] * (ref[2:3, :] / (ref[2:3, :] - 1.0)) for ref in stats))
    newm_ref[...] = (1.0 - momentum) * means_ref[...] + momentum * means
    newv_ref[...] = (1.0 - momentum) * vars_ref[...] + momentum * variances
    ngain_ref[...] = stack_rows(nsum0_ref[0:1, :], nsum1_ref[0:1, :])[:, 0:narrow]
    nbias_ref[...] = stack_rows(nsum0_ref[1:2, :], nsum1_ref[1:2, :])[:, 0:narrow]
    means = stack_rows(nsum0_ref[2:3, :], nsum1_ref[2:3, :])[:, 0:narrow]
    quarter = 0.25 * count
    variances = stack_rows(
        nsum0_ref[3:4, :] * (count / (count - 1.0)), nsum1_ref[3:4, :] * (quarter / (quarter - 1.0))
    )[:, 0:narrow]
    newnm_ref[...] = (1.0 - momentum) * nmeans_ref[...] + momentum * means
    newnv_ref[...] = (1.0 - momentum) * nvars_ref[...] + momentum * variances


def gradient_kernel(late_ref, one_ref, less_ref, factor_ref, dw_ref, dtaps_ref):
    narrow = dw_ref.shape[1]
    taps = dtaps_ref.shape[1]
    tiles = dw_ref.shape[2] // LANES
    per_tile = late_ref.shape[0] // tiles
    for block, ref in enumerate((late_ref, one_ref)):
        for tile in range(tiles):
            at = slice(tile * LANES, (tile + 1) * LANES)
            values = ref[tile * per_tile : (tile + 1) * per_tile].reshape(per_tile * 8, LANES)
            dw_ref[block, :, at] = values[0:narrow] * factor_ref[8 * block : 8 * block + 1, at] - less_ref[block, :, at]
            dtaps_ref[block, :, at] = values[narrow : narrow + taps]


AXES = ("dp", "rep")


def exchange(send):
    return lax.all_to_all(send, AXES, 0, 0, tiled=True)


def spread_sum(values):
    devices = lax.axis_size("dp") * lax.axis_size("rep")
    count = values.shape[0]
    share = -(-count // devices)
    padded = jnp.pad(values, ((0, share * devices - count), (0, 0), (0, 0)))
    pieces = padded.reshape(devices, share, *values.shape[1:])
    own = jnp.sum(exchange(pieces), axis=0)
    everyone = exchange(jnp.broadcast_to(own[None], (devices,) + own.shape))
    return everyone.reshape(devices * share, *values.shape[1:])[:count]


def shape(*dims, kind=F32):
    return jax.ShapeDtypeStruct(dims, kind)


def whole(array):
    rank = len(array.shape)
    return pl.BlockSpec(array.shape, lambda *ids: (0,) * rank)


SCALARS = pl.BlockSpec(memory_space=pltpu.SMEM)


def call(kernel, grid, in_specs, out_specs, out_shape, scratch, args):
    return pl.pallas_call(
        kernel,
        grid=grid,
        in_specs=in_specs,
        out_specs=out_specs,
        out_shape=out_shape,
        scratch_shapes=scratch,
        compiler_params=pltpu.CompilerParams(vmem_limit_bytes=VMEM_BYTES),
    )(*args)


def simple_call(kernel, scalars, args, outs):
    return call(
        kernel, (1,), [SCALARS] * scalars + [whole(array) for array in args[scalars:]], [whole(item) for item in outs],
        outs, [], args,
    )


def local(
    video, frame_counts, momentum_index, expand_weight, wide_gains, wide_biases, narrow_gains, narrow_biases, depth_weight,
    squeeze_weight, squeeze_bias, excite_weight, excite_bias, project_weight, wide_means, wide_variances, narrow_means,
    narrow_variances, cotangent,
):
    devices = lax.axis_size("dp") * lax.axis_size("rep")
    cin, pixels = video.shape
    half_pixels = cotangent.shape[1]
    width = expand_weight.shape[1]
    squeeze = squeeze_weight.shape[1]
    frames = pixels // (SIDE * SIDE)
    tiles = width // LANES
    taps = depth_weight.shape[1]
    w_t = jnp.swapaxes(expand_weight, 1, 2)
    up_t = jnp.swapaxes(excite_weight, 1, 2)
    lanes_pad = ((0, 0), (0, LANES - cin))
    ngains = jnp.pad(narrow_gains, lanes_pad)
    nbiases = jnp.pad(narrow_biases, lanes_pad)
    full_rows = frames * FULL_ROWS
    half_rows = frames * HALF_ROWS
    low = jnp.bfloat16

    def fixed(*dims):
        return pl.BlockSpec(dims, lambda *ids: (0,) * len(dims))

    def tile_rows(rows):
        return pl.BlockSpec((rows, LANES), lambda j: (0, j))

    def tile_cube(rows):
        return pl.BlockSpec((rows, 8, LANES), lambda j: (0, 0, j))

    def tile_sums(rows=2):
        return pl.BlockSpec((devices, rows, LANES), lambda j: (0, 0, j))

    def weight_tile(block, rows):
        return pl.BlockSpec((1, rows, LANES), lambda j, block=block: (block, 0, j))

    def of_block(block, rows, lanes):
        return pl.BlockSpec((1, rows, lanes), lambda *ids: (block, 0, 0))

    def early(make):
        return make(lambda p, j: j * (1 - p) + (tiles - 1) * p)

    def late(make):
        return make(lambda p, j: j * p)

    def both(make):
        return make(lambda p, j: j)

    def rows_at(rows):
        return lambda at: pl.BlockSpec((rows, LANES), lambda p, j: (0, at(p, j)))

    def cube_at(rows):
        return lambda at: pl.BlockSpec((rows, 8, LANES), lambda p, j: (0, 0, at(p, j)))

    def sums_at(rows):
        return lambda at: pl.BlockSpec((devices, rows, LANES), lambda p, j: (0, 0, at(p, j)))

    def weight_at(block, rows):
        return lambda at: pl.BlockSpec((1, rows, LANES), lambda p, j: (block, 0, at(p, j)))

    x, x_rows, x_columns, cot, gram_zero, sums = call(
        prepare_kernel, (1,), [SCALARS, whole(video), whole(cotangent), of_block(0, cin, width)],
        [fixed(pixels, LANES), fixed(pixels, 2 * LANES), fixed(2 * LANES, pixels), fixed(half_pixels, LANES),
         fixed(LANES + 8, LANES), fixed(devices, 2, width + LANES)],
        [shape(pixels, LANES), shape(pixels, 2 * LANES, kind=low), shape(2 * LANES, pixels, kind=low),
         shape(half_pixels, LANES), shape(LANES + 8, LANES), shape(devices, 2, width + LANES)],
        [], (frame_counts, video, cotangent, w_t),
    )
    sums = exchange(sums)

    def expand(block, sums, count, count_spec, rows):
        depth_rows = half_rows if block else full_rows
        return call(
            functools.partial(expand_kernel, block), (tiles,),
            [SCALARS, tile_sums(), count_spec, whole(rows), weight_tile(block, cin), tile_rows(4), tile_rows(4),
             weight_tile(block, taps)],
            [tile_cube(full_rows), tile_cube(depth_rows), tile_rows(8), tile_sums()],
            [shape(full_rows, 8, width), shape(depth_rows, 8, width), shape(8, width), shape(devices, 2, width)],
            [pltpu.VMEM((frames, 4, SIDE + 2, 8, LANES), F32), pltpu.VMEM((taps, 8, LANES), F32)],
            (frame_counts, sums, count, rows, w_t, wide_gains, wide_biases, depth_weight),
        )

    count_spec = pl.BlockSpec((devices, 2, LANES), lambda j: (0, 0, tiles))
    e_zero, d_zero, stat01, sums = expand(0, sums, sums, count_spec, x_rows)
    sums = exchange(sums)

    def squeeze_forward(block, sums, stat, depth):
        rows = half_rows if block else full_rows
        kinds = 4 if block else 2
        return call(
            functools.partial(squeeze_forward_kernel, block), (2, tiles),
            [SCALARS, early(sums_at(2)), early(rows_at(8)), early(cube_at(rows)), early(rows_at(4)), early(rows_at(4)),
             of_block(block, squeeze, width), whole(squeeze_bias), of_block(block, squeeze, width), whole(excite_bias),
             late(weight_at(block, cin)), whole(cot)],
            [fixed(rows * 8, LANES), fixed(8, width), fixed(8, width), fixed(8, squeeze), early(rows_at(8)),
             fixed(devices, kinds, LANES)],
            [shape(rows * 8, LANES), shape(8, width), shape(8, width), shape(8, squeeze), shape(8, width),
             shape(devices, kinds, LANES)],
            [pltpu.VMEM((tiles, rows, 8, LANES), F32), pltpu.VMEM((tiles, frames, LANES), F32)],
            (frame_counts, sums, stat, depth, wide_gains, wide_biases, squeeze_weight, squeeze_bias, up_t, excite_bias,
             project_weight, cot),
        )

    z_zero, gates_zero, running_zero, pre_zero, stat02, sums = squeeze_forward(0, sums, stat01, d_zero)
    sums = exchange(sums)
    narrow_args = (frame_counts, sums, stat01, gram_zero, x, z_zero, ngains, nbiases, w_t)
    narrow_outs = [
        shape(pixels, LANES), shape(pixels, 2 * LANES, kind=low), shape(2 * LANES, pixels, kind=low),
        shape(3 * LANES + 8, LANES), shape(8, LANES), shape(devices, 2, width),
    ]
    x1, x1_rows, x1_columns, gram, nstat, sums = call(
        narrow_kernel, (1,), [SCALARS] + [whole(array) for array in narrow_args[1:-1]] + [of_block(1, cin, width)],
        [whole(item) for item in narrow_outs], narrow_outs, [], narrow_args,
    )
    sums = exchange(sums)
    gram = lax.psum(gram, AXES)
    e_one, d_one, stat11, sums = expand(1, sums, nstat, pl.BlockSpec((8, LANES), lambda j: (0, 0)), x1_rows)
    sums = exchange(sums)
    z_one, gates_one, running_one, pre_one, stat12, sums = squeeze_forward(1, sums, stat11, d_one)
    third = exchange(sums)
    pack_rows = -(-(cin + 2 * squeeze + 2) // 8) * 8

    def backward_specs(block):
        rows = half_rows if block else full_rows
        ins = [both(rows_at(8)), both(cube_at(rows)), both(rows_at(4)), both(rows_at(4)), of_block(block, squeeze, width),
               of_block(block, squeeze, width), early(weight_at(block, cin)), fixed(8, width), fixed(8, width),
               fixed(8, squeeze)]
        outs = [fixed(8, LANES), late(cube_at(rows)), late(sums_at(2)), fixed(pack_rows, width)]
        shapes = [shape(8, LANES), shape(rows, 8, width), shape(devices, 2, width), shape(pack_rows, width)]
        scratch = [pltpu.VMEM((rows * 8, 2 * LANES), low), pltpu.VMEM((2 * LANES, rows * 8), low),
                   pltpu.VMEM((rows * 8, 2 * LANES), low), pltpu.VMEM((tiles, rows, 8, LANES), F32),
                   pltpu.VMEM((tiles, frames, LANES), F32)]
        return (ins, outs, shapes, scratch)

    ins, outs, shapes, scratch = backward_specs(1)
    activations, nsum_one, dy2_one, sums, pack_one = call(
        squeeze_one_backward_kernel, (2, tiles),
        [SCALARS, whole(third), whole(z_one), whole(cot), whole(ngains), whole(nbiases)] + ins,
        [fixed(cin, half_pixels)] + outs, [shape(cin, half_pixels)] + shapes, scratch,
        (frame_counts, third, z_one, cot, ngains, nbiases, stat12, d_one, wide_gains, wide_biases, squeeze_weight, up_t,
         project_weight, gates_one, running_one, pre_one),
    )
    sums = exchange(sums)
    sums, pack_one, gram = lax.optimization_barrier((sums, pack_one, gram))
    pack_one = lax.psum(pack_one, AXES)
    q_tiles = -(-cin // 8) + -(-taps // 8)

    def depth_backward(block, sums, stat2, stat, dy2, depth, expanded, columns):
        rows = half_rows if block else full_rows
        z_shape = (frames, 2, HALF_ROWS + 1, 8, LANES) if block else (frames, 4, SIDE + 2, 8, LANES)
        send = (devices, 2, width + (LANES if block else 0))
        return call(
            functools.partial(depth_backward_kernel, block), (tiles,),
            [SCALARS, tile_sums(), tile_rows(8), tile_rows(8), whole(nstat), tile_cube(rows), tile_cube(rows),
             tile_cube(full_rows), whole(columns), weight_tile(block, cin), tile_rows(4), tile_rows(4),
             weight_tile(block, taps), whole(z_zero)],
            [fixed(pixels, LANES), fixed(*send), pl.BlockSpec((q_tiles, 8, LANES), lambda j: (j, 0, 0)), tile_rows(8)],
            [shape(pixels, LANES), shape(*send), shape(tiles * q_tiles, 8, LANES), shape(8, width)],
            [pltpu.VMEM((frames, 2, SIDE + 2, 8, LANES), F32), pltpu.VMEM(z_shape, F32), pltpu.VMEM((full_rows, 8, LANES), F32),
             pltpu.VMEM((taps, 8, LANES), F32), pltpu.VMEM((taps, 8, LANES), F32), pltpu.VMEM((pixels, 2 * LANES), low)],
            (frame_counts, sums, stat2, stat, nstat, dy2, depth, expanded, columns, w_t, wide_gains, wide_biases,
             depth_weight, z_zero),
        )

    dxpre_one, sums, q_one, grad_one = depth_backward(1, sums, stat12, stat11, dy2_one, d_one, e_one, x1_columns)
    top_one = exchange(sums)
    ins, outs, shapes, scratch = backward_specs(0)
    dx1, nsum_zero, dy2_zero, sums, pack_zero = call(
        squeeze_zero_backward_kernel, (2, tiles),
        [SCALARS, whole(top_one), whole(stat11), whole(gram), whole(nstat), whole(dxpre_one), whole(x1), whole(z_zero),
         whole(ngains), of_block(1, cin, width), whole(wide_gains)] + ins,
        [fixed(pixels, LANES)] + outs, [shape(pixels, LANES)] + shapes, scratch,
        (frame_counts, top_one, stat11, gram, nstat, dxpre_one, x1, z_zero, ngains, w_t, wide_gains, stat02, d_zero,
         wide_gains, wide_biases, squeeze_weight, up_t, project_weight, gates_zero, running_zero, pre_zero),
    )
    sums = exchange(sums)
    sums, pack_zero, pack_one, q_one = lax.optimization_barrier((sums, pack_zero, pack_one, q_one))
    pack_zero, q_one = lax.psum((pack_zero, q_one), AXES)
    dxpre_zero, sums, q_zero, grad_zero = depth_backward(0, sums, stat02, stat01, dy2_zero, d_zero, e_zero, x_columns)
    top_zero = exchange(sums)
    late_tiles = spread_sum(q_zero)
    final_args = (
        frame_counts, momentum_index, gram, stat01, stat02, stat11, stat12, grad_zero, grad_one, top_one,
        top_zero, nsum_zero, nsum_one, dxpre_zero, x, dx1, w_t, wide_gains, wide_means, wide_variances, narrow_means,
        narrow_variances,
    )
    final_outs = [
        shape(cin, pixels), shape(2, cin, width), shape(16, width), shape(4, width), shape(4, width), shape(2, cin),
        shape(2, cin), shape(4, width), shape(4, width), shape(2, cin), shape(2, cin),
    ]
    video_grad, less, factor, wgain, wbias, ngain, nbias, newm, newv, newnm, newnv = simple_call(
        finish_kernel, 2, final_args, final_outs
    )
    dw_t, dtaps = simple_call(
        gradient_kernel, 0, (late_tiles, q_one, less, factor), [shape(2, cin, width), shape(2, taps, width)]
    )
    edges = (0, cin, cin + squeeze, cin + 2 * squeeze)
    dproj, ddown, dup = (
        jnp.stack([pack_zero[edges[i] : edges[i + 1]], pack_one[edges[i] : edges[i + 1]]]) for i in range(3)
    )
    dupb = jnp.stack([pack_zero[edges[3]], pack_one[edges[3]]])
    ddownb = jnp.stack([pack_zero[edges[3] + 1, :squeeze], pack_one[edges[3] + 1, :squeeze]])
    return (
        activations, video_grad, jnp.swapaxes(dw_t, 1, 2), wgain, wbias, ngain, nbias, dtaps, ddown, ddownb,
        jnp.swapaxes(dup, 1, 2), dupb, dproj, newm, newv, newnm, newnv,
    )


def solution(mesh):
    split = P(None, AXES)
    placed = (split, P(AXES)) + (P(),) * 16 + (split,)
    return jax.shard_map(
        local, mesh=mesh, in_specs=placed, out_specs=(split, split) + (P(),) * 15, check_vma=False
    )
```

```python
import functools

import jax
import jax.numpy as jnp
from jax import lax
from jax.experimental import pallas as pl
from jax.experimental.pallas import tpu as pltpu
from jax.sharding import PartitionSpec as P

SIDE = 16
LANES = 128
LAGS = 5
FULL_ROWS = 2 * SIDE
HALF_ROWS = SIDE // 2
EPSILON = 1e-05
HIGHEST = lax.Precision.HIGHEST
F32 = jnp.float32
NN = (((1,), (0,)), ((), ()))
NT = (((1,), (1,)), ((), ()))
TN = (((0,), (0,)), ((), ()))
VMEM_BYTES = 52 * 1024 * 1024


def half_tanh(half_values):
    return jnp.tanh(half_values)


def sigmoid(values):
    return 0.5 * jnp.tanh(0.5 * values) + 0.5


def silu_slope(half_values, tanh):
    return 0.5 * (1.0 + tanh + half_values * (1.0 - tanh * tanh))


def exact_dot(left, right, dims=NN):
    return lax.dot_general(left, right, dims, precision=HIGHEST, preferred_element_type=F32)


def halves(values):
    high = values.astype(jnp.bfloat16)
    return (high, (values - high.astype(F32)).astype(jnp.bfloat16))


def side_by_side(values):
    return jnp.concatenate(halves(values), axis=1)


def right_square(w):
    both = side_by_side(w)
    return jnp.concatenate([both, both], axis=0)


def right_square_t(w):
    high, low = halves(w)
    return jnp.concatenate(
        [jnp.concatenate([high, high], axis=1), jnp.concatenate([low, low], axis=1)], axis=0
    )


def plain_dot(left, right, dims=NN):
    return lax.dot_general(left, right, dims, preferred_element_type=F32)


def fold_right(values):
    lanes = values.shape[1] // 2
    return values[:, :lanes] + values[:, lanes:]


def fold_square(values):
    rows = values.shape[0] // 2
    return fold_right(values[:rows] + values[rows:])


def stacked(values):
    high = values.astype(jnp.bfloat16).astype(F32)
    return jnp.concatenate([high, values - high], axis=0).astype(jnp.bfloat16)


def skinny_dot(left, right, dims=NN):
    rows = left.shape[0]
    both = stacked(left)
    high, low = halves(right)
    values = plain_dot(both, high, dims) + plain_dot(both, low, dims)
    return values[:rows] + values[rows:]


def frame_outer(left, right):
    a_high = left.astype(jnp.bfloat16).astype(F32)
    b_high = right.astype(jnp.bfloat16).astype(F32)
    a_low = left - a_high
    b_low = right - b_high
    a = jnp.concatenate([a_high, a_high, a_low, a_low], axis=0).astype(jnp.bfloat16)
    b = jnp.concatenate([b_high, b_low, b_high, b_low], axis=0).astype(jnp.bfloat16)
    return plain_dot(a, b, TN)


def pad_rows(values):
    return jnp.concatenate([values, jnp.zeros((LANES - values.shape[0], values.shape[1]), values.dtype)], axis=0)


def column_order():
    q = lax.broadcasted_iota(jnp.int32, (LANES, LANES), 0)
    n = lax.broadcasted_iota(jnp.int32, (LANES, LANES), 1)
    source = (q // 16) * 16 + (q % 8) * 2 + (q // 8) % 2
    return (source == n).astype(jnp.bfloat16)


def live_frames(counts_ref):
    total = counts_ref[0]
    for clip in range(1, counts_ref.shape[0]):
        total = total + counts_ref[clip]
    return total


def place_of(counts_ref, frame):
    begin = jnp.int32(0)
    end = jnp.int32(0)
    for clip in range(counts_ref.shape[0]):
        end = end + counts_ref[clip]
        begin = jnp.where(frame >= end, end, begin)
    return frame - begin


def running_matrix(counts_ref, frames):
    after = lax.broadcasted_iota(jnp.int32, (frames, frames), 0)
    before = lax.broadcasted_iota(jnp.int32, (frames, frames), 1)
    begin = jnp.int32(0)
    matrix = jnp.zeros((frames, frames), F32)
    for clip in range(counts_ref.shape[0]):
        end = begin + counts_ref[clip]
        inside = (before >= begin) & (before <= after) & (after < end)
        matrix = matrix + jnp.where(inside, 1.0 / (after - begin + 1).astype(F32), 0.0)
        begin = end
    return matrix


def columns_up(values):
    spot = lax.broadcasted_iota(jnp.int32, values.shape, 1)
    return jnp.where(spot == 7, 0.0, pltpu.roll(values, 7, axis=1))


def columns_down(values):
    spot = lax.broadcasted_iota(jnp.int32, values.shape, 1)
    return jnp.where(spot == 0, 0.0, pltpu.roll(values, 1, axis=1))


def tile_sum(values):
    return jnp.sum(jnp.sum(values, axis=0), axis=0, keepdims=True)


def rows8(*rows):
    lanes = rows[0].shape[1]
    spot = lax.broadcasted_iota(jnp.int32, (8, lanes), 0)
    block = jnp.zeros((8, lanes), F32)
    for index, row in enumerate(rows):
        block = jnp.where(spot == index, row, block)
    return block


def pick_row(block, index):
    spot = lax.broadcasted_iota(jnp.int32, block.shape, 0)
    return jnp.sum(jnp.where(spot == index, block, 0.0), axis=0, keepdims=True)


def outer(left, right):
    return exact_dot(rows8(left), rows8(right), TN)


def row_dot(row, matrix, dims=NN):
    return exact_dot(rows8(row), matrix, dims)[0:1]


def clear_edges(ref):
    planes = ref.shape[1]
    edge = jnp.zeros((8, LANES), F32)
    for t in range(ref.shape[0]):
        for plane in range(planes):
            ref[t, plane, 0] = edge
            ref[t, plane, ref.shape[2] - 1] = edge


def spread_taps(taps_ref, w_ref):
    for tap in range(w_ref.shape[0]):
        w_ref[tap] = jnp.broadcast_to(taps_ref[0, tap : tap + 1, :], (8, LANES))


def conv_full(t, k, a_ref, w_ref, d_ref, fresh):
    weights = [w_ref[k * 9 + tap] for tap in range(9)]
    source = t - k
    rows = {}
    for i in range(SIDE):
        for need in (i, i + 1, i + 2):
            if need not in rows:
                rows[need] = [a_ref[source, plane, need] for plane in range(4)]
        even = None
        odd = None
        for r in range(3):
            a_even, a_odd, a_odd_down, a_even_up = rows[i + r]
            left, centre, right = weights[3 * r : 3 * r + 3]
            part_even = centre * a_even + right * a_odd + left * a_odd_down
            part_odd = centre * a_odd + left * a_even + right * a_even_up
            even = part_even if even is None else even + part_even
            odd = part_odd if odd is None else odd + part_odd
        rows.pop(i)
        at = t * FULL_ROWS + 2 * i
        if fresh:
            d_ref[at] = even
            d_ref[at + 1] = odd
        else:
            d_ref[at] = d_ref[at] + even
            d_ref[at + 1] = d_ref[at + 1] + odd


def conv_half(t, k, a_ref, w_ref, d_ref, fresh):
    weights = [w_ref[k * 9 + tap] for tap in range(9)]
    source = t - k
    carried = [a_ref[source, plane, 0] for plane in range(3)]
    for i in range(HALF_ROWS):
        rows = [carried]
        for need in (2 * i + 1, 2 * i + 2):
            rows.append([a_ref[source, plane, need] for plane in range(3)])
        carried = rows[2]
        total = None
        for r in range(3):
            a_even, a_odd, a_odd_down = rows[r]
            left, centre, right = weights[3 * r : 3 * r + 3]
            part = centre * a_even + right * a_odd + left * a_odd_down
            total = part if total is None else total + part
        at = t * HALF_ROWS + i
        d_ref[at] = total if fresh else d_ref[at] + total


def row_total(ref, lanes=None):
    values = ref[...] if lanes is None else ref[:, :, lanes]
    return jnp.sum(values, axis=0)


def send_all(send_ref, rows, lanes):
    count = rows.shape[0]

    def one(device, carry):
        send_ref[pl.ds(device, 1), 0:count, lanes] = rows[None]
        return carry

    lax.fori_loop(0, send_ref.shape[0], one, 0)


def stack_rows(*rows):
    return rows8(*rows)[0 : len(rows)]


def pick_thirds(order, values, dims, order_left):
    pieces = []
    rest = values
    for _ in range(3):
        piece = rest.astype(jnp.bfloat16)
        rest = rest - piece.astype(F32)
        args = (order, piece) if order_left else (piece, order)
        pieces.append(plain_dot(*args, dims))
    return pieces


def prepare_kernel(
    counts_ref, video_ref, cot_ref, w_ref, x_ref, rows_ref, columns_ref, cot_out_ref, gram_ref, send_ref
):
    order = column_order()
    total = live_frames(counts_ref)
    pixels = video_ref.shape[1]
    gram = jnp.zeros((2 * LANES, 2 * LANES), F32)
    summed = jnp.zeros((1, LANES), F32)
    for frame in range(pixels // 256):
        live = jnp.where(frame < total, 1.0, 0.0).astype(F32)
        for part in (2 * frame, 2 * frame + 1):
            at = slice(part * LANES, (part + 1) * LANES)
            block = pad_rows(video_ref[:, at] * live)
            high, middle, low = pick_thirds(order, block, NT, True)
            rows = high + middle + low
            x_ref[at, :] = rows
            rows_ref[at, :] = jnp.concatenate([high, middle], axis=1).astype(jnp.bfloat16)
            first, second, _ = pick_thirds(order, block, NT, False)
            columns_ref[:, at] = jnp.concatenate([first, second], axis=0).astype(jnp.bfloat16)
            summed = summed + jnp.sum(rows, axis=0, keepdims=True)
        at = slice(frame * 256, (frame + 1) * 256)
        gram = gram + plain_dot(columns_ref[:, at], rows_ref[at, :])
    gram = fold_square(gram)
    gram_ref[0:LANES, :] = gram
    gram_ref[LANES : LANES + 8, :] = rows8(summed)
    w = pad_rows(w_ref[0])
    width = w.shape[1]
    sums = stack_rows(row_dot(summed, w), jnp.sum(w * exact_dot(gram, w), axis=0, keepdims=True))
    count = jnp.full((2, LANES), 1.0, F32) * (total * (SIDE * SIDE)).astype(F32)
    send_all(send_ref, sums, slice(0, width))
    send_all(send_ref, count, slice(width, width + LANES))
    spot = lax.broadcasted_iota(jnp.int32, (LANES, LANES), 1)
    for part in range(cot_ref.shape[1] // LANES):
        at = slice(part * LANES, (part + 1) * LANES)
        frame = (spot + part * LANES) // (HALF_ROWS * 8)
        cot_out_ref[at, :] = jnp.where(frame < total, pad_rows(cot_ref[:, at]), 0.0).T


def moments_of(sums, count):
    average = sums[0:1] / count
    return (average, sums[1:2] / count - average * average)


def narrow_kernel(
    counts_ref, sums_ref, stat_ref, gram0_ref, x_ref, z_ref, ngain_ref, nbias_ref, w_ref,
    x1_ref, rows_ref, columns_ref, gram_ref, stat_out_ref, send_ref,
):
    total = live_frames(counts_ref)
    count = stat_ref[2:3, 0:LANES]
    average, variance = moments_of(row_total(sums_ref), count)
    factor = ngain_ref[0:1, :] * lax.rsqrt(variance + EPSILON)
    shift = nbias_ref[0:1, :] - factor * average
    stat_out_ref[...] = rows8(average, variance, count)
    frames = x_ref.shape[0] // 256

    def frame(t, carry):
        gram, cross, summed = carry
        at = pl.ds(pl.multiple_of(t * 256, 256), 256)
        z = z_ref[at, :]
        rows = (x_ref[at, :] + factor * z + shift) * live_value(t, total)
        x1_ref[at, :] = rows
        both = side_by_side(rows)
        rows_ref[at, :] = both
        columns = jnp.concatenate(halves(rows.T), axis=0)
        columns_ref[:, at] = columns
        gram = gram + plain_dot(columns, both)
        cross = cross + plain_dot(columns, side_by_side(z))
        return (gram, cross, summed + jnp.sum(rows, axis=0, keepdims=True))

    zero = jnp.zeros((2 * LANES, 2 * LANES), F32)
    gram, cross, summed = each_frame(frames, frame, (zero, zero, jnp.zeros((1, LANES), F32)))

    gram = fold_square(gram)
    tiles = LANES // 8
    gram_ref[0:tiles] = gram.reshape(tiles, 8, LANES)
    gram_ref[tiles : 2 * tiles] = fold_square(cross).reshape(tiles, 8, LANES)
    gram_ref[2 * tiles : 3 * tiles] = gram0_ref[0:LANES, :].reshape(tiles, 8, LANES)
    gram_ref[3 * tiles] = rows8(summed, gram0_ref[LANES : LANES + 1, :])
    w = pad_rows(w_ref[0])
    sums = stack_rows(row_dot(summed, w), jnp.sum(w * exact_dot(gram, w), axis=0, keepdims=True))
    send_all(send_ref, sums, slice(0, w.shape[1]))


def write_first(t, total, values, scale, shift, a_ref, planes):
    half_pre = values * scale + shift
    first = (half_pre + half_pre * half_tanh(half_pre)) * live_value(t, total)
    first = first.reshape(SIDE, 2, 8, LANES)
    even = first[:, 0]
    odd = first[:, 1]
    a_ref[t, 0, 1 : SIDE + 1] = even
    a_ref[t, 1, 1 : SIDE + 1] = odd
    if planes >= 3:
        a_ref[t, 2, 1 : SIDE + 1] = columns_down(odd)
    if planes >= 4:
        a_ref[t, 3, 1 : SIDE + 1] = columns_up(even)


def expand_kernel(
    block, counts_ref, sums_ref, count_ref, rows_ref, w_ref, gain_ref, bias_ref, taps_ref,
    e_ref, d_ref, stat_ref, send_ref, a_ref, taps8_ref,
):
    @pl.when(pl.program_id(0) == 0)
    def start():
        clear_edges(a_ref)

    total = live_frames(counts_ref)
    frames = a_ref.shape[0]
    count = count_ref[2:3, :] if block else row_total(count_ref)[0:1]
    average, variance = moments_of(row_total(sums_ref), count)
    stat_ref[...] = rows8(average, variance, count)
    norm_row = 2 * block
    scale = gain_ref[norm_row : norm_row + 1, :] * lax.rsqrt(variance + EPSILON)
    shift = 0.5 * (bias_ref[norm_row : norm_row + 1, :] - average * scale)
    scale = 0.5 * scale
    square = right_square(pad_rows(w_ref[0]))

    def expand(t, carry):
        at = pl.ds(pl.multiple_of(t * 256, 256), 256)
        values = fold_right(plain_dot(rows_ref[at, :], square)).reshape(FULL_ROWS, 8, LANES)
        e_ref[pl.ds(pl.multiple_of(t * FULL_ROWS, FULL_ROWS), FULL_ROWS)] = values
        write_first(t, total, values, scale, shift, a_ref, 3 if block else 4)
        return carry

    each_frame(frames, expand, 0)
    spread_taps(taps_ref, taps8_ref)
    per_frame = HALF_ROWS if block else FULL_ROWS
    conv = conv_half if block else conv_full

    def frame(t, carry):
        conv(t, 0, a_ref, taps8_ref, d_ref, True)
        last = jnp.minimum(place_of(counts_ref, t), LAGS - 1)

        def lag(k, inner):
            conv(t, k, a_ref, taps8_ref, d_ref, False)
            return inner

        lax.fori_loop(1, last + 1, lag, 0)
        values = d_ref[pl.ds(t * per_frame, per_frame)]
        return (carry[0] + jnp.sum(values, axis=0), carry[1] + jnp.sum(values * values, axis=0))

    zero = jnp.zeros((8, LANES), F32)
    summed, squares = lax.fori_loop(0, total, frame, (zero, zero))

    def dead(t, carry):
        d_ref[pl.ds(t * per_frame, per_frame)] = jnp.zeros((per_frame, 8, LANES), F32)
        return carry

    lax.fori_loop(total, frames, dead, 0)
    sums = stack_rows(jnp.sum(summed, axis=0, keepdims=True), jnp.sum(squares, axis=0, keepdims=True))
    send_all(send_ref, sums, slice(0, LANES))


def live_value(t, total):
    return jnp.where(t < total, 1.0, 0.0).astype(F32)


def each_frame(count, body, init, unroll=2):
    return lax.fori_loop(0, count, body, init, unroll=unroll)


def squeeze_forward_kernel(
    block, counts_ref, sums_ref, stat_ref, d_ref, gain_ref, bias_ref, down_ref, downb_ref, up_ref, upb_ref, proj_ref,
    cot_ref, z_ref, gates_ref, running_ref, pre_ref, stat_out_ref, send_ref, second_ref, pooled_ref,
):
    phase = pl.program_id(0)
    tile = pl.program_id(1)
    tiles = pl.num_programs(1)
    total = live_frames(counts_ref)
    per_frame = HALF_ROWS if block else FULL_ROWS
    pixels = per_frame * 8
    frames = second_ref.shape[1] // per_frame
    group = 256 // pixels
    chunks = frames // group
    norm_row = 2 * block + 1

    @pl.when(phase == 0)
    def activate():
        count = stat_ref[2:3, 0:LANES] * (0.25 if block else 1.0)
        average, variance = moments_of(row_total(sums_ref), count)
        stat_out_ref[...] = rows8(average, variance, count)
        scale = gain_ref[norm_row : norm_row + 1, :] * lax.rsqrt(variance + EPSILON)
        shift = 0.5 * (bias_ref[norm_row : norm_row + 1, :] - average * scale)
        scale = 0.5 * scale

        def chunk(index, carry):
            for inner in range(group):
                t = index * group + inner
                at = pl.ds(t * per_frame, per_frame)
                half_pre = d_ref[at] * scale + shift
                second = half_pre + half_pre * half_tanh(half_pre)
                second = second * live_value(t, total)
                second_ref[tile, at] = second
                pooled_ref[tile, pl.ds(t, 1), :] = tile_sum(second) * (1.0 / pixels)
            return carry

        each_frame(chunks, chunk, 0)

    @pl.when((phase == 1) & (tile == 0))
    def gate():
        matrix = running_matrix(counts_ref, frames)
        pooled = jnp.concatenate([pooled_ref[index] for index in range(pooled_ref.shape[0])], axis=1)
        running = exact_dot(matrix, pooled)
        running_ref[...] = running
        pre = skinny_dot(running, down_ref[0], NT) + downb_ref[block : block + 1, :]
        pre_ref[...] = pre
        gates_ref[...] = sigmoid(skinny_dot(pre * sigmoid(pre), up_ref[0]) + upb_ref[block : block + 1, :])
        z_ref[...] = jnp.zeros_like(z_ref)

    @pl.when(phase == 1)
    def project():
        square = right_square_t(pad_rows(proj_ref[0]))
        lanes = pl.ds(pl.multiple_of(tile * LANES, LANES), LANES)
        gates = gates_ref[:, lanes]

        def chunk(index, carry):
            parts = []
            for inner in range(group):
                t = index * group + inner
                second = second_ref[tile, pl.ds(t * per_frame, per_frame)].reshape(pixels, LANES)
                parts.append(second * pick_row(gates, t))
            excited = parts[0] if group == 1 else jnp.concatenate(parts, axis=0)
            at = pl.ds(pl.multiple_of(index * 256, 256), 256)
            z_ref[at, :] = z_ref[at, :] + fold_right(plain_dot(side_by_side(excited), square, NT))
            return carry

        each_frame(chunks, chunk, 0)

    @pl.when((phase == 1) & (tile == tiles - 1))
    def finish():
        def chunk(index, carry):
            at = pl.ds(pl.multiple_of(index * 256, 256), 256)
            z = z_ref[at, :].reshape(32, 8, LANES)
            values = [z, z * z]
            if block:
                dy = cot_ref[at, :].reshape(32, 8, LANES)
                values = values + [dy, dy * z]
            return tuple(old + jnp.sum(new, axis=0) for old, new in zip(carry, values))

        zero = jnp.zeros((8, LANES), F32)
        sums = each_frame(chunks, chunk, (zero,) * (4 if block else 2))
        rows = stack_rows(*(jnp.sum(value, axis=0, keepdims=True) for value in sums))
        send_all(send_ref, rows, slice(0, LANES))


def pack_tiles(narrow, squeeze):
    return narrow // 8 + 2 * (squeeze // 8) + 1


def squeeze_backward_body(
    block, counts_ref, stat_ref, d_ref, gain_ref, bias_ref, down_ref, up_ref, proj_ref, gates_ref, running_ref,
    pre_ref, dy2_ref, send_ref, pack_ref, dz3_ref, dz3t_ref, excited_ref, dexc_ref, dgate_ref, head,
):
    phase = pl.program_id(0)
    tile = pl.program_id(1)
    total = live_frames(counts_ref)
    per_frame = HALF_ROWS if block else FULL_ROWS
    pixels = per_frame * 8
    frames = dz3_ref.shape[0] // pixels
    group = 256 // pixels
    chunks = frames // group
    norm_row = 2 * block + 1
    tiles = dexc_ref.shape[0]
    narrow = proj_ref.shape[1]
    squeeze = down_ref.shape[1]
    per_tile = pack_tiles(narrow, squeeze)
    lanes = pl.ds(pl.multiple_of(tile * LANES, LANES), LANES)

    @pl.when((phase == 0) & (tile == 0))
    def start():
        head()

    average = stat_ref[0:1, :]
    root = lax.rsqrt(stat_ref[1:2, :] + EPSILON)
    scale = gain_ref[norm_row : norm_row + 1, :] * root
    shift = 0.5 * (bias_ref[norm_row : norm_row + 1, :] - average * scale)
    scale = 0.5 * scale
    gates = gates_ref[:, lanes]

    @pl.when(phase == 0)
    def excite():
        square = right_square(pad_rows(proj_ref[0]))

        def chunk(index, carry):
            flat = pl.ds(pl.multiple_of(index * 256, 256), 256)
            dexc = fold_right(plain_dot(dz3_ref[flat, :], square)).reshape(32, 8, LANES)
            dexc_ref[tile, pl.ds(pl.multiple_of(index * 32, 32), 32)] = dexc
            parts = []
            for inner in range(group):
                t = index * group + inner
                half_pre = d_ref[pl.ds(t * per_frame, per_frame)] * scale + shift
                second = half_pre + half_pre * half_tanh(half_pre)
                second = second * live_value(t, total)
                own = dexc[inner * per_frame : (inner + 1) * per_frame]
                dgate_ref[tile, pl.ds(t, 1), :] = tile_sum(own * second)
                parts.append(second.reshape(pixels, LANES) * pick_row(gates, t))
            excited = parts[0] if group == 1 else jnp.concatenate(parts, axis=0)
            excited_ref[flat, :] = side_by_side(excited)
            return carry

        each_frame(chunks, chunk, 0)
        dproj = fold_square(plain_dot(dz3t_ref[...], excited_ref[...]))
        pack_ref[pl.ds(tile * per_tile, narrow // 8)] = dproj[0:narrow].reshape(narrow // 8, 8, LANES)

    @pl.when((phase == 1) & (tile == 0))
    def squeeze_part():
        pre = pre_ref[...]
        half_pre = 0.5 * pre
        tanh = half_tanh(half_pre)
        squeezed = half_pre + half_pre * tanh
        all_gates = gates_ref[...]
        dgate = jnp.concatenate([dgate_ref[index] for index in range(tiles)], axis=1)
        du = dgate * all_gates * (1.0 - all_gates)
        dpre = skinny_dot(du, up_ref[0], NT) * silu_slope(half_pre, tanh)
        ddown = frame_outer(dpre, running_ref[...])
        dup = frame_outer(squeezed, du)
        dpre_row = jnp.sum(dpre, axis=0, keepdims=True)
        dpre_row = jnp.concatenate([dpre_row, jnp.zeros((1, du.shape[1] - squeeze), F32)], axis=1)
        biases = rows8(jnp.sum(du, axis=0, keepdims=True), dpre_row)
        for index in range(tiles):
            own = slice(index * LANES, (index + 1) * LANES)
            at = index * per_tile + narrow // 8
            pack_ref[at : at + squeeze // 8] = ddown[:, own].reshape(squeeze // 8, 8, LANES)
            at = at + squeeze // 8
            pack_ref[at : at + squeeze // 8] = dup[:, own].reshape(squeeze // 8, 8, LANES)
            pack_ref[at + squeeze // 8] = biases[:, own]
        drunning = skinny_dot(dpre, down_ref[0])
        dpooled = exact_dot(running_matrix(counts_ref, frames), drunning, TN) * (1.0 / pixels)
        for index in range(tiles):
            dgate_ref[index] = dpooled[:, index * LANES : (index + 1) * LANES]

    @pl.when(phase == 1)
    def slope():
        def chunk(index, carry):
            summed, cross = carry
            for inner in range(group):
                t = index * group + inner
                at = pl.ds(t * per_frame, per_frame)
                depth = d_ref[at]
                half_pre = depth * scale + shift
                dsecond = dexc_ref[tile, at] * pick_row(gates, t) + pick_row(dgate_ref[tile], t)
                dy = dsecond * silu_slope(half_pre, half_tanh(half_pre))
                dy = dy * live_value(t, total)
                dy2_ref[at] = dy
                summed = summed + jnp.sum(dy, axis=0)
                cross = cross + jnp.sum(dy * (depth - average), axis=0)
            return (summed, cross)

        zero = jnp.zeros((8, LANES), F32)
        summed, cross = each_frame(chunks, chunk, (zero, zero))
        rows = stack_rows(jnp.sum(summed, axis=0, keepdims=True), root * jnp.sum(cross, axis=0, keepdims=True))
        send_all(send_ref, rows, slice(0, LANES))


def squeeze_one_backward_kernel(
    counts_ref, third_ref, z_ref, cot_ref, ngain_ref, nbias_ref, stat_ref, d_ref, gain_ref, bias_ref, down_ref,
    up_ref, proj_ref, gates_ref, running_ref, pre_ref, act_ref, nsum_ref, dy2_ref, send_ref, pack_ref,
    dz3_ref, dz3t_ref, excited_ref, dexc_ref, dgate_ref,
):
    total = live_frames(counts_ref)
    pixels = HALF_ROWS * 8

    def head():
        count = stat_ref[2:3, :]
        sums = row_total(third_ref)
        mean, variance = moments_of(sums, count)
        root = lax.rsqrt(variance + EPSILON)
        gain = ngain_ref[1:2, :]
        bias_sum = sums[2:3, :]
        gain_sum = root * (sums[3:4, :] - mean * bias_sum)
        nsum_ref[...] = rows8(gain_sum, bias_sum, mean, variance)
        row = lax.broadcasted_iota(jnp.int32, z_ref.shape, 0) // pixels
        live = row < total
        normed = (z_ref[...] - mean) * root
        act = jnp.where(live, gain * normed + nbias_ref[1:2, :], 0.0)
        act_ref[...] = act.T[0 : act_ref.shape[0]]
        dz3 = gain * root * (cot_ref[...] - bias_sum / count - normed * (gain_sum / count))
        dz3 = jnp.where(live, dz3, 0.0)
        dz3_ref[...] = side_by_side(dz3)
        dz3t_ref[...] = jnp.concatenate(halves(dz3.T), axis=0)

    squeeze_backward_body(
        1, counts_ref, stat_ref, d_ref, gain_ref, bias_ref, down_ref, up_ref, proj_ref, gates_ref, running_ref,
        pre_ref, dy2_ref, send_ref, pack_ref, dz3_ref, dz3t_ref, excited_ref, dexc_ref, dgate_ref, head,
    )


def input_factors(sums, stat_ref, count, gain, w):
    root = lax.rsqrt(stat_ref[1:2, :] + EPSILON)
    factor = gain * root
    matrix = exact_dot(w * (factor * root * sums[1:2] / count), w, NT)
    return (matrix, row_dot(factor * sums[0:1] / count, w, NT))


def covariance(gram, summed, count):
    mean = summed / count
    return (mean, gram / count - outer(mean, mean))


def squeeze_zero_backward_kernel(
    counts_ref, top_ref, stat1_ref, gram_ref, nstat_ref, dxpre_ref, x1_ref, z_ref, ngain_ref, w_ref, gains_ref, q_one_ref,
    stat_ref, d_ref, gain_ref, bias_ref, down_ref, up_ref, proj_ref, gates_ref, running_ref, pre_ref,
    dx1_ref, nsum_ref, dy2_ref, send_ref, pack_ref, dz3_ref, dz3t_ref, excited_ref, dexc_ref, dgate_ref,
):
    total = live_frames(counts_ref)
    width = gains_ref.shape[1]

    def head():
        start = pack_tiles(proj_ref.shape[1], down_ref.shape[1]) * (width // LANES)
        pack_ref[start : start + q_one_ref.shape[0]] = q_one_ref[...]
        count = stat_ref[2:3, :]
        wide_count = jnp.broadcast_to(count[:, 0:1], (1, width))
        sums = row_total(top_ref, slice(0, width))
        extra = row_total(top_ref, slice(width, width + LANES))
        matrix, shift = input_factors(sums, stat1_ref, wide_count, gains_ref[2:3, :], pad_rows(w_ref[0]))
        mean = nstat_ref[0:1, :]
        root = lax.rsqrt(nstat_ref[1:2, :] + EPSILON)
        mean_x1 = gram_ref[3 * LANES : 3 * LANES + 1, :] / count
        cross = (gram_ref[LANES : 2 * LANES, :] - count * outer(mean_x1, mean)) * root
        gain_sum = extra[0:1] - jnp.sum(matrix * cross, axis=0, keepdims=True)
        bias_sum = extra[1:2] - count * shift
        nsum_ref[...] = rows8(gain_sum, bias_sum, mean, nstat_ref[1:2, :])
        factor = ngain_ref[0:1, :] * root
        square = right_square(matrix)
        bias_mean = bias_sum / count
        gain_mean = gain_sum / count

        def frame(t, carry):
            at = pl.ds(pl.multiple_of(t * 256, 256), 256)
            centred = side_by_side(x1_ref[at, :] - mean_x1)
            live = live_value(t, total)
            dx1 = (dxpre_ref[at, :] - fold_right(plain_dot(centred, square)) - shift) * live
            dx1_ref[at, :] = dx1
            normed = (z_ref[at, :] - mean) * root
            dz3 = factor * (dx1 - bias_mean - normed * gain_mean) * live
            dz3_ref[at, :] = side_by_side(dz3)
            dz3t_ref[:, at] = jnp.concatenate(halves(dz3.T), axis=0)
            return carry

        each_frame(dz3_ref.shape[0] // 256, frame, 0)

    squeeze_backward_body(
        0, counts_ref, stat_ref, d_ref, gain_ref, bias_ref, down_ref, up_ref, proj_ref, gates_ref, running_ref,
        pre_ref, dy2_ref, send_ref, pack_ref, dz3_ref, dz3t_ref, excited_ref, dexc_ref, dgate_ref, head,
    )

def back_full(t, k, a_ref, w_ref, z_ref, f_ref, dw_ref, fresh):
    weights = [w_ref[k * 9 + tap] for tap in range(9)]
    target = t - k
    sums = [None] * 9
    a_rows = {}
    z_rows = {}
    for i in range(SIDE):
        for need in (i, i + 1, i + 2):
            if need not in a_rows:
                a_rows[need] = [a_ref[target, plane, need] for plane in range(2)]
                z_rows[need] = [z_ref[t, plane, need] for plane in range(4)]
        even = None
        odd = None
        z_even, z_odd, z_odd_down, z_even_up = z_rows[i + 1]
        for r in range(3):
            b_even, b_odd, b_odd_down, b_even_up = z_rows[i + 2 - r]
            left, centre, right = weights[3 * r : 3 * r + 3]
            part_even = centre * b_even + right * b_odd_down + left * b_odd
            part_odd = centre * b_odd + right * b_even + left * b_even_up
            even = part_even if even is None else even + part_even
            odd = part_odd if odd is None else odd + part_odd
            a_even, a_odd = a_rows[i + r]
            pieces = (
                z_even_up * a_odd + z_odd * a_even,
                z_even * a_even + z_odd * a_odd,
                z_even * a_odd + z_odd_down * a_even,
            )
            for c in range(3):
                at = 3 * r + c
                sums[at] = pieces[c] if sums[at] is None else sums[at] + pieces[c]
        a_rows.pop(i)
        z_rows.pop(i)
        at = target * FULL_ROWS + 2 * i
        if fresh:
            f_ref[at] = even
            f_ref[at + 1] = odd
        else:
            f_ref[at] = f_ref[at] + even
            f_ref[at + 1] = f_ref[at + 1] + odd
    for tap in range(9):
        dw_ref[k * 9 + tap] = dw_ref[k * 9 + tap] + sums[tap]


def back_half(t, k, a_ref, w_ref, z_ref, f_ref, dw_ref, fresh):
    weights = [w_ref[k * 9 + tap] for tap in range(9)]
    target = t - k
    sums = [None] * 9

    def put(row, parity, value):
        at = target * FULL_ROWS + 2 * row + parity
        f_ref[at] = value if fresh else f_ref[at] + value

    carried = [a_ref[target, plane, 0] for plane in range(2)]
    here = [z_ref[t, plane, 0] for plane in range(2)]
    for i in range(HALF_ROWS):
        below = [z_ref[t, plane, i + 1] for plane in range(2)]
        dz, dz_up = here
        rows = [carried]
        for need in (2 * i + 1, 2 * i + 2):
            rows.append([a_ref[target, plane, need] for plane in range(2)])
        carried = rows[2]
        put(2 * i, 0, weights[4] * dz)
        put(2 * i, 1, weights[5] * dz + weights[3] * dz_up)
        put(2 * i + 1, 0, weights[7] * dz + weights[1] * below[0])
        put(
            2 * i + 1,
            1,
            weights[8] * dz + weights[6] * dz_up + (weights[2] * below[0] + weights[0] * below[1]),
        )
        for r in range(3):
            a_even, a_odd = rows[r]
            pieces = (dz_up * a_odd, dz * a_even, dz * a_odd)
            for c in range(3):
                at = 3 * r + c
                sums[at] = pieces[c] if sums[at] is None else sums[at] + pieces[c]
        here = below
    for tap in range(9):
        dw_ref[k * 9 + tap] = dw_ref[k * 9 + tap] + sums[tap]


def depth_backward_kernel(
    block, before, final, counts_ref, grads_ref, stat2_ref, stat_ref, nstat_ref, dy2_ref, d_ref, e_ref, columns_ref, w_ref,
    gain_ref, bias_ref, taps_ref, z3_ref, dx_in_ref, sums_in_ref, dxpre_ref, send_ref, q_ref, grad_rows_ref,
    a_ref, z_ref, f_ref, taps8_ref, dw_ref, pair_ref,
):
    tile = pl.program_id(0)
    tiles = pl.num_programs(0)
    total = live_frames(counts_ref)
    frames = a_ref.shape[0]
    norm_row = 2 * block
    half = block == 1
    per_frame = HALF_ROWS if half else FULL_ROWS
    taps = dw_ref.shape[0]

    @pl.when(tile == 0)
    def start():
        clear_edges(a_ref)
        clear_edges(z_ref)
        if before:
            dxpre_ref[...] = dx_in_ref[...]
            send_all(send_ref, sums_in_ref[0:2, :], slice(0, before * LANES))
        else:
            dxpre_ref[...] = jnp.zeros_like(dxpre_ref)

        def dead(t, carry):
            f_ref[pl.ds(t * FULL_ROWS, FULL_ROWS)] = jnp.zeros((FULL_ROWS, 8, LANES), F32)
            return carry

        lax.fori_loop(total, frames, dead, 0)

    count = stat2_ref[2:3, :]
    grads = row_total(grads_ref)
    grad_rows_ref[...] = rows8(grads[0:1], grads[1:2])
    average = stat2_ref[0:1, :]
    root = lax.rsqrt(stat2_ref[1:2, :] + EPSILON)
    scale_two = gain_ref[norm_row + 1 : norm_row + 2, :] * root
    slope = scale_two * root * grads[1:2] / count
    level = scale_two * grads[0:1] / count - slope * average
    average_one = stat_ref[0:1, :]
    root_one = lax.rsqrt(stat_ref[1:2, :] + EPSILON)
    scale_one = gain_ref[norm_row : norm_row + 1, :] * root_one
    shift_half = 0.5 * (bias_ref[norm_row : norm_row + 1, :] - average_one * scale_one)
    scale_half = 0.5 * scale_one

    def fill(t, carry):
        at = pl.ds(t * per_frame, per_frame)
        dz = scale_two * dy2_ref[at] - (slope * d_ref[at] + level)
        if half:
            z_ref[t, 0, 0:HALF_ROWS] = dz
            z_ref[t, 1, 0:HALF_ROWS] = columns_up(dz)
        else:
            pair = dz.reshape(SIDE, 2, 8, LANES)
            z_ref[t, 0, 1 : SIDE + 1] = pair[:, 0]
            z_ref[t, 1, 1 : SIDE + 1] = pair[:, 1]
            z_ref[t, 2, 1 : SIDE + 1] = columns_down(pair[:, 1])
            z_ref[t, 3, 1 : SIDE + 1] = columns_up(pair[:, 0])
        values = e_ref[pl.ds(pl.multiple_of(t * FULL_ROWS, FULL_ROWS), FULL_ROWS)]
        write_first(t, total, values, scale_half, shift_half, a_ref, 2)
        return carry

    each_frame(frames, fill, 0)
    spread_taps(taps_ref, taps8_ref)
    dw_ref[...] = jnp.zeros_like(dw_ref)
    back = back_half if half else back_full

    def frame(t, carry):
        back(t, 0, a_ref, taps8_ref, z_ref, f_ref, dw_ref, True)
        last = jnp.minimum(place_of(counts_ref, t), LAGS - 1)

        def lag(k, inner):
            back(t, k, a_ref, taps8_ref, z_ref, f_ref, dw_ref, False)
            return inner

        return lax.fori_loop(1, last + 1, lag, carry)

    lax.fori_loop(0, total, frame, 0)
    square = right_square_t(pad_rows(w_ref[0]))

    def finish(t, carry):
        rows = pl.ds(pl.multiple_of(t * FULL_ROWS, FULL_ROWS), FULL_ROWS)
        flat = pl.ds(pl.multiple_of(t * 256, 256), 256)
        values = e_ref[rows]
        half_pre = values * scale_half + shift_half
        dy = f_ref[rows] * silu_slope(half_pre, half_tanh(half_pre))
        summed = carry[0] + jnp.sum(dy, axis=0)
        cross = carry[1] + jnp.sum(dy * (values - average_one), axis=0)
        dy = dy.reshape(256, LANES)
        pair_ref[flat, :] = side_by_side(dy)
        scaled = side_by_side(dy * scale_one)
        dxpre_ref[flat, :] = dxpre_ref[flat, :] + fold_right(plain_dot(scaled, square, NT))
        return (summed, cross)

    zero = jnp.zeros((8, LANES), F32)
    summed, cross = each_frame(frames, finish, (zero, zero))
    rows = stack_rows(jnp.sum(summed, axis=0, keepdims=True), root_one * jnp.sum(cross, axis=0, keepdims=True))
    if final:
        send_all(send_ref, rows, pl.ds(pl.multiple_of((tile + before) * LANES, LANES), LANES))
    else:
        send_ref[...] = rows8(rows[0:1], rows[1:2])
    gathered = fold_square(plain_dot(columns_ref[...], pair_ref[...]))
    narrow = w_ref.shape[1]
    dtaps = jnp.sum(dw_ref[...], axis=1)
    unused = (-taps) % 8
    dtaps = jnp.concatenate([dtaps, jnp.zeros((unused, LANES), F32)], axis=0)
    q_ref[0 : narrow // 8] = gathered[0:narrow].reshape(narrow // 8, 8, LANES)
    q_ref[narrow // 8 :] = dtaps.reshape((taps + unused) // 8, 8, LANES)

    if half:
        @pl.when(tile == tiles - 1)
        def tail():
            mean = nstat_ref[0:1, :]
            root_three = lax.rsqrt(nstat_ref[1:2, :] + EPSILON)

            def part(t, carry):
                flat = pl.ds(pl.multiple_of(t * 256, 256), 256)
                dx = dxpre_ref[flat, :].reshape(32, 8, LANES)
                normed = ((z3_ref[flat, :] - mean) * root_three).reshape(32, 8, LANES)
                return (carry[0] + jnp.sum(dx * normed, axis=0), carry[1] + jnp.sum(dx, axis=0))

            cross_three, summed_three = each_frame(frames, part, (zero, zero))
            rows = stack_rows(
                jnp.sum(cross_three, axis=0, keepdims=True), jnp.sum(summed_three, axis=0, keepdims=True)
            )
            width = send_ref.shape[2] - LANES
            send_all(send_ref, rows, slice(width, width + LANES))


def finish_kernel(
    counts_ref, momentum_ref, gram_ref, stat01_ref, stat02_ref, stat11_ref, stat12_ref, grad0_ref,
    grad1_ref, one_ref, zero_ref, nsum0_ref, nsum1_ref, dxpre_ref, x_ref, dx1_ref, w_ref, gain_ref, means_ref, vars_ref,
    nmeans_ref, nvars_ref,
    video_ref, less_ref, factor_ref, wgain_ref, wbias_ref, ngain_ref, nbias_ref, newm_ref, newv_ref, newnm_ref, newnv_ref,
):
    total = live_frames(counts_ref)
    full = stat01_ref[2:3, :]
    count = full[:, 0:LANES]
    width = full.shape[1]
    top_zero = row_total(zero_ref)
    top_one = row_total(one_ref, slice(0, width))
    w_zero = pad_rows(w_ref[0])
    matrix, shift = input_factors(top_zero, stat01_ref, full, gain_ref[0:1, :], w_zero)
    square = right_square(matrix)
    mean_x, cov_zero = covariance(
        gram_ref[2 * LANES : 3 * LANES, :], gram_ref[3 * LANES + 1 : 3 * LANES + 2, :], count
    )
    order = column_order()
    narrow = video_ref.shape[0]

    def frame(t, carry):
        at = pl.ds(pl.multiple_of(t * 256, 256), 256)
        centred = side_by_side(x_ref[at, :] - mean_x)
        dx = (dxpre_ref[at, :] - fold_right(plain_dot(centred, square)) - shift) * live_value(t, total) + dx1_ref[at, :]
        for part in range(2):
            own = dx[part * LANES : (part + 1) * LANES].T[0:narrow]
            pieces = pick_thirds(order, own, NN, False)
            start = pl.multiple_of(t * 256 + part * LANES, LANES)
            video_ref[:, pl.ds(start, LANES)] = pieces[0] + pieces[1] + pieces[2]
        return carry

    each_frame(x_ref.shape[0] // 256, frame, 0)
    mean_one, cov_one = covariance(gram_ref[0:LANES, :], gram_ref[3 * LANES : 3 * LANES + 1, :], count)
    plan = ((mean_x, cov_zero, stat01_ref, top_zero, w_zero), (mean_one, cov_one, stat11_ref, top_one, pad_rows(w_ref[1])))
    for block, (mean_row, cov, stat_ref, top, w) in enumerate(plan):
        root = lax.rsqrt(stat_ref[1:2, :] + EPSILON)
        factor = gain_ref[2 * block : 2 * block + 1, :] * root
        less = outer(mean_row, top[0:1]) + exact_dot(cov, w) * (root * top[1:2])
        less_ref[block] = (less * factor)[0:narrow]
        factor_ref[8 * block : 8 * block + 8, :] = rows8(factor)
    momentum = momentum_ref[0].astype(F32) / 10.0
    wgain_ref[...] = stack_rows(top_zero[1:2], grad0_ref[1:2, :], top_one[1:2], grad1_ref[1:2, :])
    wbias_ref[...] = stack_rows(top_zero[0:1], grad0_ref[0:1, :], top_one[0:1], grad1_ref[0:1, :])
    stats = (stat01_ref, stat02_ref, stat11_ref, stat12_ref)
    means = stack_rows(*(ref[0:1, :] for ref in stats))
    variances = stack_rows(*(ref[1:2, :] * (ref[2:3, :] / (ref[2:3, :] - 1.0)) for ref in stats))
    newm_ref[...] = (1.0 - momentum) * means_ref[...] + momentum * means
    newv_ref[...] = (1.0 - momentum) * vars_ref[...] + momentum * variances
    ngain_ref[...] = stack_rows(nsum0_ref[0:1, :], nsum1_ref[0:1, :])[:, 0:narrow]
    nbias_ref[...] = stack_rows(nsum0_ref[1:2, :], nsum1_ref[1:2, :])[:, 0:narrow]
    means = stack_rows(nsum0_ref[2:3, :], nsum1_ref[2:3, :])[:, 0:narrow]
    quarter = 0.25 * count
    variances = stack_rows(
        nsum0_ref[3:4, :] * (count / (count - 1.0)), nsum1_ref[3:4, :] * (quarter / (quarter - 1.0))
    )[:, 0:narrow]
    newnm_ref[...] = (1.0 - momentum) * nmeans_ref[...] + momentum * means
    newnv_ref[...] = (1.0 - momentum) * nvars_ref[...] + momentum * variances


def gradient_kernel(
    pack0_ref, pack1_ref, late_ref, less_ref, factor_ref,
    dw_ref, dtaps_ref, ddown_ref, dup_ref, dproj_ref, dupb_ref, ddownb_ref,
):
    narrow = dw_ref.shape[1]
    taps = dtaps_ref.shape[1]
    squeeze = ddown_ref.shape[1]
    tiles = dw_ref.shape[2] // LANES
    per_pack = pack_tiles(narrow, squeeze)
    per_tile = narrow // 8 + -(-taps // 8)
    first = tiles - tiles // 2
    share = -(-first * per_tile // late_ref.shape[0])
    share_b = late_ref.shape[1] - share

    def late_rows(tile):
        begin, size, skip = (tile * per_tile, share, 0) if tile < first else ((tile - first) * per_tile, share_b, share)
        places = range(begin, begin + per_tile)
        return jnp.concatenate([late_ref[place // size, skip + place % size] for place in places], axis=0)

    def rows_of(ref, at, rows):
        count = -(-rows // 8)
        return ref[at : at + count].reshape(count * 8, LANES)[0:rows]

    for block, ref in enumerate((pack0_ref, pack1_ref)):
        down_rows = []
        for tile in range(tiles):
            lanes = slice(tile * LANES, (tile + 1) * LANES)
            at = tile * per_pack
            dproj_ref[block, :, lanes] = rows_of(ref, at, narrow)
            at = at + narrow // 8
            ddown_ref[block, :, lanes] = rows_of(ref, at, squeeze)
            at = at + squeeze // 8
            dup_ref[block, :, lanes] = rows_of(ref, at, squeeze)
            biases = ref[at + squeeze // 8]
            dupb_ref[block : block + 1, lanes] = biases[0:1]
            down_rows.append(biases[1:2])
            if block:
                values = rows_of(pack0_ref, per_pack * tiles + tile * per_tile, per_tile * 8)
            else:
                values = late_rows(tile)
            dw = values[0:narrow] * factor_ref[8 * block : 8 * block + 1, lanes] - less_ref[block, :, lanes]
            dw_ref[block, :, lanes] = dw
            dtaps_ref[block, :, lanes] = values[narrow : narrow + taps]
        ddownb_ref[block : block + 1, :] = jnp.concatenate(down_rows, axis=1)[:, 0:squeeze]


AXES = ("dp", "rep")


def exchange(send):
    return lax.all_to_all(send, AXES, 0, 0, tiled=True)


def after(values, *others):
    return lax.optimization_barrier((values,) + others)


def share_out(tiles):
    devices = lax.axis_size("dp") * lax.axis_size("rep")
    return exchange(tiles.reshape(devices, tiles.shape[0] // devices, *tiles.shape[1:]))


def share_back(pieces):
    own = jnp.sum(pieces, axis=0)
    everyone = exchange(jnp.broadcast_to(own[None], pieces.shape))
    return everyone.reshape(-1, *pieces.shape[2:])


def shape(*dims, kind=F32):
    return jax.ShapeDtypeStruct(dims, kind)


def whole(array):
    rank = len(array.shape)
    return pl.BlockSpec(array.shape, lambda *ids: (0,) * rank)


SCALARS = pl.BlockSpec(memory_space=pltpu.SMEM)


def call(kernel, grid, in_specs, out_specs, out_shape, scratch, args, micros=10):
    return pl.pallas_call(
        kernel,
        grid=grid,
        in_specs=in_specs,
        out_specs=out_specs,
        out_shape=out_shape,
        scratch_shapes=scratch,
        compiler_params=pltpu.CompilerParams(vmem_limit_bytes=VMEM_BYTES),
        cost_estimate=pl.CostEstimate(
            flops=micros * 1_000_000_000, bytes_accessed=micros * 3_000_000, transcendentals=0
        ),
    )(*args)


def simple_call(kernel, scalars, args, outs):
    return call(
        kernel, (1,), [SCALARS] * scalars + [whole(array) for array in args[scalars:]], [whole(item) for item in outs],
        outs, [], args,
    )


def local(
    video, frame_counts, momentum_index, expand_weight, wide_gains, wide_biases, narrow_gains, narrow_biases, depth_weight,
    squeeze_weight, squeeze_bias, excite_weight, excite_bias, project_weight, wide_means, wide_variances, narrow_means,
    narrow_variances, cotangent,
):
    devices = lax.axis_size("dp") * lax.axis_size("rep")
    cin, pixels = video.shape
    half_pixels = cotangent.shape[1]
    width = expand_weight.shape[1]
    squeeze = squeeze_weight.shape[1]
    frames = pixels // (SIDE * SIDE)
    tiles = width // LANES
    taps = depth_weight.shape[1]
    w_t = jnp.swapaxes(expand_weight, 1, 2)
    up_t = jnp.swapaxes(excite_weight, 1, 2)
    lanes_pad = ((0, 0), (0, LANES - cin))
    ngains = jnp.pad(narrow_gains, lanes_pad)
    nbiases = jnp.pad(narrow_biases, lanes_pad)
    full_rows = frames * FULL_ROWS
    half_rows = frames * HALF_ROWS
    low = jnp.bfloat16

    def round_up(count):
        return -(-count // devices) * devices

    def fixed(*dims):
        return pl.BlockSpec(dims, lambda *ids: (0,) * len(dims))

    def tile_rows(rows):
        return pl.BlockSpec((rows, LANES), lambda j: (0, j))

    def tile_cube(rows):
        return pl.BlockSpec((rows, 8, LANES), lambda j: (0, 0, j))

    def tile_sums(rows=2):
        return pl.BlockSpec((devices, rows, LANES), lambda j: (0, 0, j))

    def weight_tile(block, rows):
        return pl.BlockSpec((1, rows, LANES), lambda j, block=block: (block, 0, j))

    def of_block(block, rows, lanes):
        return pl.BlockSpec((1, rows, lanes), lambda *ids: (block, 0, 0))

    def early(make):
        return make(lambda p, j: j * (1 - p) + (tiles - 1) * p)

    def late(make):
        return make(lambda p, j: j * p)

    def both(make):
        return make(lambda p, j: j)

    def rows_at(rows):
        return lambda at: pl.BlockSpec((rows, LANES), lambda p, j: (0, at(p, j)))

    def cube_at(rows):
        return lambda at: pl.BlockSpec((rows, 8, LANES), lambda p, j: (0, 0, at(p, j)))

    def sums_at(rows):
        return lambda at: pl.BlockSpec((devices, rows, LANES), lambda p, j: (0, 0, at(p, j)))

    def weight_at(block, rows):
        return lambda at: pl.BlockSpec((1, rows, LANES), lambda p, j: (block, 0, at(p, j)))

    x, x_rows, x_columns, cot, gram_zero, sums = call(
        prepare_kernel, (1,), [SCALARS, whole(video), whole(cotangent), of_block(0, cin, width)],
        [fixed(pixels, LANES), fixed(pixels, 2 * LANES), fixed(2 * LANES, pixels), fixed(half_pixels, LANES),
         fixed(LANES + 8, LANES), fixed(devices, 2, width + LANES)],
        [shape(pixels, LANES), shape(pixels, 2 * LANES, kind=low), shape(2 * LANES, pixels, kind=low),
         shape(half_pixels, LANES), shape(LANES + 8, LANES), shape(devices, 2, width + LANES)],
        [], (frame_counts, video, cotangent, w_t),
    )
    sums = exchange(sums)

    def expand(block, sums, count, count_spec, rows):
        depth_rows = half_rows if block else full_rows
        return call(
            functools.partial(expand_kernel, block), (tiles,),
            [SCALARS, tile_sums(), count_spec, whole(rows), weight_tile(block, cin), tile_rows(4), tile_rows(4),
             weight_tile(block, taps)],
            [tile_cube(full_rows), tile_cube(depth_rows), tile_rows(8), tile_sums()],
            [shape(full_rows, 8, width), shape(depth_rows, 8, width), shape(8, width), shape(devices, 2, width)],
            [pltpu.VMEM((frames, 4, SIDE + 2, 8, LANES), F32), pltpu.VMEM((taps, 8, LANES), F32)],
            (frame_counts, sums, count, rows, w_t, wide_gains, wide_biases, depth_weight),
        )

    count_spec = pl.BlockSpec((devices, 2, LANES), lambda j: (0, 0, tiles))
    e_zero, d_zero, stat01, sums = expand(0, sums, sums, count_spec, x_rows)
    sums = exchange(sums)

    def squeeze_forward(block, sums, stat, depth):
        rows = half_rows if block else full_rows
        kinds = 4 if block else 2
        return call(
            functools.partial(squeeze_forward_kernel, block), (2, tiles),
            [SCALARS, early(sums_at(2)), early(rows_at(8)), early(cube_at(rows)), early(rows_at(4)), early(rows_at(4)),
             of_block(block, squeeze, width), whole(squeeze_bias), of_block(block, squeeze, width), whole(excite_bias),
             late(weight_at(block, cin)), whole(cot)],
            [fixed(rows * 8, LANES), fixed(8, width), fixed(8, width), fixed(8, squeeze), early(rows_at(8)),
             fixed(devices, kinds, LANES)],
            [shape(rows * 8, LANES), shape(8, width), shape(8, width), shape(8, squeeze), shape(8, width),
             shape(devices, kinds, LANES)],
            [pltpu.VMEM((tiles, rows, 8, LANES), F32), pltpu.VMEM((tiles, frames, LANES), F32)],
            (frame_counts, sums, stat, depth, wide_gains, wide_biases, squeeze_weight, squeeze_bias, up_t, excite_bias,
             project_weight, cot),
        )

    z_zero, gates_zero, running_zero, pre_zero, stat02, sums = squeeze_forward(0, sums, stat01, d_zero)
    sums = exchange(sums)
    narrow_args = (frame_counts, sums, stat01, gram_zero, x, z_zero, ngains, nbiases, w_t)
    narrow_outs = [
        shape(pixels, LANES), shape(pixels, 2 * LANES, kind=low), shape(2 * LANES, pixels, kind=low),
        shape(round_up(3 * LANES // 8 + 1), 8, LANES), shape(8, LANES), shape(devices, 2, width),
    ]
    x1, x1_rows, x1_columns, gram, nstat, sums = call(
        narrow_kernel, (1,), [SCALARS] + [whole(array) for array in narrow_args[1:-1]] + [of_block(1, cin, width)],
        [whole(item) for item in narrow_outs], narrow_outs, [], narrow_args,
    )
    sums, gram = after(exchange(sums), gram)
    gram = share_out(gram)
    e_one, d_one, stat11, sums = expand(1, sums, nstat, pl.BlockSpec((8, LANES), lambda j: (0, 0)), x1_rows)
    sums, gram = after(exchange(sums), gram)
    gram = share_back(gram).reshape(-1, LANES)
    z_one, gates_one, running_one, pre_one, stat12, sums = squeeze_forward(1, sums, stat11, d_one)
    third = exchange(sums)
    q_tiles = cin // 8 + -(-taps // 8)

    def backward_specs(block):
        rows = half_rows if block else full_rows
        ins = [both(rows_at(8)), both(cube_at(rows)), both(rows_at(4)), both(rows_at(4)), of_block(block, squeeze, width),
               of_block(block, squeeze, width), early(weight_at(block, cin)), fixed(8, width), fixed(8, width),
               fixed(8, squeeze)]
        packed = round_up(tiles * (pack_tiles(cin, squeeze) + (0 if block else q_tiles)))
        outs = [fixed(8, LANES), late(cube_at(rows)), late(sums_at(2)), fixed(packed, 8, LANES)]
        shapes = [shape(8, LANES), shape(rows, 8, width), shape(devices, 2, width), shape(packed, 8, LANES)]
        scratch = [pltpu.VMEM((rows * 8, 2 * LANES), low), pltpu.VMEM((2 * LANES, rows * 8), low),
                   pltpu.VMEM((rows * 8, 2 * LANES), low), pltpu.VMEM((tiles, rows, 8, LANES), F32),
                   pltpu.VMEM((tiles, frames, LANES), F32)]
        return (ins, outs, shapes, scratch)

    ins, outs, shapes, scratch = backward_specs(1)
    activations, nsum_one, dy2_one, sums, pack_one = call(
        squeeze_one_backward_kernel, (2, tiles),
        [SCALARS, whole(third), whole(z_one), whole(cot), whole(ngains), whole(nbiases)] + ins,
        [fixed(cin, half_pixels)] + outs, [shape(cin, half_pixels)] + shapes, scratch,
        (frame_counts, third, z_one, cot, ngains, nbiases, stat12, d_one, wide_gains, wide_biases, squeeze_weight, up_t,
         project_weight, gates_one, running_one, pre_one),
    )
    sums, pack_one = after(exchange(sums), pack_one)
    pack_one = share_out(pack_one)
    nothing = jnp.zeros((8, LANES), F32)

    def depth_backward(block, begin, end, sums, stat2, stat, dy2, depth, expanded, columns, dx_in, sums_in):
        rows = half_rows if block else full_rows
        z_shape = (frames, 2, HALF_ROWS + 1, 8, LANES) if block else (frames, 4, SIDE + 2, 8, LANES)
        count = end - begin
        final = end == tiles
        listed = count * q_tiles if block else round_up(count * q_tiles)
        if final:
            send = (devices, 2, width + (LANES if block else 0))
            send_spec = fixed(*send)
        else:
            send = (8, count * LANES)
            send_spec = tile_rows(8)

        def wide_rows(rows):
            return pl.BlockSpec((rows, LANES), lambda j: (0, j + begin))

        def wide_cube(rows):
            return pl.BlockSpec((rows, 8, LANES), lambda j: (0, 0, j + begin))

        def wide_weight(rows):
            return pl.BlockSpec((1, rows, LANES), lambda j: (block, 0, j + begin))

        return call(
            functools.partial(depth_backward_kernel, block, begin, final), (count,),
            [SCALARS, pl.BlockSpec((devices, 2, LANES), lambda j: (0, 0, j + begin)), wide_rows(8), wide_rows(8), whole(nstat),
             wide_cube(rows), wide_cube(rows), wide_cube(full_rows), whole(columns), wide_weight(cin), wide_rows(4),
             wide_rows(4), wide_weight(taps), whole(z_zero), whole(dx_in), whole(sums_in)],
            [fixed(pixels, LANES), send_spec, pl.BlockSpec((q_tiles, 8, LANES), lambda j: (j, 0, 0)), tile_rows(8)],
            [shape(pixels, LANES), shape(*send), shape(listed, 8, LANES), shape(8, count * LANES)],
            [pltpu.VMEM((frames, 2, SIDE + 2, 8, LANES), F32), pltpu.VMEM(z_shape, F32), pltpu.VMEM((full_rows, 8, LANES), F32),
             pltpu.VMEM((taps, 8, LANES), F32), pltpu.VMEM((taps, 8, LANES), F32), pltpu.VMEM((pixels, 2 * LANES), low)],
            (frame_counts, sums, stat2, stat, nstat, dy2, depth, expanded, columns, w_t, wide_gains, wide_biases,
             depth_weight, z_zero, dx_in, sums_in),
            20,
        )

    dxpre_one, sums, q_one, grad_one = depth_backward(
        1, 0, tiles, sums, stat12, stat11, dy2_one, d_one, e_one, x1_columns, nothing, nothing
    )
    top_one, pack_one = after(exchange(sums), pack_one)
    pack_one = share_back(pack_one)
    ins, outs, shapes, scratch = backward_specs(0)
    dx1, nsum_zero, dy2_zero, sums, pack_zero = call(
        squeeze_zero_backward_kernel, (2, tiles),
        [SCALARS, whole(top_one), whole(stat11), whole(gram), whole(nstat), whole(dxpre_one), whole(x1), whole(z_zero),
         whole(ngains), of_block(1, cin, width), whole(wide_gains), whole(q_one)] + ins,
        [fixed(pixels, LANES)] + outs, [shape(pixels, LANES)] + shapes, scratch,
        (frame_counts, top_one, stat11, gram, nstat, dxpre_one, x1, z_zero, ngains, w_t, wide_gains, q_one, stat02, d_zero,
         wide_gains, wide_biases, squeeze_weight, up_t, project_weight, gates_zero, running_zero, pre_zero),
    )
    sums, pack_zero, pack_one = after(exchange(sums), pack_zero, pack_one)
    pack_zero = share_out(pack_zero)
    first = tiles - tiles // 2
    dxpre_zero, sums_in, late_a, grad_a = depth_backward(
        0, 0, first, sums, stat02, stat01, dy2_zero, d_zero, e_zero, x_columns, nothing, nothing
    )
    dxpre_zero, late_a, pack_zero = after(dxpre_zero, late_a, pack_zero)
    late_a = share_out(late_a)
    pack_zero = share_back(pack_zero)
    dxpre_zero, sums, late_b, grad_b = depth_backward(
        0, first, tiles, sums, stat02, stat01, dy2_zero, d_zero, e_zero, x_columns, dxpre_zero, sums_in
    )
    grad_zero = jnp.concatenate([grad_a, grad_b], axis=1)
    top_zero, late_a, pack_zero = after(exchange(sums), late_a, pack_zero)
    shares = jnp.concatenate([jnp.sum(late_a, axis=0), jnp.sum(share_out(late_b), axis=0)], axis=0)
    late = exchange(jnp.broadcast_to(shares[None], (devices,) + shares.shape))
    final_args = (
        frame_counts, momentum_index, gram, stat01, stat02, stat11, stat12, grad_zero, grad_one, top_one,
        top_zero, nsum_zero, nsum_one, dxpre_zero, x, dx1, w_t, wide_gains, wide_means, wide_variances, narrow_means,
        narrow_variances,
    )
    final_outs = [
        shape(cin, pixels), shape(2, cin, width), shape(16, width), shape(4, width), shape(4, width), shape(2, cin),
        shape(2, cin), shape(4, width), shape(4, width), shape(2, cin), shape(2, cin),
    ]
    video_grad, less, factor, wgain, wbias, ngain, nbias, newm, newv, newnm, newnv = simple_call(
        finish_kernel, 2, final_args, final_outs
    )
    dw_t, dtaps, ddown, dup, dproj, dupb, ddownb = simple_call(
        gradient_kernel, 0, (pack_zero, pack_one, late, less, factor),
        [shape(2, cin, width), shape(2, taps, width), shape(2, squeeze, width), shape(2, squeeze, width),
         shape(2, cin, width), shape(2, width), shape(2, squeeze)],
    )
    return (
        activations, video_grad, jnp.swapaxes(dw_t, 1, 2), wgain, wbias, ngain, nbias, dtaps, ddown, ddownb,
        jnp.swapaxes(dup, 1, 2), dupb, dproj, newm, newv, newnm, newnv,
    )


def solution(mesh):
    split = P(None, AXES)
    placed = (split, P(AXES)) + (P(),) * 16 + (split,)
    return jax.shard_map(
        local, mesh=mesh, in_specs=placed, out_specs=(split, split) + (P(),) * 15, check_vma=False
    )
```

```python
import functools

import jax
import jax.numpy as jnp
from jax import lax
from jax.experimental import pallas as pl
from jax.experimental.pallas import tpu as pltpu
from jax.sharding import PartitionSpec as P

SIDE = 16
LANES = 128
LAGS = 5
FULL_ROWS = 2 * SIDE
HALF_ROWS = SIDE // 2
EPSILON = 1e-05
HIGHEST = lax.Precision.HIGHEST
F32 = jnp.float32
NN = (((1,), (0,)), ((), ()))
NT = (((1,), (1,)), ((), ()))
TN = (((0,), (0,)), ((), ()))
VMEM_BYTES = 52 * 1024 * 1024


def half_tanh(half_values):
    return jnp.tanh(half_values)


def sigmoid(values):
    return 0.5 * jnp.tanh(0.5 * values) + 0.5


def silu_slope(half_values, tanh):
    return 0.5 * (1.0 + tanh + half_values * (1.0 - tanh * tanh))


def exact_dot(left, right, dims=NN):
    return lax.dot_general(left, right, dims, precision=HIGHEST, preferred_element_type=F32)


def halves(values):
    high = values.astype(jnp.bfloat16)
    return (high, (values - high.astype(F32)).astype(jnp.bfloat16))


def side_by_side(values):
    return jnp.concatenate(halves(values), axis=1)


def right_square(w):
    both = side_by_side(w)
    return jnp.concatenate([both, both], axis=0)


def right_square_t(w):
    high, low = halves(w)
    return jnp.concatenate(
        [jnp.concatenate([high, high], axis=1), jnp.concatenate([low, low], axis=1)], axis=0
    )


def plain_dot(left, right, dims=NN):
    return lax.dot_general(left, right, dims, preferred_element_type=F32)


def fold_right(values):
    lanes = values.shape[1] // 2
    return values[:, :lanes] + values[:, lanes:]


def fold_square(values):
    rows = values.shape[0] // 2
    return fold_right(values[:rows] + values[rows:])


def stacked(values):
    high = values.astype(jnp.bfloat16).astype(F32)
    return jnp.concatenate([high, values - high], axis=0).astype(jnp.bfloat16)


def skinny_dot(left, right, dims=NN):
    rows = left.shape[0]
    both = stacked(left)
    high, low = halves(right)
    values = plain_dot(both, high, dims) + plain_dot(both, low, dims)
    return values[:rows] + values[rows:]


def frame_outer(left, right):
    a_high = left.astype(jnp.bfloat16).astype(F32)
    b_high = right.astype(jnp.bfloat16).astype(F32)
    a_low = left - a_high
    b_low = right - b_high
    a = jnp.concatenate([a_high, a_high, a_low, a_low], axis=0).astype(jnp.bfloat16)
    b = jnp.concatenate([b_high, b_low, b_high, b_low], axis=0).astype(jnp.bfloat16)
    return plain_dot(a, b, TN)


def pad_rows(values):
    return jnp.concatenate([values, jnp.zeros((LANES - values.shape[0], values.shape[1]), values.dtype)], axis=0)


def column_order():
    q = lax.broadcasted_iota(jnp.int32, (LANES, LANES), 0)
    n = lax.broadcasted_iota(jnp.int32, (LANES, LANES), 1)
    source = (q // 16) * 16 + (q % 8) * 2 + (q // 8) % 2
    return (source == n).astype(jnp.bfloat16)


def live_frames(counts_ref):
    total = counts_ref[0]
    for clip in range(1, counts_ref.shape[0]):
        total = total + counts_ref[clip]
    return total


def place_of(counts_ref, frame):
    begin = jnp.int32(0)
    end = jnp.int32(0)
    for clip in range(counts_ref.shape[0]):
        end = end + counts_ref[clip]
        begin = jnp.where(frame >= end, end, begin)
    return frame - begin


def running_matrix(counts_ref, frames):
    after = lax.broadcasted_iota(jnp.int32, (frames, frames), 0)
    before = lax.broadcasted_iota(jnp.int32, (frames, frames), 1)
    begin = jnp.int32(0)
    matrix = jnp.zeros((frames, frames), F32)
    for clip in range(counts_ref.shape[0]):
        end = begin + counts_ref[clip]
        inside = (before >= begin) & (before <= after) & (after < end)
        matrix = matrix + jnp.where(inside, 1.0 / (after - begin + 1).astype(F32), 0.0)
        begin = end
    return matrix


def columns_up(values):
    spot = lax.broadcasted_iota(jnp.int32, values.shape, 1)
    return jnp.where(spot == 7, 0.0, pltpu.roll(values, 7, axis=1))


def columns_down(values):
    spot = lax.broadcasted_iota(jnp.int32, values.shape, 1)
    return jnp.where(spot == 0, 0.0, pltpu.roll(values, 1, axis=1))


def tile_sum(values):
    return jnp.sum(jnp.sum(values, axis=0), axis=0, keepdims=True)


def rows8(*rows):
    lanes = rows[0].shape[1]
    spot = lax.broadcasted_iota(jnp.int32, (8, lanes), 0)
    block = jnp.zeros((8, lanes), F32)
    for index, row in enumerate(rows):
        block = jnp.where(spot == index, row, block)
    return block


def pick_row(block, index):
    spot = lax.broadcasted_iota(jnp.int32, block.shape, 0)
    return jnp.sum(jnp.where(spot == index, block, 0.0), axis=0, keepdims=True)


def outer(left, right):
    return exact_dot(rows8(left), rows8(right), TN)


def row_dot(row, matrix, dims=NN):
    return exact_dot(rows8(row), matrix, dims)[0:1]


def clear_edges(ref):
    planes = ref.shape[1]
    edge = jnp.zeros((8, LANES), F32)
    for t in range(ref.shape[0]):
        for plane in range(planes):
            ref[t, plane, 0] = edge
            ref[t, plane, ref.shape[2] - 1] = edge


def spread_taps(taps_ref, w_ref):
    for tap in range(w_ref.shape[0]):
        w_ref[tap] = jnp.broadcast_to(taps_ref[0, tap : tap + 1, :], (8, LANES))


def conv_full(t, k, a_ref, w_ref, d_ref, fresh):
    weights = [w_ref[k * 9 + tap] for tap in range(9)]
    source = t - k
    rows = {}
    for i in range(SIDE):
        for need in (i, i + 1, i + 2):
            if need not in rows:
                rows[need] = [a_ref[source, plane, need] for plane in range(4)]
        even = None
        odd = None
        for r in range(3):
            a_even, a_odd, a_odd_down, a_even_up = rows[i + r]
            left, centre, right = weights[3 * r : 3 * r + 3]
            part_even = centre * a_even + right * a_odd + left * a_odd_down
            part_odd = centre * a_odd + left * a_even + right * a_even_up
            even = part_even if even is None else even + part_even
            odd = part_odd if odd is None else odd + part_odd
        rows.pop(i)
        at = t * FULL_ROWS + 2 * i
        if fresh:
            d_ref[at] = even
            d_ref[at + 1] = odd
        else:
            d_ref[at] = d_ref[at] + even
            d_ref[at + 1] = d_ref[at + 1] + odd


def conv_half(t, k, a_ref, w_ref, d_ref, fresh):
    weights = [w_ref[k * 9 + tap] for tap in range(9)]
    source = t - k
    carried = [a_ref[source, plane, 0] for plane in range(3)]
    for i in range(HALF_ROWS):
        rows = [carried]
        for need in (2 * i + 1, 2 * i + 2):
            rows.append([a_ref[source, plane, need] for plane in range(3)])
        carried = rows[2]
        total = None
        for r in range(3):
            a_even, a_odd, a_odd_down = rows[r]
            left, centre, right = weights[3 * r : 3 * r + 3]
            part = centre * a_even + right * a_odd + left * a_odd_down
            total = part if total is None else total + part
        at = t * HALF_ROWS + i
        d_ref[at] = total if fresh else d_ref[at] + total


def row_total(ref, lanes=None):
    values = ref[...] if lanes is None else ref[:, :, lanes]
    return jnp.sum(values, axis=0)


def send_all(send_ref, rows, lanes):
    count = rows.shape[0]

    def one(device, carry):
        send_ref[pl.ds(device, 1), 0:count, lanes] = rows[None]
        return carry

    lax.fori_loop(0, send_ref.shape[0], one, 0)


def stack_rows(*rows):
    return rows8(*rows)[0 : len(rows)]


def pick_thirds(order, values, dims, order_left):
    pieces = []
    rest = values
    for _ in range(3):
        piece = rest.astype(jnp.bfloat16)
        rest = rest - piece.astype(F32)
        args = (order, piece) if order_left else (piece, order)
        pieces.append(plain_dot(*args, dims))
    return pieces


def prepare_kernel(
    counts_ref, video_ref, cot_ref, w_ref, x_ref, rows_ref, columns_ref, cot_out_ref, gram_ref, send_ref
):
    order = column_order()
    total = live_frames(counts_ref)
    pixels = video_ref.shape[1]
    gram = jnp.zeros((2 * LANES, 2 * LANES), F32)
    summed = jnp.zeros((1, LANES), F32)
    for frame in range(pixels // 256):
        live = jnp.where(frame < total, 1.0, 0.0).astype(F32)
        for part in (2 * frame, 2 * frame + 1):
            at = slice(part * LANES, (part + 1) * LANES)
            block = pad_rows(video_ref[:, at] * live)
            high, middle, low = pick_thirds(order, block, NT, True)
            rows = high + middle + low
            x_ref[at, :] = rows
            rows_ref[at, :] = jnp.concatenate([high, middle], axis=1).astype(jnp.bfloat16)
            first, second, _ = pick_thirds(order, block, NT, False)
            columns_ref[:, at] = jnp.concatenate([first, second], axis=0).astype(jnp.bfloat16)
            summed = summed + jnp.sum(rows, axis=0, keepdims=True)
        at = slice(frame * 256, (frame + 1) * 256)
        gram = gram + plain_dot(columns_ref[:, at], rows_ref[at, :])
    gram = fold_square(gram)
    gram_ref[0:LANES, :] = gram
    gram_ref[LANES : LANES + 8, :] = rows8(summed)
    w = pad_rows(w_ref[0])
    width = w.shape[1]
    sums = stack_rows(row_dot(summed, w), jnp.sum(w * exact_dot(gram, w), axis=0, keepdims=True))
    count = jnp.full((2, LANES), 1.0, F32) * (total * (SIDE * SIDE)).astype(F32)
    send_all(send_ref, sums, slice(0, width))
    send_all(send_ref, count, slice(width, width + LANES))
    spot = lax.broadcasted_iota(jnp.int32, (LANES, LANES), 1)
    for part in range(cot_ref.shape[1] // LANES):
        at = slice(part * LANES, (part + 1) * LANES)
        frame = (spot + part * LANES) // (HALF_ROWS * 8)
        cot_out_ref[at, :] = jnp.where(frame < total, pad_rows(cot_ref[:, at]), 0.0).T


def moments_of(sums, count):
    average = sums[0:1] / count
    return (average, sums[1:2] / count - average * average)


def narrow_kernel(
    counts_ref, sums_ref, stat_ref, gram0_ref, x_ref, z_ref, ngain_ref, nbias_ref, w_ref,
    x1_ref, rows_ref, columns_ref, gram_ref, stat_out_ref, send_ref,
):
    total = live_frames(counts_ref)
    count = stat_ref[2:3, 0:LANES]
    average, variance = moments_of(row_total(sums_ref), count)
    factor = ngain_ref[0:1, :] * lax.rsqrt(variance + EPSILON)
    shift = nbias_ref[0:1, :] - factor * average
    stat_out_ref[...] = rows8(average, variance, count)
    frames = x_ref.shape[0] // 256

    def frame(t, carry):
        gram, cross, summed = carry
        at = pl.ds(pl.multiple_of(t * 256, 256), 256)
        z = z_ref[at, :]
        rows = (x_ref[at, :] + factor * z + shift) * live_value(t, total)
        x1_ref[at, :] = rows
        both = side_by_side(rows)
        rows_ref[at, :] = both
        columns = jnp.concatenate(halves(rows.T), axis=0)
        columns_ref[:, at] = columns
        gram = gram + plain_dot(columns, both)
        cross = cross + plain_dot(columns, side_by_side(z))
        return (gram, cross, summed + jnp.sum(rows, axis=0, keepdims=True))

    zero = jnp.zeros((2 * LANES, 2 * LANES), F32)
    gram, cross, summed = each_frame(frames, frame, (zero, zero, jnp.zeros((1, LANES), F32)))

    gram = fold_square(gram)
    tiles = LANES // 8
    gram_ref[0:tiles] = gram.reshape(tiles, 8, LANES)
    gram_ref[tiles : 2 * tiles] = fold_square(cross).reshape(tiles, 8, LANES)
    gram_ref[2 * tiles : 3 * tiles] = gram0_ref[0:LANES, :].reshape(tiles, 8, LANES)
    gram_ref[3 * tiles] = rows8(summed, gram0_ref[LANES : LANES + 1, :])
    w = pad_rows(w_ref[0])
    sums = stack_rows(row_dot(summed, w), jnp.sum(w * exact_dot(gram, w), axis=0, keepdims=True))
    send_all(send_ref, sums, slice(0, w.shape[1]))


def write_first(t, total, values, scale, shift, a_ref, planes):
    half_pre = values * scale + shift
    first = (half_pre + half_pre * half_tanh(half_pre)) * live_value(t, total)
    first = first.reshape(SIDE, 2, 8, LANES)
    even = first[:, 0]
    odd = first[:, 1]
    a_ref[t, 0, 1 : SIDE + 1] = even
    a_ref[t, 1, 1 : SIDE + 1] = odd
    if planes >= 3:
        a_ref[t, 2, 1 : SIDE + 1] = columns_down(odd)
    if planes >= 4:
        a_ref[t, 3, 1 : SIDE + 1] = columns_up(even)


def expand_kernel(
    block, counts_ref, sums_ref, count_ref, rows_ref, w_ref, gain_ref, bias_ref, taps_ref,
    e_ref, d_ref, stat_ref, send_ref, a_ref, taps8_ref,
):
    @pl.when(pl.program_id(0) == 0)
    def start():
        clear_edges(a_ref)

    total = live_frames(counts_ref)
    frames = a_ref.shape[0]
    count = count_ref[2:3, :] if block else row_total(count_ref)[0:1]
    average, variance = moments_of(row_total(sums_ref), count)
    stat_ref[...] = rows8(average, variance, count)
    norm_row = 2 * block
    scale = gain_ref[norm_row : norm_row + 1, :] * lax.rsqrt(variance + EPSILON)
    shift = 0.5 * (bias_ref[norm_row : norm_row + 1, :] - average * scale)
    scale = 0.5 * scale
    square = right_square(pad_rows(w_ref[0]))

    def expand(t, carry):
        at = pl.ds(pl.multiple_of(t * 256, 256), 256)
        values = fold_right(plain_dot(rows_ref[at, :], square)).reshape(FULL_ROWS, 8, LANES)
        e_ref[pl.ds(pl.multiple_of(t * FULL_ROWS, FULL_ROWS), FULL_ROWS)] = values
        write_first(t, total, values, scale, shift, a_ref, 3 if block else 4)
        return carry

    each_frame(frames, expand, 0)
    spread_taps(taps_ref, taps8_ref)
    per_frame = HALF_ROWS if block else FULL_ROWS
    conv = conv_half if block else conv_full

    def frame(t, carry):
        conv(t, 0, a_ref, taps8_ref, d_ref, True)
        last = jnp.minimum(place_of(counts_ref, t), LAGS - 1)

        def lag(k, inner):
            conv(t, k, a_ref, taps8_ref, d_ref, False)
            return inner

        lax.fori_loop(1, last + 1, lag, 0)
        values = d_ref[pl.ds(t * per_frame, per_frame)]
        return (carry[0] + jnp.sum(values, axis=0), carry[1] + jnp.sum(values * values, axis=0))

    zero = jnp.zeros((8, LANES), F32)
    summed, squares = lax.fori_loop(0, total, frame, (zero, zero))

    def dead(t, carry):
        d_ref[pl.ds(t * per_frame, per_frame)] = jnp.zeros((per_frame, 8, LANES), F32)
        return carry

    lax.fori_loop(total, frames, dead, 0)
    sums = stack_rows(jnp.sum(summed, axis=0, keepdims=True), jnp.sum(squares, axis=0, keepdims=True))
    send_all(send_ref, sums, slice(0, LANES))


def live_value(t, total):
    return jnp.where(t < total, 1.0, 0.0).astype(F32)


def each_frame(count, body, init, unroll=2):
    return lax.fori_loop(0, count, body, init, unroll=unroll)


def squeeze_forward_kernel(
    block, counts_ref, sums_ref, stat_ref, d_ref, gain_ref, bias_ref, down_ref, downb_ref, up_ref, upb_ref, proj_ref,
    cot_ref, z_ref, gates_ref, running_ref, pre_ref, stat_out_ref, send_ref, second_ref, pooled_ref,
):
    phase = pl.program_id(0)
    tile = pl.program_id(1)
    tiles = pl.num_programs(1)
    total = live_frames(counts_ref)
    per_frame = HALF_ROWS if block else FULL_ROWS
    pixels = per_frame * 8
    frames = second_ref.shape[1] // per_frame
    group = 256 // pixels
    chunks = frames // group
    norm_row = 2 * block + 1

    @pl.when(phase == 0)
    def activate():
        count = stat_ref[2:3, 0:LANES] * (0.25 if block else 1.0)
        average, variance = moments_of(row_total(sums_ref), count)
        stat_out_ref[...] = rows8(average, variance, count)
        scale = gain_ref[norm_row : norm_row + 1, :] * lax.rsqrt(variance + EPSILON)
        shift = 0.5 * (bias_ref[norm_row : norm_row + 1, :] - average * scale)
        scale = 0.5 * scale

        def chunk(index, carry):
            for inner in range(group):
                t = index * group + inner
                at = pl.ds(t * per_frame, per_frame)
                half_pre = d_ref[at] * scale + shift
                second = half_pre + half_pre * half_tanh(half_pre)
                second = second * live_value(t, total)
                second_ref[tile, at] = second
                pooled_ref[tile, pl.ds(t, 1), :] = tile_sum(second) * (1.0 / pixels)
            return carry

        each_frame(chunks, chunk, 0)

    @pl.when((phase == 1) & (tile == 0))
    def gate():
        matrix = running_matrix(counts_ref, frames)
        pooled = jnp.concatenate([pooled_ref[index] for index in range(pooled_ref.shape[0])], axis=1)
        running = exact_dot(matrix, pooled)
        running_ref[...] = running
        pre = skinny_dot(running, down_ref[0], NT) + downb_ref[block : block + 1, :]
        pre_ref[...] = pre
        gates_ref[...] = sigmoid(skinny_dot(pre * sigmoid(pre), up_ref[0]) + upb_ref[block : block + 1, :])
        z_ref[...] = jnp.zeros_like(z_ref)

    @pl.when(phase == 1)
    def project():
        square = right_square_t(pad_rows(proj_ref[0]))
        lanes = pl.ds(pl.multiple_of(tile * LANES, LANES), LANES)
        gates = gates_ref[:, lanes]

        def chunk(index, carry):
            parts = []
            for inner in range(group):
                t = index * group + inner
                second = second_ref[tile, pl.ds(t * per_frame, per_frame)].reshape(pixels, LANES)
                parts.append(second * pick_row(gates, t))
            excited = parts[0] if group == 1 else jnp.concatenate(parts, axis=0)
            at = pl.ds(pl.multiple_of(index * 256, 256), 256)
            z_ref[at, :] = z_ref[at, :] + fold_right(plain_dot(side_by_side(excited), square, NT))
            return carry

        each_frame(chunks, chunk, 0)

    @pl.when((phase == 1) & (tile == tiles - 1))
    def finish():
        def chunk(index, carry):
            at = pl.ds(pl.multiple_of(index * 256, 256), 256)
            z = z_ref[at, :].reshape(32, 8, LANES)
            values = [z, z * z]
            if block:
                dy = cot_ref[at, :].reshape(32, 8, LANES)
                values = values + [dy, dy * z]
            return tuple(old + jnp.sum(new, axis=0) for old, new in zip(carry, values))

        zero = jnp.zeros((8, LANES), F32)
        sums = each_frame(chunks, chunk, (zero,) * (4 if block else 2))
        rows = stack_rows(*(jnp.sum(value, axis=0, keepdims=True) for value in sums))
        send_all(send_ref, rows, slice(0, LANES))


def pack_tiles(narrow, squeeze):
    return narrow // 8 + 2 * (squeeze // 8) + 1


def squeeze_backward_body(
    block, counts_ref, stat_ref, d_ref, gain_ref, bias_ref, down_ref, up_ref, proj_ref, gates_ref, running_ref,
    pre_ref, dy2_ref, send_ref, pack_ref, dz3_ref, dz3t_ref, excited_ref, dexc_ref, dgate_ref, head,
):
    phase = pl.program_id(0)
    tile = pl.program_id(1)
    total = live_frames(counts_ref)
    per_frame = HALF_ROWS if block else FULL_ROWS
    pixels = per_frame * 8
    frames = dz3_ref.shape[0] // pixels
    group = 256 // pixels
    chunks = frames // group
    norm_row = 2 * block + 1
    tiles = dexc_ref.shape[0]
    narrow = proj_ref.shape[1]
    squeeze = down_ref.shape[1]
    per_tile = pack_tiles(narrow, squeeze)
    lanes = pl.ds(pl.multiple_of(tile * LANES, LANES), LANES)

    @pl.when((phase == 0) & (tile == 0))
    def start():
        head()

    average = stat_ref[0:1, :]
    root = lax.rsqrt(stat_ref[1:2, :] + EPSILON)
    scale = gain_ref[norm_row : norm_row + 1, :] * root
    shift = 0.5 * (bias_ref[norm_row : norm_row + 1, :] - average * scale)
    scale = 0.5 * scale
    gates = gates_ref[:, lanes]

    @pl.when(phase == 0)
    def excite():
        square = right_square(pad_rows(proj_ref[0]))

        def chunk(index, carry):
            flat = pl.ds(pl.multiple_of(index * 256, 256), 256)
            dexc = fold_right(plain_dot(dz3_ref[flat, :], square)).reshape(32, 8, LANES)
            dexc_ref[tile, pl.ds(pl.multiple_of(index * 32, 32), 32)] = dexc
            parts = []
            for inner in range(group):
                t = index * group + inner
                half_pre = d_ref[pl.ds(t * per_frame, per_frame)] * scale + shift
                second = half_pre + half_pre * half_tanh(half_pre)
                second = second * live_value(t, total)
                own = dexc[inner * per_frame : (inner + 1) * per_frame]
                dgate_ref[tile, pl.ds(t, 1), :] = tile_sum(own * second)
                parts.append(second.reshape(pixels, LANES) * pick_row(gates, t))
            excited = parts[0] if group == 1 else jnp.concatenate(parts, axis=0)
            excited_ref[flat, :] = side_by_side(excited)
            return carry

        each_frame(chunks, chunk, 0)
        dproj = fold_square(plain_dot(dz3t_ref[...], excited_ref[...]))
        pack_ref[pl.ds(tile * per_tile, narrow // 8)] = dproj[0:narrow].reshape(narrow // 8, 8, LANES)

    @pl.when((phase == 1) & (tile == 0))
    def squeeze_part():
        pre = pre_ref[...]
        half_pre = 0.5 * pre
        tanh = half_tanh(half_pre)
        squeezed = half_pre + half_pre * tanh
        all_gates = gates_ref[...]
        dgate = jnp.concatenate([dgate_ref[index] for index in range(tiles)], axis=1)
        du = dgate * all_gates * (1.0 - all_gates)
        dpre = skinny_dot(du, up_ref[0], NT) * silu_slope(half_pre, tanh)
        ddown = frame_outer(dpre, running_ref[...])
        dup = frame_outer(squeezed, du)
        dpre_row = jnp.sum(dpre, axis=0, keepdims=True)
        dpre_row = jnp.concatenate([dpre_row, jnp.zeros((1, du.shape[1] - squeeze), F32)], axis=1)
        biases = rows8(jnp.sum(du, axis=0, keepdims=True), dpre_row)
        for index in range(tiles):
            own = slice(index * LANES, (index + 1) * LANES)
            at = index * per_tile + narrow // 8
            pack_ref[at : at + squeeze // 8] = ddown[:, own].reshape(squeeze // 8, 8, LANES)
            at = at + squeeze // 8
            pack_ref[at : at + squeeze // 8] = dup[:, own].reshape(squeeze // 8, 8, LANES)
            pack_ref[at + squeeze // 8] = biases[:, own]
        drunning = skinny_dot(dpre, down_ref[0])
        dpooled = exact_dot(running_matrix(counts_ref, frames), drunning, TN) * (1.0 / pixels)
        for index in range(tiles):
            dgate_ref[index] = dpooled[:, index * LANES : (index + 1) * LANES]

    @pl.when(phase == 1)
    def slope():
        def chunk(index, carry):
            summed, cross = carry
            for inner in range(group):
                t = index * group + inner
                at = pl.ds(t * per_frame, per_frame)
                depth = d_ref[at]
                half_pre = depth * scale + shift
                dsecond = dexc_ref[tile, at] * pick_row(gates, t) + pick_row(dgate_ref[tile], t)
                dy = dsecond * silu_slope(half_pre, half_tanh(half_pre))
                dy = dy * live_value(t, total)
                dy2_ref[at] = dy
                summed = summed + jnp.sum(dy, axis=0)
                cross = cross + jnp.sum(dy * (depth - average), axis=0)
            return (summed, cross)

        zero = jnp.zeros((8, LANES), F32)
        summed, cross = each_frame(chunks, chunk, (zero, zero))
        rows = stack_rows(jnp.sum(summed, axis=0, keepdims=True), root * jnp.sum(cross, axis=0, keepdims=True))
        send_all(send_ref, rows, slice(0, LANES))


def squeeze_one_backward_kernel(
    counts_ref, third_ref, z_ref, cot_ref, ngain_ref, nbias_ref, stat_ref, d_ref, gain_ref, bias_ref, down_ref,
    up_ref, proj_ref, gates_ref, running_ref, pre_ref, act_ref, nsum_ref, dy2_ref, send_ref, pack_ref,
    dz3_ref, dz3t_ref, excited_ref, dexc_ref, dgate_ref,
):
    total = live_frames(counts_ref)
    pixels = HALF_ROWS * 8

    def head():
        count = stat_ref[2:3, :]
        sums = row_total(third_ref)
        mean, variance = moments_of(sums, count)
        root = lax.rsqrt(variance + EPSILON)
        gain = ngain_ref[1:2, :]
        bias_sum = sums[2:3, :]
        gain_sum = root * (sums[3:4, :] - mean * bias_sum)
        nsum_ref[...] = rows8(gain_sum, bias_sum, mean, variance)
        row = lax.broadcasted_iota(jnp.int32, z_ref.shape, 0) // pixels
        live = row < total
        normed = (z_ref[...] - mean) * root
        act = jnp.where(live, gain * normed + nbias_ref[1:2, :], 0.0)
        act_ref[...] = act.T[0 : act_ref.shape[0]]
        dz3 = gain * root * (cot_ref[...] - bias_sum / count - normed * (gain_sum / count))
        dz3 = jnp.where(live, dz3, 0.0)
        dz3_ref[...] = side_by_side(dz3)
        dz3t_ref[...] = jnp.concatenate(halves(dz3.T), axis=0)

    squeeze_backward_body(
        1, counts_ref, stat_ref, d_ref, gain_ref, bias_ref, down_ref, up_ref, proj_ref, gates_ref, running_ref,
        pre_ref, dy2_ref, send_ref, pack_ref, dz3_ref, dz3t_ref, excited_ref, dexc_ref, dgate_ref, head,
    )


def input_factors(sums, stat_ref, count, gain, w):
    root = lax.rsqrt(stat_ref[1:2, :] + EPSILON)
    factor = gain * root
    matrix = exact_dot(w * (factor * root * sums[1:2] / count), w, NT)
    return (matrix, row_dot(factor * sums[0:1] / count, w, NT))


def covariance(gram, summed, count):
    mean = summed / count
    return (mean, gram / count - outer(mean, mean))


def squeeze_zero_backward_kernel(
    counts_ref, top_ref, stat1_ref, gram_ref, nstat_ref, dxpre_ref, x1_ref, z_ref, ngain_ref, w_ref, gains_ref, q_one_ref,
    stat_ref, d_ref, gain_ref, bias_ref, down_ref, up_ref, proj_ref, gates_ref, running_ref, pre_ref,
    dx1_ref, nsum_ref, dy2_ref, send_ref, pack_ref, dz3_ref, dz3t_ref, excited_ref, dexc_ref, dgate_ref,
):
    total = live_frames(counts_ref)
    width = gains_ref.shape[1]

    def head():
        start = pack_tiles(proj_ref.shape[1], down_ref.shape[1]) * (width // LANES)
        pack_ref[start : start + q_one_ref.shape[0]] = q_one_ref[...]
        count = stat_ref[2:3, :]
        wide_count = jnp.broadcast_to(count[:, 0:1], (1, width))
        sums = row_total(top_ref, slice(0, width))
        extra = row_total(top_ref, slice(width, width + LANES))
        matrix, shift = input_factors(sums, stat1_ref, wide_count, gains_ref[2:3, :], pad_rows(w_ref[0]))
        mean = nstat_ref[0:1, :]
        root = lax.rsqrt(nstat_ref[1:2, :] + EPSILON)
        mean_x1 = gram_ref[3 * LANES : 3 * LANES + 1, :] / count
        cross = (gram_ref[LANES : 2 * LANES, :] - count * outer(mean_x1, mean)) * root
        gain_sum = extra[0:1] - jnp.sum(matrix * cross, axis=0, keepdims=True)
        bias_sum = extra[1:2] - count * shift
        nsum_ref[...] = rows8(gain_sum, bias_sum, mean, nstat_ref[1:2, :])
        factor = ngain_ref[0:1, :] * root
        square = right_square(matrix)
        bias_mean = bias_sum / count
        gain_mean = gain_sum / count

        def frame(t, carry):
            at = pl.ds(pl.multiple_of(t * 256, 256), 256)
            centred = side_by_side(x1_ref[at, :] - mean_x1)
            live = live_value(t, total)
            dx1 = (dxpre_ref[at, :] - fold_right(plain_dot(centred, square)) - shift) * live
            dx1_ref[at, :] = dx1
            normed = (z_ref[at, :] - mean) * root
            dz3 = factor * (dx1 - bias_mean - normed * gain_mean) * live
            dz3_ref[at, :] = side_by_side(dz3)
            dz3t_ref[:, at] = jnp.concatenate(halves(dz3.T), axis=0)
            return carry

        each_frame(dz3_ref.shape[0] // 256, frame, 0)

    squeeze_backward_body(
        0, counts_ref, stat_ref, d_ref, gain_ref, bias_ref, down_ref, up_ref, proj_ref, gates_ref, running_ref,
        pre_ref, dy2_ref, send_ref, pack_ref, dz3_ref, dz3t_ref, excited_ref, dexc_ref, dgate_ref, head,
    )

def back_full(t, k, a_ref, w_ref, z_ref, f_ref, dw_ref, fresh):
    weights = [w_ref[k * 9 + tap] for tap in range(9)]
    target = t - k
    sums = [None] * 9
    a_rows = {}
    z_rows = {}
    for i in range(SIDE):
        for need in (i, i + 1, i + 2):
            if need not in a_rows:
                a_rows[need] = [a_ref[target, plane, need] for plane in range(2)]
                z_rows[need] = [z_ref[t, plane, need] for plane in range(4)]
        even = None
        odd = None
        z_even, z_odd, z_odd_down, z_even_up = z_rows[i + 1]
        for r in range(3):
            b_even, b_odd, b_odd_down, b_even_up = z_rows[i + 2 - r]
            left, centre, right = weights[3 * r : 3 * r + 3]
            part_even = centre * b_even + right * b_odd_down + left * b_odd
            part_odd = centre * b_odd + right * b_even + left * b_even_up
            even = part_even if even is None else even + part_even
            odd = part_odd if odd is None else odd + part_odd
            a_even, a_odd = a_rows[i + r]
            pieces = (
                z_even_up * a_odd + z_odd * a_even,
                z_even * a_even + z_odd * a_odd,
                z_even * a_odd + z_odd_down * a_even,
            )
            for c in range(3):
                at = 3 * r + c
                sums[at] = pieces[c] if sums[at] is None else sums[at] + pieces[c]
        a_rows.pop(i)
        z_rows.pop(i)
        at = target * FULL_ROWS + 2 * i
        if fresh:
            f_ref[at] = even
            f_ref[at + 1] = odd
        else:
            f_ref[at] = f_ref[at] + even
            f_ref[at + 1] = f_ref[at + 1] + odd
    for tap in range(9):
        dw_ref[k * 9 + tap] = dw_ref[k * 9 + tap] + sums[tap]


def back_half(t, k, a_ref, w_ref, z_ref, f_ref, dw_ref, fresh):
    weights = [w_ref[k * 9 + tap] for tap in range(9)]
    target = t - k
    sums = [None] * 9

    def put(row, parity, value):
        at = target * FULL_ROWS + 2 * row + parity
        f_ref[at] = value if fresh else f_ref[at] + value

    carried = [a_ref[target, plane, 0] for plane in range(2)]
    here = [z_ref[t, plane, 0] for plane in range(2)]
    for i in range(HALF_ROWS):
        below = [z_ref[t, plane, i + 1] for plane in range(2)]
        dz, dz_up = here
        rows = [carried]
        for need in (2 * i + 1, 2 * i + 2):
            rows.append([a_ref[target, plane, need] for plane in range(2)])
        carried = rows[2]
        put(2 * i, 0, weights[4] * dz)
        put(2 * i, 1, weights[5] * dz + weights[3] * dz_up)
        put(2 * i + 1, 0, weights[7] * dz + weights[1] * below[0])
        put(
            2 * i + 1,
            1,
            weights[8] * dz + weights[6] * dz_up + (weights[2] * below[0] + weights[0] * below[1]),
        )
        for r in range(3):
            a_even, a_odd = rows[r]
            pieces = (dz_up * a_odd, dz * a_even, dz * a_odd)
            for c in range(3):
                at = 3 * r + c
                sums[at] = pieces[c] if sums[at] is None else sums[at] + pieces[c]
        here = below
    for tap in range(9):
        dw_ref[k * 9 + tap] = dw_ref[k * 9 + tap] + sums[tap]


def depth_backward_kernel(
    block, before, final, counts_ref, grads_ref, stat2_ref, stat_ref, nstat_ref, dy2_ref, d_ref, e_ref, columns_ref, w_ref,
    gain_ref, bias_ref, taps_ref, z3_ref, dx_in_ref, sums_in_ref, list_in_ref, dxpre_ref, send_ref, q_ref, grad_rows_ref,
    a_ref, z_ref, f_ref, taps8_ref, dw_ref, pair_ref,
):
    tile = pl.program_id(0)
    tiles = pl.num_programs(0)
    total = live_frames(counts_ref)
    frames = a_ref.shape[0]
    norm_row = 2 * block
    half = block == 1
    per_frame = HALF_ROWS if half else FULL_ROWS
    taps = dw_ref.shape[0]

    @pl.when(tile == 0)
    def start():
        clear_edges(a_ref)
        clear_edges(z_ref)
        if before:
            dxpre_ref[...] = dx_in_ref[...]
            send_all(send_ref, sums_in_ref[0:2, :], slice(0, before * LANES))
            q_ref[0 : list_in_ref.shape[0]] = list_in_ref[...]
        else:
            dxpre_ref[...] = jnp.zeros_like(dxpre_ref)

        def dead(t, carry):
            f_ref[pl.ds(t * FULL_ROWS, FULL_ROWS)] = jnp.zeros((FULL_ROWS, 8, LANES), F32)
            return carry

        lax.fori_loop(total, frames, dead, 0)

    count = stat2_ref[2:3, :]
    grads = row_total(grads_ref)
    grad_rows_ref[...] = rows8(grads[0:1], grads[1:2])
    average = stat2_ref[0:1, :]
    root = lax.rsqrt(stat2_ref[1:2, :] + EPSILON)
    scale_two = gain_ref[norm_row + 1 : norm_row + 2, :] * root
    slope = scale_two * root * grads[1:2] / count
    level = scale_two * grads[0:1] / count - slope * average
    average_one = stat_ref[0:1, :]
    root_one = lax.rsqrt(stat_ref[1:2, :] + EPSILON)
    scale_one = gain_ref[norm_row : norm_row + 1, :] * root_one
    shift_half = 0.5 * (bias_ref[norm_row : norm_row + 1, :] - average_one * scale_one)
    scale_half = 0.5 * scale_one

    def fill(t, carry):
        at = pl.ds(t * per_frame, per_frame)
        dz = scale_two * dy2_ref[at] - (slope * d_ref[at] + level)
        if half:
            z_ref[t, 0, 0:HALF_ROWS] = dz
            z_ref[t, 1, 0:HALF_ROWS] = columns_up(dz)
        else:
            pair = dz.reshape(SIDE, 2, 8, LANES)
            z_ref[t, 0, 1 : SIDE + 1] = pair[:, 0]
            z_ref[t, 1, 1 : SIDE + 1] = pair[:, 1]
            z_ref[t, 2, 1 : SIDE + 1] = columns_down(pair[:, 1])
            z_ref[t, 3, 1 : SIDE + 1] = columns_up(pair[:, 0])
        values = e_ref[pl.ds(pl.multiple_of(t * FULL_ROWS, FULL_ROWS), FULL_ROWS)]
        write_first(t, total, values, scale_half, shift_half, a_ref, 2)
        return carry

    each_frame(frames, fill, 0)
    spread_taps(taps_ref, taps8_ref)
    dw_ref[...] = jnp.zeros_like(dw_ref)
    back = back_half if half else back_full

    def frame(t, carry):
        back(t, 0, a_ref, taps8_ref, z_ref, f_ref, dw_ref, True)
        last = jnp.minimum(place_of(counts_ref, t), LAGS - 1)

        def lag(k, inner):
            back(t, k, a_ref, taps8_ref, z_ref, f_ref, dw_ref, False)
            return inner

        return lax.fori_loop(1, last + 1, lag, carry)

    lax.fori_loop(0, total, frame, 0)
    square = right_square_t(pad_rows(w_ref[0]))

    def finish(t, carry):
        rows = pl.ds(pl.multiple_of(t * FULL_ROWS, FULL_ROWS), FULL_ROWS)
        flat = pl.ds(pl.multiple_of(t * 256, 256), 256)
        values = e_ref[rows]
        half_pre = values * scale_half + shift_half
        dy = f_ref[rows] * silu_slope(half_pre, half_tanh(half_pre))
        summed = carry[0] + jnp.sum(dy, axis=0)
        cross = carry[1] + jnp.sum(dy * (values - average_one), axis=0)
        dy = dy.reshape(256, LANES)
        pair_ref[flat, :] = side_by_side(dy)
        scaled = side_by_side(dy * scale_one)
        dxpre_ref[flat, :] = dxpre_ref[flat, :] + fold_right(plain_dot(scaled, square, NT))
        return (summed, cross)

    zero = jnp.zeros((8, LANES), F32)
    summed, cross = each_frame(frames, finish, (zero, zero))
    rows = stack_rows(jnp.sum(summed, axis=0, keepdims=True), root_one * jnp.sum(cross, axis=0, keepdims=True))
    if final:
        send_all(send_ref, rows, pl.ds(pl.multiple_of((tile + before) * LANES, LANES), LANES))
    else:
        send_ref[...] = rows8(rows[0:1], rows[1:2])
    gathered = fold_square(plain_dot(columns_ref[...], pair_ref[...]))
    narrow = w_ref.shape[1]
    dtaps = jnp.sum(dw_ref[...], axis=1)
    unused = (-taps) % 8
    dtaps = jnp.concatenate([dtaps, jnp.zeros((unused, LANES), F32)], axis=0)
    values = jnp.concatenate([gathered[0:narrow], dtaps], axis=0)
    listed = values.shape[0] // 8
    q_ref[pl.ds((tile + before) * listed, listed)] = values.reshape(listed, 8, LANES)

    if half:
        @pl.when(tile == tiles - 1)
        def tail():
            mean = nstat_ref[0:1, :]
            root_three = lax.rsqrt(nstat_ref[1:2, :] + EPSILON)

            def part(t, carry):
                flat = pl.ds(pl.multiple_of(t * 256, 256), 256)
                dx = dxpre_ref[flat, :].reshape(32, 8, LANES)
                normed = ((z3_ref[flat, :] - mean) * root_three).reshape(32, 8, LANES)
                return (carry[0] + jnp.sum(dx * normed, axis=0), carry[1] + jnp.sum(dx, axis=0))

            cross_three, summed_three = each_frame(frames, part, (zero, zero))
            rows = stack_rows(
                jnp.sum(cross_three, axis=0, keepdims=True), jnp.sum(summed_three, axis=0, keepdims=True)
            )
            width = send_ref.shape[2] - LANES
            send_all(send_ref, rows, slice(width, width + LANES))


def finish_kernel(
    counts_ref, momentum_ref, gram_ref, stat01_ref, stat02_ref, stat11_ref, stat12_ref, grad0_ref,
    grad1_ref, one_ref, zero_ref, nsum0_ref, nsum1_ref, dxpre_ref, x_ref, dx1_ref, w_ref, gain_ref, means_ref, vars_ref,
    nmeans_ref, nvars_ref,
    video_ref, less_ref, factor_ref, wgain_ref, wbias_ref, ngain_ref, nbias_ref, newm_ref, newv_ref, newnm_ref, newnv_ref,
):
    total = live_frames(counts_ref)
    full = stat01_ref[2:3, :]
    count = full[:, 0:LANES]
    width = full.shape[1]
    top_zero = row_total(zero_ref)
    top_one = row_total(one_ref, slice(0, width))
    w_zero = pad_rows(w_ref[0])
    matrix, shift = input_factors(top_zero, stat01_ref, full, gain_ref[0:1, :], w_zero)
    square = right_square(matrix)
    mean_x, cov_zero = covariance(
        gram_ref[2 * LANES : 3 * LANES, :], gram_ref[3 * LANES + 1 : 3 * LANES + 2, :], count
    )
    order = column_order()
    narrow = video_ref.shape[0]

    def frame(t, carry):
        at = pl.ds(pl.multiple_of(t * 256, 256), 256)
        centred = side_by_side(x_ref[at, :] - mean_x)
        dx = (dxpre_ref[at, :] - fold_right(plain_dot(centred, square)) - shift) * live_value(t, total) + dx1_ref[at, :]
        for part in range(2):
            own = dx[part * LANES : (part + 1) * LANES].T[0:narrow]
            pieces = pick_thirds(order, own, NN, False)
            start = pl.multiple_of(t * 256 + part * LANES, LANES)
            video_ref[:, pl.ds(start, LANES)] = pieces[0] + pieces[1] + pieces[2]
        return carry

    each_frame(x_ref.shape[0] // 256, frame, 0)
    mean_one, cov_one = covariance(gram_ref[0:LANES, :], gram_ref[3 * LANES : 3 * LANES + 1, :], count)
    plan = ((mean_x, cov_zero, stat01_ref, top_zero, w_zero), (mean_one, cov_one, stat11_ref, top_one, pad_rows(w_ref[1])))
    for block, (mean_row, cov, stat_ref, top, w) in enumerate(plan):
        root = lax.rsqrt(stat_ref[1:2, :] + EPSILON)
        factor = gain_ref[2 * block : 2 * block + 1, :] * root
        less = outer(mean_row, top[0:1]) + exact_dot(cov, w) * (root * top[1:2])
        less_ref[block] = (less * factor)[0:narrow]
        factor_ref[8 * block : 8 * block + 8, :] = rows8(factor)
    momentum = momentum_ref[0].astype(F32) / 10.0
    wgain_ref[...] = stack_rows(top_zero[1:2], grad0_ref[1:2, :], top_one[1:2], grad1_ref[1:2, :])
    wbias_ref[...] = stack_rows(top_zero[0:1], grad0_ref[0:1, :], top_one[0:1], grad1_ref[0:1, :])
    stats = (stat01_ref, stat02_ref, stat11_ref, stat12_ref)
    means = stack_rows(*(ref[0:1, :] for ref in stats))
    variances = stack_rows(*(ref[1:2, :] * (ref[2:3, :] / (ref[2:3, :] - 1.0)) for ref in stats))
    newm_ref[...] = (1.0 - momentum) * means_ref[...] + momentum * means
    newv_ref[...] = (1.0 - momentum) * vars_ref[...] + momentum * variances
    ngain_ref[...] = stack_rows(nsum0_ref[0:1, :], nsum1_ref[0:1, :])[:, 0:narrow]
    nbias_ref[...] = stack_rows(nsum0_ref[1:2, :], nsum1_ref[1:2, :])[:, 0:narrow]
    means = stack_rows(nsum0_ref[2:3, :], nsum1_ref[2:3, :])[:, 0:narrow]
    quarter = 0.25 * count
    variances = stack_rows(
        nsum0_ref[3:4, :] * (count / (count - 1.0)), nsum1_ref[3:4, :] * (quarter / (quarter - 1.0))
    )[:, 0:narrow]
    newnm_ref[...] = (1.0 - momentum) * nmeans_ref[...] + momentum * means
    newnv_ref[...] = (1.0 - momentum) * nvars_ref[...] + momentum * variances


def gradient_kernel(
    core_ref, pack0_ref, pack0_other_ref, pack1_ref, pack1_other_ref, late_ref, late_other_ref, less_ref, factor_ref,
    dw_ref, dtaps_ref, ddown_ref, dup_ref, dproj_ref, dupb_ref, ddownb_ref,
):
    narrow = dw_ref.shape[1]
    taps = dtaps_ref.shape[1]
    squeeze = ddown_ref.shape[1]
    tiles = dw_ref.shape[2] // LANES
    per_pack = pack_tiles(narrow, squeeze)
    per_tile = narrow // 8 + -(-taps // 8)
    first_core = core_ref[0] == 0

    def rows_of(pair, at, count):
        mine, other = pair
        half = mine.shape[0]
        pieces = []
        if at < half:
            size = min(count, half - at)
            here = slice(at, at + size)
            pieces.append(jnp.where(first_core, mine[here], other[here]))
            count = count - size
            at = at + size
        if count:
            here = slice(at - half, at - half + count)
            pieces.append(jnp.where(first_core, other[here], mine[here]))
        values = pieces[0] if len(pieces) == 1 else jnp.concatenate(pieces, axis=0)
        return values.reshape(-1, LANES)

    packs = ((pack0_ref, pack0_other_ref), (pack1_ref, pack1_other_ref))
    lists = ((late_ref, late_other_ref), packs[0])
    for block in range(2):
        down_rows = []
        for tile in range(tiles):
            lanes = slice(tile * LANES, (tile + 1) * LANES)
            at = tile * per_pack
            dproj_ref[block, :, lanes] = rows_of(packs[block], at, narrow // 8)
            at = at + narrow // 8
            ddown_ref[block, :, lanes] = rows_of(packs[block], at, squeeze // 8)
            at = at + squeeze // 8
            dup_ref[block, :, lanes] = rows_of(packs[block], at, squeeze // 8)
            biases = rows_of(packs[block], at + squeeze // 8, 1)
            dupb_ref[block : block + 1, lanes] = biases[0:1]
            down_rows.append(biases[1:2])
            values = rows_of(lists[block], (per_pack * tiles if block else 0) + tile * per_tile, per_tile)
            dw = values[0:narrow] * factor_ref[8 * block : 8 * block + 1, lanes] - less_ref[block, :, lanes]
            dw_ref[block, :, lanes] = dw
            dtaps_ref[block, :, lanes] = values[narrow : narrow + taps]
        ddownb_ref[block : block + 1, :] = jnp.concatenate(down_rows, axis=1)[:, 0:squeeze]


AXES = ("dp", "z", "core")
CHIPS = ("dp", "z")


def exchange(send):
    return lax.all_to_all(send, AXES, 0, 0, tiled=True)


def together(*values):
    return lax.optimization_barrier(values)


def swap_cores(values):
    return lax.ppermute(values, "core", [(0, 1), (1, 0)])


def add_cores(tiles):
    core = lax.axis_index("core")
    pair = tiles.reshape(2, tiles.shape[0] // 2, *tiles.shape[1:])
    mine = lax.dynamic_index_in_dim(pair, core, 0, keepdims=False)
    return mine + swap_cores(lax.dynamic_index_in_dim(pair, 1 - core, 0, keepdims=False))


def share_out(tiles, names=CHIPS):
    count = 1
    for name in names:
        count = count * lax.axis_size(name)
    return lax.all_to_all(tiles.reshape(count, -1, *tiles.shape[1:]), names, 0, 0, tiled=True)


def share_back(pieces, names=CHIPS):
    own = jnp.sum(pieces, axis=0)
    everyone = lax.all_to_all(jnp.broadcast_to(own[None], pieces.shape), names, 0, 0, tiled=True)
    return everyone.reshape(-1, *pieces.shape[2:])


def shape(*dims, kind=F32):
    return jax.ShapeDtypeStruct(dims, kind)


def whole(array):
    rank = len(array.shape)
    return pl.BlockSpec(array.shape, lambda *ids: (0,) * rank)


SCALARS = pl.BlockSpec(memory_space=pltpu.SMEM)


def call(kernel, grid, in_specs, out_specs, out_shape, scratch, args, micros=10):
    return pl.pallas_call(
        kernel,
        grid=grid,
        in_specs=in_specs,
        out_specs=out_specs,
        out_shape=out_shape,
        scratch_shapes=scratch,
        compiler_params=pltpu.CompilerParams(vmem_limit_bytes=VMEM_BYTES),
        cost_estimate=pl.CostEstimate(
            flops=micros * 1_000_000_000, bytes_accessed=micros * 3_000_000, transcendentals=0
        ),
    )(*args)


def simple_call(kernel, scalars, args, outs):
    return call(
        kernel, (1,), [SCALARS] * scalars + [whole(array) for array in args[scalars:]], [whole(item) for item in outs],
        outs, [], args,
    )


def local(
    video, frame_counts, momentum_index, expand_weight, wide_gains, wide_biases, narrow_gains, narrow_biases, depth_weight,
    squeeze_weight, squeeze_bias, excite_weight, excite_bias, project_weight, wide_means, wide_variances, narrow_means,
    narrow_variances, cotangent,
):
    devices = lax.axis_size("dp") * lax.axis_size("z") * lax.axis_size("core")
    cin, pixels = video.shape
    half_pixels = cotangent.shape[1]
    width = expand_weight.shape[1]
    squeeze = squeeze_weight.shape[1]
    frames = pixels // (SIDE * SIDE)
    tiles = width // LANES
    taps = depth_weight.shape[1]
    w_t = jnp.swapaxes(expand_weight, 1, 2)
    up_t = jnp.swapaxes(excite_weight, 1, 2)
    lanes_pad = ((0, 0), (0, LANES - cin))
    ngains = jnp.pad(narrow_gains, lanes_pad)
    nbiases = jnp.pad(narrow_biases, lanes_pad)
    full_rows = frames * FULL_ROWS
    half_rows = frames * HALF_ROWS
    low = jnp.bfloat16

    def round_up(count):
        return -(-count // devices) * devices

    def fixed(*dims):
        return pl.BlockSpec(dims, lambda *ids: (0,) * len(dims))

    def tile_rows(rows):
        return pl.BlockSpec((rows, LANES), lambda j: (0, j))

    def tile_cube(rows):
        return pl.BlockSpec((rows, 8, LANES), lambda j: (0, 0, j))

    def tile_sums(rows=2):
        return pl.BlockSpec((devices, rows, LANES), lambda j: (0, 0, j))

    def weight_tile(block, rows):
        return pl.BlockSpec((1, rows, LANES), lambda j, block=block: (block, 0, j))

    def of_block(block, rows, lanes):
        return pl.BlockSpec((1, rows, lanes), lambda *ids: (block, 0, 0))

    def early(make):
        return make(lambda p, j: j * (1 - p) + (tiles - 1) * p)

    def late(make):
        return make(lambda p, j: j * p)

    def both(make):
        return make(lambda p, j: j)

    def rows_at(rows):
        return lambda at: pl.BlockSpec((rows, LANES), lambda p, j: (0, at(p, j)))

    def cube_at(rows):
        return lambda at: pl.BlockSpec((rows, 8, LANES), lambda p, j: (0, 0, at(p, j)))

    def sums_at(rows):
        return lambda at: pl.BlockSpec((devices, rows, LANES), lambda p, j: (0, 0, at(p, j)))

    def weight_at(block, rows):
        return lambda at: pl.BlockSpec((1, rows, LANES), lambda p, j: (block, 0, at(p, j)))

    x, x_rows, x_columns, cot, gram_zero, sums = call(
        prepare_kernel, (1,), [SCALARS, whole(video), whole(cotangent), of_block(0, cin, width)],
        [fixed(pixels, LANES), fixed(pixels, 2 * LANES), fixed(2 * LANES, pixels), fixed(half_pixels, LANES),
         fixed(LANES + 8, LANES), fixed(devices, 2, width + LANES)],
        [shape(pixels, LANES), shape(pixels, 2 * LANES, kind=low), shape(2 * LANES, pixels, kind=low),
         shape(half_pixels, LANES), shape(LANES + 8, LANES), shape(devices, 2, width + LANES)],
        [], (frame_counts, video, cotangent, w_t),
    )
    sums = exchange(sums)

    def expand(block, sums, count, count_spec, rows):
        depth_rows = half_rows if block else full_rows
        return call(
            functools.partial(expand_kernel, block), (tiles,),
            [SCALARS, tile_sums(), count_spec, whole(rows), weight_tile(block, cin), tile_rows(4), tile_rows(4),
             weight_tile(block, taps)],
            [tile_cube(full_rows), tile_cube(depth_rows), tile_rows(8), tile_sums()],
            [shape(full_rows, 8, width), shape(depth_rows, 8, width), shape(8, width), shape(devices, 2, width)],
            [pltpu.VMEM((frames, 4, SIDE + 2, 8, LANES), F32), pltpu.VMEM((taps, 8, LANES), F32)],
            (frame_counts, sums, count, rows, w_t, wide_gains, wide_biases, depth_weight),
        )

    count_spec = pl.BlockSpec((devices, 2, LANES), lambda j: (0, 0, tiles))
    e_zero, d_zero, stat01, sums = expand(0, sums, sums, count_spec, x_rows)
    sums = exchange(sums)

    def squeeze_forward(block, sums, stat, depth):
        rows = half_rows if block else full_rows
        kinds = 4 if block else 2
        return call(
            functools.partial(squeeze_forward_kernel, block), (2, tiles),
            [SCALARS, early(sums_at(2)), early(rows_at(8)), early(cube_at(rows)), early(rows_at(4)), early(rows_at(4)),
             of_block(block, squeeze, width), whole(squeeze_bias), of_block(block, squeeze, width), whole(excite_bias),
             late(weight_at(block, cin)), whole(cot)],
            [fixed(rows * 8, LANES), fixed(8, width), fixed(8, width), fixed(8, squeeze), early(rows_at(8)),
             fixed(devices, kinds, LANES)],
            [shape(rows * 8, LANES), shape(8, width), shape(8, width), shape(8, squeeze), shape(8, width),
             shape(devices, kinds, LANES)],
            [pltpu.VMEM((tiles, rows, 8, LANES), F32), pltpu.VMEM((tiles, frames, LANES), F32)],
            (frame_counts, sums, stat, depth, wide_gains, wide_biases, squeeze_weight, squeeze_bias, up_t, excite_bias,
             project_weight, cot),
        )

    z_zero, gates_zero, running_zero, pre_zero, stat02, sums = squeeze_forward(0, sums, stat01, d_zero)
    sums = exchange(sums)
    narrow_args = (frame_counts, sums, stat01, gram_zero, x, z_zero, ngains, nbiases, w_t)
    narrow_outs = [
        shape(pixels, LANES), shape(pixels, 2 * LANES, kind=low), shape(2 * LANES, pixels, kind=low),
        shape(round_up(3 * LANES // 8 + 1), 8, LANES), shape(8, LANES), shape(devices, 2, width),
    ]
    x1, x1_rows, x1_columns, gram, nstat, sums = call(
        narrow_kernel, (1,), [SCALARS] + [whole(array) for array in narrow_args[1:-1]] + [of_block(1, cin, width)],
        [whole(item) for item in narrow_outs], narrow_outs, [], narrow_args,
    )
    sums, gram = together(exchange(sums), gram)
    gram = share_out(gram, AXES)
    e_one, d_one, stat11, sums = expand(1, sums, nstat, pl.BlockSpec((8, LANES), lambda j: (0, 0)), x1_rows)
    sums, gram = together(sums, gram)
    sums = exchange(sums)
    z_one, gates_one, running_one, pre_one, stat12, sums = squeeze_forward(1, sums, stat11, d_one)
    third, gram = together(exchange(sums), gram)
    gram = share_back(gram, AXES).reshape(-1, LANES)
    q_tiles = cin // 8 + -(-taps // 8)

    def backward_specs(block):
        rows = half_rows if block else full_rows
        ins = [both(rows_at(8)), both(cube_at(rows)), both(rows_at(4)), both(rows_at(4)), of_block(block, squeeze, width),
               of_block(block, squeeze, width), early(weight_at(block, cin)), fixed(8, width), fixed(8, width),
               fixed(8, squeeze)]
        packed = round_up(tiles * (pack_tiles(cin, squeeze) + (0 if block else q_tiles)))
        outs = [fixed(8, LANES), late(cube_at(rows)), late(sums_at(2)), fixed(packed, 8, LANES)]
        shapes = [shape(8, LANES), shape(rows, 8, width), shape(devices, 2, width), shape(packed, 8, LANES)]
        scratch = [pltpu.VMEM((rows * 8, 2 * LANES), low), pltpu.VMEM((2 * LANES, rows * 8), low),
                   pltpu.VMEM((rows * 8, 2 * LANES), low), pltpu.VMEM((tiles, rows, 8, LANES), F32),
                   pltpu.VMEM((tiles, frames, LANES), F32)]
        return (ins, outs, shapes, scratch)

    ins, outs, shapes, scratch = backward_specs(1)
    activations, nsum_one, dy2_one, sums, pack_one = call(
        squeeze_one_backward_kernel, (2, tiles),
        [SCALARS, whole(third), whole(z_one), whole(cot), whole(ngains), whole(nbiases)] + ins,
        [fixed(cin, half_pixels)] + outs, [shape(cin, half_pixels)] + shapes, scratch,
        (frame_counts, third, z_one, cot, ngains, nbiases, stat12, d_one, wide_gains, wide_biases, squeeze_weight, up_t,
         project_weight, gates_one, running_one, pre_one),
    )
    sums, gram = together(sums, gram)
    sums, pack_one = together(exchange(sums), add_cores(pack_one))
    pack_one = share_out(pack_one)
    nothing = jnp.zeros((8, LANES), F32)

    def depth_backward(block, begin, end, sums, stat2, stat, dy2, depth, expanded, columns, dx_in, sums_in, list_in):
        rows = half_rows if block else full_rows
        z_shape = (frames, 2, HALF_ROWS + 1, 8, LANES) if block else (frames, 4, SIDE + 2, 8, LANES)
        count = end - begin
        final = end == tiles
        listed = round_up(end * q_tiles) if final and not block else end * q_tiles
        if final:
            send = (devices, 2, width + (LANES if block else 0))
            send_spec = fixed(*send)
        else:
            send = (8, count * LANES)
            send_spec = tile_rows(8)

        def wide_rows(rows):
            return pl.BlockSpec((rows, LANES), lambda j: (0, j + begin))

        def wide_cube(rows):
            return pl.BlockSpec((rows, 8, LANES), lambda j: (0, 0, j + begin))

        def wide_weight(rows):
            return pl.BlockSpec((1, rows, LANES), lambda j: (block, 0, j + begin))

        return call(
            functools.partial(depth_backward_kernel, block, begin, final), (count,),
            [SCALARS, pl.BlockSpec((devices, 2, LANES), lambda j: (0, 0, j + begin)), wide_rows(8), wide_rows(8), whole(nstat),
             wide_cube(rows), wide_cube(rows), wide_cube(full_rows), whole(columns), wide_weight(cin), wide_rows(4),
             wide_rows(4), wide_weight(taps), whole(z_zero), whole(dx_in), whole(sums_in), whole(list_in)],
            [fixed(pixels, LANES), send_spec, fixed(listed, 8, LANES), tile_rows(8)],
            [shape(pixels, LANES), shape(*send), shape(listed, 8, LANES), shape(8, count * LANES)],
            [pltpu.VMEM((frames, 2, SIDE + 2, 8, LANES), F32), pltpu.VMEM(z_shape, F32), pltpu.VMEM((full_rows, 8, LANES), F32),
             pltpu.VMEM((taps, 8, LANES), F32), pltpu.VMEM((taps, 8, LANES), F32), pltpu.VMEM((pixels, 2 * LANES), low)],
            (frame_counts, sums, stat2, stat, nstat, dy2, depth, expanded, columns, w_t, wide_gains, wide_biases,
             depth_weight, z_zero, dx_in, sums_in, list_in),
            20,
        )

    dxpre_one, sums, q_one, grad_one = depth_backward(
        1, 0, tiles, sums, stat12, stat11, dy2_one, d_one, e_one, x1_columns, nothing, nothing, nothing
    )
    sums, pack_one = together(sums, pack_one)
    top_one, pack_one = together(exchange(sums), pack_one)
    pack_one = share_back(pack_one)
    ins, outs, shapes, scratch = backward_specs(0)
    dx1, nsum_zero, dy2_zero, sums, pack_zero = call(
        squeeze_zero_backward_kernel, (2, tiles),
        [SCALARS, whole(top_one), whole(stat11), whole(gram), whole(nstat), whole(dxpre_one), whole(x1), whole(z_zero),
         whole(ngains), of_block(1, cin, width), whole(wide_gains), whole(q_one)] + ins,
        [fixed(pixels, LANES)] + outs, [shape(pixels, LANES)] + shapes, scratch,
        (frame_counts, top_one, stat11, gram, nstat, dxpre_one, x1, z_zero, ngains, w_t, wide_gains, q_one, stat02, d_zero,
         wide_gains, wide_biases, squeeze_weight, up_t, project_weight, gates_zero, running_zero, pre_zero),
    )
    sums, pack_one = together(sums, pack_one)
    pack_one_other = swap_cores(pack_one)
    sums, pack_zero, pack_one_other = together(exchange(sums), add_cores(pack_zero), pack_one_other)
    pack_zero = share_out(pack_zero)
    first = tiles - tiles // 2
    dxpre_zero, sums_in, late, grad_a = depth_backward(
        0, 0, first, sums, stat02, stat01, dy2_zero, d_zero, e_zero, x_columns, nothing, nothing, nothing
    )
    dxpre_zero, pack_zero = together(dxpre_zero, pack_zero)
    pack_zero = share_back(pack_zero)
    dxpre_zero, sums, late, grad_b = depth_backward(
        0, first, tiles, sums, stat02, stat01, dy2_zero, d_zero, e_zero, x_columns, dxpre_zero, sums_in, late
    )
    grad_zero = jnp.concatenate([grad_a, grad_b], axis=1)
    sums, pack_zero = together(sums, pack_zero)
    pack_zero_other = swap_cores(pack_zero)
    top_zero, late, pack_zero_other = together(exchange(sums), add_cores(late), pack_zero_other)
    late = share_back(share_out(late))
    late_other = swap_cores(late)
    core = lax.axis_index("core").astype(jnp.int32).reshape(1)
    final_args = (
        frame_counts, momentum_index, gram, stat01, stat02, stat11, stat12, grad_zero, grad_one, top_one,
        top_zero, nsum_zero, nsum_one, dxpre_zero, x, dx1, w_t, wide_gains, wide_means, wide_variances, narrow_means,
        narrow_variances,
    )
    final_outs = [
        shape(cin, pixels), shape(2, cin, width), shape(16, width), shape(4, width), shape(4, width), shape(2, cin),
        shape(2, cin), shape(4, width), shape(4, width), shape(2, cin), shape(2, cin),
    ]
    video_grad, less, factor, wgain, wbias, ngain, nbias, newm, newv, newnm, newnv = simple_call(
        finish_kernel, 2, final_args, final_outs
    )
    dw_t, dtaps, ddown, dup, dproj, dupb, ddownb = simple_call(
        gradient_kernel, 1,
        (core, pack_zero, pack_zero_other, pack_one, pack_one_other, late, late_other, less, factor),
        [shape(2, cin, width), shape(2, taps, width), shape(2, squeeze, width), shape(2, squeeze, width),
         shape(2, cin, width), shape(2, width), shape(2, squeeze)],
    )
    return (
        activations, video_grad, jnp.swapaxes(dw_t, 1, 2), wgain, wbias, ngain, nbias, dtaps, ddown, ddownb,
        jnp.swapaxes(dup, 1, 2), dupb, dproj, newm, newv, newnm, newnv,
    )


def solution(mesh):
    sizes = (mesh.shape["dp"], mesh.shape["rep"] // 2, 2)
    split_mesh = jax.sharding.Mesh(mesh.devices.reshape(sizes), AXES)
    split = P(None, AXES)
    placed = (split, P(AXES)) + (P(),) * 16 + (split,)
    return jax.shard_map(
        local, mesh=split_mesh, in_specs=placed, out_specs=(split, split) + (P(),) * 15, check_vma=False
    )
```

```python
import functools

import jax
import jax.numpy as jnp
from jax import lax
from jax.experimental import pallas as pl
from jax.experimental.pallas import tpu as pltpu
from jax.sharding import PartitionSpec as P

SIDE = 16
LANES = 128
LAGS = 5
FULL_ROWS = 2 * SIDE
HALF_ROWS = SIDE // 2
EPSILON = 1e-05
HIGHEST = lax.Precision.HIGHEST
F32 = jnp.float32
NN = (((1,), (0,)), ((), ()))
NT = (((1,), (1,)), ((), ()))
TN = (((0,), (0,)), ((), ()))
VMEM_BYTES = 52 * 1024 * 1024


def half_tanh(half_values):
    return jnp.tanh(half_values)


def sigmoid(values):
    return 0.5 * jnp.tanh(0.5 * values) + 0.5


def silu_slope(half_values, tanh):
    return 0.5 * (1.0 + tanh + half_values * (1.0 - tanh * tanh))


def exact_dot(left, right, dims=NN):
    return lax.dot_general(left, right, dims, precision=HIGHEST, preferred_element_type=F32)


def halves(values):
    high = values.astype(jnp.bfloat16)
    return (high, (values - high.astype(F32)).astype(jnp.bfloat16))


def side_by_side(values):
    return jnp.concatenate(halves(values), axis=1)


def right_square(w):
    both = side_by_side(w)
    return jnp.concatenate([both, both], axis=0)


def right_square_t(w):
    high, low = halves(w)
    return jnp.concatenate(
        [jnp.concatenate([high, high], axis=1), jnp.concatenate([low, low], axis=1)], axis=0
    )


def plain_dot(left, right, dims=NN):
    return lax.dot_general(left, right, dims, preferred_element_type=F32)


def fold_right(values):
    lanes = values.shape[1] // 2
    return values[:, :lanes] + values[:, lanes:]


def fold_square(values):
    rows = values.shape[0] // 2
    return fold_right(values[:rows] + values[rows:])


def stacked(values):
    high = values.astype(jnp.bfloat16).astype(F32)
    return jnp.concatenate([high, values - high], axis=0).astype(jnp.bfloat16)


def skinny_dot(left, right, dims=NN):
    rows = left.shape[0]
    both = stacked(left)
    high, low = halves(right)
    values = plain_dot(both, high, dims) + plain_dot(both, low, dims)
    return values[:rows] + values[rows:]


def frame_outer(left, right):
    a_high = left.astype(jnp.bfloat16).astype(F32)
    b_high = right.astype(jnp.bfloat16).astype(F32)
    a_low = left - a_high
    b_low = right - b_high
    a = jnp.concatenate([a_high, a_high, a_low, a_low], axis=0).astype(jnp.bfloat16)
    b = jnp.concatenate([b_high, b_low, b_high, b_low], axis=0).astype(jnp.bfloat16)
    return plain_dot(a, b, TN)


def pad_rows(values):
    return jnp.concatenate([values, jnp.zeros((LANES - values.shape[0], values.shape[1]), values.dtype)], axis=0)


def column_order():
    q = lax.broadcasted_iota(jnp.int32, (LANES, LANES), 0)
    n = lax.broadcasted_iota(jnp.int32, (LANES, LANES), 1)
    source = (q // 16) * 16 + (q % 8) * 2 + (q // 8) % 2
    return (source == n).astype(jnp.bfloat16)


def live_frames(counts_ref):
    total = counts_ref[0]
    for clip in range(1, counts_ref.shape[0]):
        total = total + counts_ref[clip]
    return total


def place_of(counts_ref, frame):
    begin = jnp.int32(0)
    end = jnp.int32(0)
    for clip in range(counts_ref.shape[0]):
        end = end + counts_ref[clip]
        begin = jnp.where(frame >= end, end, begin)
    return frame - begin


def running_matrix(counts_ref, frames):
    after = lax.broadcasted_iota(jnp.int32, (frames, frames), 0)
    before = lax.broadcasted_iota(jnp.int32, (frames, frames), 1)
    begin = jnp.int32(0)
    matrix = jnp.zeros((frames, frames), F32)
    for clip in range(counts_ref.shape[0]):
        end = begin + counts_ref[clip]
        inside = (before >= begin) & (before <= after) & (after < end)
        matrix = matrix + jnp.where(inside, 1.0 / (after - begin + 1).astype(F32), 0.0)
        begin = end
    return matrix


def columns_up(values):
    spot = lax.broadcasted_iota(jnp.int32, values.shape, 1)
    return jnp.where(spot == 7, 0.0, pltpu.roll(values, 7, axis=1))


def columns_down(values):
    spot = lax.broadcasted_iota(jnp.int32, values.shape, 1)
    return jnp.where(spot == 0, 0.0, pltpu.roll(values, 1, axis=1))


def tile_sum(values):
    return jnp.sum(jnp.sum(values, axis=0), axis=0, keepdims=True)


def rows8(*rows):
    lanes = rows[0].shape[1]
    spot = lax.broadcasted_iota(jnp.int32, (8, lanes), 0)
    block = jnp.zeros((8, lanes), F32)
    for index, row in enumerate(rows):
        block = jnp.where(spot == index, row, block)
    return block


def pick_row(block, index):
    spot = lax.broadcasted_iota(jnp.int32, block.shape, 0)
    return jnp.sum(jnp.where(spot == index, block, 0.0), axis=0, keepdims=True)


def outer(left, right):
    return exact_dot(rows8(left), rows8(right), TN)


def row_dot(row, matrix, dims=NN):
    return exact_dot(rows8(row), matrix, dims)[0:1]


def clear_edges(ref):
    planes = ref.shape[1]
    edge = jnp.zeros((8, LANES), F32)
    for t in range(ref.shape[0]):
        for plane in range(planes):
            ref[t, plane, 0] = edge
            ref[t, plane, ref.shape[2] - 1] = edge


def spread_taps(taps_ref, w_ref):
    for tap in range(w_ref.shape[0]):
        w_ref[tap] = jnp.broadcast_to(taps_ref[0, tap : tap + 1, :], (8, LANES))


def conv_full(t, k, a_ref, w_ref, d_ref, fresh):
    weights = [w_ref[k * 9 + tap] for tap in range(9)]
    source = t - k
    rows = {}
    for i in range(SIDE):
        for need in (i, i + 1, i + 2):
            if need not in rows:
                rows[need] = [a_ref[source, plane, need] for plane in range(4)]
        even = None
        odd = None
        for r in range(3):
            a_even, a_odd, a_odd_down, a_even_up = rows[i + r]
            left, centre, right = weights[3 * r : 3 * r + 3]
            part_even = centre * a_even + right * a_odd + left * a_odd_down
            part_odd = centre * a_odd + left * a_even + right * a_even_up
            even = part_even if even is None else even + part_even
            odd = part_odd if odd is None else odd + part_odd
        rows.pop(i)
        at = t * FULL_ROWS + 2 * i
        if fresh:
            d_ref[at] = even
            d_ref[at + 1] = odd
        else:
            d_ref[at] = d_ref[at] + even
            d_ref[at + 1] = d_ref[at + 1] + odd


def conv_half(t, k, a_ref, w_ref, d_ref, fresh):
    weights = [w_ref[k * 9 + tap] for tap in range(9)]
    source = t - k
    carried = [a_ref[source, plane, 0] for plane in range(3)]
    for i in range(HALF_ROWS):
        rows = [carried]
        for need in (2 * i + 1, 2 * i + 2):
            rows.append([a_ref[source, plane, need] for plane in range(3)])
        carried = rows[2]
        total = None
        for r in range(3):
            a_even, a_odd, a_odd_down = rows[r]
            left, centre, right = weights[3 * r : 3 * r + 3]
            part = centre * a_even + right * a_odd + left * a_odd_down
            total = part if total is None else total + part
        at = t * HALF_ROWS + i
        d_ref[at] = total if fresh else d_ref[at] + total


def row_total(ref, lanes=None):
    values = ref[...] if lanes is None or lanes == slice(None) else ref[:, :, lanes]
    return jnp.sum(values, axis=0)


def send_all(send_ref, rows, lanes):
    count = rows.shape[0]

    def one(device, carry):
        send_ref[pl.ds(device, 1), 0:count, lanes] = rows[None]
        return carry

    lax.fori_loop(0, send_ref.shape[0], one, 0)


def stack_rows(*rows):
    return rows8(*rows)[0 : len(rows)]


def pick_thirds(order, values, dims, order_left):
    pieces = []
    rest = values
    for _ in range(3):
        piece = rest.astype(jnp.bfloat16)
        rest = rest - piece.astype(F32)
        args = (order, piece) if order_left else (piece, order)
        pieces.append(plain_dot(*args, dims))
    return pieces


def prepare_kernel(
    counts_ref, video_ref, cot_ref, w_ref, x_ref, rows_ref, columns_ref, cot_out_ref, gram_ref, send_ref
):
    order = column_order()
    total = live_frames(counts_ref)
    pixels = video_ref.shape[1]
    gram = jnp.zeros((2 * LANES, 2 * LANES), F32)
    summed = jnp.zeros((1, LANES), F32)
    for frame in range(pixels // 256):
        live = jnp.where(frame < total, 1.0, 0.0).astype(F32)
        for part in (2 * frame, 2 * frame + 1):
            at = slice(part * LANES, (part + 1) * LANES)
            block = pad_rows(video_ref[:, at] * live)
            high, middle, low = pick_thirds(order, block, NT, True)
            rows = high + middle + low
            x_ref[at, :] = rows
            rows_ref[at, :] = jnp.concatenate([high, middle], axis=1).astype(jnp.bfloat16)
            first, second, _ = pick_thirds(order, block, NT, False)
            columns_ref[:, at] = jnp.concatenate([first, second], axis=0).astype(jnp.bfloat16)
            summed = summed + jnp.sum(rows, axis=0, keepdims=True)
        at = slice(frame * 256, (frame + 1) * 256)
        gram = gram + plain_dot(columns_ref[:, at], rows_ref[at, :])
    gram = fold_square(gram)
    gram_ref[0:LANES, :] = gram
    gram_ref[LANES : LANES + 8, :] = rows8(summed)
    w = pad_rows(w_ref[0])
    width = w.shape[1]
    sums = stack_rows(row_dot(summed, w), jnp.sum(w * exact_dot(gram, w), axis=0, keepdims=True))
    count = jnp.full((2, LANES), 1.0, F32) * (total * (SIDE * SIDE)).astype(F32)
    send_all(send_ref, sums, slice(0, width))
    send_all(send_ref, count, slice(width, width + LANES))
    spot = lax.broadcasted_iota(jnp.int32, (LANES, LANES), 1)
    for part in range(cot_ref.shape[1] // LANES):
        at = slice(part * LANES, (part + 1) * LANES)
        frame = (spot + part * LANES) // (HALF_ROWS * 8)
        cot_out_ref[at, :] = jnp.where(frame < total, pad_rows(cot_ref[:, at]), 0.0).T


def moments_of(sums, count):
    average = sums[0:1] / count
    return (average, sums[1:2] / count - average * average)


def narrow_kernel(
    counts_ref, sums_ref, stat_ref, gram0_ref, x_ref, z_ref, ngain_ref, nbias_ref, w_ref,
    x1_ref, rows_ref, columns_ref, gram_ref, stat_out_ref, send_ref,
):
    total = live_frames(counts_ref)
    count = stat_ref[2:3, 0:LANES]
    average, variance = moments_of(row_total(sums_ref), count)
    factor = ngain_ref[0:1, :] * lax.rsqrt(variance + EPSILON)
    shift = nbias_ref[0:1, :] - factor * average
    stat_out_ref[...] = rows8(average, variance, count)
    frames = x_ref.shape[0] // 256

    def frame(t, carry):
        gram, cross, summed = carry
        at = pl.ds(pl.multiple_of(t * 256, 256), 256)
        z = z_ref[at, :]
        rows = (x_ref[at, :] + factor * z + shift) * live_value(t, total)
        x1_ref[at, :] = rows
        both = side_by_side(rows)
        rows_ref[at, :] = both
        columns = jnp.concatenate(halves(rows.T), axis=0)
        columns_ref[:, at] = columns
        gram = gram + plain_dot(columns, both)
        cross = cross + plain_dot(columns, side_by_side(z))
        return (gram, cross, summed + jnp.sum(rows, axis=0, keepdims=True))

    zero = jnp.zeros((2 * LANES, 2 * LANES), F32)
    gram, cross, summed = each_frame(frames, frame, (zero, zero, jnp.zeros((1, LANES), F32)))

    gram = fold_square(gram)
    tiles = LANES // 8
    gram_ref[0:tiles] = gram.reshape(tiles, 8, LANES)
    gram_ref[tiles : 2 * tiles] = fold_square(cross).reshape(tiles, 8, LANES)
    gram_ref[2 * tiles : 3 * tiles] = gram0_ref[0:LANES, :].reshape(tiles, 8, LANES)
    gram_ref[3 * tiles] = rows8(summed, gram0_ref[LANES : LANES + 1, :])
    w = pad_rows(w_ref[0])
    sums = stack_rows(row_dot(summed, w), jnp.sum(w * exact_dot(gram, w), axis=0, keepdims=True))
    send_all(send_ref, sums, slice(0, w.shape[1]))


def write_first(t, total, values, scale, shift, a_ref, planes):
    half_pre = values * scale + shift
    first = (half_pre + half_pre * half_tanh(half_pre)) * live_value(t, total)
    first = first.reshape(SIDE, 2, 8, LANES)
    even = first[:, 0]
    odd = first[:, 1]
    a_ref[t, 0, 1 : SIDE + 1] = even
    a_ref[t, 1, 1 : SIDE + 1] = odd
    if planes >= 3:
        a_ref[t, 2, 1 : SIDE + 1] = columns_down(odd)
    if planes >= 4:
        a_ref[t, 3, 1 : SIDE + 1] = columns_up(even)


def expand_kernel(
    block, counts_ref, sums_ref, count_ref, rows_ref, w_ref, gain_ref, bias_ref, taps_ref,
    e_ref, d_ref, stat_ref, send_ref, a_ref, taps8_ref,
):
    @pl.when(pl.program_id(0) == 0)
    def start():
        clear_edges(a_ref)

    total = live_frames(counts_ref)
    frames = a_ref.shape[0]
    count = count_ref[2:3, :] if block else row_total(count_ref)[0:1]
    average, variance = moments_of(row_total(sums_ref), count)
    stat_ref[...] = rows8(average, variance, count)
    norm_row = 2 * block
    scale = gain_ref[norm_row : norm_row + 1, :] * lax.rsqrt(variance + EPSILON)
    shift = 0.5 * (bias_ref[norm_row : norm_row + 1, :] - average * scale)
    scale = 0.5 * scale
    square = right_square(pad_rows(w_ref[0]))

    def expand(t, carry):
        at = pl.ds(pl.multiple_of(t * 256, 256), 256)
        values = fold_right(plain_dot(rows_ref[at, :], square)).reshape(FULL_ROWS, 8, LANES)
        e_ref[pl.ds(pl.multiple_of(t * FULL_ROWS, FULL_ROWS), FULL_ROWS)] = values
        write_first(t, total, values, scale, shift, a_ref, 3 if block else 4)
        return carry

    each_frame(frames, expand, 0)
    spread_taps(taps_ref, taps8_ref)
    per_frame = HALF_ROWS if block else FULL_ROWS
    conv = conv_half if block else conv_full

    def frame(t, carry):
        conv(t, 0, a_ref, taps8_ref, d_ref, True)
        last = jnp.minimum(place_of(counts_ref, t), LAGS - 1)

        def lag(k, inner):
            conv(t, k, a_ref, taps8_ref, d_ref, False)
            return inner

        lax.fori_loop(1, last + 1, lag, 0)
        values = d_ref[pl.ds(t * per_frame, per_frame)]
        return (carry[0] + jnp.sum(values, axis=0), carry[1] + jnp.sum(values * values, axis=0))

    zero = jnp.zeros((8, LANES), F32)
    summed, squares = lax.fori_loop(0, total, frame, (zero, zero))

    def dead(t, carry):
        d_ref[pl.ds(t * per_frame, per_frame)] = jnp.zeros((per_frame, 8, LANES), F32)
        return carry

    lax.fori_loop(total, frames, dead, 0)
    sums = stack_rows(jnp.sum(summed, axis=0, keepdims=True), jnp.sum(squares, axis=0, keepdims=True))
    send_all(send_ref, sums, slice(0, LANES))


def live_value(t, total):
    return jnp.where(t < total, 1.0, 0.0).astype(F32)


def each_frame(count, body, init, unroll=2):
    return lax.fori_loop(0, count, body, init, unroll=unroll)


def lanes_of(ref, tile):
    if ref.shape[-1] == LANES:
        return slice(None)
    return pl.ds(pl.multiple_of(tile * LANES, LANES), LANES)


def squeeze_forward_kernel(
    block, counts_ref, sums_ref, stat_ref, d_ref, gain_ref, bias_ref, down_ref, downb_ref, up_ref, upb_ref, proj_ref,
    cot_ref, z_ref, gates_ref, running_ref, pre_ref, stat_out_ref, send_ref, second_ref, pooled_ref,
):
    step = pl.program_id(0)
    steps = pl.num_programs(0)
    tiles = second_ref.shape[0]
    total = live_frames(counts_ref)
    per_frame = HALF_ROWS if block else FULL_ROWS
    pixels = per_frame * 8
    frames = second_ref.shape[1] // per_frame
    group = 256 // pixels
    chunks = frames // group
    norm_row = 2 * block + 1

    def activate(tile, carry):
        lanes = lanes_of(d_ref, tile)
        count = stat_ref[2:3, lanes] * (0.25 if block else 1.0)
        average, variance = moments_of(row_total(sums_ref, lanes), count)
        stat_out_ref[:, lanes] = rows8(average, variance, count)
        scale = gain_ref[norm_row : norm_row + 1, lanes] * lax.rsqrt(variance + EPSILON)
        shift = 0.5 * (bias_ref[norm_row : norm_row + 1, lanes] - average * scale)
        scale = 0.5 * scale

        def chunk(index, inside):
            for inner in range(group):
                t = index * group + inner
                at = pl.ds(t * per_frame, per_frame)
                half_pre = d_ref[at, :, lanes] * scale + shift
                second = half_pre + half_pre * half_tanh(half_pre)
                second = second * live_value(t, total)
                second_ref[tile, at] = second
                pooled_ref[tile, pl.ds(t, 1), :] = tile_sum(second) * (1.0 / pixels)
            return inside

        each_frame(chunks, chunk, 0)
        return carry

    if block:
        lax.fori_loop(0, tiles, activate, 0)
    else:
        activate(step, 0)

    def project(tile, carry):
        lanes = lanes_of(gates_ref, tile)
        square = right_square_t(pad_rows(proj_ref[0, :, lanes]))
        gates = gates_ref[:, lanes]

        def chunk(index, inside):
            parts = []
            for inner in range(group):
                t = index * group + inner
                second = second_ref[tile, pl.ds(t * per_frame, per_frame)].reshape(pixels, LANES)
                parts.append(second * pick_row(gates, t))
            excited = parts[0] if group == 1 else jnp.concatenate(parts, axis=0)
            at = pl.ds(pl.multiple_of(index * 256, 256), 256)
            z_ref[at, :] = z_ref[at, :] + fold_right(plain_dot(side_by_side(excited), square, NT))
            return inside

        each_frame(chunks, chunk, 0)
        return carry

    @pl.when(step == steps - 1)
    def gate_and_project():
        matrix = running_matrix(counts_ref, frames)
        pooled = jnp.concatenate([pooled_ref[index] for index in range(tiles)], axis=1)
        running = exact_dot(matrix, pooled)
        running_ref[...] = running
        pre = skinny_dot(running, down_ref[0], NT) + downb_ref[block : block + 1, :]
        pre_ref[...] = pre
        gates_ref[...] = sigmoid(skinny_dot(pre * sigmoid(pre), up_ref[0]) + upb_ref[block : block + 1, :])
        z_ref[...] = jnp.zeros_like(z_ref)
        lax.fori_loop(0, tiles, project, 0)

        def chunk(index, carry):
            at = pl.ds(pl.multiple_of(index * 256, 256), 256)
            z = z_ref[at, :].reshape(32, 8, LANES)
            values = [z, z * z]
            if block:
                dy = cot_ref[at, :].reshape(32, 8, LANES)
                values = values + [dy, dy * z]
            return tuple(old + jnp.sum(new, axis=0) for old, new in zip(carry, values))

        zero = jnp.zeros((8, LANES), F32)
        sums = each_frame(chunks, chunk, (zero,) * (4 if block else 2))
        rows = stack_rows(*(jnp.sum(value, axis=0, keepdims=True) for value in sums))
        send_all(send_ref, rows, slice(0, LANES))


def pack_tiles(narrow, squeeze):
    return narrow // 8 + 2 * (squeeze // 8) + 1


def squeeze_backward_body(
    block, counts_ref, stat_ref, d_ref, gain_ref, bias_ref, down_ref, up_ref, proj_ref, gates_ref, running_ref,
    pre_ref, dy2_ref, send_ref, pack_ref, dz3_ref, dz3t_ref, excited_ref, dexc_ref, dgate_ref, head,
):
    total = live_frames(counts_ref)
    per_frame = HALF_ROWS if block else FULL_ROWS
    pixels = per_frame * 8
    frames = dz3_ref.shape[0] // pixels
    group = 256 // pixels
    chunks = frames // group
    norm_row = 2 * block + 1
    tiles = dexc_ref.shape[0]
    narrow = proj_ref.shape[1]
    squeeze = down_ref.shape[1]
    per_tile = pack_tiles(narrow, squeeze)

    def norm_of(tile):
        lanes = lanes_of(d_ref, tile)
        average = stat_ref[0:1, lanes]
        root = lax.rsqrt(stat_ref[1:2, lanes] + EPSILON)
        scale = gain_ref[norm_row : norm_row + 1, lanes] * root
        shift = 0.5 * (bias_ref[norm_row : norm_row + 1, lanes] - average * scale)
        return (lanes, average, root, 0.5 * scale, shift)

    def excite(tile, carry):
        lanes, _, _, scale, shift = norm_of(tile)
        gates = gates_ref[:, lanes_of(gates_ref, tile)]
        square = right_square(pad_rows(proj_ref[0, :, lanes]))

        def chunk(index, inside):
            flat = pl.ds(pl.multiple_of(index * 256, 256), 256)
            dexc = fold_right(plain_dot(dz3_ref[flat, :], square)).reshape(32, 8, LANES)
            dexc_ref[tile, pl.ds(pl.multiple_of(index * 32, 32), 32)] = dexc
            parts = []
            for inner in range(group):
                t = index * group + inner
                half_pre = d_ref[pl.ds(t * per_frame, per_frame), :, lanes] * scale + shift
                second = half_pre + half_pre * half_tanh(half_pre)
                second = second * live_value(t, total)
                own = dexc[inner * per_frame : (inner + 1) * per_frame]
                dgate_ref[tile, pl.ds(t, 1), :] = tile_sum(own * second)
                parts.append(second.reshape(pixels, LANES) * pick_row(gates, t))
            excited = parts[0] if group == 1 else jnp.concatenate(parts, axis=0)
            excited_ref[flat, :] = side_by_side(excited)
            return inside

        each_frame(chunks, chunk, 0)
        dproj = fold_square(plain_dot(dz3t_ref[...], excited_ref[...]))
        pack_ref[pl.ds(tile * per_tile, narrow // 8)] = dproj[0:narrow].reshape(narrow // 8, 8, LANES)
        return carry

    def squeeze_part():
        pre = pre_ref[...]
        half_pre = 0.5 * pre
        tanh = half_tanh(half_pre)
        squeezed = half_pre + half_pre * tanh
        all_gates = gates_ref[...]
        dgate = jnp.concatenate([dgate_ref[index] for index in range(tiles)], axis=1)
        du = dgate * all_gates * (1.0 - all_gates)
        dpre = skinny_dot(du, up_ref[0], NT) * silu_slope(half_pre, tanh)
        ddown = frame_outer(dpre, running_ref[...])
        dup = frame_outer(squeezed, du)
        dpre_row = jnp.sum(dpre, axis=0, keepdims=True)
        dpre_row = jnp.concatenate([dpre_row, jnp.zeros((1, du.shape[1] - squeeze), F32)], axis=1)
        biases = rows8(jnp.sum(du, axis=0, keepdims=True), dpre_row)
        for index in range(tiles):
            own = slice(index * LANES, (index + 1) * LANES)
            at = index * per_tile + narrow // 8
            pack_ref[at : at + squeeze // 8] = ddown[:, own].reshape(squeeze // 8, 8, LANES)
            at = at + squeeze // 8
            pack_ref[at : at + squeeze // 8] = dup[:, own].reshape(squeeze // 8, 8, LANES)
            pack_ref[at + squeeze // 8] = biases[:, own]
        drunning = skinny_dot(dpre, down_ref[0])
        dpooled = exact_dot(running_matrix(counts_ref, frames), drunning, TN) * (1.0 / pixels)
        for index in range(tiles):
            dgate_ref[index] = dpooled[:, index * LANES : (index + 1) * LANES]

    def slope(tile, carry):
        lanes, average, root, scale, shift = norm_of(tile)
        gates = gates_ref[:, lanes_of(gates_ref, tile)]

        def chunk(index, inside):
            summed, cross = inside
            for inner in range(group):
                t = index * group + inner
                at = pl.ds(t * per_frame, per_frame)
                depth = d_ref[at, :, lanes]
                half_pre = depth * scale + shift
                dsecond = dexc_ref[tile, at] * pick_row(gates, t) + pick_row(dgate_ref[tile], t)
                dy = dsecond * silu_slope(half_pre, half_tanh(half_pre))
                dy = dy * live_value(t, total)
                dy2_ref[at, :, lanes] = dy
                summed = summed + jnp.sum(dy, axis=0)
                cross = cross + jnp.sum(dy * (depth - average), axis=0)
            return (summed, cross)

        zero = jnp.zeros((8, LANES), F32)
        summed, cross = each_frame(chunks, chunk, (zero, zero))
        rows = stack_rows(jnp.sum(summed, axis=0, keepdims=True), root * jnp.sum(cross, axis=0, keepdims=True))
        send_all(send_ref, rows, lanes)
        return carry

    if block:
        head()
        lax.fori_loop(0, tiles, excite, 0)
        squeeze_part()
        lax.fori_loop(0, tiles, slope, 0)
    else:
        phase = pl.program_id(0)
        tile = pl.program_id(1)

        @pl.when((phase == 0) & (tile == 0))
        def start():
            head()

        @pl.when(phase == 0)
        def first():
            excite(tile, 0)

        @pl.when((phase == 1) & (tile == 0))
        def between():
            squeeze_part()

        @pl.when(phase == 1)
        def second():
            slope(tile, 0)


def squeeze_one_backward_kernel(
    counts_ref, third_ref, z_ref, cot_ref, ngain_ref, nbias_ref, stat_ref, d_ref, gain_ref, bias_ref, down_ref,
    up_ref, proj_ref, gates_ref, running_ref, pre_ref, act_ref, nsum_ref, dy2_ref, send_ref, pack_ref,
    dz3_ref, dz3t_ref, excited_ref, dexc_ref, dgate_ref,
):
    total = live_frames(counts_ref)
    pixels = HALF_ROWS * 8

    def head():
        count = stat_ref[2:3, 0:LANES]
        sums = row_total(third_ref)
        mean, variance = moments_of(sums, count)
        root = lax.rsqrt(variance + EPSILON)
        gain = ngain_ref[1:2, :]
        bias_sum = sums[2:3, :]
        gain_sum = root * (sums[3:4, :] - mean * bias_sum)
        nsum_ref[...] = rows8(gain_sum, bias_sum, mean, variance)
        row = lax.broadcasted_iota(jnp.int32, z_ref.shape, 0) // pixels
        live = row < total
        normed = (z_ref[...] - mean) * root
        act = jnp.where(live, gain * normed + nbias_ref[1:2, :], 0.0)
        act_ref[...] = act.T[0 : act_ref.shape[0]]
        dz3 = gain * root * (cot_ref[...] - bias_sum / count - normed * (gain_sum / count))
        dz3 = jnp.where(live, dz3, 0.0)
        dz3_ref[...] = side_by_side(dz3)
        dz3t_ref[...] = jnp.concatenate(halves(dz3.T), axis=0)

    squeeze_backward_body(
        1, counts_ref, stat_ref, d_ref, gain_ref, bias_ref, down_ref, up_ref, proj_ref, gates_ref, running_ref,
        pre_ref, dy2_ref, send_ref, pack_ref, dz3_ref, dz3t_ref, excited_ref, dexc_ref, dgate_ref, head,
    )


def input_factors(sums, stat_ref, count, gain, w):
    root = lax.rsqrt(stat_ref[1:2, :] + EPSILON)
    factor = gain * root
    matrix = exact_dot(w * (factor * root * sums[1:2] / count), w, NT)
    return (matrix, row_dot(factor * sums[0:1] / count, w, NT))


def covariance(gram, summed, count):
    mean = summed / count
    return (mean, gram / count - outer(mean, mean))


def squeeze_zero_backward_kernel(
    counts_ref, top_ref, stat1_ref, gram_ref, nstat_ref, dxpre_ref, x1_ref, z_ref, ngain_ref, w_ref, gains_ref, q_one_ref,
    stat_ref, d_ref, gain_ref, bias_ref, down_ref, up_ref, proj_ref, gates_ref, running_ref, pre_ref,
    dx1_ref, nsum_ref, dy2_ref, send_ref, pack_ref, dz3_ref, dz3t_ref, excited_ref, dexc_ref, dgate_ref,
):
    total = live_frames(counts_ref)
    width = gains_ref.shape[1]

    def head():
        start = pack_tiles(proj_ref.shape[1], down_ref.shape[1]) * (width // LANES)
        pack_ref[start : start + q_one_ref.shape[0]] = q_one_ref[...]
        count = stat_ref[2:3, :]
        wide_count = jnp.broadcast_to(count[:, 0:1], (1, width))
        sums = row_total(top_ref, slice(0, width))
        extra = row_total(top_ref, slice(width, width + LANES))
        matrix, shift = input_factors(sums, stat1_ref, wide_count, gains_ref[2:3, :], pad_rows(w_ref[0]))
        mean = nstat_ref[0:1, :]
        root = lax.rsqrt(nstat_ref[1:2, :] + EPSILON)
        mean_x1 = gram_ref[3 * LANES : 3 * LANES + 1, :] / count
        cross = (gram_ref[LANES : 2 * LANES, :] - count * outer(mean_x1, mean)) * root
        gain_sum = extra[0:1] - jnp.sum(matrix * cross, axis=0, keepdims=True)
        bias_sum = extra[1:2] - count * shift
        nsum_ref[...] = rows8(gain_sum, bias_sum, mean, nstat_ref[1:2, :])
        factor = ngain_ref[0:1, :] * root
        square = right_square(matrix)
        bias_mean = bias_sum / count
        gain_mean = gain_sum / count

        def frame(t, carry):
            at = pl.ds(pl.multiple_of(t * 256, 256), 256)
            centred = side_by_side(x1_ref[at, :] - mean_x1)
            live = live_value(t, total)
            dx1 = (dxpre_ref[at, :] - fold_right(plain_dot(centred, square)) - shift) * live
            dx1_ref[at, :] = dx1
            normed = (z_ref[at, :] - mean) * root
            dz3 = factor * (dx1 - bias_mean - normed * gain_mean) * live
            dz3_ref[at, :] = side_by_side(dz3)
            dz3t_ref[:, at] = jnp.concatenate(halves(dz3.T), axis=0)
            return carry

        each_frame(dz3_ref.shape[0] // 256, frame, 0)

    squeeze_backward_body(
        0, counts_ref, stat_ref, d_ref, gain_ref, bias_ref, down_ref, up_ref, proj_ref, gates_ref, running_ref,
        pre_ref, dy2_ref, send_ref, pack_ref, dz3_ref, dz3t_ref, excited_ref, dexc_ref, dgate_ref, head,
    )

def back_full(t, k, a_ref, w_ref, z_ref, f_ref, dw_ref, fresh):
    weights = [w_ref[k * 9 + tap] for tap in range(9)]
    target = t - k
    sums = [None] * 9
    a_rows = {}
    z_rows = {}
    for i in range(SIDE):
        for need in (i, i + 1, i + 2):
            if need not in a_rows:
                a_rows[need] = [a_ref[target, plane, need] for plane in range(2)]
                z_rows[need] = [z_ref[t, plane, need] for plane in range(4)]
        even = None
        odd = None
        z_even, z_odd, z_odd_down, z_even_up = z_rows[i + 1]
        for r in range(3):
            b_even, b_odd, b_odd_down, b_even_up = z_rows[i + 2 - r]
            left, centre, right = weights[3 * r : 3 * r + 3]
            part_even = centre * b_even + right * b_odd_down + left * b_odd
            part_odd = centre * b_odd + right * b_even + left * b_even_up
            even = part_even if even is None else even + part_even
            odd = part_odd if odd is None else odd + part_odd
            a_even, a_odd = a_rows[i + r]
            pieces = (
                z_even_up * a_odd + z_odd * a_even,
                z_even * a_even + z_odd * a_odd,
                z_even * a_odd + z_odd_down * a_even,
            )
            for c in range(3):
                at = 3 * r + c
                sums[at] = pieces[c] if sums[at] is None else sums[at] + pieces[c]
        a_rows.pop(i)
        z_rows.pop(i)
        at = target * FULL_ROWS + 2 * i
        if fresh:
            f_ref[at] = even
            f_ref[at + 1] = odd
        else:
            f_ref[at] = f_ref[at] + even
            f_ref[at + 1] = f_ref[at + 1] + odd
    for tap in range(9):
        dw_ref[k * 9 + tap] = dw_ref[k * 9 + tap] + sums[tap]


def back_half(t, k, a_ref, w_ref, z_ref, f_ref, dw_ref, fresh):
    weights = [w_ref[k * 9 + tap] for tap in range(9)]
    target = t - k
    sums = [None] * 9

    def put(row, parity, value):
        at = target * FULL_ROWS + 2 * row + parity
        f_ref[at] = value if fresh else f_ref[at] + value

    carried = [a_ref[target, plane, 0] for plane in range(2)]
    here = [z_ref[t, plane, 0] for plane in range(2)]
    for i in range(HALF_ROWS):
        below = [z_ref[t, plane, i + 1] for plane in range(2)]
        dz, dz_up = here
        rows = [carried]
        for need in (2 * i + 1, 2 * i + 2):
            rows.append([a_ref[target, plane, need] for plane in range(2)])
        carried = rows[2]
        put(2 * i, 0, weights[4] * dz)
        put(2 * i, 1, weights[5] * dz + weights[3] * dz_up)
        put(2 * i + 1, 0, weights[7] * dz + weights[1] * below[0])
        put(
            2 * i + 1,
            1,
            weights[8] * dz + weights[6] * dz_up + (weights[2] * below[0] + weights[0] * below[1]),
        )
        for r in range(3):
            a_even, a_odd = rows[r]
            pieces = (dz_up * a_odd, dz * a_even, dz * a_odd)
            for c in range(3):
                at = 3 * r + c
                sums[at] = pieces[c] if sums[at] is None else sums[at] + pieces[c]
        here = below
    for tap in range(9):
        dw_ref[k * 9 + tap] = dw_ref[k * 9 + tap] + sums[tap]


def depth_backward_kernel(
    block, before, final, counts_ref, grads_ref, stat2_ref, stat_ref, nstat_ref, dy2_ref, d_ref, e_ref, columns_ref, w_ref,
    gain_ref, bias_ref, taps_ref, z3_ref, dx_in_ref, sums_in_ref, list_in_ref, dxpre_ref, send_ref, q_ref, grad_rows_ref,
    a_ref, z_ref, f_ref, taps8_ref, dw_ref, pair_ref,
):
    tile = pl.program_id(0)
    tiles = pl.num_programs(0)
    total = live_frames(counts_ref)
    frames = a_ref.shape[0]
    norm_row = 2 * block
    half = block == 1
    per_frame = HALF_ROWS if half else FULL_ROWS
    taps = dw_ref.shape[0]

    @pl.when(tile == 0)
    def start():
        clear_edges(a_ref)
        clear_edges(z_ref)
        if before:
            dxpre_ref[...] = dx_in_ref[...]
            send_all(send_ref, sums_in_ref[0:2, :], slice(0, before * LANES))
            q_ref[0 : list_in_ref.shape[0]] = list_in_ref[...]
        else:
            dxpre_ref[...] = jnp.zeros_like(dxpre_ref)

        def dead(t, carry):
            f_ref[pl.ds(t * FULL_ROWS, FULL_ROWS)] = jnp.zeros((FULL_ROWS, 8, LANES), F32)
            return carry

        lax.fori_loop(total, frames, dead, 0)

    count = stat2_ref[2:3, :]
    grads = row_total(grads_ref)
    grad_rows_ref[...] = rows8(grads[0:1], grads[1:2])
    average = stat2_ref[0:1, :]
    root = lax.rsqrt(stat2_ref[1:2, :] + EPSILON)
    scale_two = gain_ref[norm_row + 1 : norm_row + 2, :] * root
    slope = scale_two * root * grads[1:2] / count
    level = scale_two * grads[0:1] / count - slope * average
    average_one = stat_ref[0:1, :]
    root_one = lax.rsqrt(stat_ref[1:2, :] + EPSILON)
    scale_one = gain_ref[norm_row : norm_row + 1, :] * root_one
    shift_half = 0.5 * (bias_ref[norm_row : norm_row + 1, :] - average_one * scale_one)
    scale_half = 0.5 * scale_one

    def fill(t, carry):
        at = pl.ds(t * per_frame, per_frame)
        dz = scale_two * dy2_ref[at] - (slope * d_ref[at] + level)
        if half:
            z_ref[t, 0, 0:HALF_ROWS] = dz
            z_ref[t, 1, 0:HALF_ROWS] = columns_up(dz)
        else:
            pair = dz.reshape(SIDE, 2, 8, LANES)
            z_ref[t, 0, 1 : SIDE + 1] = pair[:, 0]
            z_ref[t, 1, 1 : SIDE + 1] = pair[:, 1]
            z_ref[t, 2, 1 : SIDE + 1] = columns_down(pair[:, 1])
            z_ref[t, 3, 1 : SIDE + 1] = columns_up(pair[:, 0])
        values = e_ref[pl.ds(pl.multiple_of(t * FULL_ROWS, FULL_ROWS), FULL_ROWS)]
        write_first(t, total, values, scale_half, shift_half, a_ref, 2)
        return carry

    each_frame(frames, fill, 0)
    spread_taps(taps_ref, taps8_ref)
    dw_ref[...] = jnp.zeros_like(dw_ref)
    back = back_half if half else back_full

    def frame(t, carry):
        back(t, 0, a_ref, taps8_ref, z_ref, f_ref, dw_ref, True)
        last = jnp.minimum(place_of(counts_ref, t), LAGS - 1)

        def lag(k, inner):
            back(t, k, a_ref, taps8_ref, z_ref, f_ref, dw_ref, False)
            return inner

        return lax.fori_loop(1, last + 1, lag, carry)

    lax.fori_loop(0, total, frame, 0)
    square = right_square_t(pad_rows(w_ref[0]))

    def finish(t, carry):
        rows = pl.ds(pl.multiple_of(t * FULL_ROWS, FULL_ROWS), FULL_ROWS)
        flat = pl.ds(pl.multiple_of(t * 256, 256), 256)
        values = e_ref[rows]
        half_pre = values * scale_half + shift_half
        dy = f_ref[rows] * silu_slope(half_pre, half_tanh(half_pre))
        summed = carry[0] + jnp.sum(dy, axis=0)
        cross = carry[1] + jnp.sum(dy * (values - average_one), axis=0)
        dy = dy.reshape(256, LANES)
        pair_ref[flat, :] = side_by_side(dy)
        scaled = side_by_side(dy * scale_one)
        dxpre_ref[flat, :] = dxpre_ref[flat, :] + fold_right(plain_dot(scaled, square, NT))
        return (summed, cross)

    zero = jnp.zeros((8, LANES), F32)
    summed, cross = each_frame(frames, finish, (zero, zero))
    rows = stack_rows(jnp.sum(summed, axis=0, keepdims=True), root_one * jnp.sum(cross, axis=0, keepdims=True))
    if final:
        send_all(send_ref, rows, pl.ds(pl.multiple_of((tile + before) * LANES, LANES), LANES))
    else:
        send_ref[...] = rows8(rows[0:1], rows[1:2])
    gathered = fold_square(plain_dot(columns_ref[...], pair_ref[...]))
    narrow = w_ref.shape[1]
    dtaps = jnp.sum(dw_ref[...], axis=1)
    unused = (-taps) % 8
    dtaps = jnp.concatenate([dtaps, jnp.zeros((unused, LANES), F32)], axis=0)
    values = jnp.concatenate([gathered[0:narrow], dtaps], axis=0)
    listed = values.shape[0] // 8
    q_ref[pl.ds((tile + before) * listed, listed)] = values.reshape(listed, 8, LANES)

    if half:
        @pl.when(tile == tiles - 1)
        def tail():
            mean = nstat_ref[0:1, :]
            root_three = lax.rsqrt(nstat_ref[1:2, :] + EPSILON)

            def part(t, carry):
                flat = pl.ds(pl.multiple_of(t * 256, 256), 256)
                dx = dxpre_ref[flat, :].reshape(32, 8, LANES)
                normed = ((z3_ref[flat, :] - mean) * root_three).reshape(32, 8, LANES)
                return (carry[0] + jnp.sum(dx * normed, axis=0), carry[1] + jnp.sum(dx, axis=0))

            cross_three, summed_three = each_frame(frames, part, (zero, zero))
            rows = stack_rows(
                jnp.sum(cross_three, axis=0, keepdims=True), jnp.sum(summed_three, axis=0, keepdims=True)
            )
            width = send_ref.shape[2] - LANES
            send_all(send_ref, rows, slice(width, width + LANES))


def finish_kernel(
    counts_ref, momentum_ref, gram_ref, stat01_ref, stat02_ref, stat11_ref, stat12_ref, grad0_ref,
    grad1_ref, one_ref, zero_ref, nsum0_ref, nsum1_ref, dxpre_ref, x_ref, dx1_ref, w_ref, gain_ref, means_ref, vars_ref,
    nmeans_ref, nvars_ref,
    video_ref, less_ref, factor_ref, wgain_ref, wbias_ref, ngain_ref, nbias_ref, newm_ref, newv_ref, newnm_ref, newnv_ref,
):
    total = live_frames(counts_ref)
    full = stat01_ref[2:3, :]
    count = full[:, 0:LANES]
    width = full.shape[1]
    top_zero = row_total(zero_ref)
    top_one = row_total(one_ref, slice(0, width))
    w_zero = pad_rows(w_ref[0])
    matrix, shift = input_factors(top_zero, stat01_ref, full, gain_ref[0:1, :], w_zero)
    square = right_square(matrix)
    mean_x, cov_zero = covariance(
        gram_ref[2 * LANES : 3 * LANES, :], gram_ref[3 * LANES + 1 : 3 * LANES + 2, :], count
    )
    order = column_order()
    narrow = video_ref.shape[0]

    def frame(t, carry):
        at = pl.ds(pl.multiple_of(t * 256, 256), 256)
        centred = side_by_side(x_ref[at, :] - mean_x)
        dx = (dxpre_ref[at, :] - fold_right(plain_dot(centred, square)) - shift) * live_value(t, total) + dx1_ref[at, :]
        for part in range(2):
            own = dx[part * LANES : (part + 1) * LANES].T[0:narrow]
            pieces = pick_thirds(order, own, NN, False)
            start = pl.multiple_of(t * 256 + part * LANES, LANES)
            video_ref[:, pl.ds(start, LANES)] = pieces[0] + pieces[1] + pieces[2]
        return carry

    each_frame(x_ref.shape[0] // 256, frame, 0)
    mean_one, cov_one = covariance(gram_ref[0:LANES, :], gram_ref[3 * LANES : 3 * LANES + 1, :], count)
    plan = ((mean_x, cov_zero, stat01_ref, top_zero, w_zero), (mean_one, cov_one, stat11_ref, top_one, pad_rows(w_ref[1])))
    for block, (mean_row, cov, stat_ref, top, w) in enumerate(plan):
        root = lax.rsqrt(stat_ref[1:2, :] + EPSILON)
        factor = gain_ref[2 * block : 2 * block + 1, :] * root
        less = outer(mean_row, top[0:1]) + exact_dot(cov, w) * (root * top[1:2])
        less_ref[block] = (less * factor)[0:narrow]
        factor_ref[8 * block : 8 * block + 8, :] = rows8(factor)
    momentum = momentum_ref[0].astype(F32) / 10.0
    wgain_ref[...] = stack_rows(top_zero[1:2], grad0_ref[1:2, :], top_one[1:2], grad1_ref[1:2, :])
    wbias_ref[...] = stack_rows(top_zero[0:1], grad0_ref[0:1, :], top_one[0:1], grad1_ref[0:1, :])
    stats = (stat01_ref, stat02_ref, stat11_ref, stat12_ref)
    means = stack_rows(*(ref[0:1, :] for ref in stats))
    variances = stack_rows(*(ref[1:2, :] * (ref[2:3, :] / (ref[2:3, :] - 1.0)) for ref in stats))
    newm_ref[...] = (1.0 - momentum) * means_ref[...] + momentum * means
    newv_ref[...] = (1.0 - momentum) * vars_ref[...] + momentum * variances
    ngain_ref[...] = stack_rows(nsum0_ref[0:1, :], nsum1_ref[0:1, :])[:, 0:narrow]
    nbias_ref[...] = stack_rows(nsum0_ref[1:2, :], nsum1_ref[1:2, :])[:, 0:narrow]
    means = stack_rows(nsum0_ref[2:3, :], nsum1_ref[2:3, :])[:, 0:narrow]
    quarter = 0.25 * count
    variances = stack_rows(
        nsum0_ref[3:4, :] * (count / (count - 1.0)), nsum1_ref[3:4, :] * (quarter / (quarter - 1.0))
    )[:, 0:narrow]
    newnm_ref[...] = (1.0 - momentum) * nmeans_ref[...] + momentum * means
    newnv_ref[...] = (1.0 - momentum) * nvars_ref[...] + momentum * variances


def gradient_kernel(
    core_ref, pack0_ref, pack0_other_ref, pack1_ref, late_ref, late_other_ref, less_ref, factor_ref,
    dw_ref, dtaps_ref, ddown_ref, dup_ref, dproj_ref, dupb_ref, ddownb_ref,
):
    narrow = dw_ref.shape[1]
    taps = dtaps_ref.shape[1]
    squeeze = ddown_ref.shape[1]
    tiles = dw_ref.shape[2] // LANES
    per_pack = pack_tiles(narrow, squeeze)
    per_tile = narrow // 8 + -(-taps // 8)
    first_core = core_ref[0] == 0

    def rows_of(pair, at, count):
        mine, other = pair
        if other is None:
            return mine[at : at + count].reshape(-1, LANES)
        half = mine.shape[0]
        pieces = []
        if at < half:
            size = min(count, half - at)
            here = slice(at, at + size)
            pieces.append(jnp.where(first_core, mine[here], other[here]))
            count = count - size
            at = at + size
        if count:
            here = slice(at - half, at - half + count)
            pieces.append(jnp.where(first_core, other[here], mine[here]))
        values = pieces[0] if len(pieces) == 1 else jnp.concatenate(pieces, axis=0)
        return values.reshape(-1, LANES)

    packs = ((pack0_ref, pack0_other_ref), (pack1_ref, None))
    lists = ((late_ref, late_other_ref), packs[0])
    for block in range(2):
        down_rows = []
        for tile in range(tiles):
            lanes = slice(tile * LANES, (tile + 1) * LANES)
            at = tile * per_pack
            dproj_ref[block, :, lanes] = rows_of(packs[block], at, narrow // 8)
            at = at + narrow // 8
            ddown_ref[block, :, lanes] = rows_of(packs[block], at, squeeze // 8)
            at = at + squeeze // 8
            dup_ref[block, :, lanes] = rows_of(packs[block], at, squeeze // 8)
            biases = rows_of(packs[block], at + squeeze // 8, 1)
            dupb_ref[block : block + 1, lanes] = biases[0:1]
            down_rows.append(biases[1:2])
            values = rows_of(lists[block], (per_pack * tiles if block else 0) + tile * per_tile, per_tile)
            dw = values[0:narrow] * factor_ref[8 * block : 8 * block + 1, lanes] - less_ref[block, :, lanes]
            dw_ref[block, :, lanes] = dw
            dtaps_ref[block, :, lanes] = values[narrow : narrow + taps]
        ddownb_ref[block : block + 1, :] = jnp.concatenate(down_rows, axis=1)[:, 0:squeeze]


AXES = ("dp", "z", "core")
CHIPS = ("dp", "z")


def exchange(send):
    return lax.all_to_all(send, AXES, 0, 0, tiled=True)


def together(*values):
    return lax.optimization_barrier(values)


def swap_cores(values):
    return lax.ppermute(values, "core", [(0, 1), (1, 0)])


def add_cores(tiles):
    core = lax.axis_index("core")
    pair = tiles.reshape(2, tiles.shape[0] // 2, *tiles.shape[1:])
    mine = lax.dynamic_index_in_dim(pair, core, 0, keepdims=False)
    return mine + swap_cores(lax.dynamic_index_in_dim(pair, 1 - core, 0, keepdims=False))


def share_out(tiles, names=CHIPS):
    count = 1
    for name in names:
        count = count * lax.axis_size(name)
    return lax.all_to_all(tiles.reshape(count, -1, *tiles.shape[1:]), names, 0, 0, tiled=True)


def share_back(pieces, names=CHIPS):
    own = jnp.sum(pieces, axis=0)
    everyone = lax.all_to_all(jnp.broadcast_to(own[None], pieces.shape), names, 0, 0, tiled=True)
    return everyone.reshape(-1, *pieces.shape[2:])


def shape(*dims, kind=F32):
    return jax.ShapeDtypeStruct(dims, kind)


def whole(array):
    rank = len(array.shape)
    return pl.BlockSpec(array.shape, lambda *ids: (0,) * rank)


SCALARS = pl.BlockSpec(memory_space=pltpu.SMEM)


def call(kernel, grid, in_specs, out_specs, out_shape, scratch, args):
    return pl.pallas_call(
        kernel,
        grid=grid,
        in_specs=in_specs,
        out_specs=out_specs,
        out_shape=out_shape,
        scratch_shapes=scratch,
        compiler_params=pltpu.CompilerParams(vmem_limit_bytes=VMEM_BYTES),
        cost_estimate=pl.CostEstimate(
            flops=1_000_000_000, bytes_accessed=1_000_000, transcendentals=0
        ),
    )(*args)


def simple_call(kernel, scalars, args, outs):
    return call(
        kernel, (1,), [SCALARS] * scalars + [whole(array) for array in args[scalars:]], [whole(item) for item in outs],
        outs, [], args,
    )


def local(
    video, frame_counts, momentum_index, expand_weight, wide_gains, wide_biases, narrow_gains, narrow_biases, depth_weight,
    squeeze_weight, squeeze_bias, excite_weight, excite_bias, project_weight, wide_means, wide_variances, narrow_means,
    narrow_variances, cotangent,
):
    devices = lax.axis_size("dp") * lax.axis_size("z") * lax.axis_size("core")
    cin, pixels = video.shape
    half_pixels = cotangent.shape[1]
    width = expand_weight.shape[1]
    squeeze = squeeze_weight.shape[1]
    frames = pixels // (SIDE * SIDE)
    tiles = width // LANES
    taps = depth_weight.shape[1]
    w_t = jnp.swapaxes(expand_weight, 1, 2)
    up_t = jnp.swapaxes(excite_weight, 1, 2)
    lanes_pad = ((0, 0), (0, LANES - cin))
    ngains = jnp.pad(narrow_gains, lanes_pad)
    nbiases = jnp.pad(narrow_biases, lanes_pad)
    full_rows = frames * FULL_ROWS
    half_rows = frames * HALF_ROWS
    low = jnp.bfloat16

    def round_up(count):
        return -(-count // devices) * devices

    def fixed(*dims):
        return pl.BlockSpec(dims, lambda *ids: (0,) * len(dims))

    def tile_rows(rows):
        return pl.BlockSpec((rows, LANES), lambda j: (0, j))

    def tile_cube(rows):
        return pl.BlockSpec((rows, 8, LANES), lambda j: (0, 0, j))

    def tile_sums(rows=2):
        return pl.BlockSpec((devices, rows, LANES), lambda j: (0, 0, j))

    def weight_tile(block, rows):
        return pl.BlockSpec((1, rows, LANES), lambda j, block=block: (block, 0, j))

    def of_block(block, rows, lanes):
        return pl.BlockSpec((1, rows, lanes), lambda *ids: (block, 0, 0))

    def early(make):
        return make(lambda p, j: j * (1 - p) + (tiles - 1) * p)

    def late(make):
        return make(lambda p, j: j * p)

    def both(make):
        return make(lambda p, j: j)

    def rows_at(rows):
        return lambda at: pl.BlockSpec((rows, LANES), lambda p, j: (0, at(p, j)))

    def cube_at(rows):
        return lambda at: pl.BlockSpec((rows, 8, LANES), lambda p, j: (0, 0, at(p, j)))

    def sums_at(rows):
        return lambda at: pl.BlockSpec((devices, rows, LANES), lambda p, j: (0, 0, at(p, j)))

    def weight_at(block, rows):
        return lambda at: pl.BlockSpec((1, rows, LANES), lambda p, j: (block, 0, at(p, j)))

    x, x_rows, x_columns, cot, gram_zero, sums = call(
        prepare_kernel, (1,), [SCALARS, whole(video), whole(cotangent), of_block(0, cin, width)],
        [fixed(pixels, LANES), fixed(pixels, 2 * LANES), fixed(2 * LANES, pixels), fixed(half_pixels, LANES),
         fixed(LANES + 8, LANES), fixed(devices, 2, width + LANES)],
        [shape(pixels, LANES), shape(pixels, 2 * LANES, kind=low), shape(2 * LANES, pixels, kind=low),
         shape(half_pixels, LANES), shape(LANES + 8, LANES), shape(devices, 2, width + LANES)],
        [], (frame_counts, video, cotangent, w_t),
    )
    sums = exchange(sums)

    def expand(block, sums, count, count_spec, rows):
        depth_rows = half_rows if block else full_rows
        return call(
            functools.partial(expand_kernel, block), (tiles,),
            [SCALARS, tile_sums(), count_spec, whole(rows), weight_tile(block, cin), tile_rows(4), tile_rows(4),
             weight_tile(block, taps)],
            [tile_cube(full_rows), tile_cube(depth_rows), tile_rows(8), tile_sums()],
            [shape(full_rows, 8, width), shape(depth_rows, 8, width), shape(8, width), shape(devices, 2, width)],
            [pltpu.VMEM((frames, 4, SIDE + 2, 8, LANES), F32), pltpu.VMEM((taps, 8, LANES), F32)],
            (frame_counts, sums, count, rows, w_t, wide_gains, wide_biases, depth_weight),
        )

    count_spec = pl.BlockSpec((devices, 2, LANES), lambda j: (0, 0, tiles))
    e_zero, d_zero, stat01, sums = expand(0, sums, sums, count_spec, x_rows)
    sums = exchange(sums)

    def squeeze_forward(block, sums, stat, depth):
        rows = half_rows if block else full_rows
        kinds = 4 if block else 2
        moving = [tile_sums(), tile_rows(8), tile_cube(rows), tile_rows(4), tile_rows(4)]
        if block:
            moving = [whole(array) for array in (sums, stat, depth, wide_gains, wide_biases)]
        return call(
            functools.partial(squeeze_forward_kernel, block), (1 if block else tiles,),
            [SCALARS] + moving
            + [of_block(block, squeeze, width), whole(squeeze_bias), of_block(block, squeeze, width), whole(excite_bias),
               of_block(block, cin, width), whole(cot)],
            [fixed(rows * 8, LANES), fixed(8, width), fixed(8, width), fixed(8, squeeze),
             fixed(8, width) if block else tile_rows(8), fixed(devices, kinds, LANES)],
            [shape(rows * 8, LANES), shape(8, width), shape(8, width), shape(8, squeeze), shape(8, width),
             shape(devices, kinds, LANES)],
            [pltpu.VMEM((tiles, rows, 8, LANES), F32), pltpu.VMEM((tiles, frames, LANES), F32)],
            (frame_counts, sums, stat, depth, wide_gains, wide_biases, squeeze_weight, squeeze_bias, up_t, excite_bias,
             project_weight, cot),
        )

    z_zero, gates_zero, running_zero, pre_zero, stat02, sums = squeeze_forward(0, sums, stat01, d_zero)
    sums = exchange(sums)
    narrow_args = (frame_counts, sums, stat01, gram_zero, x, z_zero, ngains, nbiases, w_t)
    narrow_outs = [
        shape(pixels, LANES), shape(pixels, 2 * LANES, kind=low), shape(2 * LANES, pixels, kind=low),
        shape(round_up(3 * LANES // 8 + 1), 8, LANES), shape(8, LANES), shape(devices, 2, width),
    ]
    x1, x1_rows, x1_columns, gram, nstat, sums = call(
        narrow_kernel, (1,), [SCALARS] + [whole(array) for array in narrow_args[1:-1]] + [of_block(1, cin, width)],
        [whole(item) for item in narrow_outs], narrow_outs, [], narrow_args,
    )
    sums, gram = together(exchange(sums), gram)
    gram = share_out(gram, AXES)
    e_one, d_one, stat11, sums = expand(1, sums, nstat, pl.BlockSpec((8, LANES), lambda j: (0, 0)), x1_rows)
    sums, gram = together(sums, gram)
    sums = exchange(sums)
    z_one, gates_one, running_one, pre_one, stat12, sums = squeeze_forward(1, sums, stat11, d_one)
    third, gram = together(exchange(sums), gram)
    gram = share_back(gram, AXES).reshape(-1, LANES)
    q_tiles = cin // 8 + -(-taps // 8)

    def backward_specs(block):
        rows = half_rows if block else full_rows
        ins = [fixed(8, width), fixed(rows, 8, width), fixed(4, width), fixed(4, width), of_block(block, squeeze, width),
               of_block(block, squeeze, width), of_block(block, cin, width), fixed(8, width), fixed(8, width),
               fixed(8, squeeze)]
        if not block:
            ins[0:4] = [both(rows_at(8)), both(cube_at(rows)), both(rows_at(4)), both(rows_at(4))]
            ins[6] = early(weight_at(block, cin))
        packed = tiles * pack_tiles(cin, squeeze)
        packed = packed if block else round_up(packed + tiles * q_tiles)
        wide_outs = [fixed(rows, 8, width), fixed(devices, 2, width)] if block else [late(cube_at(rows)), late(sums_at(2))]
        outs = [fixed(8, LANES)] + wide_outs + [fixed(packed, 8, LANES)]
        shapes = [shape(8, LANES), shape(rows, 8, width), shape(devices, 2, width), shape(packed, 8, LANES)]
        scratch = [pltpu.VMEM((rows * 8, 2 * LANES), low), pltpu.VMEM((2 * LANES, rows * 8), low),
                   pltpu.VMEM((rows * 8, 2 * LANES), low), pltpu.VMEM((tiles, rows, 8, LANES), F32),
                   pltpu.VMEM((tiles, frames, LANES), F32)]
        return (ins, outs, shapes, scratch)

    ins, outs, shapes, scratch = backward_specs(1)
    activations, nsum_one, dy2_one, sums, pack_one = call(
        squeeze_one_backward_kernel, (1,),
        [SCALARS, whole(third), whole(z_one), whole(cot), whole(ngains), whole(nbiases)] + ins,
        [fixed(cin, half_pixels)] + outs, [shape(cin, half_pixels)] + shapes, scratch,
        (frame_counts, third, z_one, cot, ngains, nbiases, stat12, d_one, wide_gains, wide_biases, squeeze_weight, up_t,
         project_weight, gates_one, running_one, pre_one),
    )
    sums, gram = together(sums, gram)
    pack_one = lax.psum(pack_one, AXES)
    sums = exchange(sums)
    nothing = jnp.zeros((8, LANES), F32)

    def depth_backward(block, begin, end, sums, stat2, stat, dy2, depth, expanded, columns, dx_in, sums_in, list_in):
        rows = half_rows if block else full_rows
        z_shape = (frames, 2, HALF_ROWS + 1, 8, LANES) if block else (frames, 4, SIDE + 2, 8, LANES)
        count = end - begin
        final = end == tiles
        listed = round_up(end * q_tiles) if final and not block else end * q_tiles
        if final:
            send = (devices, 2, width + (LANES if block else 0))
            send_spec = fixed(*send)
        else:
            send = (8, count * LANES)
            send_spec = tile_rows(8)

        def wide_rows(rows):
            return pl.BlockSpec((rows, LANES), lambda j: (0, j + begin))

        def wide_cube(rows):
            return pl.BlockSpec((rows, 8, LANES), lambda j: (0, 0, j + begin))

        def wide_weight(rows):
            return pl.BlockSpec((1, rows, LANES), lambda j: (block, 0, j + begin))

        return call(
            functools.partial(depth_backward_kernel, block, begin, final), (count,),
            [SCALARS, pl.BlockSpec((devices, 2, LANES), lambda j: (0, 0, j + begin)), wide_rows(8), wide_rows(8), whole(nstat),
             wide_cube(rows), wide_cube(rows), wide_cube(full_rows), whole(columns), wide_weight(cin), wide_rows(4),
             wide_rows(4), wide_weight(taps), whole(z_zero), whole(dx_in), whole(sums_in), whole(list_in)],
            [fixed(pixels, LANES), send_spec, fixed(listed, 8, LANES), tile_rows(8)],
            [shape(pixels, LANES), shape(*send), shape(listed, 8, LANES), shape(8, count * LANES)],
            [pltpu.VMEM((frames, 2, SIDE + 2, 8, LANES), F32), pltpu.VMEM(z_shape, F32), pltpu.VMEM((full_rows, 8, LANES), F32),
             pltpu.VMEM((taps, 8, LANES), F32), pltpu.VMEM((taps, 8, LANES), F32), pltpu.VMEM((pixels, 2 * LANES), low)],
            (frame_counts, sums, stat2, stat, nstat, dy2, depth, expanded, columns, w_t, wide_gains, wide_biases,
             depth_weight, z_zero, dx_in, sums_in, list_in),
        )

    dxpre_one, sums, q_one, grad_one = depth_backward(
        1, 0, tiles, sums, stat12, stat11, dy2_one, d_one, e_one, x1_columns, nothing, nothing, nothing
    )
    top_one = exchange(sums)
    ins, outs, shapes, scratch = backward_specs(0)
    dx1, nsum_zero, dy2_zero, sums, pack_zero = call(
        squeeze_zero_backward_kernel, (2, tiles),
        [SCALARS, whole(top_one), whole(stat11), whole(gram), whole(nstat), whole(dxpre_one), whole(x1), whole(z_zero),
         whole(ngains), of_block(1, cin, width), whole(wide_gains), whole(q_one)] + ins,
        [fixed(pixels, LANES)] + outs, [shape(pixels, LANES)] + shapes, scratch,
        (frame_counts, top_one, stat11, gram, nstat, dxpre_one, x1, z_zero, ngains, w_t, wide_gains, q_one, stat02, d_zero,
         wide_gains, wide_biases, squeeze_weight, up_t, project_weight, gates_zero, running_zero, pre_zero),
    )
    sums, pack_zero = together(exchange(sums), add_cores(pack_zero))
    pack_zero = share_out(pack_zero)
    first = tiles - tiles // 2
    dxpre_zero, sums_in, late, grad_a = depth_backward(
        0, 0, first, sums, stat02, stat01, dy2_zero, d_zero, e_zero, x_columns, nothing, nothing, nothing
    )
    dxpre_zero, pack_zero = together(dxpre_zero, pack_zero)
    pack_zero = share_back(pack_zero)
    dxpre_zero, sums, late, grad_b = depth_backward(
        0, first, tiles, sums, stat02, stat01, dy2_zero, d_zero, e_zero, x_columns, dxpre_zero, sums_in, late
    )
    grad_zero = jnp.concatenate([grad_a, grad_b], axis=1)
    sums, pack_zero = together(sums, pack_zero)
    pack_zero_other = swap_cores(pack_zero)
    top_zero, late, pack_zero_other = together(exchange(sums), add_cores(late), pack_zero_other)
    late = share_out(late)
    core = lax.axis_index("core").astype(jnp.int32).reshape(1)
    final_args = (
        frame_counts, momentum_index, gram, stat01, stat02, stat11, stat12, grad_zero, grad_one, top_one,
        top_zero, nsum_zero, nsum_one, dxpre_zero, x, dx1, w_t, wide_gains, wide_means, wide_variances, narrow_means,
        narrow_variances,
    )
    final_outs = [
        shape(cin, pixels), shape(2, cin, width), shape(16, width), shape(4, width), shape(4, width), shape(2, cin),
        shape(2, cin), shape(4, width), shape(4, width), shape(2, cin), shape(2, cin),
    ]
    video_grad, less, factor, wgain, wbias, ngain, nbias, newm, newv, newnm, newnv = simple_call(
        finish_kernel, 2, final_args, final_outs
    )
    less, late = together(less, late)
    late = share_back(late)
    late_other = swap_cores(late)
    dw_t, dtaps, ddown, dup, dproj, dupb, ddownb = simple_call(
        gradient_kernel, 1,
        (core, pack_zero, pack_zero_other, pack_one, late, late_other, less, factor),
        [shape(2, cin, width), shape(2, taps, width), shape(2, squeeze, width), shape(2, squeeze, width),
         shape(2, cin, width), shape(2, width), shape(2, squeeze)],
    )
    return (
        activations, video_grad, jnp.swapaxes(dw_t, 1, 2), wgain, wbias, ngain, nbias, dtaps, ddown, ddownb,
        jnp.swapaxes(dup, 1, 2), dupb, dproj, newm, newv, newnm, newnv,
    )


def solution(mesh):
    sizes = (mesh.shape["dp"], mesh.shape["rep"] // 2, 2)
    split_mesh = jax.sharding.Mesh(mesh.devices.reshape(sizes), AXES)
    split = P(None, AXES)
    placed = (split, P(AXES)) + (P(),) * 16 + (split,)
    return jax.shard_map(
        local, mesh=split_mesh, in_specs=placed, out_specs=(split, split) + (P(),) * 15, check_vma=False
    )
```

```python
import functools

import jax
import jax.numpy as jnp
from jax import lax
from jax.experimental import pallas as pl
from jax.experimental.pallas import tpu as pltpu
from jax.sharding import PartitionSpec as P

SIDE = 16
LANES = 128
LAGS = 5
FULL_ROWS = 2 * SIDE
HALF_ROWS = SIDE // 2
EPSILON = 1e-05
HIGHEST = lax.Precision.HIGHEST
F32 = jnp.float32
NN = (((1,), (0,)), ((), ()))
NT = (((1,), (1,)), ((), ()))
TN = (((0,), (0,)), ((), ()))
VMEM_BYTES = 52 * 1024 * 1024


def half_tanh(half_values):
    return jnp.tanh(half_values)


def sigmoid(values):
    return 0.5 * jnp.tanh(0.5 * values) + 0.5


def silu_slope(half_values, tanh):
    return 0.5 * (1.0 + tanh + half_values * (1.0 - tanh * tanh))


def exact_dot(left, right, dims=NN):
    return lax.dot_general(left, right, dims, precision=HIGHEST, preferred_element_type=F32)


def halves(values):
    high = values.astype(jnp.bfloat16)
    return (high, (values - high.astype(F32)).astype(jnp.bfloat16))


def side_by_side(values):
    return jnp.concatenate(halves(values), axis=1)


def right_square(w):
    both = side_by_side(w)
    return jnp.concatenate([both, both], axis=0)


def right_square_t(w):
    high, low = halves(w)
    return jnp.concatenate(
        [jnp.concatenate([high, high], axis=1), jnp.concatenate([low, low], axis=1)], axis=0
    )


def plain_dot(left, right, dims=NN):
    return lax.dot_general(left, right, dims, preferred_element_type=F32)


def fold_right(values):
    lanes = values.shape[1] // 2
    return values[:, :lanes] + values[:, lanes:]


def fold_square(values):
    rows = values.shape[0] // 2
    return fold_right(values[:rows] + values[rows:])


def stacked(values):
    high = values.astype(jnp.bfloat16).astype(F32)
    return jnp.concatenate([high, values - high], axis=0).astype(jnp.bfloat16)


def skinny_dot(left, right, dims=NN):
    rows = left.shape[0]
    both = stacked(left)
    high, low = halves(right)
    values = plain_dot(both, high, dims) + plain_dot(both, low, dims)
    return values[:rows] + values[rows:]


def frame_outer(left, right):
    a_high = left.astype(jnp.bfloat16).astype(F32)
    b_high = right.astype(jnp.bfloat16).astype(F32)
    a_low = left - a_high
    b_low = right - b_high
    a = jnp.concatenate([a_high, a_high, a_low, a_low], axis=0).astype(jnp.bfloat16)
    b = jnp.concatenate([b_high, b_low, b_high, b_low], axis=0).astype(jnp.bfloat16)
    return plain_dot(a, b, TN)


def pad_rows(values):
    return jnp.concatenate([values, jnp.zeros((LANES - values.shape[0], values.shape[1]), values.dtype)], axis=0)


def column_order():
    q = lax.broadcasted_iota(jnp.int32, (LANES, LANES), 0)
    n = lax.broadcasted_iota(jnp.int32, (LANES, LANES), 1)
    source = (q // 16) * 16 + (q % 8) * 2 + (q // 8) % 2
    return (source == n).astype(jnp.bfloat16)


def live_frames(counts_ref):
    total = counts_ref[0]
    for clip in range(1, counts_ref.shape[0]):
        total = total + counts_ref[clip]
    return total


def place_of(counts_ref, frame):
    begin = jnp.int32(0)
    end = jnp.int32(0)
    for clip in range(counts_ref.shape[0]):
        end = end + counts_ref[clip]
        begin = jnp.where(frame >= end, end, begin)
    return frame - begin


def running_matrix(counts_ref, frames):
    after = lax.broadcasted_iota(jnp.int32, (frames, frames), 0)
    before = lax.broadcasted_iota(jnp.int32, (frames, frames), 1)
    begin = jnp.int32(0)
    matrix = jnp.zeros((frames, frames), F32)
    for clip in range(counts_ref.shape[0]):
        end = begin + counts_ref[clip]
        inside = (before >= begin) & (before <= after) & (after < end)
        matrix = matrix + jnp.where(inside, 1.0 / (after - begin + 1).astype(F32), 0.0)
        begin = end
    return matrix


def columns_up(values):
    spot = lax.broadcasted_iota(jnp.int32, values.shape, 1)
    return jnp.where(spot == 7, 0.0, pltpu.roll(values, 7, axis=1))


def columns_down(values):
    spot = lax.broadcasted_iota(jnp.int32, values.shape, 1)
    return jnp.where(spot == 0, 0.0, pltpu.roll(values, 1, axis=1))


def tile_sum(values):
    return jnp.sum(jnp.sum(values, axis=0), axis=0, keepdims=True)


def rows8(*rows):
    lanes = rows[0].shape[1]
    spot = lax.broadcasted_iota(jnp.int32, (8, lanes), 0)
    block = jnp.zeros((8, lanes), F32)
    for index, row in enumerate(rows):
        block = jnp.where(spot == index, row, block)
    return block


def pick_row(block, index):
    spot = lax.broadcasted_iota(jnp.int32, block.shape, 0)
    return jnp.sum(jnp.where(spot == index, block, 0.0), axis=0, keepdims=True)


def outer(left, right):
    return exact_dot(rows8(left), rows8(right), TN)


def row_dot(row, matrix, dims=NN):
    return exact_dot(rows8(row), matrix, dims)[0:1]


def clear_edges(ref):
    planes = ref.shape[1]
    edge = jnp.zeros((8, LANES), F32)
    for t in range(ref.shape[0]):
        for plane in range(planes):
            ref[t, plane, 0] = edge
            ref[t, plane, ref.shape[2] - 1] = edge


def spread_taps(taps_ref, w_ref):
    for tap in range(w_ref.shape[0]):
        w_ref[tap] = jnp.broadcast_to(taps_ref[0, tap : tap + 1, :], (8, LANES))


def conv_full(t, k, a_ref, w_ref, d_ref, fresh):
    weights = [w_ref[k * 9 + tap] for tap in range(9)]
    source = t - k
    rows = {}
    for i in range(SIDE):
        for need in (i, i + 1, i + 2):
            if need not in rows:
                rows[need] = [a_ref[source, plane, need] for plane in range(4)]
        even = None
        odd = None
        for r in range(3):
            a_even, a_odd, a_odd_down, a_even_up = rows[i + r]
            left, centre, right = weights[3 * r : 3 * r + 3]
            part_even = centre * a_even + right * a_odd + left * a_odd_down
            part_odd = centre * a_odd + left * a_even + right * a_even_up
            even = part_even if even is None else even + part_even
            odd = part_odd if odd is None else odd + part_odd
        rows.pop(i)
        at = t * FULL_ROWS + 2 * i
        if fresh:
            d_ref[at] = even
            d_ref[at + 1] = odd
        else:
            d_ref[at] = d_ref[at] + even
            d_ref[at + 1] = d_ref[at + 1] + odd


def conv_half(t, k, a_ref, w_ref, d_ref, fresh):
    weights = [w_ref[k * 9 + tap] for tap in range(9)]
    source = t - k
    carried = [a_ref[source, plane, 0] for plane in range(3)]
    for i in range(HALF_ROWS):
        rows = [carried]
        for need in (2 * i + 1, 2 * i + 2):
            rows.append([a_ref[source, plane, need] for plane in range(3)])
        carried = rows[2]
        total = None
        for r in range(3):
            a_even, a_odd, a_odd_down = rows[r]
            left, centre, right = weights[3 * r : 3 * r + 3]
            part = centre * a_even + right * a_odd + left * a_odd_down
            total = part if total is None else total + part
        at = t * HALF_ROWS + i
        d_ref[at] = total if fresh else d_ref[at] + total


def row_total(ref, lanes=None):
    values = ref[...] if lanes is None or lanes == slice(None) else ref[:, :, lanes]
    return jnp.sum(values, axis=0)


def send_all(send_ref, rows, lanes):
    count = rows.shape[0]

    def one(device, carry):
        send_ref[pl.ds(device, 1), 0:count, lanes] = rows[None]
        return carry

    lax.fori_loop(0, send_ref.shape[0], one, 0)


def stack_rows(*rows):
    return rows8(*rows)[0 : len(rows)]


def pick_thirds(order, values, dims, order_left):
    pieces = []
    rest = values
    for _ in range(3):
        piece = rest.astype(jnp.bfloat16)
        rest = rest - piece.astype(F32)
        args = (order, piece) if order_left else (piece, order)
        pieces.append(plain_dot(*args, dims))
    return pieces


def gram_kernel(counts_ref, video_ref, w_ref, gram_ref, send_ref):
    total = live_frames(counts_ref)
    frames = video_ref.shape[1] // 256
    ones = jnp.ones((8, 256), jnp.bfloat16)

    def frame(t, carry):
        at = pl.ds(pl.multiple_of(t * 256, 256), 256)
        both = jnp.concatenate(halves(pad_rows(video_ref[:, at] * live_value(t, total))), axis=0)
        return (carry[0] + plain_dot(both, both, NT), carry[1] + plain_dot(ones, both, NT))

    init = (jnp.zeros((2 * LANES, 2 * LANES), F32), jnp.zeros((8, 2 * LANES), F32))
    gram, summed = each_frame(frames, frame, init)
    gram = fold_square(gram)
    summed = fold_right(summed)[0:1]
    gram_ref[0:LANES, :] = gram
    gram_ref[LANES : LANES + 8, :] = rows8(summed)
    w = pad_rows(w_ref[0])
    width = w.shape[1]
    sums = stack_rows(row_dot(summed, w), jnp.sum(w * exact_dot(gram, w), axis=0, keepdims=True))
    count = jnp.full((2, LANES), 1.0, F32) * (total * (SIDE * SIDE)).astype(F32)
    send_all(send_ref, sums, slice(0, width))
    send_all(send_ref, count, slice(width, width + LANES))


def prepare_kernel(counts_ref, video_ref, cot_ref, x_ref, rows_ref, columns_ref, cot_out_ref):
    order = column_order()
    total = live_frames(counts_ref)
    for part in range(video_ref.shape[1] // LANES):
        at = slice(part * LANES, (part + 1) * LANES)
        block = pad_rows(video_ref[:, at] * live_value(part // 2, total))
        high, middle, low = pick_thirds(order, block, NT, True)
        x_ref[at, :] = high + middle + low
        rows_ref[at, :] = jnp.concatenate([high, middle], axis=1).astype(jnp.bfloat16)
        columns_ref[:, at] = jnp.concatenate([high.T, middle.T], axis=0).astype(jnp.bfloat16)
    spot = lax.broadcasted_iota(jnp.int32, (LANES, LANES), 1)
    for part in range(cot_ref.shape[1] // LANES):
        at = slice(part * LANES, (part + 1) * LANES)
        frame = (spot + part * LANES) // (HALF_ROWS * 8)
        cot_out_ref[at, :] = jnp.where(frame < total, pad_rows(cot_ref[:, at]), 0.0).T


def moments_of(sums, count):
    average = sums[0:1] / count
    return (average, sums[1:2] / count - average * average)


def narrow_kernel(
    counts_ref, sums_ref, stat_ref, gram0_ref, x_ref, z_ref, ngain_ref, nbias_ref, w_ref,
    x1_ref, rows_ref, columns_ref, gram_ref, stat_out_ref, send_ref,
):
    total = live_frames(counts_ref)
    count = stat_ref[2:3, 0:LANES]
    average, variance = moments_of(row_total(sums_ref), count)
    factor = ngain_ref[0:1, :] * lax.rsqrt(variance + EPSILON)
    shift = nbias_ref[0:1, :] - factor * average
    stat_out_ref[...] = rows8(average, variance, count)
    frames = x_ref.shape[0] // 256

    def frame(t, carry):
        gram, cross, summed = carry
        at = pl.ds(pl.multiple_of(t * 256, 256), 256)
        z = z_ref[at, :]
        rows = (x_ref[at, :] + factor * z + shift) * live_value(t, total)
        x1_ref[at, :] = rows
        both = side_by_side(rows)
        rows_ref[at, :] = both
        columns = jnp.concatenate(halves(rows.T), axis=0)
        columns_ref[:, at] = columns
        gram = gram + plain_dot(columns, both)
        cross = cross + plain_dot(columns, side_by_side(z))
        return (gram, cross, summed + jnp.sum(rows, axis=0, keepdims=True))

    zero = jnp.zeros((2 * LANES, 2 * LANES), F32)
    gram, cross, summed = each_frame(frames, frame, (zero, zero, jnp.zeros((1, LANES), F32)))

    gram = fold_square(gram)
    tiles = LANES // 8
    gram_ref[0:tiles] = gram.reshape(tiles, 8, LANES)
    gram_ref[tiles : 2 * tiles] = fold_square(cross).reshape(tiles, 8, LANES)
    gram_ref[2 * tiles : 3 * tiles] = gram0_ref[0:LANES, :].reshape(tiles, 8, LANES)
    gram_ref[3 * tiles] = rows8(summed, gram0_ref[LANES : LANES + 1, :])
    w = pad_rows(w_ref[0])
    sums = stack_rows(row_dot(summed, w), jnp.sum(w * exact_dot(gram, w), axis=0, keepdims=True))
    send_all(send_ref, sums, slice(0, w.shape[1]))


def write_first(t, total, values, scale, shift, a_ref, planes):
    half_pre = values * scale + shift
    first = (half_pre + half_pre * half_tanh(half_pre)) * live_value(t, total)
    first = first.reshape(SIDE, 2, 8, LANES)
    even = first[:, 0]
    odd = first[:, 1]
    a_ref[t, 0, 1 : SIDE + 1] = even
    a_ref[t, 1, 1 : SIDE + 1] = odd
    if planes >= 3:
        a_ref[t, 2, 1 : SIDE + 1] = columns_down(odd)
    if planes >= 4:
        a_ref[t, 3, 1 : SIDE + 1] = columns_up(even)


def expand_kernel(
    block, counts_ref, sums_ref, count_ref, rows_ref, w_ref, gain_ref, bias_ref, taps_ref,
    e_ref, d_ref, stat_ref, send_ref, a_ref, taps8_ref,
):
    clear_edges(a_ref)
    total = live_frames(counts_ref)
    frames = a_ref.shape[0]
    count = count_ref[2:3, :] if block else row_total(count_ref)[0:1]
    average, variance = moments_of(row_total(sums_ref), count)
    stat_ref[...] = rows8(average, variance, count)
    norm_row = 2 * block
    scale = gain_ref[norm_row : norm_row + 1, :] * lax.rsqrt(variance + EPSILON)
    shift = 0.5 * (bias_ref[norm_row : norm_row + 1, :] - average * scale)
    scale = 0.5 * scale
    square = right_square(pad_rows(w_ref[0]))

    def expand(t, carry):
        at = pl.ds(pl.multiple_of(t * 256, 256), 256)
        values = fold_right(plain_dot(rows_ref[at, :], square)).reshape(FULL_ROWS, 8, LANES)
        e_ref[pl.ds(pl.multiple_of(t * FULL_ROWS, FULL_ROWS), FULL_ROWS)] = values
        write_first(t, total, values, scale, shift, a_ref, 3 if block else 4)
        return carry

    each_frame(frames, expand, 0)
    spread_taps(taps_ref, taps8_ref)
    per_frame = HALF_ROWS if block else FULL_ROWS
    conv = conv_half if block else conv_full

    def frame(t, carry):
        conv(t, 0, a_ref, taps8_ref, d_ref, True)
        last = jnp.minimum(place_of(counts_ref, t), LAGS - 1)

        def lag(k, inner):
            conv(t, k, a_ref, taps8_ref, d_ref, False)
            return inner

        lax.fori_loop(1, last + 1, lag, 0)
        values = d_ref[pl.ds(t * per_frame, per_frame)]
        return (carry[0] + jnp.sum(values, axis=0), carry[1] + jnp.sum(values * values, axis=0))

    zero = jnp.zeros((8, LANES), F32)
    summed, squares = lax.fori_loop(0, total, frame, (zero, zero))

    def dead(t, carry):
        d_ref[pl.ds(t * per_frame, per_frame)] = jnp.zeros((per_frame, 8, LANES), F32)
        return carry

    lax.fori_loop(total, frames, dead, 0)
    sums = stack_rows(jnp.sum(summed, axis=0, keepdims=True), jnp.sum(squares, axis=0, keepdims=True))
    send_all(send_ref, sums, slice(0, LANES))


def live_value(t, total):
    return jnp.where(t < total, 1.0, 0.0).astype(F32)


def each_frame(count, body, init, unroll=2):
    return lax.fori_loop(0, count, body, init, unroll=unroll)


def lanes_of(ref, tile):
    if ref.shape[-1] == LANES:
        return slice(None)
    return pl.ds(pl.multiple_of(tile * LANES, LANES), LANES)


def squeeze_forward_kernel(
    block, counts_ref, sums_ref, stat_ref, d_ref, gain_ref, bias_ref, down_ref, downb_ref, up_ref, upb_ref, proj_ref,
    cot_ref, z_ref, gates_ref, running_ref, pre_ref, stat_out_ref, send_ref, second_ref, pooled_ref,
):
    step = pl.program_id(0)
    steps = pl.num_programs(0)
    tiles = second_ref.shape[0]
    total = live_frames(counts_ref)
    per_frame = HALF_ROWS if block else FULL_ROWS
    pixels = per_frame * 8
    frames = second_ref.shape[1] // per_frame
    group = 256 // pixels
    chunks = frames // group
    norm_row = 2 * block + 1

    def activate(tile, carry):
        lanes = lanes_of(d_ref, tile)
        count = stat_ref[2:3, lanes] * (0.25 if block else 1.0)
        average, variance = moments_of(row_total(sums_ref, lanes), count)
        stat_out_ref[:, lanes] = rows8(average, variance, count)
        scale = gain_ref[norm_row : norm_row + 1, lanes] * lax.rsqrt(variance + EPSILON)
        shift = 0.5 * (bias_ref[norm_row : norm_row + 1, lanes] - average * scale)
        scale = 0.5 * scale

        def chunk(index, inside):
            for inner in range(group):
                t = index * group + inner
                at = pl.ds(t * per_frame, per_frame)
                half_pre = d_ref[at, :, lanes] * scale + shift
                second = half_pre + half_pre * half_tanh(half_pre)
                second = second * live_value(t, total)
                second_ref[tile, at] = second
                pooled_ref[tile, pl.ds(t, 1), :] = tile_sum(second) * (1.0 / pixels)
            return inside

        each_frame(chunks, chunk, 0)
        return carry

    if block:
        lax.fori_loop(0, tiles, activate, 0)
    else:
        activate(step, 0)

    def project(tile, carry):
        lanes = lanes_of(gates_ref, tile)
        square = right_square_t(pad_rows(proj_ref[0, :, lanes]))
        gates = gates_ref[:, lanes]

        def chunk(index, inside):
            parts = []
            for inner in range(group):
                t = index * group + inner
                second = second_ref[tile, pl.ds(t * per_frame, per_frame)].reshape(pixels, LANES)
                parts.append(second * pick_row(gates, t))
            excited = parts[0] if group == 1 else jnp.concatenate(parts, axis=0)
            at = pl.ds(pl.multiple_of(index * 256, 256), 256)
            z_ref[at, :] = z_ref[at, :] + fold_right(plain_dot(side_by_side(excited), square, NT))
            return inside

        each_frame(chunks, chunk, 0)
        return carry

    @pl.when(step == steps - 1)
    def gate_and_project():
        matrix = running_matrix(counts_ref, frames)
        pooled = jnp.concatenate([pooled_ref[index] for index in range(tiles)], axis=1)
        running = exact_dot(matrix, pooled)
        running_ref[...] = running
        pre = skinny_dot(running, down_ref[0], NT) + downb_ref[block : block + 1, :]
        pre_ref[...] = pre
        gates_ref[...] = sigmoid(skinny_dot(pre * sigmoid(pre), up_ref[0]) + upb_ref[block : block + 1, :])
        z_ref[...] = jnp.zeros_like(z_ref)
        lax.fori_loop(0, tiles, project, 0)

        def chunk(index, carry):
            at = pl.ds(pl.multiple_of(index * 256, 256), 256)
            z = z_ref[at, :].reshape(32, 8, LANES)
            values = [z, z * z]
            if block:
                dy = cot_ref[at, :].reshape(32, 8, LANES)
                values = values + [dy, dy * z]
            return tuple(old + jnp.sum(new, axis=0) for old, new in zip(carry, values))

        zero = jnp.zeros((8, LANES), F32)
        sums = each_frame(chunks, chunk, (zero,) * (4 if block else 2))
        rows = stack_rows(*(jnp.sum(value, axis=0, keepdims=True) for value in sums))
        send_all(send_ref, rows, slice(0, LANES))


def pack_tiles(narrow, squeeze):
    return narrow // 8 + 2 * (squeeze // 8) + 1


def squeeze_backward_body(
    block, counts_ref, stat_ref, d_ref, gain_ref, bias_ref, down_ref, up_ref, proj_ref, gates_ref, running_ref,
    pre_ref, dy2_ref, send_ref, pack_ref, dz3_ref, dz3t_ref, excited_ref, dexc_ref, dgate_ref, head,
):
    total = live_frames(counts_ref)
    per_frame = HALF_ROWS if block else FULL_ROWS
    pixels = per_frame * 8
    frames = dz3_ref.shape[0] // pixels
    group = 256 // pixels
    chunks = frames // group
    norm_row = 2 * block + 1
    tiles = dexc_ref.shape[0]
    narrow = proj_ref.shape[1]
    squeeze = down_ref.shape[1]
    per_tile = pack_tiles(narrow, squeeze)

    def norm_of(tile):
        lanes = lanes_of(d_ref, tile)
        average = stat_ref[0:1, lanes]
        root = lax.rsqrt(stat_ref[1:2, lanes] + EPSILON)
        scale = gain_ref[norm_row : norm_row + 1, lanes] * root
        shift = 0.5 * (bias_ref[norm_row : norm_row + 1, lanes] - average * scale)
        return (lanes, average, root, 0.5 * scale, shift)

    def excite(tile, carry):
        lanes, _, _, scale, shift = norm_of(tile)
        gates = gates_ref[:, lanes_of(gates_ref, tile)]
        square = right_square(pad_rows(proj_ref[0, :, lanes]))

        def chunk(index, inside):
            flat = pl.ds(pl.multiple_of(index * 256, 256), 256)
            dexc = fold_right(plain_dot(dz3_ref[flat, :], square)).reshape(32, 8, LANES)
            dexc_ref[tile, pl.ds(pl.multiple_of(index * 32, 32), 32)] = dexc
            parts = []
            for inner in range(group):
                t = index * group + inner
                half_pre = d_ref[pl.ds(t * per_frame, per_frame), :, lanes] * scale + shift
                second = half_pre + half_pre * half_tanh(half_pre)
                second = second * live_value(t, total)
                own = dexc[inner * per_frame : (inner + 1) * per_frame]
                dgate_ref[tile, pl.ds(t, 1), :] = tile_sum(own * second)
                parts.append(second.reshape(pixels, LANES) * pick_row(gates, t))
            excited = parts[0] if group == 1 else jnp.concatenate(parts, axis=0)
            excited_ref[flat, :] = side_by_side(excited)
            return inside

        each_frame(chunks, chunk, 0)
        dproj = fold_square(plain_dot(dz3t_ref[...], excited_ref[...]))
        pack_ref[pl.ds(tile * per_tile, narrow // 8)] = dproj[0:narrow].reshape(narrow // 8, 8, LANES)
        return carry

    def squeeze_part():
        pre = pre_ref[...]
        half_pre = 0.5 * pre
        tanh = half_tanh(half_pre)
        squeezed = half_pre + half_pre * tanh
        all_gates = gates_ref[...]
        dgate = jnp.concatenate([dgate_ref[index] for index in range(tiles)], axis=1)
        du = dgate * all_gates * (1.0 - all_gates)
        dpre = skinny_dot(du, up_ref[0], NT) * silu_slope(half_pre, tanh)
        ddown = frame_outer(dpre, running_ref[...])
        dup = frame_outer(squeezed, du)
        dpre_row = jnp.sum(dpre, axis=0, keepdims=True)
        dpre_row = jnp.concatenate([dpre_row, jnp.zeros((1, du.shape[1] - squeeze), F32)], axis=1)
        biases = rows8(jnp.sum(du, axis=0, keepdims=True), dpre_row)
        for index in range(tiles):
            own = slice(index * LANES, (index + 1) * LANES)
            at = index * per_tile + narrow // 8
            pack_ref[at : at + squeeze // 8] = ddown[:, own].reshape(squeeze // 8, 8, LANES)
            at = at + squeeze // 8
            pack_ref[at : at + squeeze // 8] = dup[:, own].reshape(squeeze // 8, 8, LANES)
            pack_ref[at + squeeze // 8] = biases[:, own]
        drunning = skinny_dot(dpre, down_ref[0])
        dpooled = exact_dot(running_matrix(counts_ref, frames), drunning, TN) * (1.0 / pixels)
        for index in range(tiles):
            dgate_ref[index] = dpooled[:, index * LANES : (index + 1) * LANES]

    def slope(tile, carry):
        lanes, average, root, scale, shift = norm_of(tile)
        gates = gates_ref[:, lanes_of(gates_ref, tile)]

        def chunk(index, inside):
            summed, cross = inside
            for inner in range(group):
                t = index * group + inner
                at = pl.ds(t * per_frame, per_frame)
                depth = d_ref[at, :, lanes]
                half_pre = depth * scale + shift
                dsecond = dexc_ref[tile, at] * pick_row(gates, t) + pick_row(dgate_ref[tile], t)
                dy = dsecond * silu_slope(half_pre, half_tanh(half_pre))
                dy = dy * live_value(t, total)
                dy2_ref[at, :, lanes] = dy
                summed = summed + jnp.sum(dy, axis=0)
                cross = cross + jnp.sum(dy * (depth - average), axis=0)
            return (summed, cross)

        zero = jnp.zeros((8, LANES), F32)
        summed, cross = each_frame(chunks, chunk, (zero, zero))
        rows = stack_rows(jnp.sum(summed, axis=0, keepdims=True), root * jnp.sum(cross, axis=0, keepdims=True))
        send_all(send_ref, rows, lanes)
        return carry

    if block:
        head()
        lax.fori_loop(0, tiles, excite, 0)
        squeeze_part()
        lax.fori_loop(0, tiles, slope, 0)
    else:
        phase = pl.program_id(0)
        tile = pl.program_id(1)

        @pl.when((phase == 0) & (tile == 0))
        def start():
            head()

        @pl.when(phase == 0)
        def first():
            excite(tile, 0)

        @pl.when((phase == 1) & (tile == 0))
        def between():
            squeeze_part()

        @pl.when(phase == 1)
        def second():
            slope(tile, 0)


def squeeze_one_backward_kernel(
    counts_ref, third_ref, z_ref, cot_ref, ngain_ref, nbias_ref, stat_ref, d_ref, gain_ref, bias_ref, down_ref,
    up_ref, proj_ref, gates_ref, running_ref, pre_ref, act_ref, nsum_ref, dy2_ref, send_ref, pack_ref,
    dz3_ref, dz3t_ref, excited_ref, dexc_ref, dgate_ref,
):
    total = live_frames(counts_ref)
    pixels = HALF_ROWS * 8

    def head():
        count = stat_ref[2:3, 0:LANES]
        sums = row_total(third_ref)
        mean, variance = moments_of(sums, count)
        root = lax.rsqrt(variance + EPSILON)
        gain = ngain_ref[1:2, :]
        bias_sum = sums[2:3, :]
        gain_sum = root * (sums[3:4, :] - mean * bias_sum)
        nsum_ref[...] = rows8(gain_sum, bias_sum, mean, variance)
        row = lax.broadcasted_iota(jnp.int32, z_ref.shape, 0) // pixels
        live = row < total
        normed = (z_ref[...] - mean) * root
        act = jnp.where(live, gain * normed + nbias_ref[1:2, :], 0.0)
        act_ref[...] = act.T[0 : act_ref.shape[0]]
        dz3 = gain * root * (cot_ref[...] - bias_sum / count - normed * (gain_sum / count))
        dz3 = jnp.where(live, dz3, 0.0)
        dz3_ref[...] = side_by_side(dz3)
        dz3t_ref[...] = jnp.concatenate(halves(dz3.T), axis=0)

    squeeze_backward_body(
        1, counts_ref, stat_ref, d_ref, gain_ref, bias_ref, down_ref, up_ref, proj_ref, gates_ref, running_ref,
        pre_ref, dy2_ref, send_ref, pack_ref, dz3_ref, dz3t_ref, excited_ref, dexc_ref, dgate_ref, head,
    )


def input_factors(sums, stat_ref, count, gain, w):
    root = lax.rsqrt(stat_ref[1:2, :] + EPSILON)
    factor = gain * root
    matrix = exact_dot(w * (factor * root * sums[1:2] / count), w, NT)
    return (matrix, row_dot(factor * sums[0:1] / count, w, NT))


def covariance(gram, summed, count):
    mean = summed / count
    return (mean, gram / count - outer(mean, mean))


def squeeze_zero_backward_kernel(
    counts_ref, top_ref, stat1_ref, gram_ref, nstat_ref, dxpre_ref, x1_ref, z_ref, ngain_ref, w_ref, gains_ref, q_one_ref,
    stat_ref, d_ref, gain_ref, bias_ref, down_ref, up_ref, proj_ref, gates_ref, running_ref, pre_ref,
    dx1_ref, nsum_ref, dy2_ref, send_ref, pack_ref, dz3_ref, dz3t_ref, excited_ref, dexc_ref, dgate_ref,
):
    total = live_frames(counts_ref)
    width = gains_ref.shape[1]

    def head():
        start = pack_tiles(proj_ref.shape[1], down_ref.shape[1]) * (width // LANES)
        pack_ref[start : start + q_one_ref.shape[0]] = q_one_ref[...]
        count = stat_ref[2:3, :]
        wide_count = jnp.broadcast_to(count[:, 0:1], (1, width))
        sums = row_total(top_ref, slice(0, width))
        extra = row_total(top_ref, slice(width, width + LANES))
        matrix, shift = input_factors(sums, stat1_ref, wide_count, gains_ref[2:3, :], pad_rows(w_ref[0]))
        mean = nstat_ref[0:1, :]
        root = lax.rsqrt(nstat_ref[1:2, :] + EPSILON)
        mean_x1 = gram_ref[3 * LANES : 3 * LANES + 1, :] / count
        cross = (gram_ref[LANES : 2 * LANES, :] - count * outer(mean_x1, mean)) * root
        gain_sum = extra[0:1] - jnp.sum(matrix * cross, axis=0, keepdims=True)
        bias_sum = extra[1:2] - count * shift
        nsum_ref[...] = rows8(gain_sum, bias_sum, mean, nstat_ref[1:2, :])
        factor = ngain_ref[0:1, :] * root
        square = right_square(matrix)
        bias_mean = bias_sum / count
        gain_mean = gain_sum / count

        def frame(t, carry):
            at = pl.ds(pl.multiple_of(t * 256, 256), 256)
            centred = side_by_side(x1_ref[at, :] - mean_x1)
            live = live_value(t, total)
            dx1 = (dxpre_ref[at, :] - fold_right(plain_dot(centred, square)) - shift) * live
            dx1_ref[at, :] = dx1
            normed = (z_ref[at, :] - mean) * root
            dz3 = factor * (dx1 - bias_mean - normed * gain_mean) * live
            dz3_ref[at, :] = side_by_side(dz3)
            dz3t_ref[:, at] = jnp.concatenate(halves(dz3.T), axis=0)
            return carry

        each_frame(dz3_ref.shape[0] // 256, frame, 0)

    squeeze_backward_body(
        0, counts_ref, stat_ref, d_ref, gain_ref, bias_ref, down_ref, up_ref, proj_ref, gates_ref, running_ref,
        pre_ref, dy2_ref, send_ref, pack_ref, dz3_ref, dz3t_ref, excited_ref, dexc_ref, dgate_ref, head,
    )

def back_full(t, k, a_ref, w_ref, z_ref, f_ref, dw_ref, fresh):
    weights = [w_ref[k * 9 + tap] for tap in range(9)]
    target = t - k
    sums = [None] * 9
    a_rows = {}
    z_rows = {}
    for i in range(SIDE):
        for need in (i, i + 1, i + 2):
            if need not in a_rows:
                a_rows[need] = [a_ref[target, plane, need] for plane in range(2)]
                z_rows[need] = [z_ref[t, plane, need] for plane in range(4)]
        even = None
        odd = None
        z_even, z_odd, z_odd_down, z_even_up = z_rows[i + 1]
        for r in range(3):
            b_even, b_odd, b_odd_down, b_even_up = z_rows[i + 2 - r]
            left, centre, right = weights[3 * r : 3 * r + 3]
            part_even = centre * b_even + right * b_odd_down + left * b_odd
            part_odd = centre * b_odd + right * b_even + left * b_even_up
            even = part_even if even is None else even + part_even
            odd = part_odd if odd is None else odd + part_odd
            a_even, a_odd = a_rows[i + r]
            pieces = (
                z_even_up * a_odd + z_odd * a_even,
                z_even * a_even + z_odd * a_odd,
                z_even * a_odd + z_odd_down * a_even,
            )
            for c in range(3):
                at = 3 * r + c
                sums[at] = pieces[c] if sums[at] is None else sums[at] + pieces[c]
        a_rows.pop(i)
        z_rows.pop(i)
        at = target * FULL_ROWS + 2 * i
        if fresh:
            f_ref[at] = even
            f_ref[at + 1] = odd
        else:
            f_ref[at] = f_ref[at] + even
            f_ref[at + 1] = f_ref[at + 1] + odd
    for tap in range(9):
        dw_ref[k * 9 + tap] = dw_ref[k * 9 + tap] + sums[tap]


def back_half(t, k, a_ref, w_ref, z_ref, f_ref, dw_ref, fresh):
    weights = [w_ref[k * 9 + tap] for tap in range(9)]
    target = t - k
    sums = [None] * 9

    def put(row, parity, value):
        at = target * FULL_ROWS + 2 * row + parity
        f_ref[at] = value if fresh else f_ref[at] + value

    carried = [a_ref[target, plane, 0] for plane in range(2)]
    here = [z_ref[t, plane, 0] for plane in range(2)]
    for i in range(HALF_ROWS):
        below = [z_ref[t, plane, i + 1] for plane in range(2)]
        dz, dz_up = here
        rows = [carried]
        for need in (2 * i + 1, 2 * i + 2):
            rows.append([a_ref[target, plane, need] for plane in range(2)])
        carried = rows[2]
        put(2 * i, 0, weights[4] * dz)
        put(2 * i, 1, weights[5] * dz + weights[3] * dz_up)
        put(2 * i + 1, 0, weights[7] * dz + weights[1] * below[0])
        put(
            2 * i + 1,
            1,
            weights[8] * dz + weights[6] * dz_up + (weights[2] * below[0] + weights[0] * below[1]),
        )
        for r in range(3):
            a_even, a_odd = rows[r]
            pieces = (dz_up * a_odd, dz * a_even, dz * a_odd)
            for c in range(3):
                at = 3 * r + c
                sums[at] = pieces[c] if sums[at] is None else sums[at] + pieces[c]
        here = below
    for tap in range(9):
        dw_ref[k * 9 + tap] = dw_ref[k * 9 + tap] + sums[tap]


def depth_backward_kernel(
    block, before, final, counts_ref, grads_ref, stat2_ref, stat_ref, nstat_ref, dy2_ref, d_ref, e_ref, a_ref, columns_ref, w_ref,
    gain_ref, bias_ref, taps_ref, z3_ref, dx_in_ref, sums_in_ref, list_in_ref, dxpre_ref, send_ref, q_ref, grad_rows_ref,
    z_ref, f_ref, taps8_ref, dw_ref, pair_ref,
):
    tile = pl.program_id(0)
    tiles = pl.num_programs(0)
    total = live_frames(counts_ref)
    frames = a_ref.shape[0]
    norm_row = 2 * block
    half = block == 1
    per_frame = HALF_ROWS if half else FULL_ROWS
    taps = dw_ref.shape[0]

    @pl.when(tile == 0)
    def start():
        clear_edges(z_ref)
        if before:
            dxpre_ref[...] = dx_in_ref[...]
            send_all(send_ref, sums_in_ref[0:2, :], slice(0, before * LANES))
            q_ref[0 : list_in_ref.shape[0]] = list_in_ref[...]
        else:
            dxpre_ref[...] = jnp.zeros_like(dxpre_ref)

        def dead(t, carry):
            f_ref[pl.ds(t * FULL_ROWS, FULL_ROWS)] = jnp.zeros((FULL_ROWS, 8, LANES), F32)
            return carry

        lax.fori_loop(total, frames, dead, 0)

    count = stat2_ref[2:3, :]
    grads = row_total(grads_ref)
    grad_rows_ref[...] = rows8(grads[0:1], grads[1:2])
    average = stat2_ref[0:1, :]
    root = lax.rsqrt(stat2_ref[1:2, :] + EPSILON)
    scale_two = gain_ref[norm_row + 1 : norm_row + 2, :] * root
    slope = scale_two * root * grads[1:2] / count
    level = scale_two * grads[0:1] / count - slope * average
    average_one = stat_ref[0:1, :]
    root_one = lax.rsqrt(stat_ref[1:2, :] + EPSILON)
    scale_one = gain_ref[norm_row : norm_row + 1, :] * root_one
    shift_half = 0.5 * (bias_ref[norm_row : norm_row + 1, :] - average_one * scale_one)
    scale_half = 0.5 * scale_one

    def fill(t, carry):
        at = pl.ds(t * per_frame, per_frame)
        dz = scale_two * dy2_ref[at] - (slope * d_ref[at] + level)
        if half:
            z_ref[t, 0, 0:HALF_ROWS] = dz
            z_ref[t, 1, 0:HALF_ROWS] = columns_up(dz)
        else:
            pair = dz.reshape(SIDE, 2, 8, LANES)
            z_ref[t, 0, 1 : SIDE + 1] = pair[:, 0]
            z_ref[t, 1, 1 : SIDE + 1] = pair[:, 1]
            z_ref[t, 2, 1 : SIDE + 1] = columns_down(pair[:, 1])
            z_ref[t, 3, 1 : SIDE + 1] = columns_up(pair[:, 0])
        return carry

    each_frame(frames, fill, 0)
    spread_taps(taps_ref, taps8_ref)
    dw_ref[...] = jnp.zeros_like(dw_ref)
    back = back_half if half else back_full

    def frame(t, carry):
        back(t, 0, a_ref, taps8_ref, z_ref, f_ref, dw_ref, True)
        last = jnp.minimum(place_of(counts_ref, t), LAGS - 1)

        def lag(k, inner):
            back(t, k, a_ref, taps8_ref, z_ref, f_ref, dw_ref, False)
            return inner

        return lax.fori_loop(1, last + 1, lag, carry)

    lax.fori_loop(0, total, frame, 0)
    square = right_square_t(pad_rows(w_ref[0]))

    def finish(t, carry):
        rows = pl.ds(pl.multiple_of(t * FULL_ROWS, FULL_ROWS), FULL_ROWS)
        flat = pl.ds(pl.multiple_of(t * 256, 256), 256)
        values = e_ref[rows]
        half_pre = values * scale_half + shift_half
        dy = f_ref[rows] * silu_slope(half_pre, half_tanh(half_pre))
        summed = carry[0] + jnp.sum(dy, axis=0)
        cross = carry[1] + jnp.sum(dy * (values - average_one), axis=0)
        dy = dy.reshape(256, LANES)
        pair_ref[flat, :] = side_by_side(dy)
        scaled = side_by_side(dy * scale_one)
        dxpre_ref[flat, :] = dxpre_ref[flat, :] + fold_right(plain_dot(scaled, square, NT))
        return (summed, cross)

    zero = jnp.zeros((8, LANES), F32)
    summed, cross = each_frame(frames, finish, (zero, zero))
    rows = stack_rows(jnp.sum(summed, axis=0, keepdims=True), root_one * jnp.sum(cross, axis=0, keepdims=True))
    if final:
        send_all(send_ref, rows, pl.ds(pl.multiple_of((tile + before) * LANES, LANES), LANES))
    else:
        send_ref[...] = rows8(rows[0:1], rows[1:2])
    gathered = fold_square(plain_dot(columns_ref[...], pair_ref[...]))
    narrow = w_ref.shape[1]
    dtaps = jnp.sum(dw_ref[...], axis=1)
    unused = (-taps) % 8
    dtaps = jnp.concatenate([dtaps, jnp.zeros((unused, LANES), F32)], axis=0)
    values = jnp.concatenate([gathered[0:narrow], dtaps], axis=0)
    listed = values.shape[0] // 8
    q_ref[pl.ds((tile + before) * listed, listed)] = values.reshape(listed, 8, LANES)

    if half:
        @pl.when(tile == tiles - 1)
        def tail():
            mean = nstat_ref[0:1, :]
            root_three = lax.rsqrt(nstat_ref[1:2, :] + EPSILON)

            def part(t, carry):
                flat = pl.ds(pl.multiple_of(t * 256, 256), 256)
                dx = dxpre_ref[flat, :].reshape(32, 8, LANES)
                normed = ((z3_ref[flat, :] - mean) * root_three).reshape(32, 8, LANES)
                return (carry[0] + jnp.sum(dx * normed, axis=0), carry[1] + jnp.sum(dx, axis=0))

            cross_three, summed_three = each_frame(frames, part, (zero, zero))
            rows = stack_rows(
                jnp.sum(cross_three, axis=0, keepdims=True), jnp.sum(summed_three, axis=0, keepdims=True)
            )
            width = send_ref.shape[2] - LANES
            send_all(send_ref, rows, slice(width, width + LANES))


def finish_kernel(
    counts_ref, momentum_ref, gram_ref, stat01_ref, stat02_ref, stat11_ref, stat12_ref, grad0_ref,
    grad1_ref, one_ref, zero_ref, nsum0_ref, nsum1_ref, dxpre_ref, x_ref, dx1_ref, w_ref, gain_ref, means_ref, vars_ref,
    nmeans_ref, nvars_ref,
    video_ref, less_ref, factor_ref, wgain_ref, wbias_ref, ngain_ref, nbias_ref, newm_ref, newv_ref, newnm_ref, newnv_ref,
):
    total = live_frames(counts_ref)
    full = stat01_ref[2:3, :]
    count = full[:, 0:LANES]
    width = full.shape[1]
    top_zero = row_total(zero_ref)
    top_one = row_total(one_ref, slice(0, width))
    w_zero = pad_rows(w_ref[0])
    matrix, shift = input_factors(top_zero, stat01_ref, full, gain_ref[0:1, :], w_zero)
    square = right_square(matrix)
    mean_x, cov_zero = covariance(
        gram_ref[2 * LANES : 3 * LANES, :], gram_ref[3 * LANES + 1 : 3 * LANES + 2, :], count
    )
    order = column_order()
    narrow = video_ref.shape[0]

    def frame(t, carry):
        at = pl.ds(pl.multiple_of(t * 256, 256), 256)
        centred = side_by_side(x_ref[at, :] - mean_x)
        dx = (dxpre_ref[at, :] - fold_right(plain_dot(centred, square)) - shift) * live_value(t, total) + dx1_ref[at, :]
        for part in range(2):
            own = dx[part * LANES : (part + 1) * LANES].T[0:narrow]
            pieces = pick_thirds(order, own, NN, False)
            start = pl.multiple_of(t * 256 + part * LANES, LANES)
            video_ref[:, pl.ds(start, LANES)] = pieces[0] + pieces[1] + pieces[2]
        return carry

    each_frame(x_ref.shape[0] // 256, frame, 0)
    mean_one, cov_one = covariance(gram_ref[0:LANES, :], gram_ref[3 * LANES : 3 * LANES + 1, :], count)
    plan = ((mean_x, cov_zero, stat01_ref, top_zero, w_zero), (mean_one, cov_one, stat11_ref, top_one, pad_rows(w_ref[1])))
    for block, (mean_row, cov, stat_ref, top, w) in enumerate(plan):
        root = lax.rsqrt(stat_ref[1:2, :] + EPSILON)
        factor = gain_ref[2 * block : 2 * block + 1, :] * root
        less = outer(mean_row, top[0:1]) + exact_dot(cov, w) * (root * top[1:2])
        less_ref[block] = (less * factor)[0:narrow]
        factor_ref[8 * block : 8 * block + 8, :] = rows8(factor)
    momentum = momentum_ref[0].astype(F32) / 10.0
    wgain_ref[...] = stack_rows(top_zero[1:2], grad0_ref[1:2, :], top_one[1:2], grad1_ref[1:2, :])
    wbias_ref[...] = stack_rows(top_zero[0:1], grad0_ref[0:1, :], top_one[0:1], grad1_ref[0:1, :])
    stats = (stat01_ref, stat02_ref, stat11_ref, stat12_ref)
    means = stack_rows(*(ref[0:1, :] for ref in stats))
    variances = stack_rows(*(ref[1:2, :] * (ref[2:3, :] / (ref[2:3, :] - 1.0)) for ref in stats))
    newm_ref[...] = (1.0 - momentum) * means_ref[...] + momentum * means
    newv_ref[...] = (1.0 - momentum) * vars_ref[...] + momentum * variances
    ngain_ref[...] = stack_rows(nsum0_ref[0:1, :], nsum1_ref[0:1, :])[:, 0:narrow]
    nbias_ref[...] = stack_rows(nsum0_ref[1:2, :], nsum1_ref[1:2, :])[:, 0:narrow]
    means = stack_rows(nsum0_ref[2:3, :], nsum1_ref[2:3, :])[:, 0:narrow]
    quarter = 0.25 * count
    variances = stack_rows(
        nsum0_ref[3:4, :] * (count / (count - 1.0)), nsum1_ref[3:4, :] * (quarter / (quarter - 1.0))
    )[:, 0:narrow]
    newnm_ref[...] = (1.0 - momentum) * nmeans_ref[...] + momentum * means
    newnv_ref[...] = (1.0 - momentum) * nvars_ref[...] + momentum * variances


def gradient_kernel(
    core_ref, pack0_ref, pack0_other_ref, pack1_ref, pack1_other_ref, late_ref, late_other_ref, less_ref, factor_ref,
    dw_ref, dtaps_ref, ddown_ref, dup_ref, dproj_ref, dupb_ref, ddownb_ref,
):
    narrow = dw_ref.shape[1]
    taps = dtaps_ref.shape[1]
    squeeze = ddown_ref.shape[1]
    tiles = dw_ref.shape[2] // LANES
    per_pack = pack_tiles(narrow, squeeze)
    per_tile = narrow // 8 + -(-taps // 8)
    first_core = core_ref[0] == 0

    def rows_of(pair, at, count):
        mine, other = pair
        half = mine.shape[0]
        pieces = []
        if at < half:
            size = min(count, half - at)
            here = slice(at, at + size)
            pieces.append(jnp.where(first_core, mine[here], other[here]))
            count = count - size
            at = at + size
        if count:
            here = slice(at - half, at - half + count)
            pieces.append(jnp.where(first_core, other[here], mine[here]))
        values = pieces[0] if len(pieces) == 1 else jnp.concatenate(pieces, axis=0)
        return values.reshape(-1, LANES)

    packs = ((pack0_ref, pack0_other_ref), (pack1_ref, pack1_other_ref))
    lists = ((late_ref, late_other_ref), packs[0])
    for block in range(2):
        down_rows = []
        for tile in range(tiles):
            lanes = slice(tile * LANES, (tile + 1) * LANES)
            at = tile * per_pack
            dproj_ref[block, :, lanes] = rows_of(packs[block], at, narrow // 8)
            at = at + narrow // 8
            ddown_ref[block, :, lanes] = rows_of(packs[block], at, squeeze // 8)
            at = at + squeeze // 8
            dup_ref[block, :, lanes] = rows_of(packs[block], at, squeeze // 8)
            biases = rows_of(packs[block], at + squeeze // 8, 1)
            dupb_ref[block : block + 1, lanes] = biases[0:1]
            down_rows.append(biases[1:2])
            values = rows_of(lists[block], (per_pack * tiles if block else 0) + tile * per_tile, per_tile)
            dw = values[0:narrow] * factor_ref[8 * block : 8 * block + 1, lanes] - less_ref[block, :, lanes]
            dw_ref[block, :, lanes] = dw
            dtaps_ref[block, :, lanes] = values[narrow : narrow + taps]
        ddownb_ref[block : block + 1, :] = jnp.concatenate(down_rows, axis=1)[:, 0:squeeze]


AXES = ("dp", "z", "core")
CHIPS = ("dp", "z")


def exchange(send):
    return lax.all_to_all(send, AXES, 0, 0, tiled=True)


def together(*values):
    return lax.optimization_barrier(values)


def swap_cores(values):
    return lax.ppermute(values, "core", [(0, 1), (1, 0)])


def add_cores(tiles):
    core = lax.axis_index("core")
    pair = tiles.reshape(2, tiles.shape[0] // 2, *tiles.shape[1:])
    mine = lax.dynamic_index_in_dim(pair, core, 0, keepdims=False)
    return mine + swap_cores(lax.dynamic_index_in_dim(pair, 1 - core, 0, keepdims=False))


def share_out(tiles, names=CHIPS):
    count = 1
    for name in names:
        count = count * lax.axis_size(name)
    return lax.all_to_all(tiles.reshape(count, -1, *tiles.shape[1:]), names, 0, 0, tiled=True)


def share_back(pieces, names=CHIPS):
    own = jnp.sum(pieces, axis=0)
    everyone = lax.all_to_all(jnp.broadcast_to(own[None], pieces.shape), names, 0, 0, tiled=True)
    return everyone.reshape(-1, *pieces.shape[2:])


def shape(*dims, kind=F32):
    return jax.ShapeDtypeStruct(dims, kind)


def whole(array):
    rank = len(array.shape)
    return pl.BlockSpec(array.shape, lambda *ids: (0,) * rank)


SCALARS = pl.BlockSpec(memory_space=pltpu.SMEM)


def call(kernel, grid, in_specs, out_specs, out_shape, scratch, args):
    return pl.pallas_call(
        kernel,
        grid=grid,
        in_specs=in_specs,
        out_specs=out_specs,
        out_shape=out_shape,
        scratch_shapes=scratch,
        compiler_params=pltpu.CompilerParams(vmem_limit_bytes=VMEM_BYTES),
        cost_estimate=pl.CostEstimate(
            flops=1_000_000_000, bytes_accessed=1_000_000, transcendentals=0
        ),
    )(*args)


def simple_call(kernel, scalars, args, outs):
    return call(
        kernel, (1,), [SCALARS] * scalars + [whole(array) for array in args[scalars:]], [whole(item) for item in outs],
        outs, [], args,
    )


def local(
    video, frame_counts, momentum_index, expand_weight, wide_gains, wide_biases, narrow_gains, narrow_biases, depth_weight,
    squeeze_weight, squeeze_bias, excite_weight, excite_bias, project_weight, wide_means, wide_variances, narrow_means,
    narrow_variances, cotangent,
):
    devices = lax.axis_size("dp") * lax.axis_size("z") * lax.axis_size("core")
    cin, pixels = video.shape
    half_pixels = cotangent.shape[1]
    width = expand_weight.shape[1]
    squeeze = squeeze_weight.shape[1]
    frames = pixels // (SIDE * SIDE)
    tiles = width // LANES
    taps = depth_weight.shape[1]
    w_t = jnp.swapaxes(expand_weight, 1, 2)
    up_t = jnp.swapaxes(excite_weight, 1, 2)
    lanes_pad = ((0, 0), (0, LANES - cin))
    ngains = jnp.pad(narrow_gains, lanes_pad)
    nbiases = jnp.pad(narrow_biases, lanes_pad)
    full_rows = frames * FULL_ROWS
    half_rows = frames * HALF_ROWS
    low = jnp.bfloat16

    def round_up(count):
        return -(-count // devices) * devices

    def fixed(*dims):
        return pl.BlockSpec(dims, lambda *ids: (0,) * len(dims))

    def tile_rows(rows):
        return pl.BlockSpec((rows, LANES), lambda j: (0, j))

    def tile_cube(rows):
        return pl.BlockSpec((rows, 8, LANES), lambda j: (0, 0, j))

    def tile_sums(rows=2):
        return pl.BlockSpec((devices, rows, LANES), lambda j: (0, 0, j))

    def weight_tile(block, rows):
        return pl.BlockSpec((1, rows, LANES), lambda j, block=block: (block, 0, j))

    def of_block(block, rows, lanes):
        return pl.BlockSpec((1, rows, lanes), lambda *ids: (block, 0, 0))

    def early(make):
        return make(lambda p, j: j * (1 - p) + (tiles - 1) * p)

    def late(make):
        return make(lambda p, j: j * p)

    def both(make):
        return make(lambda p, j: j)

    def rows_at(rows):
        return lambda at: pl.BlockSpec((rows, LANES), lambda p, j: (0, at(p, j)))

    def cube_at(rows):
        return lambda at: pl.BlockSpec((rows, 8, LANES), lambda p, j: (0, 0, at(p, j)))

    def sums_at(rows):
        return lambda at: pl.BlockSpec((devices, rows, LANES), lambda p, j: (0, 0, at(p, j)))

    def weight_at(block, rows):
        return lambda at: pl.BlockSpec((1, rows, LANES), lambda p, j: (block, 0, at(p, j)))

    gram_zero, sums = call(
        gram_kernel, (1,), [SCALARS, whole(video), of_block(0, cin, width)],
        [fixed(LANES + 8, LANES), fixed(devices, 2, width + LANES)],
        [shape(LANES + 8, LANES), shape(devices, 2, width + LANES)],
        [], (frame_counts, video, w_t),
    )
    x, x_rows, x_columns, cot = simple_call(
        prepare_kernel, 1, (frame_counts, video, cotangent),
        [shape(pixels, LANES), shape(pixels, 2 * LANES, kind=low), shape(2 * LANES, pixels, kind=low),
         shape(half_pixels, LANES)],
    )
    sums = exchange(sums)

    def planes_of(planes, begin=0):
        return pl.BlockSpec((frames, planes, SIDE + 2, 8, LANES), lambda j: (0, 0, 0, 0, j + begin))

    def expand(block, sums, count, count_spec, rows):
        depth_rows = half_rows if block else full_rows
        planes = 3 if block else 4
        return call(
            functools.partial(expand_kernel, block), (tiles,),
            [SCALARS, tile_sums(), count_spec, whole(rows), weight_tile(block, cin), tile_rows(4), tile_rows(4),
             weight_tile(block, taps)],
            [tile_cube(full_rows), tile_cube(depth_rows), tile_rows(8), tile_sums(), planes_of(planes)],
            [shape(full_rows, 8, width), shape(depth_rows, 8, width), shape(8, width), shape(devices, 2, width),
             shape(frames, planes, SIDE + 2, 8, width)],
            [pltpu.VMEM((taps, 8, LANES), F32)],
            (frame_counts, sums, count, rows, w_t, wide_gains, wide_biases, depth_weight),
        )

    count_spec = pl.BlockSpec((devices, 2, LANES), lambda j: (0, 0, tiles))
    e_zero, d_zero, stat01, sums, planes_zero = expand(0, sums, sums, count_spec, x_rows)
    sums = exchange(sums)

    def squeeze_forward(block, sums, stat, depth):
        rows = half_rows if block else full_rows
        kinds = 4 if block else 2
        moving = [tile_sums(), tile_rows(8), tile_cube(rows), tile_rows(4), tile_rows(4)]
        if block:
            moving = [whole(array) for array in (sums, stat, depth, wide_gains, wide_biases)]
        return call(
            functools.partial(squeeze_forward_kernel, block), (1 if block else tiles,),
            [SCALARS] + moving
            + [of_block(block, squeeze, width), whole(squeeze_bias), of_block(block, squeeze, width), whole(excite_bias),
               of_block(block, cin, width), whole(cot)],
            [fixed(rows * 8, LANES), fixed(8, width), fixed(8, width), fixed(8, squeeze),
             fixed(8, width) if block else tile_rows(8), fixed(devices, kinds, LANES)],
            [shape(rows * 8, LANES), shape(8, width), shape(8, width), shape(8, squeeze), shape(8, width),
             shape(devices, kinds, LANES)],
            [pltpu.VMEM((tiles, rows, 8, LANES), F32), pltpu.VMEM((tiles, frames, LANES), F32)],
            (frame_counts, sums, stat, depth, wide_gains, wide_biases, squeeze_weight, squeeze_bias, up_t, excite_bias,
             project_weight, cot),
        )

    z_zero, gates_zero, running_zero, pre_zero, stat02, sums = squeeze_forward(0, sums, stat01, d_zero)
    sums = exchange(sums)
    narrow_args = (frame_counts, sums, stat01, gram_zero, x, z_zero, ngains, nbiases, w_t)
    narrow_outs = [
        shape(pixels, LANES), shape(pixels, 2 * LANES, kind=low), shape(2 * LANES, pixels, kind=low),
        shape(round_up(3 * LANES // 8 + 1), 8, LANES), shape(8, LANES), shape(devices, 2, width),
    ]
    x1, x1_rows, x1_columns, gram, nstat, sums = call(
        narrow_kernel, (1,), [SCALARS] + [whole(array) for array in narrow_args[1:-1]] + [of_block(1, cin, width)],
        [whole(item) for item in narrow_outs], narrow_outs, [], narrow_args,
    )
    sums, gram = together(exchange(sums), gram)
    gram = share_out(gram, AXES)
    e_one, d_one, stat11, sums, planes_one = expand(1, sums, nstat, pl.BlockSpec((8, LANES), lambda j: (0, 0)), x1_rows)
    sums, gram = together(sums, gram)
    sums = exchange(sums)
    z_one, gates_one, running_one, pre_one, stat12, sums = squeeze_forward(1, sums, stat11, d_one)
    third, gram = together(exchange(sums), gram)
    gram = share_back(gram, AXES).reshape(-1, LANES)
    q_tiles = cin // 8 + -(-taps // 8)

    def backward_specs(block):
        rows = half_rows if block else full_rows
        ins = [fixed(8, width), fixed(rows, 8, width), fixed(4, width), fixed(4, width), of_block(block, squeeze, width),
               of_block(block, squeeze, width), of_block(block, cin, width), fixed(8, width), fixed(8, width),
               fixed(8, squeeze)]
        if not block:
            ins[0:4] = [both(rows_at(8)), both(cube_at(rows)), both(rows_at(4)), both(rows_at(4))]
            ins[6] = early(weight_at(block, cin))
        packed = round_up(tiles * (pack_tiles(cin, squeeze) + (0 if block else q_tiles)))
        wide_outs = [fixed(rows, 8, width), fixed(devices, 2, width)] if block else [late(cube_at(rows)), late(sums_at(2))]
        outs = [fixed(8, LANES)] + wide_outs + [fixed(packed, 8, LANES)]
        shapes = [shape(8, LANES), shape(rows, 8, width), shape(devices, 2, width), shape(packed, 8, LANES)]
        scratch = [pltpu.VMEM((rows * 8, 2 * LANES), low), pltpu.VMEM((2 * LANES, rows * 8), low),
                   pltpu.VMEM((rows * 8, 2 * LANES), low), pltpu.VMEM((tiles, rows, 8, LANES), F32),
                   pltpu.VMEM((tiles, frames, LANES), F32)]
        return (ins, outs, shapes, scratch)

    ins, outs, shapes, scratch = backward_specs(1)
    activations, nsum_one, dy2_one, sums, pack_one = call(
        squeeze_one_backward_kernel, (1,),
        [SCALARS, whole(third), whole(z_one), whole(cot), whole(ngains), whole(nbiases)] + ins,
        [fixed(cin, half_pixels)] + outs, [shape(cin, half_pixels)] + shapes, scratch,
        (frame_counts, third, z_one, cot, ngains, nbiases, stat12, d_one, wide_gains, wide_biases, squeeze_weight, up_t,
         project_weight, gates_one, running_one, pre_one),
    )
    sums, gram = together(sums, gram)
    sums, pack_one = together(exchange(sums), add_cores(pack_one))
    pack_one = share_out(pack_one)
    nothing = jnp.zeros((8, LANES), F32)

    def depth_backward(block, begin, end, sums, stat2, stat, dy2, depth, expanded, planes, columns, dx_in, sums_in, list_in):
        rows = half_rows if block else full_rows
        z_shape = (frames, 2, HALF_ROWS + 1, 8, LANES) if block else (frames, 4, SIDE + 2, 8, LANES)
        count = end - begin
        final = end == tiles
        listed = round_up(end * q_tiles) if final and not block else end * q_tiles
        if final:
            send = (devices, 2, width + (LANES if block else 0))
            send_spec = fixed(*send)
        else:
            send = (8, count * LANES)
            send_spec = tile_rows(8)

        def wide_rows(rows):
            return pl.BlockSpec((rows, LANES), lambda j: (0, j + begin))

        def wide_cube(rows):
            return pl.BlockSpec((rows, 8, LANES), lambda j: (0, 0, j + begin))

        def wide_weight(rows):
            return pl.BlockSpec((1, rows, LANES), lambda j: (block, 0, j + begin))

        return call(
            functools.partial(depth_backward_kernel, block, begin, final), (count,),
            [SCALARS, pl.BlockSpec((devices, 2, LANES), lambda j: (0, 0, j + begin)), wide_rows(8), wide_rows(8), whole(nstat),
             wide_cube(rows), wide_cube(rows), wide_cube(full_rows), planes_of(2, begin), whole(columns), wide_weight(cin), wide_rows(4),
             wide_rows(4), wide_weight(taps), whole(z_zero), whole(dx_in), whole(sums_in), whole(list_in)],
            [fixed(pixels, LANES), send_spec, fixed(listed, 8, LANES), tile_rows(8)],
            [shape(pixels, LANES), shape(*send), shape(listed, 8, LANES), shape(8, count * LANES)],
            [pltpu.VMEM(z_shape, F32), pltpu.VMEM((full_rows, 8, LANES), F32),
             pltpu.VMEM((taps, 8, LANES), F32), pltpu.VMEM((taps, 8, LANES), F32), pltpu.VMEM((pixels, 2 * LANES), low)],
            (frame_counts, sums, stat2, stat, nstat, dy2, depth, expanded, planes, columns, w_t, wide_gains, wide_biases,
             depth_weight, z_zero, dx_in, sums_in, list_in),
        )

    dxpre_one, sums, q_one, grad_one = depth_backward(
        1, 0, tiles, sums, stat12, stat11, dy2_one, d_one, e_one, planes_one, x1_columns, nothing, nothing, nothing
    )
    sums, pack_one = together(sums, pack_one)
    top_one, pack_one = together(exchange(sums), pack_one)
    pack_one = share_back(pack_one)
    ins, outs, shapes, scratch = backward_specs(0)
    dx1, nsum_zero, dy2_zero, sums, pack_zero = call(
        squeeze_zero_backward_kernel, (2, tiles),
        [SCALARS, whole(top_one), whole(stat11), whole(gram), whole(nstat), whole(dxpre_one), whole(x1), whole(z_zero),
         whole(ngains), of_block(1, cin, width), whole(wide_gains), whole(q_one)] + ins,
        [fixed(pixels, LANES)] + outs, [shape(pixels, LANES)] + shapes, scratch,
        (frame_counts, top_one, stat11, gram, nstat, dxpre_one, x1, z_zero, ngains, w_t, wide_gains, q_one, stat02, d_zero,
         wide_gains, wide_biases, squeeze_weight, up_t, project_weight, gates_zero, running_zero, pre_zero),
    )
    sums, pack_one = together(sums, pack_one)
    pack_one_other = swap_cores(pack_one)
    sums, pack_zero, pack_one_other = together(exchange(sums), add_cores(pack_zero), pack_one_other)
    pack_zero = share_out(pack_zero)
    first = tiles - tiles // 2
    dxpre_zero, sums_in, late, grad_a = depth_backward(
        0, 0, first, sums, stat02, stat01, dy2_zero, d_zero, e_zero, planes_zero, x_columns, nothing, nothing, nothing
    )
    dxpre_zero, pack_zero = together(dxpre_zero, pack_zero)
    pack_zero = share_back(pack_zero)
    dxpre_zero, sums, late, grad_b = depth_backward(
        0, first, tiles, sums, stat02, stat01, dy2_zero, d_zero, e_zero, planes_zero, x_columns, dxpre_zero, sums_in, late
    )
    grad_zero = jnp.concatenate([grad_a, grad_b], axis=1)
    sums, pack_zero = together(sums, pack_zero)
    pack_zero_other = swap_cores(pack_zero)
    top_zero, late, pack_zero_other = together(exchange(sums), add_cores(late), pack_zero_other)
    late = share_out(late)
    core = lax.axis_index("core").astype(jnp.int32).reshape(1)
    final_args = (
        frame_counts, momentum_index, gram, stat01, stat02, stat11, stat12, grad_zero, grad_one, top_one,
        top_zero, nsum_zero, nsum_one, dxpre_zero, x, dx1, w_t, wide_gains, wide_means, wide_variances, narrow_means,
        narrow_variances,
    )
    final_outs = [
        shape(cin, pixels), shape(2, cin, width), shape(16, width), shape(4, width), shape(4, width), shape(2, cin),
        shape(2, cin), shape(4, width), shape(4, width), shape(2, cin), shape(2, cin),
    ]
    video_grad, less, factor, wgain, wbias, ngain, nbias, newm, newv, newnm, newnv = simple_call(
        finish_kernel, 2, final_args, final_outs
    )
    less, late = together(less, late)
    late = share_back(late)
    late_other = swap_cores(late)
    dw_t, dtaps, ddown, dup, dproj, dupb, ddownb = simple_call(
        gradient_kernel, 1,
        (core, pack_zero, pack_zero_other, pack_one, pack_one_other, late, late_other, less, factor),
        [shape(2, cin, width), shape(2, taps, width), shape(2, squeeze, width), shape(2, squeeze, width),
         shape(2, cin, width), shape(2, width), shape(2, squeeze)],
    )
    return (
        activations, video_grad, jnp.swapaxes(dw_t, 1, 2), wgain, wbias, ngain, nbias, dtaps, ddown, ddownb,
        jnp.swapaxes(dup, 1, 2), dupb, dproj, newm, newv, newnm, newnv,
    )


def solution(mesh):
    sizes = (mesh.shape["dp"], mesh.shape["rep"] // 2, 2)
    split_mesh = jax.sharding.Mesh(mesh.devices.reshape(sizes), AXES)
    split = P(None, AXES)
    placed = (split, P(AXES)) + (P(),) * 16 + (split,)
    return jax.shard_map(
        local, mesh=split_mesh, in_specs=placed, out_specs=(split, split) + (P(),) * 15, check_vma=False
    )
```

```python
import functools

import jax
import jax.numpy as jnp
from jax import lax
from jax.experimental import pallas as pl
from jax.experimental.pallas import tpu as pltpu
from jax.sharding import PartitionSpec as P

SIDE = 16
LANES = 128
LAGS = 5
FULL_ROWS = 2 * SIDE
HALF_ROWS = SIDE // 2
EPSILON = 1e-05
HIGHEST = lax.Precision.HIGHEST
F32 = jnp.float32
NN = (((1,), (0,)), ((), ()))
NT = (((1,), (1,)), ((), ()))
TN = (((0,), (0,)), ((), ()))
VMEM_BYTES = 52 * 1024 * 1024


def half_tanh(half_values):
    return jnp.tanh(half_values)


def sigmoid(values):
    return 0.5 * jnp.tanh(0.5 * values) + 0.5


def silu_slope(half_values, tanh):
    return 0.5 * (1.0 + tanh + half_values * (1.0 - tanh * tanh))


def exact_dot(left, right, dims=NN):
    return lax.dot_general(left, right, dims, precision=HIGHEST, preferred_element_type=F32)


def halves(values):
    high = values.astype(jnp.bfloat16)
    return (high, (values - high.astype(F32)).astype(jnp.bfloat16))


def side_by_side(values):
    return jnp.concatenate(halves(values), axis=1)


def right_square(w):
    both = side_by_side(w)
    return jnp.concatenate([both, both], axis=0)


def right_square_t(w):
    high, low = halves(w)
    return jnp.concatenate(
        [jnp.concatenate([high, high], axis=1), jnp.concatenate([low, low], axis=1)], axis=0
    )


def plain_dot(left, right, dims=NN):
    return lax.dot_general(left, right, dims, preferred_element_type=F32)


def fold_right(values):
    lanes = values.shape[1] // 2
    return values[:, :lanes] + values[:, lanes:]


def fold_square(values):
    rows = values.shape[0] // 2
    return fold_right(values[:rows] + values[rows:])


def stacked(values):
    high = values.astype(jnp.bfloat16).astype(F32)
    return jnp.concatenate([high, values - high], axis=0).astype(jnp.bfloat16)


def skinny_dot(left, right, dims=NN):
    rows = left.shape[0]
    both = stacked(left)
    high, low = halves(right)
    values = plain_dot(both, high, dims) + plain_dot(both, low, dims)
    return values[:rows] + values[rows:]


def frame_outer(left, right):
    a_high = left.astype(jnp.bfloat16).astype(F32)
    b_high = right.astype(jnp.bfloat16).astype(F32)
    a_low = left - a_high
    b_low = right - b_high
    a = jnp.concatenate([a_high, a_high, a_low, a_low], axis=0).astype(jnp.bfloat16)
    b = jnp.concatenate([b_high, b_low, b_high, b_low], axis=0).astype(jnp.bfloat16)
    return plain_dot(a, b, TN)


def pad_rows(values):
    return jnp.concatenate([values, jnp.zeros((LANES - values.shape[0], values.shape[1]), values.dtype)], axis=0)


def column_order():
    q = lax.broadcasted_iota(jnp.int32, (LANES, LANES), 0)
    n = lax.broadcasted_iota(jnp.int32, (LANES, LANES), 1)
    source = (q // 16) * 16 + (q % 8) * 2 + (q // 8) % 2
    return (source == n).astype(jnp.bfloat16)


def live_frames(counts_ref):
    total = counts_ref[0]
    for clip in range(1, counts_ref.shape[0]):
        total = total + counts_ref[clip]
    return total


def place_of(counts_ref, frame):
    begin = jnp.int32(0)
    end = jnp.int32(0)
    for clip in range(counts_ref.shape[0]):
        end = end + counts_ref[clip]
        begin = jnp.where(frame >= end, end, begin)
    return frame - begin


def running_matrix(counts_ref, frames):
    after = lax.broadcasted_iota(jnp.int32, (frames, frames), 0)
    before = lax.broadcasted_iota(jnp.int32, (frames, frames), 1)
    begin = jnp.int32(0)
    matrix = jnp.zeros((frames, frames), F32)
    for clip in range(counts_ref.shape[0]):
        end = begin + counts_ref[clip]
        inside = (before >= begin) & (before <= after) & (after < end)
        matrix = matrix + jnp.where(inside, 1.0 / (after - begin + 1).astype(F32), 0.0)
        begin = end
    return matrix


def columns_up(values):
    spot = lax.broadcasted_iota(jnp.int32, values.shape, 1)
    return jnp.where(spot == 7, 0.0, pltpu.roll(values, 7, axis=1))


def columns_down(values):
    spot = lax.broadcasted_iota(jnp.int32, values.shape, 1)
    return jnp.where(spot == 0, 0.0, pltpu.roll(values, 1, axis=1))


def tile_sum(values):
    return jnp.sum(jnp.sum(values, axis=0), axis=0, keepdims=True)


def rows8(*rows):
    lanes = rows[0].shape[1]
    spot = lax.broadcasted_iota(jnp.int32, (8, lanes), 0)
    block = jnp.zeros((8, lanes), F32)
    for index, row in enumerate(rows):
        block = jnp.where(spot == index, row, block)
    return block


def pick_row(block, index):
    spot = lax.broadcasted_iota(jnp.int32, block.shape, 0)
    return jnp.sum(jnp.where(spot == index, block, 0.0), axis=0, keepdims=True)


def outer(left, right):
    return exact_dot(rows8(left), rows8(right), TN)


def row_dot(row, matrix, dims=NN):
    return exact_dot(rows8(row), matrix, dims)[0:1]


def clear_edges(ref):
    planes = ref.shape[1]
    edge = jnp.zeros((8, LANES), F32)
    for t in range(ref.shape[0]):
        for plane in range(planes):
            ref[t, plane, 0] = edge
            ref[t, plane, ref.shape[2] - 1] = edge


def spread_taps(taps_ref, w_ref):
    for tap in range(w_ref.shape[0]):
        w_ref[tap] = jnp.broadcast_to(taps_ref[0, tap : tap + 1, :], (8, LANES))


PAIRS = SIDE // 2


def row_pairs(plane):
    pair = plane.reshape(PAIRS, 2, 8, LANES)
    d1 = pair[:, 0]
    d2 = pair[:, 1]
    edge = jnp.zeros((1, 8, LANES), F32)
    d0 = jnp.concatenate([edge, d2[:-1]], axis=0)
    d3 = jnp.concatenate([d1[1:], edge], axis=0)
    return (d0 - d2, d1 + d2, d2 - d1, d1 - d3)


def pair_rows(parts):
    upper = parts[:, 0] + parts[:, 1] + parts[:, 2]
    lower = parts[:, 1] - parts[:, 2] - parts[:, 3]
    return jnp.stack([upper, lower], axis=1).reshape(FULL_ROWS, 8, LANES)


def spread_pairs(taps_ref, w_ref):
    for k in range(LAGS):
        for c in range(3):
            g0, g1, g2 = (taps_ref[0, k * 9 + 3 * r + c : k * 9 + 3 * r + c + 1, :] for r in range(3))
            outside = 0.5 * (g0 + g2)
            combined = (g0, outside + 0.5 * g1, outside - 0.5 * g1, g2)
            for place in range(4):
                w_ref[k * 12 + 3 * place + c] = jnp.broadcast_to(combined[place], (8, LANES))


def conv_full(t, k, a_ref, b_ref, w_ref, m_ref, fresh):
    weights = [w_ref[k * 12 + tap] for tap in range(12)]
    source = t - k
    for m in range(PAIRS):
        for place in range(4):
            left, centre, right = weights[3 * place : 3 * place + 3]
            a_even, a_odd = (a_ref[source, plane, place, m] for plane in range(2))
            a_odd_down, a_even_up = (b_ref[source, plane, place, m] for plane in range(2))
            even = centre * a_even + right * a_odd + left * a_odd_down
            odd = centre * a_odd + left * a_even + right * a_even_up
            if fresh:
                m_ref[m, place, 0] = even
                m_ref[m, place, 1] = odd
            else:
                m_ref[m, place, 0] = m_ref[m, place, 0] + even
                m_ref[m, place, 1] = m_ref[m, place, 1] + odd


def conv_half(t, k, a_ref, w_ref, d_ref, fresh):
    weights = [w_ref[k * 9 + tap] for tap in range(9)]
    source = t - k
    carried = [a_ref[source, plane, 0] for plane in range(3)]
    for i in range(HALF_ROWS):
        rows = [carried]
        for need in (2 * i + 1, 2 * i + 2):
            rows.append([a_ref[source, plane, need] for plane in range(3)])
        carried = rows[2]
        total = None
        for r in range(3):
            a_even, a_odd, a_odd_down = rows[r]
            left, centre, right = weights[3 * r : 3 * r + 3]
            part = centre * a_even + right * a_odd + left * a_odd_down
            total = part if total is None else total + part
        at = t * HALF_ROWS + i
        d_ref[at] = total if fresh else d_ref[at] + total


def row_total(ref, lanes=None):
    values = ref[...] if lanes is None or lanes == slice(None) else ref[:, :, lanes]
    return jnp.sum(values, axis=0)


def send_all(send_ref, rows, lanes):
    count = rows.shape[0]

    def one(device, carry):
        send_ref[pl.ds(device, 1), 0:count, lanes] = rows[None]
        return carry

    lax.fori_loop(0, send_ref.shape[0], one, 0)


def stack_rows(*rows):
    return rows8(*rows)[0 : len(rows)]


def pick_thirds(order, values, dims, order_left):
    pieces = []
    rest = values
    for _ in range(3):
        piece = rest.astype(jnp.bfloat16)
        rest = rest - piece.astype(F32)
        args = (order, piece) if order_left else (piece, order)
        pieces.append(plain_dot(*args, dims))
    return pieces


def gram_kernel(counts_ref, video_ref, w_ref, gram_ref, send_ref):
    total = live_frames(counts_ref)
    frames = video_ref.shape[1] // 256
    ones = jnp.ones((8, 256), jnp.bfloat16)

    def frame(t, carry):
        at = pl.ds(pl.multiple_of(t * 256, 256), 256)
        both = jnp.concatenate(halves(pad_rows(video_ref[:, at] * live_value(t, total))), axis=0)
        return (carry[0] + plain_dot(both, both, NT), carry[1] + plain_dot(ones, both, NT))

    init = (jnp.zeros((2 * LANES, 2 * LANES), F32), jnp.zeros((8, 2 * LANES), F32))
    gram, summed = each_frame(frames, frame, init)
    gram = fold_square(gram)
    summed = fold_right(summed)[0:1]
    gram_ref[0:LANES, :] = gram
    gram_ref[LANES : LANES + 8, :] = rows8(summed)
    w = pad_rows(w_ref[0])
    width = w.shape[1]
    sums = stack_rows(row_dot(summed, w), jnp.sum(w * exact_dot(gram, w), axis=0, keepdims=True))
    count = jnp.full((2, LANES), 1.0, F32) * (total * (SIDE * SIDE)).astype(F32)
    send_all(send_ref, sums, slice(0, width))
    send_all(send_ref, count, slice(width, width + LANES))


def prepare_kernel(counts_ref, video_ref, cot_ref, x_ref, rows_ref, columns_ref, cot_out_ref):
    order = column_order()
    total = live_frames(counts_ref)
    for part in range(video_ref.shape[1] // LANES):
        at = slice(part * LANES, (part + 1) * LANES)
        block = pad_rows(video_ref[:, at] * live_value(part // 2, total))
        high, middle, low = pick_thirds(order, block, NT, True)
        x_ref[at, :] = high + middle + low
        rows_ref[at, :] = jnp.concatenate([high, middle], axis=1).astype(jnp.bfloat16)
        columns_ref[:, at] = jnp.concatenate([high.T, middle.T], axis=0).astype(jnp.bfloat16)
    spot = lax.broadcasted_iota(jnp.int32, (LANES, LANES), 1)
    for part in range(cot_ref.shape[1] // LANES):
        at = slice(part * LANES, (part + 1) * LANES)
        frame = (spot + part * LANES) // (HALF_ROWS * 8)
        cot_out_ref[at, :] = jnp.where(frame < total, pad_rows(cot_ref[:, at]), 0.0).T


def moments_of(sums, count):
    average = sums[0:1] / count
    return (average, sums[1:2] / count - average * average)


def narrow_kernel(
    counts_ref, sums_ref, stat_ref, gram0_ref, x_ref, z_ref, ngain_ref, nbias_ref, w_ref,
    x1_ref, rows_ref, columns_ref, gram_ref, stat_out_ref, send_ref,
):
    total = live_frames(counts_ref)
    count = stat_ref[2:3, 0:LANES]
    average, variance = moments_of(row_total(sums_ref), count)
    factor = ngain_ref[0:1, :] * lax.rsqrt(variance + EPSILON)
    shift = nbias_ref[0:1, :] - factor * average
    stat_out_ref[...] = rows8(average, variance, count)
    frames = x_ref.shape[0] // 256

    def frame(t, carry):
        gram, cross, summed = carry
        at = pl.ds(pl.multiple_of(t * 256, 256), 256)
        z = z_ref[at, :]
        rows = (x_ref[at, :] + factor * z + shift) * live_value(t, total)
        x1_ref[at, :] = rows
        both = side_by_side(rows)
        rows_ref[at, :] = both
        columns = jnp.concatenate(halves(rows.T), axis=0)
        columns_ref[:, at] = columns
        gram = gram + plain_dot(columns, both)
        cross = cross + plain_dot(columns, side_by_side(z))
        return (gram, cross, summed + jnp.sum(rows, axis=0, keepdims=True))

    zero = jnp.zeros((2 * LANES, 2 * LANES), F32)
    gram, cross, summed = each_frame(frames, frame, (zero, zero, jnp.zeros((1, LANES), F32)))

    gram = fold_square(gram)
    tiles = LANES // 8
    gram_ref[0:tiles] = gram.reshape(tiles, 8, LANES)
    gram_ref[tiles : 2 * tiles] = fold_square(cross).reshape(tiles, 8, LANES)
    gram_ref[2 * tiles : 3 * tiles] = gram0_ref[0:LANES, :].reshape(tiles, 8, LANES)
    gram_ref[3 * tiles] = rows8(summed, gram0_ref[LANES : LANES + 1, :])
    w = pad_rows(w_ref[0])
    sums = stack_rows(row_dot(summed, w), jnp.sum(w * exact_dot(gram, w), axis=0, keepdims=True))
    send_all(send_ref, sums, slice(0, w.shape[1]))


def write_first(t, total, values, scale, shift, a_ref, b_ref):
    half_pre = values * scale + shift
    first = (half_pre + half_pre * half_tanh(half_pre)) * live_value(t, total)
    first = first.reshape(SIDE, 2, 8, LANES)
    even = first[:, 0]
    odd = first[:, 1]
    if b_ref is None:
        a_ref[t, 0, 1 : SIDE + 1] = even
        a_ref[t, 1, 1 : SIDE + 1] = odd
        a_ref[t, 2, 1 : SIDE + 1] = columns_down(odd)
        return
    for ref, plane, values in ((a_ref, 0, even), (a_ref, 1, odd), (b_ref, 0, columns_down(odd)), (b_ref, 1, columns_up(even))):
        for place, part in enumerate(row_pairs(values)):
            ref[t, plane, place] = part


def expand_kernel(
    block, counts_ref, sums_ref, count_ref, rows_ref, w_ref, gain_ref, bias_ref, taps_ref,
    e_ref, d_ref, stat_ref, send_ref, a_ref, taps8_ref, *pair_refs,
):
    b_ref, m_ref = pair_refs if pair_refs else (None, None)
    if block:
        clear_edges(a_ref)
    total = live_frames(counts_ref)
    frames = a_ref.shape[0]
    count = count_ref[2:3, :] if block else row_total(count_ref)[0:1]
    average, variance = moments_of(row_total(sums_ref), count)
    stat_ref[...] = rows8(average, variance, count)
    norm_row = 2 * block
    scale = gain_ref[norm_row : norm_row + 1, :] * lax.rsqrt(variance + EPSILON)
    shift = 0.5 * (bias_ref[norm_row : norm_row + 1, :] - average * scale)
    scale = 0.5 * scale
    square = right_square(pad_rows(w_ref[0]))

    def expand(t, carry):
        at = pl.ds(pl.multiple_of(t * 256, 256), 256)
        values = fold_right(plain_dot(rows_ref[at, :], square)).reshape(FULL_ROWS, 8, LANES)
        e_ref[pl.ds(pl.multiple_of(t * FULL_ROWS, FULL_ROWS), FULL_ROWS)] = values
        write_first(t, total, values, scale, shift, a_ref, b_ref)
        return carry

    each_frame(frames, expand, 0)
    per_frame = HALF_ROWS if block else FULL_ROWS
    if block:
        spread_taps(taps_ref, taps8_ref)
        conv = functools.partial(conv_half, a_ref=a_ref, w_ref=taps8_ref, d_ref=d_ref)
    else:
        spread_pairs(taps_ref, taps8_ref)
        conv = functools.partial(conv_full, a_ref=a_ref, b_ref=b_ref, w_ref=taps8_ref, m_ref=m_ref)

    def frame(t, carry):
        conv(t, 0, fresh=True)
        last = jnp.minimum(place_of(counts_ref, t), LAGS - 1)

        def lag(k, inner):
            conv(t, k, fresh=False)
            return inner

        lax.fori_loop(1, last + 1, lag, 0)
        if not block:
            d_ref[pl.ds(t * per_frame, per_frame)] = pair_rows(m_ref[...])
        values = d_ref[pl.ds(t * per_frame, per_frame)]
        return (carry[0] + jnp.sum(values, axis=0), carry[1] + jnp.sum(values * values, axis=0))

    zero = jnp.zeros((8, LANES), F32)
    summed, squares = lax.fori_loop(0, total, frame, (zero, zero))

    def dead(t, carry):
        d_ref[pl.ds(t * per_frame, per_frame)] = jnp.zeros((per_frame, 8, LANES), F32)
        return carry

    lax.fori_loop(total, frames, dead, 0)
    sums = stack_rows(jnp.sum(summed, axis=0, keepdims=True), jnp.sum(squares, axis=0, keepdims=True))
    send_all(send_ref, sums, slice(0, LANES))


def live_value(t, total):
    return jnp.where(t < total, 1.0, 0.0).astype(F32)


def each_frame(count, body, init, unroll=2):
    return lax.fori_loop(0, count, body, init, unroll=unroll)


def lanes_of(ref, tile):
    if ref.shape[-1] == LANES:
        return slice(None)
    return pl.ds(pl.multiple_of(tile * LANES, LANES), LANES)


def squeeze_forward_kernel(
    block, counts_ref, sums_ref, stat_ref, d_ref, gain_ref, bias_ref, down_ref, downb_ref, up_ref, upb_ref, proj_ref,
    cot_ref, z_ref, gates_ref, running_ref, pre_ref, stat_out_ref, send_ref, second_ref, pooled_ref,
):
    step = pl.program_id(0)
    steps = pl.num_programs(0)
    tiles = second_ref.shape[0]
    total = live_frames(counts_ref)
    per_frame = HALF_ROWS if block else FULL_ROWS
    pixels = per_frame * 8
    frames = second_ref.shape[1] // per_frame
    group = 256 // pixels
    chunks = frames // group
    norm_row = 2 * block + 1

    def activate(tile, carry):
        lanes = lanes_of(d_ref, tile)
        count = stat_ref[2:3, lanes] * (0.25 if block else 1.0)
        average, variance = moments_of(row_total(sums_ref, lanes), count)
        stat_out_ref[:, lanes] = rows8(average, variance, count)
        scale = gain_ref[norm_row : norm_row + 1, lanes] * lax.rsqrt(variance + EPSILON)
        shift = 0.5 * (bias_ref[norm_row : norm_row + 1, lanes] - average * scale)
        scale = 0.5 * scale

        def chunk(index, inside):
            for inner in range(group):
                t = index * group + inner
                at = pl.ds(t * per_frame, per_frame)
                half_pre = d_ref[at, :, lanes] * scale + shift
                second = half_pre + half_pre * half_tanh(half_pre)
                second = second * live_value(t, total)
                second_ref[tile, at] = second
                pooled_ref[tile, pl.ds(t, 1), :] = tile_sum(second) * (1.0 / pixels)
            return inside

        each_frame(chunks, chunk, 0)
        return carry

    if block:
        lax.fori_loop(0, tiles, activate, 0)
    else:
        activate(step, 0)

    def project(tile, carry):
        lanes = lanes_of(gates_ref, tile)
        square = right_square_t(pad_rows(proj_ref[0, :, lanes]))
        gates = gates_ref[:, lanes]

        def chunk(index, inside):
            parts = []
            for inner in range(group):
                t = index * group + inner
                second = second_ref[tile, pl.ds(t * per_frame, per_frame)].reshape(pixels, LANES)
                parts.append(second * pick_row(gates, t))
            excited = parts[0] if group == 1 else jnp.concatenate(parts, axis=0)
            at = pl.ds(pl.multiple_of(index * 256, 256), 256)
            z_ref[at, :] = z_ref[at, :] + fold_right(plain_dot(side_by_side(excited), square, NT))
            return inside

        each_frame(chunks, chunk, 0)
        return carry

    @pl.when(step == steps - 1)
    def gate_and_project():
        matrix = running_matrix(counts_ref, frames)
        pooled = jnp.concatenate([pooled_ref[index] for index in range(tiles)], axis=1)
        running = exact_dot(matrix, pooled)
        running_ref[...] = running
        pre = skinny_dot(running, down_ref[0], NT) + downb_ref[block : block + 1, :]
        pre_ref[...] = pre
        gates_ref[...] = sigmoid(skinny_dot(pre * sigmoid(pre), up_ref[0]) + upb_ref[block : block + 1, :])
        z_ref[...] = jnp.zeros_like(z_ref)
        lax.fori_loop(0, tiles, project, 0)

        def chunk(index, carry):
            at = pl.ds(pl.multiple_of(index * 256, 256), 256)
            z = z_ref[at, :].reshape(32, 8, LANES)
            values = [z, z * z]
            if block:
                dy = cot_ref[at, :].reshape(32, 8, LANES)
                values = values + [dy, dy * z]
            return tuple(old + jnp.sum(new, axis=0) for old, new in zip(carry, values))

        zero = jnp.zeros((8, LANES), F32)
        sums = each_frame(chunks, chunk, (zero,) * (4 if block else 2))
        rows = stack_rows(*(jnp.sum(value, axis=0, keepdims=True) for value in sums))
        send_all(send_ref, rows, slice(0, LANES))


def pack_tiles(narrow, squeeze):
    return narrow // 8 + 2 * (squeeze // 8) + 1


def squeeze_backward_body(
    block, counts_ref, stat_ref, d_ref, gain_ref, bias_ref, down_ref, up_ref, proj_ref, gates_ref, running_ref,
    pre_ref, dy2_ref, send_ref, pack_ref, dz3_ref, dz3t_ref, excited_ref, dexc_ref, dgate_ref, head,
):
    total = live_frames(counts_ref)
    per_frame = HALF_ROWS if block else FULL_ROWS
    pixels = per_frame * 8
    frames = dz3_ref.shape[0] // pixels
    group = 256 // pixels
    chunks = frames // group
    norm_row = 2 * block + 1
    tiles = dexc_ref.shape[0]
    narrow = proj_ref.shape[1]
    squeeze = down_ref.shape[1]
    per_tile = pack_tiles(narrow, squeeze)

    def norm_of(tile):
        lanes = lanes_of(d_ref, tile)
        average = stat_ref[0:1, lanes]
        root = lax.rsqrt(stat_ref[1:2, lanes] + EPSILON)
        scale = gain_ref[norm_row : norm_row + 1, lanes] * root
        shift = 0.5 * (bias_ref[norm_row : norm_row + 1, lanes] - average * scale)
        return (lanes, average, root, 0.5 * scale, shift)

    def excite(tile, carry):
        lanes, _, _, scale, shift = norm_of(tile)
        gates = gates_ref[:, lanes_of(gates_ref, tile)]
        square = right_square(pad_rows(proj_ref[0, :, lanes]))

        def chunk(index, inside):
            flat = pl.ds(pl.multiple_of(index * 256, 256), 256)
            dexc = fold_right(plain_dot(dz3_ref[flat, :], square)).reshape(32, 8, LANES)
            dexc_ref[tile, pl.ds(pl.multiple_of(index * 32, 32), 32)] = dexc
            parts = []
            for inner in range(group):
                t = index * group + inner
                half_pre = d_ref[pl.ds(t * per_frame, per_frame), :, lanes] * scale + shift
                second = half_pre + half_pre * half_tanh(half_pre)
                second = second * live_value(t, total)
                own = dexc[inner * per_frame : (inner + 1) * per_frame]
                dgate_ref[tile, pl.ds(t, 1), :] = tile_sum(own * second)
                parts.append(second.reshape(pixels, LANES) * pick_row(gates, t))
            excited = parts[0] if group == 1 else jnp.concatenate(parts, axis=0)
            excited_ref[flat, :] = side_by_side(excited)
            return inside

        each_frame(chunks, chunk, 0)
        dproj = fold_square(plain_dot(dz3t_ref[...], excited_ref[...]))
        pack_ref[pl.ds(tile * per_tile, narrow // 8)] = dproj[0:narrow].reshape(narrow // 8, 8, LANES)
        return carry

    def squeeze_part():
        pre = pre_ref[...]
        half_pre = 0.5 * pre
        tanh = half_tanh(half_pre)
        squeezed = half_pre + half_pre * tanh
        all_gates = gates_ref[...]
        dgate = jnp.concatenate([dgate_ref[index] for index in range(tiles)], axis=1)
        du = dgate * all_gates * (1.0 - all_gates)
        dpre = skinny_dot(du, up_ref[0], NT) * silu_slope(half_pre, tanh)
        ddown = frame_outer(dpre, running_ref[...])
        dup = frame_outer(squeezed, du)
        dpre_row = jnp.sum(dpre, axis=0, keepdims=True)
        dpre_row = jnp.concatenate([dpre_row, jnp.zeros((1, du.shape[1] - squeeze), F32)], axis=1)
        biases = rows8(jnp.sum(du, axis=0, keepdims=True), dpre_row)
        for index in range(tiles):
            own = slice(index * LANES, (index + 1) * LANES)
            at = index * per_tile + narrow // 8
            pack_ref[at : at + squeeze // 8] = ddown[:, own].reshape(squeeze // 8, 8, LANES)
            at = at + squeeze // 8
            pack_ref[at : at + squeeze // 8] = dup[:, own].reshape(squeeze // 8, 8, LANES)
            pack_ref[at + squeeze // 8] = biases[:, own]
        drunning = skinny_dot(dpre, down_ref[0])
        dpooled = exact_dot(running_matrix(counts_ref, frames), drunning, TN) * (1.0 / pixels)
        for index in range(tiles):
            dgate_ref[index] = dpooled[:, index * LANES : (index + 1) * LANES]

    def slope(tile, carry):
        lanes, average, root, scale, shift = norm_of(tile)
        gates = gates_ref[:, lanes_of(gates_ref, tile)]

        def chunk(index, inside):
            summed, cross = inside
            for inner in range(group):
                t = index * group + inner
                at = pl.ds(t * per_frame, per_frame)
                depth = d_ref[at, :, lanes]
                half_pre = depth * scale + shift
                dsecond = dexc_ref[tile, at] * pick_row(gates, t) + pick_row(dgate_ref[tile], t)
                dy = dsecond * silu_slope(half_pre, half_tanh(half_pre))
                dy = dy * live_value(t, total)
                dy2_ref[at, :, lanes] = dy
                summed = summed + jnp.sum(dy, axis=0)
                cross = cross + jnp.sum(dy * (depth - average), axis=0)
            return (summed, cross)

        zero = jnp.zeros((8, LANES), F32)
        summed, cross = each_frame(chunks, chunk, (zero, zero))
        rows = stack_rows(jnp.sum(summed, axis=0, keepdims=True), root * jnp.sum(cross, axis=0, keepdims=True))
        send_all(send_ref, rows, lanes)
        return carry

    if block:
        head()
        lax.fori_loop(0, tiles, excite, 0)
        squeeze_part()
        lax.fori_loop(0, tiles, slope, 0)
    else:
        phase = pl.program_id(0)
        tile = pl.program_id(1)

        @pl.when((phase == 0) & (tile == 0))
        def start():
            head()

        @pl.when(phase == 0)
        def first():
            excite(tile, 0)

        @pl.when((phase == 1) & (tile == 0))
        def between():
            squeeze_part()

        @pl.when(phase == 1)
        def second():
            slope(tile, 0)


def squeeze_one_backward_kernel(
    counts_ref, third_ref, z_ref, cot_ref, ngain_ref, nbias_ref, stat_ref, d_ref, gain_ref, bias_ref, down_ref,
    up_ref, proj_ref, gates_ref, running_ref, pre_ref, act_ref, nsum_ref, dy2_ref, send_ref, pack_ref,
    dz3_ref, dz3t_ref, excited_ref, dexc_ref, dgate_ref,
):
    total = live_frames(counts_ref)
    pixels = HALF_ROWS * 8

    def head():
        count = stat_ref[2:3, 0:LANES]
        sums = row_total(third_ref)
        mean, variance = moments_of(sums, count)
        root = lax.rsqrt(variance + EPSILON)
        gain = ngain_ref[1:2, :]
        bias_sum = sums[2:3, :]
        gain_sum = root * (sums[3:4, :] - mean * bias_sum)
        nsum_ref[...] = rows8(gain_sum, bias_sum, mean, variance)
        row = lax.broadcasted_iota(jnp.int32, z_ref.shape, 0) // pixels
        live = row < total
        normed = (z_ref[...] - mean) * root
        act = jnp.where(live, gain * normed + nbias_ref[1:2, :], 0.0)
        act_ref[...] = act.T[0 : act_ref.shape[0]]
        dz3 = gain * root * (cot_ref[...] - bias_sum / count - normed * (gain_sum / count))
        dz3 = jnp.where(live, dz3, 0.0)
        dz3_ref[...] = side_by_side(dz3)
        dz3t_ref[...] = jnp.concatenate(halves(dz3.T), axis=0)

    squeeze_backward_body(
        1, counts_ref, stat_ref, d_ref, gain_ref, bias_ref, down_ref, up_ref, proj_ref, gates_ref, running_ref,
        pre_ref, dy2_ref, send_ref, pack_ref, dz3_ref, dz3t_ref, excited_ref, dexc_ref, dgate_ref, head,
    )


def input_factors(sums, stat_ref, count, gain, w):
    root = lax.rsqrt(stat_ref[1:2, :] + EPSILON)
    factor = gain * root
    matrix = exact_dot(w * (factor * root * sums[1:2] / count), w, NT)
    return (matrix, row_dot(factor * sums[0:1] / count, w, NT))


def covariance(gram, summed, count):
    mean = summed / count
    return (mean, gram / count - outer(mean, mean))


def squeeze_zero_backward_kernel(
    counts_ref, top_ref, stat1_ref, gram_ref, nstat_ref, dxpre_ref, x1_ref, z_ref, ngain_ref, w_ref, gains_ref, q_one_ref,
    stat_ref, d_ref, gain_ref, bias_ref, down_ref, up_ref, proj_ref, gates_ref, running_ref, pre_ref,
    dx1_ref, nsum_ref, dy2_ref, send_ref, pack_ref, dz3_ref, dz3t_ref, excited_ref, dexc_ref, dgate_ref,
):
    total = live_frames(counts_ref)
    width = gains_ref.shape[1]

    def head():
        start = pack_tiles(proj_ref.shape[1], down_ref.shape[1]) * (width // LANES)
        pack_ref[start : start + q_one_ref.shape[0]] = q_one_ref[...]
        count = stat_ref[2:3, :]
        wide_count = jnp.broadcast_to(count[:, 0:1], (1, width))
        sums = row_total(top_ref, slice(0, width))
        extra = row_total(top_ref, slice(width, width + LANES))
        matrix, shift = input_factors(sums, stat1_ref, wide_count, gains_ref[2:3, :], pad_rows(w_ref[0]))
        mean = nstat_ref[0:1, :]
        root = lax.rsqrt(nstat_ref[1:2, :] + EPSILON)
        mean_x1 = gram_ref[3 * LANES : 3 * LANES + 1, :] / count
        cross = (gram_ref[LANES : 2 * LANES, :] - count * outer(mean_x1, mean)) * root
        gain_sum = extra[0:1] - jnp.sum(matrix * cross, axis=0, keepdims=True)
        bias_sum = extra[1:2] - count * shift
        nsum_ref[...] = rows8(gain_sum, bias_sum, mean, nstat_ref[1:2, :])
        factor = ngain_ref[0:1, :] * root
        square = right_square(matrix)
        bias_mean = bias_sum / count
        gain_mean = gain_sum / count

        def frame(t, carry):
            at = pl.ds(pl.multiple_of(t * 256, 256), 256)
            centred = side_by_side(x1_ref[at, :] - mean_x1)
            live = live_value(t, total)
            dx1 = (dxpre_ref[at, :] - fold_right(plain_dot(centred, square)) - shift) * live
            dx1_ref[at, :] = dx1
            normed = (z_ref[at, :] - mean) * root
            dz3 = factor * (dx1 - bias_mean - normed * gain_mean) * live
            dz3_ref[at, :] = side_by_side(dz3)
            dz3t_ref[:, at] = jnp.concatenate(halves(dz3.T), axis=0)
            return carry

        each_frame(dz3_ref.shape[0] // 256, frame, 0)

    squeeze_backward_body(
        0, counts_ref, stat_ref, d_ref, gain_ref, bias_ref, down_ref, up_ref, proj_ref, gates_ref, running_ref,
        pre_ref, dy2_ref, send_ref, pack_ref, dz3_ref, dz3t_ref, excited_ref, dexc_ref, dgate_ref, head,
    )

def back_full(t, k, a_ref, w_ref, z_ref, raw_ref, f_ref, dw_ref, fresh):
    weights = [w_ref[k * 12 + tap] for tap in range(12)]
    target = t - k
    sums = [None] * 12
    for m in range(PAIRS):
        for place in range(4):
            flipped = (3, 1, 2, 0)[place]
            left, centre, right = weights[3 * flipped : 3 * flipped + 3]
            b_even, b_odd, b_odd_down, b_even_up = (z_ref[t, plane, place, m] for plane in range(4))
            even = centre * b_even + right * b_odd_down + left * b_odd
            odd = centre * b_odd + right * b_even + left * b_even_up
            if fresh:
                f_ref[target, m, place, 0] = even
                f_ref[target, m, place, 1] = odd
            else:
                f_ref[target, m, place, 0] = f_ref[target, m, place, 0] + even
                f_ref[target, m, place, 1] = f_ref[target, m, place, 1] + odd
            if place in (0, 3):
                row = 0 if place == 0 else 1
                b_even, b_odd, b_odd_down, b_even_up = (raw_ref[t, plane, row, m] for plane in range(4))
            a_even, a_odd = (a_ref[target, plane, place, m] for plane in range(2))
            pieces = (
                b_even_up * a_odd + b_odd * a_even,
                b_even * a_even + b_odd * a_odd,
                b_even * a_odd + b_odd_down * a_even,
            )
            for c in range(3):
                at = 3 * place + c
                sums[at] = pieces[c] if sums[at] is None else sums[at] + pieces[c]
    for place in range(4):
        for c in range(3):
            at = place * 3 * LAGS + k * 3 + c
            dw_ref[at] = dw_ref[at] + sums[3 * place + c]


def pair_taps(totals):
    count = 3 * LAGS
    first, second, third, last = (totals[place * count : (place + 1) * count] for place in range(4))
    middle = 0.5 * (second - third)
    return (first + middle, 0.5 * (second + third), middle - last)


def back_half(t, k, a_ref, w_ref, z_ref, f_ref, dw_ref, fresh):
    weights = [w_ref[k * 9 + tap] for tap in range(9)]
    target = t - k
    sums = [None] * 9

    def put(row, parity, value):
        at = target * FULL_ROWS + 2 * row + parity
        f_ref[at] = value if fresh else f_ref[at] + value

    carried = [a_ref[target, plane, 0] for plane in range(2)]
    here = [z_ref[t, plane, 0] for plane in range(2)]
    for i in range(HALF_ROWS):
        below = [z_ref[t, plane, i + 1] for plane in range(2)]
        dz, dz_up = here
        rows = [carried]
        for need in (2 * i + 1, 2 * i + 2):
            rows.append([a_ref[target, plane, need] for plane in range(2)])
        carried = rows[2]
        put(2 * i, 0, weights[4] * dz)
        put(2 * i, 1, weights[5] * dz + weights[3] * dz_up)
        put(2 * i + 1, 0, weights[7] * dz + weights[1] * below[0])
        put(
            2 * i + 1,
            1,
            weights[8] * dz + weights[6] * dz_up + (weights[2] * below[0] + weights[0] * below[1]),
        )
        for r in range(3):
            a_even, a_odd = rows[r]
            pieces = (dz_up * a_odd, dz * a_even, dz * a_odd)
            for c in range(3):
                at = 3 * r + c
                sums[at] = pieces[c] if sums[at] is None else sums[at] + pieces[c]
        here = below
    for tap in range(9):
        dw_ref[k * 9 + tap] = dw_ref[k * 9 + tap] + sums[tap]


def depth_backward_kernel(
    block, before, final, counts_ref, grads_ref, stat2_ref, stat_ref, nstat_ref, dy2_ref, d_ref, e_ref, a_ref, columns_ref, w_ref,
    gain_ref, bias_ref, taps_ref, z3_ref, dx_in_ref, sums_in_ref, list_in_ref, dxpre_ref, send_ref, q_ref, grad_rows_ref,
    z_ref, f_ref, taps8_ref, dw_ref, pair_ref, *raw_refs,
):
    tile = pl.program_id(0)
    tiles = pl.num_programs(0)
    total = live_frames(counts_ref)
    frames = a_ref.shape[0]
    norm_row = 2 * block
    half = block == 1
    per_frame = HALF_ROWS if half else FULL_ROWS
    taps = taps_ref.shape[1]

    @pl.when(tile == 0)
    def start():
        if half:
            clear_edges(z_ref)
        if before:
            dxpre_ref[...] = dx_in_ref[...]
            send_all(send_ref, sums_in_ref[0:2, :], slice(0, before * LANES))
            q_ref[0 : list_in_ref.shape[0]] = list_in_ref[...]
        else:
            dxpre_ref[...] = jnp.zeros_like(dxpre_ref)

        def dead(t, carry):
            if half:
                f_ref[pl.ds(t * FULL_ROWS, FULL_ROWS)] = jnp.zeros((FULL_ROWS, 8, LANES), F32)
            else:
                f_ref[t] = jnp.zeros(f_ref.shape[1:], F32)
            return carry

        lax.fori_loop(total, frames, dead, 0)

    count = stat2_ref[2:3, :]
    grads = row_total(grads_ref)
    grad_rows_ref[...] = rows8(grads[0:1], grads[1:2])
    average = stat2_ref[0:1, :]
    root = lax.rsqrt(stat2_ref[1:2, :] + EPSILON)
    scale_two = gain_ref[norm_row + 1 : norm_row + 2, :] * root
    slope = scale_two * root * grads[1:2] / count
    level = scale_two * grads[0:1] / count - slope * average
    average_one = stat_ref[0:1, :]
    root_one = lax.rsqrt(stat_ref[1:2, :] + EPSILON)
    scale_one = gain_ref[norm_row : norm_row + 1, :] * root_one
    shift_half = 0.5 * (bias_ref[norm_row : norm_row + 1, :] - average_one * scale_one)
    scale_half = 0.5 * scale_one

    def fill(t, carry):
        at = pl.ds(t * per_frame, per_frame)
        dz = scale_two * dy2_ref[at] - (slope * d_ref[at] + level)
        if half:
            z_ref[t, 0, 0:HALF_ROWS] = dz
            z_ref[t, 1, 0:HALF_ROWS] = columns_up(dz)
        else:
            pair = dz.reshape(SIDE, 2, 8, LANES)
            even = pair[:, 0]
            odd = pair[:, 1]
            for plane, values in enumerate((even, odd, columns_down(odd), columns_up(even))):
                for place, part in enumerate(row_pairs(values)):
                    z_ref[t, plane, place] = part
                rows = values.reshape(PAIRS, 2, 8, LANES)
                raw_refs[0][t, plane, 0] = rows[:, 0]
                raw_refs[0][t, plane, 1] = rows[:, 1]
        return carry

    each_frame(frames, fill, 0)
    dw_ref[...] = jnp.zeros_like(dw_ref)
    refs = dict(a_ref=a_ref, w_ref=taps8_ref, z_ref=z_ref, f_ref=f_ref, dw_ref=dw_ref)
    if half:
        spread_taps(taps_ref, taps8_ref)
        back = functools.partial(back_half, **refs)
    else:
        spread_pairs(taps_ref, taps8_ref)
        back = functools.partial(back_full, raw_ref=raw_refs[0], **refs)

    def frame(t, carry):
        back(t, 0, fresh=True)
        last = jnp.minimum(place_of(counts_ref, t), LAGS - 1)

        def lag(k, inner):
            back(t, k, fresh=False)
            return inner

        return lax.fori_loop(1, last + 1, lag, carry)

    lax.fori_loop(0, total, frame, 0)
    square = right_square_t(pad_rows(w_ref[0]))

    def finish(t, carry):
        rows = pl.ds(pl.multiple_of(t * FULL_ROWS, FULL_ROWS), FULL_ROWS)
        flat = pl.ds(pl.multiple_of(t * 256, 256), 256)
        values = e_ref[rows]
        half_pre = values * scale_half + shift_half
        dfirst = f_ref[rows] if half else pair_rows(f_ref[t])
        dy = dfirst * silu_slope(half_pre, half_tanh(half_pre))
        summed = carry[0] + jnp.sum(dy, axis=0)
        cross = carry[1] + jnp.sum(dy * (values - average_one), axis=0)
        dy = dy.reshape(256, LANES)
        pair_ref[flat, :] = side_by_side(dy)
        scaled = side_by_side(dy * scale_one)
        dxpre_ref[flat, :] = dxpre_ref[flat, :] + fold_right(plain_dot(scaled, square, NT))
        return (summed, cross)

    zero = jnp.zeros((8, LANES), F32)
    summed, cross = each_frame(frames, finish, (zero, zero))
    rows = stack_rows(jnp.sum(summed, axis=0, keepdims=True), root_one * jnp.sum(cross, axis=0, keepdims=True))
    if final:
        send_all(send_ref, rows, pl.ds(pl.multiple_of((tile + before) * LANES, LANES), LANES))
    else:
        send_ref[...] = rows8(rows[0:1], rows[1:2])
    gathered = fold_square(plain_dot(columns_ref[...], pair_ref[...]))
    narrow = w_ref.shape[1]
    dtaps = jnp.sum(dw_ref[...], axis=1)
    parts = (dtaps,) if half else pair_taps(dtaps)
    unused = jnp.zeros(((-taps) % 8, LANES), F32)
    values = jnp.concatenate((gathered[0:narrow],) + parts + (unused,), axis=0)
    listed = values.shape[0] // 8
    q_ref[pl.ds((tile + before) * listed, listed)] = values.reshape(listed, 8, LANES)

    if half:
        @pl.when(tile == tiles - 1)
        def tail():
            mean = nstat_ref[0:1, :]
            root_three = lax.rsqrt(nstat_ref[1:2, :] + EPSILON)

            def part(t, carry):
                flat = pl.ds(pl.multiple_of(t * 256, 256), 256)
                dx = dxpre_ref[flat, :].reshape(32, 8, LANES)
                normed = ((z3_ref[flat, :] - mean) * root_three).reshape(32, 8, LANES)
                return (carry[0] + jnp.sum(dx * normed, axis=0), carry[1] + jnp.sum(dx, axis=0))

            cross_three, summed_three = each_frame(frames, part, (zero, zero))
            rows = stack_rows(
                jnp.sum(cross_three, axis=0, keepdims=True), jnp.sum(summed_three, axis=0, keepdims=True)
            )
            width = send_ref.shape[2] - LANES
            send_all(send_ref, rows, slice(width, width + LANES))


def finish_kernel(
    counts_ref, momentum_ref, gram_ref, stat01_ref, stat02_ref, stat11_ref, stat12_ref, grad0_ref,
    grad1_ref, one_ref, zero_ref, nsum0_ref, nsum1_ref, dxpre_ref, x_ref, dx1_ref, w_ref, gain_ref, means_ref, vars_ref,
    nmeans_ref, nvars_ref,
    video_ref, less_ref, factor_ref, wgain_ref, wbias_ref, ngain_ref, nbias_ref, newm_ref, newv_ref, newnm_ref, newnv_ref,
):
    total = live_frames(counts_ref)
    full = stat01_ref[2:3, :]
    count = full[:, 0:LANES]
    width = full.shape[1]
    top_zero = row_total(zero_ref)
    top_one = row_total(one_ref, slice(0, width))
    w_zero = pad_rows(w_ref[0])
    matrix, shift = input_factors(top_zero, stat01_ref, full, gain_ref[0:1, :], w_zero)
    square = right_square(matrix)
    mean_x, cov_zero = covariance(
        gram_ref[2 * LANES : 3 * LANES, :], gram_ref[3 * LANES + 1 : 3 * LANES + 2, :], count
    )
    order = column_order()
    narrow = video_ref.shape[0]

    def frame(t, carry):
        at = pl.ds(pl.multiple_of(t * 256, 256), 256)
        centred = side_by_side(x_ref[at, :] - mean_x)
        dx = (dxpre_ref[at, :] - fold_right(plain_dot(centred, square)) - shift) * live_value(t, total) + dx1_ref[at, :]
        for part in range(2):
            own = dx[part * LANES : (part + 1) * LANES].T[0:narrow]
            pieces = pick_thirds(order, own, NN, False)
            start = pl.multiple_of(t * 256 + part * LANES, LANES)
            video_ref[:, pl.ds(start, LANES)] = pieces[0] + pieces[1] + pieces[2]
        return carry

    each_frame(x_ref.shape[0] // 256, frame, 0)
    mean_one, cov_one = covariance(gram_ref[0:LANES, :], gram_ref[3 * LANES : 3 * LANES + 1, :], count)
    plan = ((mean_x, cov_zero, stat01_ref, top_zero, w_zero), (mean_one, cov_one, stat11_ref, top_one, pad_rows(w_ref[1])))
    for block, (mean_row, cov, stat_ref, top, w) in enumerate(plan):
        root = lax.rsqrt(stat_ref[1:2, :] + EPSILON)
        factor = gain_ref[2 * block : 2 * block + 1, :] * root
        less = outer(mean_row, top[0:1]) + exact_dot(cov, w) * (root * top[1:2])
        less_ref[block] = (less * factor)[0:narrow]
        factor_ref[8 * block : 8 * block + 8, :] = rows8(factor)
    momentum = momentum_ref[0].astype(F32) / 10.0
    wgain_ref[...] = stack_rows(top_zero[1:2], grad0_ref[1:2, :], top_one[1:2], grad1_ref[1:2, :])
    wbias_ref[...] = stack_rows(top_zero[0:1], grad0_ref[0:1, :], top_one[0:1], grad1_ref[0:1, :])
    stats = (stat01_ref, stat02_ref, stat11_ref, stat12_ref)
    means = stack_rows(*(ref[0:1, :] for ref in stats))
    variances = stack_rows(*(ref[1:2, :] * (ref[2:3, :] / (ref[2:3, :] - 1.0)) for ref in stats))
    newm_ref[...] = (1.0 - momentum) * means_ref[...] + momentum * means
    newv_ref[...] = (1.0 - momentum) * vars_ref[...] + momentum * variances
    ngain_ref[...] = stack_rows(nsum0_ref[0:1, :], nsum1_ref[0:1, :])[:, 0:narrow]
    nbias_ref[...] = stack_rows(nsum0_ref[1:2, :], nsum1_ref[1:2, :])[:, 0:narrow]
    means = stack_rows(nsum0_ref[2:3, :], nsum1_ref[2:3, :])[:, 0:narrow]
    quarter = 0.25 * count
    variances = stack_rows(
        nsum0_ref[3:4, :] * (count / (count - 1.0)), nsum1_ref[3:4, :] * (quarter / (quarter - 1.0))
    )[:, 0:narrow]
    newnm_ref[...] = (1.0 - momentum) * nmeans_ref[...] + momentum * means
    newnv_ref[...] = (1.0 - momentum) * nvars_ref[...] + momentum * variances


def gradient_kernel(
    core_ref, pack0_ref, pack0_other_ref, pack1_ref, pack1_other_ref, late_ref, late_other_ref, less_ref, factor_ref,
    dw_ref, dtaps_ref, ddown_ref, dup_ref, dproj_ref, dupb_ref, ddownb_ref,
):
    narrow = dw_ref.shape[1]
    taps = dtaps_ref.shape[1]
    squeeze = ddown_ref.shape[1]
    tiles = dw_ref.shape[2] // LANES
    per_pack = pack_tiles(narrow, squeeze)
    per_tile = narrow // 8 + -(-taps // 8)
    first_core = core_ref[0] == 0

    def rows_of(pair, at, count):
        mine, other = pair
        half = mine.shape[0]
        pieces = []
        if at < half:
            size = min(count, half - at)
            here = slice(at, at + size)
            pieces.append(jnp.where(first_core, mine[here], other[here]))
            count = count - size
            at = at + size
        if count:
            here = slice(at - half, at - half + count)
            pieces.append(jnp.where(first_core, other[here], mine[here]))
        values = pieces[0] if len(pieces) == 1 else jnp.concatenate(pieces, axis=0)
        return values.reshape(-1, LANES)

    packs = ((pack0_ref, pack0_other_ref), (pack1_ref, pack1_other_ref))
    lists = ((late_ref, late_other_ref), packs[0])
    for block in range(2):
        down_rows = []
        for tile in range(tiles):
            lanes = slice(tile * LANES, (tile + 1) * LANES)
            at = tile * per_pack
            dproj_ref[block, :, lanes] = rows_of(packs[block], at, narrow // 8)
            at = at + narrow // 8
            ddown_ref[block, :, lanes] = rows_of(packs[block], at, squeeze // 8)
            at = at + squeeze // 8
            dup_ref[block, :, lanes] = rows_of(packs[block], at, squeeze // 8)
            biases = rows_of(packs[block], at + squeeze // 8, 1)
            dupb_ref[block : block + 1, lanes] = biases[0:1]
            down_rows.append(biases[1:2])
            values = rows_of(lists[block], (per_pack * tiles if block else 0) + tile * per_tile, per_tile)
            dw = values[0:narrow] * factor_ref[8 * block : 8 * block + 1, lanes] - less_ref[block, :, lanes]
            dw_ref[block, :, lanes] = dw
            if block:
                dtaps_ref[block, :, lanes] = values[narrow : narrow + taps]
                continue
            for r in range(3):
                for k in range(LAGS):
                    source = narrow + r * 3 * LAGS + 3 * k
                    dtaps_ref[block, k * 9 + 3 * r : k * 9 + 3 * r + 3, lanes] = values[source : source + 3]
        ddownb_ref[block : block + 1, :] = jnp.concatenate(down_rows, axis=1)[:, 0:squeeze]


AXES = ("dp", "z", "core")
CHIPS = ("dp", "z")


def exchange(send):
    return lax.all_to_all(send, AXES, 0, 0, tiled=True)


def together(*values):
    return lax.optimization_barrier(values)


def swap_cores(values):
    return lax.ppermute(values, "core", [(0, 1), (1, 0)])


def add_cores(tiles):
    core = lax.axis_index("core")
    pair = tiles.reshape(2, tiles.shape[0] // 2, *tiles.shape[1:])
    mine = lax.dynamic_index_in_dim(pair, core, 0, keepdims=False)
    return mine + swap_cores(lax.dynamic_index_in_dim(pair, 1 - core, 0, keepdims=False))


def share_out(tiles, names=CHIPS):
    count = 1
    for name in names:
        count = count * lax.axis_size(name)
    return lax.all_to_all(tiles.reshape(count, -1, *tiles.shape[1:]), names, 0, 0, tiled=True)


def share_back(pieces, names=CHIPS):
    own = jnp.sum(pieces, axis=0)
    everyone = lax.all_to_all(jnp.broadcast_to(own[None], pieces.shape), names, 0, 0, tiled=True)
    return everyone.reshape(-1, *pieces.shape[2:])


def shape(*dims, kind=F32):
    return jax.ShapeDtypeStruct(dims, kind)


def whole(array):
    rank = len(array.shape)
    return pl.BlockSpec(array.shape, lambda *ids: (0,) * rank)


SCALARS = pl.BlockSpec(memory_space=pltpu.SMEM)


def call(kernel, grid, in_specs, out_specs, out_shape, scratch, args):
    return pl.pallas_call(
        kernel,
        grid=grid,
        in_specs=in_specs,
        out_specs=out_specs,
        out_shape=out_shape,
        scratch_shapes=scratch,
        compiler_params=pltpu.CompilerParams(vmem_limit_bytes=VMEM_BYTES),
        cost_estimate=pl.CostEstimate(
            flops=1_000_000_000, bytes_accessed=1_000_000, transcendentals=0
        ),
    )(*args)


def simple_call(kernel, scalars, args, outs):
    return call(
        kernel, (1,), [SCALARS] * scalars + [whole(array) for array in args[scalars:]], [whole(item) for item in outs],
        outs, [], args,
    )


def local(
    video, frame_counts, momentum_index, expand_weight, wide_gains, wide_biases, narrow_gains, narrow_biases, depth_weight,
    squeeze_weight, squeeze_bias, excite_weight, excite_bias, project_weight, wide_means, wide_variances, narrow_means,
    narrow_variances, cotangent,
):
    devices = lax.axis_size("dp") * lax.axis_size("z") * lax.axis_size("core")
    cin, pixels = video.shape
    half_pixels = cotangent.shape[1]
    width = expand_weight.shape[1]
    squeeze = squeeze_weight.shape[1]
    frames = pixels // (SIDE * SIDE)
    tiles = width // LANES
    taps = depth_weight.shape[1]
    w_t = jnp.swapaxes(expand_weight, 1, 2)
    up_t = jnp.swapaxes(excite_weight, 1, 2)
    lanes_pad = ((0, 0), (0, LANES - cin))
    ngains = jnp.pad(narrow_gains, lanes_pad)
    nbiases = jnp.pad(narrow_biases, lanes_pad)
    full_rows = frames * FULL_ROWS
    half_rows = frames * HALF_ROWS
    low = jnp.bfloat16

    def round_up(count):
        return -(-count // devices) * devices

    def fixed(*dims):
        return pl.BlockSpec(dims, lambda *ids: (0,) * len(dims))

    def tile_rows(rows):
        return pl.BlockSpec((rows, LANES), lambda j: (0, j))

    def tile_cube(rows):
        return pl.BlockSpec((rows, 8, LANES), lambda j: (0, 0, j))

    def tile_sums(rows=2):
        return pl.BlockSpec((devices, rows, LANES), lambda j: (0, 0, j))

    def weight_tile(block, rows):
        return pl.BlockSpec((1, rows, LANES), lambda j, block=block: (block, 0, j))

    def of_block(block, rows, lanes):
        return pl.BlockSpec((1, rows, lanes), lambda *ids: (block, 0, 0))

    def early(make):
        return make(lambda p, j: j * (1 - p) + (tiles - 1) * p)

    def late(make):
        return make(lambda p, j: j * p)

    def both(make):
        return make(lambda p, j: j)

    def rows_at(rows):
        return lambda at: pl.BlockSpec((rows, LANES), lambda p, j: (0, at(p, j)))

    def cube_at(rows):
        return lambda at: pl.BlockSpec((rows, 8, LANES), lambda p, j: (0, 0, at(p, j)))

    def sums_at(rows):
        return lambda at: pl.BlockSpec((devices, rows, LANES), lambda p, j: (0, 0, at(p, j)))

    def weight_at(block, rows):
        return lambda at: pl.BlockSpec((1, rows, LANES), lambda p, j: (block, 0, at(p, j)))

    gram_zero, sums = call(
        gram_kernel, (1,), [SCALARS, whole(video), of_block(0, cin, width)],
        [fixed(LANES + 8, LANES), fixed(devices, 2, width + LANES)],
        [shape(LANES + 8, LANES), shape(devices, 2, width + LANES)],
        [], (frame_counts, video, w_t),
    )
    x, x_rows, x_columns, cot = simple_call(
        prepare_kernel, 1, (frame_counts, video, cotangent),
        [shape(pixels, LANES), shape(pixels, 2 * LANES, kind=low), shape(2 * LANES, pixels, kind=low),
         shape(half_pixels, LANES)],
    )
    sums = exchange(sums)

    def planes_shape(block, lanes, planes):
        if block:
            return (frames, planes, SIDE + 2, 8, lanes)
        return (frames, planes, 4, PAIRS, 8, lanes)

    def planes_of(block, planes, begin=0):
        dims = planes_shape(block, LANES, planes)
        zeros = (0,) * (len(dims) - 1)
        return pl.BlockSpec(dims, lambda j: zeros + (j + begin,))

    def expand(block, sums, count, count_spec, rows):
        depth_rows = half_rows if block else full_rows
        planes = 3 if block else 2
        scratch = [pltpu.VMEM((taps if block else 12 * LAGS, 8, LANES), F32)]
        if not block:
            scratch = scratch + [pltpu.VMEM(planes_shape(0, LANES, 2), F32), pltpu.VMEM((PAIRS, 4, 2, 8, LANES), F32)]
        return call(
            functools.partial(expand_kernel, block), (tiles,),
            [SCALARS, tile_sums(), count_spec, whole(rows), weight_tile(block, cin), tile_rows(4), tile_rows(4),
             weight_tile(block, taps)],
            [tile_cube(full_rows), tile_cube(depth_rows), tile_rows(8), tile_sums(), planes_of(block, planes)],
            [shape(full_rows, 8, width), shape(depth_rows, 8, width), shape(8, width), shape(devices, 2, width),
             shape(*planes_shape(block, width, planes))],
            scratch,
            (frame_counts, sums, count, rows, w_t, wide_gains, wide_biases, depth_weight),
        )

    count_spec = pl.BlockSpec((devices, 2, LANES), lambda j: (0, 0, tiles))
    e_zero, d_zero, stat01, sums, planes_zero = expand(0, sums, sums, count_spec, x_rows)
    sums = exchange(sums)

    def squeeze_forward(block, sums, stat, depth):
        rows = half_rows if block else full_rows
        kinds = 4 if block else 2
        moving = [tile_sums(), tile_rows(8), tile_cube(rows), tile_rows(4), tile_rows(4)]
        if block:
            moving = [whole(array) for array in (sums, stat, depth, wide_gains, wide_biases)]
        return call(
            functools.partial(squeeze_forward_kernel, block), (1 if block else tiles,),
            [SCALARS] + moving
            + [of_block(block, squeeze, width), whole(squeeze_bias), of_block(block, squeeze, width), whole(excite_bias),
               of_block(block, cin, width), whole(cot)],
            [fixed(rows * 8, LANES), fixed(8, width), fixed(8, width), fixed(8, squeeze),
             fixed(8, width) if block else tile_rows(8), fixed(devices, kinds, LANES)],
            [shape(rows * 8, LANES), shape(8, width), shape(8, width), shape(8, squeeze), shape(8, width),
             shape(devices, kinds, LANES)],
            [pltpu.VMEM((tiles, rows, 8, LANES), F32), pltpu.VMEM((tiles, frames, LANES), F32)],
            (frame_counts, sums, stat, depth, wide_gains, wide_biases, squeeze_weight, squeeze_bias, up_t, excite_bias,
             project_weight, cot),
        )

    z_zero, gates_zero, running_zero, pre_zero, stat02, sums = squeeze_forward(0, sums, stat01, d_zero)
    sums = exchange(sums)
    narrow_args = (frame_counts, sums, stat01, gram_zero, x, z_zero, ngains, nbiases, w_t)
    narrow_outs = [
        shape(pixels, LANES), shape(pixels, 2 * LANES, kind=low), shape(2 * LANES, pixels, kind=low),
        shape(round_up(3 * LANES // 8 + 1), 8, LANES), shape(8, LANES), shape(devices, 2, width),
    ]
    x1, x1_rows, x1_columns, gram, nstat, sums = call(
        narrow_kernel, (1,), [SCALARS] + [whole(array) for array in narrow_args[1:-1]] + [of_block(1, cin, width)],
        [whole(item) for item in narrow_outs], narrow_outs, [], narrow_args,
    )
    sums, gram = together(exchange(sums), gram)
    gram = share_out(gram, AXES)
    e_one, d_one, stat11, sums, planes_one = expand(1, sums, nstat, pl.BlockSpec((8, LANES), lambda j: (0, 0)), x1_rows)
    sums, gram = together(sums, gram)
    sums = exchange(sums)
    z_one, gates_one, running_one, pre_one, stat12, sums = squeeze_forward(1, sums, stat11, d_one)
    third, gram = together(exchange(sums), gram)
    gram = share_back(gram, AXES).reshape(-1, LANES)
    q_tiles = cin // 8 + -(-taps // 8)

    def backward_specs(block):
        rows = half_rows if block else full_rows
        ins = [fixed(8, width), fixed(rows, 8, width), fixed(4, width), fixed(4, width), of_block(block, squeeze, width),
               of_block(block, squeeze, width), of_block(block, cin, width), fixed(8, width), fixed(8, width),
               fixed(8, squeeze)]
        if not block:
            ins[0:4] = [both(rows_at(8)), both(cube_at(rows)), both(rows_at(4)), both(rows_at(4))]
            ins[6] = early(weight_at(block, cin))
        packed = round_up(tiles * (pack_tiles(cin, squeeze) + (0 if block else q_tiles)))
        wide_outs = [fixed(rows, 8, width), fixed(devices, 2, width)] if block else [late(cube_at(rows)), late(sums_at(2))]
        outs = [fixed(8, LANES)] + wide_outs + [fixed(packed, 8, LANES)]
        shapes = [shape(8, LANES), shape(rows, 8, width), shape(devices, 2, width), shape(packed, 8, LANES)]
        scratch = [pltpu.VMEM((rows * 8, 2 * LANES), low), pltpu.VMEM((2 * LANES, rows * 8), low),
                   pltpu.VMEM((rows * 8, 2 * LANES), low), pltpu.VMEM((tiles, rows, 8, LANES), F32),
                   pltpu.VMEM((tiles, frames, LANES), F32)]
        return (ins, outs, shapes, scratch)

    ins, outs, shapes, scratch = backward_specs(1)
    activations, nsum_one, dy2_one, sums, pack_one = call(
        squeeze_one_backward_kernel, (1,),
        [SCALARS, whole(third), whole(z_one), whole(cot), whole(ngains), whole(nbiases)] + ins,
        [fixed(cin, half_pixels)] + outs, [shape(cin, half_pixels)] + shapes, scratch,
        (frame_counts, third, z_one, cot, ngains, nbiases, stat12, d_one, wide_gains, wide_biases, squeeze_weight, up_t,
         project_weight, gates_one, running_one, pre_one),
    )
    sums, pack_one, gram = together(sums, pack_one, gram)
    sums, pack_one = together(exchange(sums), add_cores(pack_one))
    pack_one = share_out(pack_one)
    nothing = jnp.zeros((8, LANES), F32)

    def depth_backward(block, begin, end, sums, stat2, stat, dy2, depth, expanded, planes, columns, dx_in, sums_in, list_in):
        rows = half_rows if block else full_rows
        if block:
            taps_shape = (taps, 8, LANES)
            z_shape = (frames, 2, HALF_ROWS + 1, 8, LANES)
            f_shape = (full_rows, 8, LANES)
        else:
            taps_shape = (12 * LAGS, 8, LANES)
            z_shape = planes_shape(0, LANES, 4)
            f_shape = (frames, PAIRS, 4, 2, 8, LANES)
        count = end - begin
        final = end == tiles
        listed = round_up(end * q_tiles) if final and not block else end * q_tiles
        if final:
            send = (devices, 2, width + (LANES if block else 0))
            send_spec = fixed(*send)
        else:
            send = (8, count * LANES)
            send_spec = tile_rows(8)

        def wide_rows(rows):
            return pl.BlockSpec((rows, LANES), lambda j: (0, j + begin))

        def wide_cube(rows):
            return pl.BlockSpec((rows, 8, LANES), lambda j: (0, 0, j + begin))

        def wide_weight(rows):
            return pl.BlockSpec((1, rows, LANES), lambda j: (block, 0, j + begin))

        return call(
            functools.partial(depth_backward_kernel, block, begin, final), (count,),
            [SCALARS, pl.BlockSpec((devices, 2, LANES), lambda j: (0, 0, j + begin)), wide_rows(8), wide_rows(8), whole(nstat),
             wide_cube(rows), wide_cube(rows), wide_cube(full_rows), planes_of(block, 2, begin), whole(columns), wide_weight(cin), wide_rows(4),
             wide_rows(4), wide_weight(taps), whole(z_zero), whole(dx_in), whole(sums_in), whole(list_in)],
            [fixed(pixels, LANES), send_spec, fixed(listed, 8, LANES), tile_rows(8)],
            [shape(pixels, LANES), shape(*send), shape(listed, 8, LANES), shape(8, count * LANES)],
            [pltpu.VMEM(z_shape, F32), pltpu.VMEM(f_shape, F32), pltpu.VMEM(taps_shape, F32), pltpu.VMEM(taps_shape, F32),
             pltpu.VMEM((pixels, 2 * LANES), low)]
            + ([] if block else [pltpu.VMEM((frames, 4, 2, PAIRS, 8, LANES), F32)]),
            (frame_counts, sums, stat2, stat, nstat, dy2, depth, expanded, planes, columns, w_t, wide_gains, wide_biases,
             depth_weight, z_zero, dx_in, sums_in, list_in),
        )

    dxpre_one, sums, q_one, grad_one = depth_backward(
        1, 0, tiles, sums, stat12, stat11, dy2_one, d_one, e_one, planes_one, x1_columns, nothing, nothing, nothing
    )
    sums, pack_one = together(sums, pack_one)
    top_one, pack_one = together(exchange(sums), pack_one)
    pack_one = share_back(pack_one)
    ins, outs, shapes, scratch = backward_specs(0)
    dx1, nsum_zero, dy2_zero, sums, pack_zero = call(
        squeeze_zero_backward_kernel, (2, tiles),
        [SCALARS, whole(top_one), whole(stat11), whole(gram), whole(nstat), whole(dxpre_one), whole(x1), whole(z_zero),
         whole(ngains), of_block(1, cin, width), whole(wide_gains), whole(q_one)] + ins,
        [fixed(pixels, LANES)] + outs, [shape(pixels, LANES)] + shapes, scratch,
        (frame_counts, top_one, stat11, gram, nstat, dxpre_one, x1, z_zero, ngains, w_t, wide_gains, q_one, stat02, d_zero,
         wide_gains, wide_biases, squeeze_weight, up_t, project_weight, gates_zero, running_zero, pre_zero),
    )
    sums, pack_one = together(sums, pack_one)
    pack_one_other = swap_cores(pack_one)
    sums, pack_zero, pack_one_other = together(exchange(sums), add_cores(pack_zero), pack_one_other)
    pack_zero = share_out(pack_zero)
    first = tiles - tiles // 2
    dxpre_zero, sums_in, late, grad_a = depth_backward(
        0, 0, first, sums, stat02, stat01, dy2_zero, d_zero, e_zero, planes_zero, x_columns, nothing, nothing, nothing
    )
    dxpre_zero, pack_zero = together(dxpre_zero, pack_zero)
    pack_zero = share_back(pack_zero)
    dxpre_zero, sums, late, grad_b = depth_backward(
        0, first, tiles, sums, stat02, stat01, dy2_zero, d_zero, e_zero, planes_zero, x_columns, dxpre_zero, sums_in, late
    )
    grad_zero = jnp.concatenate([grad_a, grad_b], axis=1)
    sums, pack_zero = together(sums, pack_zero)
    pack_zero_other = swap_cores(pack_zero)
    top_zero, late, pack_zero_other = together(exchange(sums), add_cores(late), pack_zero_other)
    late = share_out(late)
    core = lax.axis_index("core").astype(jnp.int32).reshape(1)
    final_args = (
        frame_counts, momentum_index, gram, stat01, stat02, stat11, stat12, grad_zero, grad_one, top_one,
        top_zero, nsum_zero, nsum_one, dxpre_zero, x, dx1, w_t, wide_gains, wide_means, wide_variances, narrow_means,
        narrow_variances,
    )
    final_outs = [
        shape(cin, pixels), shape(2, cin, width), shape(16, width), shape(4, width), shape(4, width), shape(2, cin),
        shape(2, cin), shape(4, width), shape(4, width), shape(2, cin), shape(2, cin),
    ]
    video_grad, less, factor, wgain, wbias, ngain, nbias, newm, newv, newnm, newnv = simple_call(
        finish_kernel, 2, final_args, final_outs
    )
    less, late = together(less, late)
    late = share_back(late)
    late_other = swap_cores(late)
    dw_t, dtaps, ddown, dup, dproj, dupb, ddownb = simple_call(
        gradient_kernel, 1,
        (core, pack_zero, pack_zero_other, pack_one, pack_one_other, late, late_other, less, factor),
        [shape(2, cin, width), shape(2, taps, width), shape(2, squeeze, width), shape(2, squeeze, width),
         shape(2, cin, width), shape(2, width), shape(2, squeeze)],
    )
    return (
        activations, video_grad, jnp.swapaxes(dw_t, 1, 2), wgain, wbias, ngain, nbias, dtaps, ddown, ddownb,
        jnp.swapaxes(dup, 1, 2), dupb, dproj, newm, newv, newnm, newnv,
    )


def solution(mesh):
    sizes = (mesh.shape["dp"], mesh.shape["rep"] // 2, 2)
    split_mesh = jax.sharding.Mesh(mesh.devices.reshape(sizes), AXES)
    split = P(None, AXES)
    placed = (split, P(AXES)) + (P(),) * 16 + (split,)
    return jax.shard_map(
        local, mesh=split_mesh, in_specs=placed, out_specs=(split, split) + (P(),) * 15, check_vma=False
    )
```

```python
import functools

import jax
import jax.numpy as jnp
from jax import lax
from jax.experimental import pallas as pl
from jax.experimental.pallas import tpu as pltpu
from jax.sharding import PartitionSpec as P

SIDE = 16
LANES = 128
LAGS = 5
FULL_ROWS = 2 * SIDE
HALF_ROWS = SIDE // 2
EPSILON = 1e-05
HIGHEST = lax.Precision.HIGHEST
F32 = jnp.float32
NN = (((1,), (0,)), ((), ()))
NT = (((1,), (1,)), ((), ()))
TN = (((0,), (0,)), ((), ()))
VMEM_BYTES = 52 * 1024 * 1024


def half_tanh(half_values):
    return jnp.tanh(half_values)


def sigmoid(values):
    return 0.5 * jnp.tanh(0.5 * values) + 0.5


def silu_slope(half_values, tanh):
    return 0.5 * (1.0 + tanh + half_values * (1.0 - tanh * tanh))


def exact_dot(left, right, dims=NN):
    return lax.dot_general(left, right, dims, precision=HIGHEST, preferred_element_type=F32)


def halves(values):
    high = values.astype(jnp.bfloat16)
    return (high, (values - high.astype(F32)).astype(jnp.bfloat16))


def side_by_side(values):
    return jnp.concatenate(halves(values), axis=1)


def right_square(w):
    both = side_by_side(w)
    return jnp.concatenate([both, both], axis=0)


def right_square_t(w):
    high, low = halves(w)
    return jnp.concatenate(
        [jnp.concatenate([high, high], axis=1), jnp.concatenate([low, low], axis=1)], axis=0
    )


def plain_dot(left, right, dims=NN):
    return lax.dot_general(left, right, dims, preferred_element_type=F32)


def fold_right(values):
    lanes = values.shape[1] // 2
    return values[:, :lanes] + values[:, lanes:]


def fold_square(values):
    rows = values.shape[0] // 2
    return fold_right(values[:rows] + values[rows:])


def stacked(values):
    high = values.astype(jnp.bfloat16).astype(F32)
    return jnp.concatenate([high, values - high], axis=0).astype(jnp.bfloat16)


def skinny_dot(left, right, dims=NN):
    rows = left.shape[0]
    both = stacked(left)
    high, low = halves(right)
    values = plain_dot(both, high, dims) + plain_dot(both, low, dims)
    return values[:rows] + values[rows:]


def frame_outer(left, right):
    a_high = left.astype(jnp.bfloat16).astype(F32)
    b_high = right.astype(jnp.bfloat16).astype(F32)
    a_low = left - a_high
    b_low = right - b_high
    a = jnp.concatenate([a_high, a_high, a_low, a_low], axis=0).astype(jnp.bfloat16)
    b = jnp.concatenate([b_high, b_low, b_high, b_low], axis=0).astype(jnp.bfloat16)
    return plain_dot(a, b, TN)


def pad_rows(values):
    return jnp.concatenate([values, jnp.zeros((LANES - values.shape[0], values.shape[1]), values.dtype)], axis=0)


def column_order():
    q = lax.broadcasted_iota(jnp.int32, (LANES, LANES), 0)
    n = lax.broadcasted_iota(jnp.int32, (LANES, LANES), 1)
    source = (q // 16) * 16 + (q % 8) * 2 + (q // 8) % 2
    return (source == n).astype(jnp.bfloat16)


def live_frames(counts_ref):
    total = counts_ref[0]
    for clip in range(1, counts_ref.shape[0]):
        total = total + counts_ref[clip]
    return total


def place_of(counts_ref, frame):
    begin = jnp.int32(0)
    end = jnp.int32(0)
    for clip in range(counts_ref.shape[0]):
        end = end + counts_ref[clip]
        begin = jnp.where(frame >= end, end, begin)
    return frame - begin


def running_matrix(counts_ref, frames):
    after = lax.broadcasted_iota(jnp.int32, (frames, frames), 0)
    before = lax.broadcasted_iota(jnp.int32, (frames, frames), 1)
    begin = jnp.int32(0)
    matrix = jnp.zeros((frames, frames), F32)
    for clip in range(counts_ref.shape[0]):
        end = begin + counts_ref[clip]
        inside = (before >= begin) & (before <= after) & (after < end)
        matrix = matrix + jnp.where(inside, 1.0 / (after - begin + 1).astype(F32), 0.0)
        begin = end
    return matrix


def columns_up(values):
    spot = lax.broadcasted_iota(jnp.int32, values.shape, 1)
    return jnp.where(spot == 7, 0.0, pltpu.roll(values, 7, axis=1))


def columns_down(values):
    spot = lax.broadcasted_iota(jnp.int32, values.shape, 1)
    return jnp.where(spot == 0, 0.0, pltpu.roll(values, 1, axis=1))


def tile_sum(values):
    return jnp.sum(jnp.sum(values, axis=0), axis=0, keepdims=True)


def rows8(*rows):
    lanes = rows[0].shape[1]
    spot = lax.broadcasted_iota(jnp.int32, (8, lanes), 0)
    block = jnp.zeros((8, lanes), F32)
    for index, row in enumerate(rows):
        block = jnp.where(spot == index, row, block)
    return block


def pick_row(block, index):
    spot = lax.broadcasted_iota(jnp.int32, block.shape, 0)
    return jnp.sum(jnp.where(spot == index, block, 0.0), axis=0, keepdims=True)


def outer(left, right):
    return exact_dot(rows8(left), rows8(right), TN)


def row_dot(row, matrix, dims=NN):
    return exact_dot(rows8(row), matrix, dims)[0:1]


def clear_edges(ref):
    planes = ref.shape[1]
    edge = jnp.zeros((8, LANES), F32)
    for t in range(ref.shape[0]):
        for plane in range(planes):
            ref[t, plane, 0] = edge
            ref[t, plane, ref.shape[2] - 1] = edge


def spread_taps(taps_ref, w_ref):
    for tap in range(w_ref.shape[0]):
        w_ref[tap] = jnp.broadcast_to(taps_ref[0, tap : tap + 1, :], (8, LANES))


PAIRS = SIDE // 2


def row_pairs(plane):
    pair = plane.reshape(PAIRS, 2, 8, LANES)
    d1 = pair[:, 0]
    d2 = pair[:, 1]
    edge = jnp.zeros((1, 8, LANES), F32)
    d0 = jnp.concatenate([edge, d2[:-1]], axis=0)
    d3 = jnp.concatenate([d1[1:], edge], axis=0)
    return (d0 - d2, d1 + d2, d2 - d1, d1 - d3)


def pair_rows(parts):
    upper = parts[:, 0] + parts[:, 1] + parts[:, 2]
    lower = parts[:, 1] - parts[:, 2] - parts[:, 3]
    return jnp.stack([upper, lower], axis=1).reshape(FULL_ROWS, 8, LANES)


def spread_pairs(taps_ref, w_ref):
    for k in range(LAGS):
        for c in range(3):
            g0, g1, g2 = (taps_ref[0, k * 9 + 3 * r + c : k * 9 + 3 * r + c + 1, :] for r in range(3))
            outside = 0.5 * (g0 + g2)
            combined = (g0, outside + 0.5 * g1, outside - 0.5 * g1, g2)
            for place in range(4):
                w_ref[k * 12 + 3 * place + c] = jnp.broadcast_to(combined[place], (8, LANES))


def conv_full(t, k, a_ref, b_ref, w_ref, m_ref, fresh):
    weights = [w_ref[k * 12 + tap] for tap in range(12)]
    source = t - k
    for m in range(PAIRS):
        for place in range(4):
            left, centre, right = weights[3 * place : 3 * place + 3]
            a_even, a_odd = (a_ref[source, plane, place, m] for plane in range(2))
            a_odd_down, a_even_up = (b_ref[source, plane, place, m] for plane in range(2))
            even = centre * a_even + right * a_odd + left * a_odd_down
            odd = centre * a_odd + left * a_even + right * a_even_up
            if fresh:
                m_ref[m, place, 0] = even
                m_ref[m, place, 1] = odd
            else:
                m_ref[m, place, 0] = m_ref[m, place, 0] + even
                m_ref[m, place, 1] = m_ref[m, place, 1] + odd


def conv_half(t, k, a_ref, w_ref, d_ref, fresh):
    weights = [w_ref[k * 9 + tap] for tap in range(9)]
    source = t - k
    carried = [a_ref[source, plane, 0] for plane in range(3)]
    for i in range(HALF_ROWS):
        rows = [carried]
        for need in (2 * i + 1, 2 * i + 2):
            rows.append([a_ref[source, plane, need] for plane in range(3)])
        carried = rows[2]
        total = None
        for r in range(3):
            a_even, a_odd, a_odd_down = rows[r]
            left, centre, right = weights[3 * r : 3 * r + 3]
            part = centre * a_even + right * a_odd + left * a_odd_down
            total = part if total is None else total + part
        at = t * HALF_ROWS + i
        d_ref[at] = total if fresh else d_ref[at] + total


def row_total(ref, lanes=None):
    values = ref[...] if lanes is None or lanes == slice(None) else ref[:, :, lanes]
    return jnp.sum(values, axis=0)


def send_all(send_ref, rows, lanes):
    count = rows.shape[0]

    def one(device, carry):
        send_ref[pl.ds(device, 1), 0:count, lanes] = rows[None]
        return carry

    lax.fori_loop(0, send_ref.shape[0], one, 0)


def stack_rows(*rows):
    return rows8(*rows)[0 : len(rows)]


def pick_thirds(order, values, dims, order_left):
    pieces = []
    rest = values
    for _ in range(3):
        piece = rest.astype(jnp.bfloat16)
        rest = rest - piece.astype(F32)
        args = (order, piece) if order_left else (piece, order)
        pieces.append(plain_dot(*args, dims))
    return pieces


def gram_kernel(counts_ref, video_ref, w_ref, gram_ref, send_ref):
    total = live_frames(counts_ref)
    frames = video_ref.shape[1] // 256
    ones = jnp.ones((8, 256), jnp.bfloat16)

    def frame(t, carry):
        at = pl.ds(pl.multiple_of(t * 256, 256), 256)
        both = jnp.concatenate(halves(pad_rows(video_ref[:, at] * live_value(t, total))), axis=0)
        return (carry[0] + plain_dot(both, both, NT), carry[1] + plain_dot(ones, both, NT))

    init = (jnp.zeros((2 * LANES, 2 * LANES), F32), jnp.zeros((8, 2 * LANES), F32))
    gram, summed = each_frame(frames, frame, init)
    gram = fold_square(gram)
    summed = fold_right(summed)[0:1]
    gram_ref[0:LANES, :] = gram
    gram_ref[LANES : LANES + 8, :] = rows8(summed)
    w = pad_rows(w_ref[0])
    width = w.shape[1]
    sums = stack_rows(row_dot(summed, w), jnp.sum(w * exact_dot(gram, w), axis=0, keepdims=True))
    count = jnp.full((2, LANES), 1.0, F32) * (total * (SIDE * SIDE)).astype(F32)
    send_all(send_ref, sums, slice(0, width))
    send_all(send_ref, count, slice(width, width + LANES))


def prepare_kernel(counts_ref, video_ref, cot_ref, x_ref, rows_ref, columns_ref, cot_out_ref):
    order = column_order()
    total = live_frames(counts_ref)
    for part in range(video_ref.shape[1] // LANES):
        at = slice(part * LANES, (part + 1) * LANES)
        block = pad_rows(video_ref[:, at] * live_value(part // 2, total))
        high, middle, low = pick_thirds(order, block, NT, True)
        x_ref[at, :] = high + middle + low
        rows_ref[at, :] = jnp.concatenate([high, middle], axis=1).astype(jnp.bfloat16)
        columns_ref[:, at] = jnp.concatenate([high.T, middle.T], axis=0).astype(jnp.bfloat16)
    spot = lax.broadcasted_iota(jnp.int32, (LANES, LANES), 1)
    for part in range(cot_ref.shape[1] // LANES):
        at = slice(part * LANES, (part + 1) * LANES)
        frame = (spot + part * LANES) // (HALF_ROWS * 8)
        cot_out_ref[at, :] = jnp.where(frame < total, pad_rows(cot_ref[:, at]), 0.0).T


def moments_of(sums, count):
    average = sums[0:1] / count
    return (average, sums[1:2] / count - average * average)


def narrow_kernel(
    counts_ref, sums_ref, stat_ref, gram0_ref, x_ref, z_ref, ngain_ref, nbias_ref, w_ref,
    x1_ref, rows_ref, columns_ref, gram_ref, stat_out_ref, send_ref,
):
    total = live_frames(counts_ref)
    count = stat_ref[2:3, 0:LANES]
    average, variance = moments_of(row_total(sums_ref), count)
    factor = ngain_ref[0:1, :] * lax.rsqrt(variance + EPSILON)
    shift = nbias_ref[0:1, :] - factor * average
    stat_out_ref[...] = rows8(average, variance, count)
    frames = x_ref.shape[0] // 256

    def frame(t, carry):
        gram, cross, summed = carry
        at = pl.ds(pl.multiple_of(t * 256, 256), 256)
        z = z_ref[at, :]
        rows = (x_ref[at, :] + factor * z + shift) * live_value(t, total)
        x1_ref[at, :] = rows
        both = side_by_side(rows)
        rows_ref[at, :] = both
        columns = jnp.concatenate(halves(rows.T), axis=0)
        columns_ref[:, at] = columns
        gram = gram + plain_dot(columns, both)
        cross = cross + plain_dot(columns, side_by_side(z))
        return (gram, cross, summed + jnp.sum(rows, axis=0, keepdims=True))

    zero = jnp.zeros((2 * LANES, 2 * LANES), F32)
    gram, cross, summed = each_frame(frames, frame, (zero, zero, jnp.zeros((1, LANES), F32)))

    gram = fold_square(gram)
    tiles = LANES // 8
    gram_ref[0:tiles] = gram.reshape(tiles, 8, LANES)
    gram_ref[tiles : 2 * tiles] = fold_square(cross).reshape(tiles, 8, LANES)
    gram_ref[2 * tiles : 3 * tiles] = gram0_ref[0:LANES, :].reshape(tiles, 8, LANES)
    gram_ref[3 * tiles] = rows8(summed, gram0_ref[LANES : LANES + 1, :])
    w = pad_rows(w_ref[0])
    sums = stack_rows(row_dot(summed, w), jnp.sum(w * exact_dot(gram, w), axis=0, keepdims=True))
    send_all(send_ref, sums, slice(0, w.shape[1]))


def write_first(t, total, values, scale, shift, a_ref, b_ref):
    half_pre = values * scale + shift
    first = (half_pre + half_pre * half_tanh(half_pre)) * live_value(t, total)
    first = first.reshape(SIDE, 2, 8, LANES)
    even = first[:, 0]
    odd = first[:, 1]
    if b_ref is None:
        a_ref[t, 0, 1 : SIDE + 1] = even
        a_ref[t, 1, 1 : SIDE + 1] = odd
        a_ref[t, 2, 1 : SIDE + 1] = columns_down(odd)
        return
    for ref, plane, values in ((a_ref, 0, even), (a_ref, 1, odd), (b_ref, 0, columns_down(odd)), (b_ref, 1, columns_up(even))):
        for place, part in enumerate(row_pairs(values)):
            ref[t, plane, place] = part


def expand_kernel(
    block, counts_ref, sums_ref, count_ref, rows_ref, w_ref, gain_ref, bias_ref, taps_ref,
    e_ref, d_ref, stat_ref, send_ref, a_ref, taps8_ref, *pair_refs,
):
    b_ref, m_ref = pair_refs if pair_refs else (None, None)
    if block:
        clear_edges(a_ref)
    total = live_frames(counts_ref)
    frames = a_ref.shape[0]
    count = count_ref[2:3, :] if block else row_total(count_ref)[0:1]
    average, variance = moments_of(row_total(sums_ref), count)
    stat_ref[...] = rows8(average, variance, count)
    norm_row = 2 * block
    scale = gain_ref[norm_row : norm_row + 1, :] * lax.rsqrt(variance + EPSILON)
    shift = 0.5 * (bias_ref[norm_row : norm_row + 1, :] - average * scale)
    scale = 0.5 * scale
    square = right_square(pad_rows(w_ref[0]))

    def expand(t, carry):
        at = pl.ds(pl.multiple_of(t * 256, 256), 256)
        values = fold_right(plain_dot(rows_ref[at, :], square)).reshape(FULL_ROWS, 8, LANES)
        e_ref[pl.ds(pl.multiple_of(t * FULL_ROWS, FULL_ROWS), FULL_ROWS)] = values
        write_first(t, total, values, scale, shift, a_ref, b_ref)
        return carry

    each_frame(frames, expand, 0)
    per_frame = HALF_ROWS if block else FULL_ROWS
    if block:
        spread_taps(taps_ref, taps8_ref)
        conv = functools.partial(conv_half, a_ref=a_ref, w_ref=taps8_ref, d_ref=d_ref)
    else:
        spread_pairs(taps_ref, taps8_ref)
        conv = functools.partial(conv_full, a_ref=a_ref, b_ref=b_ref, w_ref=taps8_ref, m_ref=m_ref)

    def frame(t, carry):
        conv(t, 0, fresh=True)
        last = jnp.minimum(place_of(counts_ref, t), LAGS - 1)

        def lag(k, inner):
            conv(t, k, fresh=False)
            return inner

        lax.fori_loop(1, last + 1, lag, 0)
        if not block:
            d_ref[pl.ds(t * per_frame, per_frame)] = pair_rows(m_ref[...])
        values = d_ref[pl.ds(t * per_frame, per_frame)]
        return (carry[0] + jnp.sum(values, axis=0), carry[1] + jnp.sum(values * values, axis=0))

    zero = jnp.zeros((8, LANES), F32)
    summed, squares = lax.fori_loop(0, total, frame, (zero, zero))

    def dead(t, carry):
        d_ref[pl.ds(t * per_frame, per_frame)] = jnp.zeros((per_frame, 8, LANES), F32)
        return carry

    lax.fori_loop(total, frames, dead, 0)
    sums = stack_rows(jnp.sum(summed, axis=0, keepdims=True), jnp.sum(squares, axis=0, keepdims=True))
    send_all(send_ref, sums, slice(0, LANES))


def live_value(t, total):
    return jnp.where(t < total, 1.0, 0.0).astype(F32)


def each_frame(count, body, init):
    return lax.fori_loop(0, count, body, init, unroll=min(4, count))


def lanes_of(ref, tile):
    if ref.shape[-1] == LANES:
        return slice(None)
    return pl.ds(pl.multiple_of(tile * LANES, LANES), LANES)


def squeeze_forward_kernel(
    block, counts_ref, sums_ref, stat_ref, d_ref, gain_ref, bias_ref, down_ref, downb_ref, up_ref, upb_ref, proj_ref,
    cot_ref, z_ref, gates_ref, running_ref, pre_ref, stat_out_ref, send_ref, second_ref, pooled_ref,
):
    step = pl.program_id(0)
    steps = pl.num_programs(0)
    tiles = second_ref.shape[0]
    total = live_frames(counts_ref)
    per_frame = HALF_ROWS if block else FULL_ROWS
    pixels = per_frame * 8
    frames = second_ref.shape[1] // per_frame
    group = 256 // pixels
    chunks = frames // group
    norm_row = 2 * block + 1

    def activate(tile, carry):
        lanes = lanes_of(d_ref, tile)
        count = stat_ref[2:3, lanes] * (0.25 if block else 1.0)
        average, variance = moments_of(row_total(sums_ref, lanes), count)
        stat_out_ref[:, lanes] = rows8(average, variance, count)
        scale = gain_ref[norm_row : norm_row + 1, lanes] * lax.rsqrt(variance + EPSILON)
        shift = 0.5 * (bias_ref[norm_row : norm_row + 1, lanes] - average * scale)
        scale = 0.5 * scale

        def chunk(index, inside):
            for inner in range(group):
                t = index * group + inner
                at = pl.ds(t * per_frame, per_frame)
                half_pre = d_ref[at, :, lanes] * scale + shift
                second = half_pre + half_pre * half_tanh(half_pre)
                second = second * live_value(t, total)
                second_ref[tile, at] = second
                pooled_ref[tile, pl.ds(t, 1), :] = tile_sum(second) * (1.0 / pixels)
            return inside

        each_frame(chunks, chunk, 0)
        return carry

    if block:
        lax.fori_loop(0, tiles, activate, 0)
    else:
        activate(step, 0)

    def project(tile, carry):
        lanes = lanes_of(gates_ref, tile)
        square = right_square_t(pad_rows(proj_ref[0, :, lanes]))
        gates = gates_ref[:, lanes]

        def chunk(index, inside):
            parts = []
            for inner in range(group):
                t = index * group + inner
                second = second_ref[tile, pl.ds(t * per_frame, per_frame)].reshape(pixels, LANES)
                parts.append(second * pick_row(gates, t))
            excited = parts[0] if group == 1 else jnp.concatenate(parts, axis=0)
            at = pl.ds(pl.multiple_of(index * 256, 256), 256)
            z_ref[at, :] = z_ref[at, :] + fold_right(plain_dot(side_by_side(excited), square, NT))
            return inside

        each_frame(chunks, chunk, 0)
        return carry

    @pl.when(step == steps - 1)
    def gate_and_project():
        matrix = running_matrix(counts_ref, frames)
        pooled = jnp.concatenate([pooled_ref[index] for index in range(tiles)], axis=1)
        running = exact_dot(matrix, pooled)
        running_ref[...] = running
        pre = skinny_dot(running, down_ref[0], NT) + downb_ref[block : block + 1, :]
        pre_ref[...] = pre
        gates_ref[...] = sigmoid(skinny_dot(pre * sigmoid(pre), up_ref[0]) + upb_ref[block : block + 1, :])
        z_ref[...] = jnp.zeros_like(z_ref)
        lax.fori_loop(0, tiles, project, 0)

        def chunk(index, carry):
            at = pl.ds(pl.multiple_of(index * 256, 256), 256)
            z = z_ref[at, :].reshape(32, 8, LANES)
            values = [z, z * z]
            if block:
                dy = cot_ref[at, :].reshape(32, 8, LANES)
                values = values + [dy, dy * z]
            return tuple(old + jnp.sum(new, axis=0) for old, new in zip(carry, values))

        zero = jnp.zeros((8, LANES), F32)
        sums = each_frame(chunks, chunk, (zero,) * (4 if block else 2))
        rows = stack_rows(*(jnp.sum(value, axis=0, keepdims=True) for value in sums))
        send_all(send_ref, rows, slice(0, LANES))


def pack_tiles(narrow, squeeze):
    return narrow // 8 + 2 * (squeeze // 8) + 1


def squeeze_backward_body(
    block, counts_ref, stat_ref, d_ref, gain_ref, bias_ref, down_ref, up_ref, proj_ref, gates_ref, running_ref,
    pre_ref, dy2_ref, send_ref, pack_ref, dz3_ref, dz3t_ref, total_ref, dexc_ref, dgate_ref, head,
):
    total = live_frames(counts_ref)
    per_frame = HALF_ROWS if block else FULL_ROWS
    pixels = per_frame * 8
    frames = dz3_ref.shape[0] // pixels
    group = 256 // pixels
    chunks = frames // group
    norm_row = 2 * block + 1
    tiles = dexc_ref.shape[0]
    narrow = proj_ref.shape[1]
    squeeze = down_ref.shape[1]
    per_tile = pack_tiles(narrow, squeeze)

    def norm_of(tile):
        lanes = lanes_of(d_ref, tile)
        average = stat_ref[0:1, lanes]
        root = lax.rsqrt(stat_ref[1:2, lanes] + EPSILON)
        scale = gain_ref[norm_row : norm_row + 1, lanes] * root
        shift = 0.5 * (bias_ref[norm_row : norm_row + 1, lanes] - average * scale)
        return (lanes, average, root, 0.5 * scale, shift)

    def excite(tile, carry):
        lanes, _, _, scale, shift = norm_of(tile)
        gates = gates_ref[:, lanes_of(gates_ref, tile)]
        square = right_square(pad_rows(proj_ref[0, :, lanes]))

        def chunk(index, inside):
            flat = pl.ds(pl.multiple_of(index * 256, 256), 256)
            dexc = fold_right(plain_dot(dz3_ref[flat, :], square)).reshape(32, 8, LANES)
            dexc_ref[tile, pl.ds(pl.multiple_of(index * 32, 32), 32)] = dexc
            parts = []
            for inner in range(group):
                t = index * group + inner
                half_pre = d_ref[pl.ds(t * per_frame, per_frame), :, lanes] * scale + shift
                second = half_pre + half_pre * half_tanh(half_pre)
                second = second * live_value(t, total)
                own = dexc[inner * per_frame : (inner + 1) * per_frame]
                dgate_ref[tile, pl.ds(t, 1), :] = tile_sum(own * second)
                parts.append(second.reshape(pixels, LANES) * pick_row(gates, t))
            excited = parts[0] if group == 1 else jnp.concatenate(parts, axis=0)
            total_ref[...] = total_ref[...] + plain_dot(dz3t_ref[:, flat], side_by_side(excited))
            return inside

        total_ref[...] = jnp.zeros_like(total_ref)
        each_frame(chunks, chunk, 0)
        dproj = fold_square(total_ref[...])
        pack_ref[pl.ds(tile * per_tile, narrow // 8)] = dproj[0:narrow].reshape(narrow // 8, 8, LANES)
        return carry

    def squeeze_part():
        pre = pre_ref[...]
        half_pre = 0.5 * pre
        tanh = half_tanh(half_pre)
        squeezed = half_pre + half_pre * tanh
        all_gates = gates_ref[...]
        dgate = jnp.concatenate([dgate_ref[index] for index in range(tiles)], axis=1)
        du = dgate * all_gates * (1.0 - all_gates)
        dpre = skinny_dot(du, up_ref[0], NT) * silu_slope(half_pre, tanh)
        ddown = frame_outer(dpre, running_ref[...])
        dup = frame_outer(squeezed, du)
        dpre_row = jnp.sum(dpre, axis=0, keepdims=True)
        dpre_row = jnp.concatenate([dpre_row, jnp.zeros((1, du.shape[1] - squeeze), F32)], axis=1)
        biases = rows8(jnp.sum(du, axis=0, keepdims=True), dpre_row)
        for index in range(tiles):
            own = slice(index * LANES, (index + 1) * LANES)
            at = index * per_tile + narrow // 8
            pack_ref[at : at + squeeze // 8] = ddown[:, own].reshape(squeeze // 8, 8, LANES)
            at = at + squeeze // 8
            pack_ref[at : at + squeeze // 8] = dup[:, own].reshape(squeeze // 8, 8, LANES)
            pack_ref[at + squeeze // 8] = biases[:, own]
        drunning = skinny_dot(dpre, down_ref[0])
        dpooled = exact_dot(running_matrix(counts_ref, frames), drunning, TN) * (1.0 / pixels)
        for index in range(tiles):
            dgate_ref[index] = dpooled[:, index * LANES : (index + 1) * LANES]

    def slope(tile, carry):
        lanes, average, root, scale, shift = norm_of(tile)
        gates = gates_ref[:, lanes_of(gates_ref, tile)]

        def chunk(index, inside):
            summed, cross = inside
            for inner in range(group):
                t = index * group + inner
                at = pl.ds(t * per_frame, per_frame)
                depth = d_ref[at, :, lanes]
                half_pre = depth * scale + shift
                dsecond = dexc_ref[tile, at] * pick_row(gates, t) + pick_row(dgate_ref[tile], t)
                dy = dsecond * silu_slope(half_pre, half_tanh(half_pre))
                dy = dy * live_value(t, total)
                dy2_ref[at, :, lanes] = dy
                summed = summed + jnp.sum(dy, axis=0)
                cross = cross + jnp.sum(dy * (depth - average), axis=0)
            return (summed, cross)

        zero = jnp.zeros((8, LANES), F32)
        summed, cross = each_frame(chunks, chunk, (zero, zero))
        rows = stack_rows(jnp.sum(summed, axis=0, keepdims=True), root * jnp.sum(cross, axis=0, keepdims=True))
        send_all(send_ref, rows, lanes)
        return carry

    if block:
        head()
        lax.fori_loop(0, tiles, excite, 0)
        squeeze_part()
        lax.fori_loop(0, tiles, slope, 0)
    else:
        phase = pl.program_id(0)
        tile = pl.program_id(1)

        @pl.when((phase == 0) & (tile == 0))
        def start():
            head()

        @pl.when(phase == 0)
        def first():
            excite(tile, 0)

        @pl.when((phase == 1) & (tile == 0))
        def between():
            squeeze_part()

        @pl.when(phase == 1)
        def second():
            slope(tile, 0)


def squeeze_one_backward_kernel(
    counts_ref, third_ref, z_ref, cot_ref, ngain_ref, nbias_ref, stat_ref, d_ref, gain_ref, bias_ref, down_ref,
    up_ref, proj_ref, gates_ref, running_ref, pre_ref, act_ref, nsum_ref, dy2_ref, send_ref, pack_ref,
    dz3_ref, dz3t_ref, total_ref, dexc_ref, dgate_ref,
):
    total = live_frames(counts_ref)
    pixels = HALF_ROWS * 8

    def head():
        count = stat_ref[2:3, 0:LANES]
        sums = row_total(third_ref)
        mean, variance = moments_of(sums, count)
        root = lax.rsqrt(variance + EPSILON)
        gain = ngain_ref[1:2, :]
        bias_sum = sums[2:3, :]
        gain_sum = root * (sums[3:4, :] - mean * bias_sum)
        nsum_ref[...] = rows8(gain_sum, bias_sum, mean, variance)
        row = lax.broadcasted_iota(jnp.int32, z_ref.shape, 0) // pixels
        live = row < total
        normed = (z_ref[...] - mean) * root
        act = jnp.where(live, gain * normed + nbias_ref[1:2, :], 0.0)
        act_ref[...] = act.T[0 : act_ref.shape[0]]
        dz3 = gain * root * (cot_ref[...] - bias_sum / count - normed * (gain_sum / count))
        dz3 = jnp.where(live, dz3, 0.0)
        dz3_ref[...] = side_by_side(dz3)
        dz3t_ref[...] = jnp.concatenate(halves(dz3.T), axis=0)

    squeeze_backward_body(
        1, counts_ref, stat_ref, d_ref, gain_ref, bias_ref, down_ref, up_ref, proj_ref, gates_ref, running_ref,
        pre_ref, dy2_ref, send_ref, pack_ref, dz3_ref, dz3t_ref, total_ref, dexc_ref, dgate_ref, head,
    )


def input_factors(sums, stat_ref, count, gain, w):
    root = lax.rsqrt(stat_ref[1:2, :] + EPSILON)
    factor = gain * root
    matrix = exact_dot(w * (factor * root * sums[1:2] / count), w, NT)
    return (matrix, row_dot(factor * sums[0:1] / count, w, NT))


def covariance(gram, summed, count):
    mean = summed / count
    return (mean, gram / count - outer(mean, mean))


def squeeze_zero_backward_kernel(
    counts_ref, top_ref, stat1_ref, gram_ref, nstat_ref, dxpre_ref, x1_ref, z_ref, ngain_ref, w_ref, gains_ref, q_one_ref,
    stat_ref, d_ref, gain_ref, bias_ref, down_ref, up_ref, proj_ref, gates_ref, running_ref, pre_ref,
    dx1_ref, nsum_ref, dy2_ref, send_ref, pack_ref, dz3_ref, dz3t_ref, total_ref, dexc_ref, dgate_ref,
):
    total = live_frames(counts_ref)
    width = gains_ref.shape[1]

    def head():
        start = pack_tiles(proj_ref.shape[1], down_ref.shape[1]) * (width // LANES)
        pack_ref[start : start + q_one_ref.shape[0]] = q_one_ref[...]
        count = stat_ref[2:3, :]
        wide_count = jnp.broadcast_to(count[:, 0:1], (1, width))
        sums = row_total(top_ref, slice(0, width))
        extra = row_total(top_ref, slice(width, width + LANES))
        matrix, shift = input_factors(sums, stat1_ref, wide_count, gains_ref[2:3, :], pad_rows(w_ref[0]))
        mean = nstat_ref[0:1, :]
        root = lax.rsqrt(nstat_ref[1:2, :] + EPSILON)
        mean_x1 = gram_ref[3 * LANES : 3 * LANES + 1, :] / count
        cross = (gram_ref[LANES : 2 * LANES, :] - count * outer(mean_x1, mean)) * root
        gain_sum = extra[0:1] - jnp.sum(matrix * cross, axis=0, keepdims=True)
        bias_sum = extra[1:2] - count * shift
        nsum_ref[...] = rows8(gain_sum, bias_sum, mean, nstat_ref[1:2, :])
        factor = ngain_ref[0:1, :] * root
        square = right_square(matrix)
        bias_mean = bias_sum / count
        gain_mean = gain_sum / count

        def frame(t, carry):
            at = pl.ds(pl.multiple_of(t * 256, 256), 256)
            centred = side_by_side(x1_ref[at, :] - mean_x1)
            live = live_value(t, total)
            dx1 = (dxpre_ref[at, :] - fold_right(plain_dot(centred, square)) - shift) * live
            dx1_ref[at, :] = dx1
            normed = (z_ref[at, :] - mean) * root
            dz3 = factor * (dx1 - bias_mean - normed * gain_mean) * live
            dz3_ref[at, :] = side_by_side(dz3)
            dz3t_ref[:, at] = jnp.concatenate(halves(dz3.T), axis=0)
            return carry

        each_frame(dz3_ref.shape[0] // 256, frame, 0)

    squeeze_backward_body(
        0, counts_ref, stat_ref, d_ref, gain_ref, bias_ref, down_ref, up_ref, proj_ref, gates_ref, running_ref,
        pre_ref, dy2_ref, send_ref, pack_ref, dz3_ref, dz3t_ref, total_ref, dexc_ref, dgate_ref, head,
    )

def back_full(t, k, a_ref, w_ref, z_ref, raw_ref, f_ref, dw_ref, fresh):
    weights = [w_ref[k * 12 + tap] for tap in range(12)]
    target = t - k
    sums = [None] * 12
    for m in range(PAIRS):
        for place in range(4):
            flipped = (3, 1, 2, 0)[place]
            left, centre, right = weights[3 * flipped : 3 * flipped + 3]
            b_even, b_odd, b_odd_down, b_even_up = (z_ref[t, plane, place, m] for plane in range(4))
            even = centre * b_even + right * b_odd_down + left * b_odd
            odd = centre * b_odd + right * b_even + left * b_even_up
            if fresh:
                f_ref[target, m, place, 0] = even
                f_ref[target, m, place, 1] = odd
            else:
                f_ref[target, m, place, 0] = f_ref[target, m, place, 0] + even
                f_ref[target, m, place, 1] = f_ref[target, m, place, 1] + odd
            if place in (0, 3):
                row = 0 if place == 0 else 1
                b_even, b_odd, b_odd_down, b_even_up = (raw_ref[t, plane, row, m] for plane in range(4))
            a_even, a_odd = (a_ref[target, plane, place, m] for plane in range(2))
            pieces = (
                b_even_up * a_odd + b_odd * a_even,
                b_even * a_even + b_odd * a_odd,
                b_even * a_odd + b_odd_down * a_even,
            )
            for c in range(3):
                at = 3 * place + c
                sums[at] = pieces[c] if sums[at] is None else sums[at] + pieces[c]
    for place in range(4):
        for c in range(3):
            at = place * 3 * LAGS + k * 3 + c
            dw_ref[at] = dw_ref[at] + sums[3 * place + c]


def pair_taps(totals):
    count = 3 * LAGS
    first, second, third, last = (totals[place * count : (place + 1) * count] for place in range(4))
    middle = 0.5 * (second - third)
    return (first + middle, 0.5 * (second + third), middle - last)


def back_half(t, k, a_ref, w_ref, z_ref, f_ref, dw_ref, fresh):
    weights = [w_ref[k * 9 + tap] for tap in range(9)]
    target = t - k
    sums = [None] * 9

    def put(row, parity, value):
        at = target * FULL_ROWS + 2 * row + parity
        f_ref[at] = value if fresh else f_ref[at] + value

    carried = [a_ref[target, plane, 0] for plane in range(2)]
    here = [z_ref[t, plane, 0] for plane in range(2)]
    for i in range(HALF_ROWS):
        below = [z_ref[t, plane, i + 1] for plane in range(2)]
        dz, dz_up = here
        rows = [carried]
        for need in (2 * i + 1, 2 * i + 2):
            rows.append([a_ref[target, plane, need] for plane in range(2)])
        carried = rows[2]
        put(2 * i, 0, weights[4] * dz)
        put(2 * i, 1, weights[5] * dz + weights[3] * dz_up)
        put(2 * i + 1, 0, weights[7] * dz + weights[1] * below[0])
        put(
            2 * i + 1,
            1,
            weights[8] * dz + weights[6] * dz_up + (weights[2] * below[0] + weights[0] * below[1]),
        )
        for r in range(3):
            a_even, a_odd = rows[r]
            pieces = (dz_up * a_odd, dz * a_even, dz * a_odd)
            for c in range(3):
                at = 3 * r + c
                sums[at] = pieces[c] if sums[at] is None else sums[at] + pieces[c]
        here = below
    for tap in range(9):
        dw_ref[k * 9 + tap] = dw_ref[k * 9 + tap] + sums[tap]


def depth_backward_kernel(
    block, before, final, counts_ref, grads_ref, stat2_ref, stat_ref, nstat_ref, dy2_ref, d_ref, e_ref, a_ref, columns_ref, w_ref,
    gain_ref, bias_ref, taps_ref, z3_ref, dx_in_ref, sums_in_ref, list_in_ref, dxpre_ref, send_ref, q_ref, grad_rows_ref,
    z_ref, f_ref, taps8_ref, dw_ref, total_ref, *raw_refs,
):
    tile = pl.program_id(0)
    tiles = pl.num_programs(0)
    total = live_frames(counts_ref)
    frames = a_ref.shape[0]
    norm_row = 2 * block
    half = block == 1
    per_frame = HALF_ROWS if half else FULL_ROWS
    taps = taps_ref.shape[1]

    @pl.when(tile == 0)
    def start():
        if half:
            clear_edges(z_ref)
        if before:
            dxpre_ref[...] = dx_in_ref[...]
            send_all(send_ref, sums_in_ref[0:2, :], slice(0, before * LANES))
            q_ref[0 : list_in_ref.shape[0]] = list_in_ref[...]
        else:
            dxpre_ref[...] = jnp.zeros_like(dxpre_ref)

        def dead(t, carry):
            if half:
                f_ref[pl.ds(t * FULL_ROWS, FULL_ROWS)] = jnp.zeros((FULL_ROWS, 8, LANES), F32)
            else:
                f_ref[t] = jnp.zeros(f_ref.shape[1:], F32)
            return carry

        lax.fori_loop(total, frames, dead, 0)

    count = stat2_ref[2:3, :]
    grads = row_total(grads_ref)
    grad_rows_ref[...] = rows8(grads[0:1], grads[1:2])
    average = stat2_ref[0:1, :]
    root = lax.rsqrt(stat2_ref[1:2, :] + EPSILON)
    scale_two = gain_ref[norm_row + 1 : norm_row + 2, :] * root
    slope = scale_two * root * grads[1:2] / count
    level = scale_two * grads[0:1] / count - slope * average
    average_one = stat_ref[0:1, :]
    root_one = lax.rsqrt(stat_ref[1:2, :] + EPSILON)
    scale_one = gain_ref[norm_row : norm_row + 1, :] * root_one
    shift_half = 0.5 * (bias_ref[norm_row : norm_row + 1, :] - average_one * scale_one)
    scale_half = 0.5 * scale_one

    def fill(t, carry):
        at = pl.ds(t * per_frame, per_frame)
        dz = scale_two * dy2_ref[at] - (slope * d_ref[at] + level)
        if half:
            z_ref[t, 0, 0:HALF_ROWS] = dz
            z_ref[t, 1, 0:HALF_ROWS] = columns_up(dz)
        else:
            pair = dz.reshape(SIDE, 2, 8, LANES)
            even = pair[:, 0]
            odd = pair[:, 1]
            for plane, values in enumerate((even, odd, columns_down(odd), columns_up(even))):
                for place, part in enumerate(row_pairs(values)):
                    z_ref[t, plane, place] = part
                rows = values.reshape(PAIRS, 2, 8, LANES)
                raw_refs[0][t, plane, 0] = rows[:, 0]
                raw_refs[0][t, plane, 1] = rows[:, 1]
        return carry

    each_frame(frames, fill, 0)
    dw_ref[...] = jnp.zeros_like(dw_ref)
    refs = dict(a_ref=a_ref, w_ref=taps8_ref, z_ref=z_ref, f_ref=f_ref, dw_ref=dw_ref)
    if half:
        spread_taps(taps_ref, taps8_ref)
        back = functools.partial(back_half, **refs)
    else:
        spread_pairs(taps_ref, taps8_ref)
        back = functools.partial(back_full, raw_ref=raw_refs[0], **refs)

    def frame(t, carry):
        back(t, 0, fresh=True)
        last = jnp.minimum(place_of(counts_ref, t), LAGS - 1)

        def lag(k, inner):
            back(t, k, fresh=False)
            return inner

        return lax.fori_loop(1, last + 1, lag, carry)

    lax.fori_loop(0, total, frame, 0)
    square = right_square_t(pad_rows(w_ref[0]) * scale_one)
    total_ref[...] = jnp.zeros_like(total_ref)

    def finish(t, carry):
        rows = pl.ds(pl.multiple_of(t * FULL_ROWS, FULL_ROWS), FULL_ROWS)
        flat = pl.ds(pl.multiple_of(t * 256, 256), 256)
        values = e_ref[rows]
        half_pre = values * scale_half + shift_half
        dfirst = f_ref[rows] if half else pair_rows(f_ref[t])
        dy = dfirst * silu_slope(half_pre, half_tanh(half_pre))
        summed = carry[0] + jnp.sum(dy, axis=0)
        cross = carry[1] + jnp.sum(dy * (values - average_one), axis=0)
        dy = dy.reshape(256, LANES)
        both = side_by_side(dy)
        total_ref[...] = total_ref[...] + plain_dot(columns_ref[:, flat], both)
        dxpre_ref[flat, :] = dxpre_ref[flat, :] + fold_right(plain_dot(both, square, NT))
        return (summed, cross)

    zero = jnp.zeros((8, LANES), F32)
    summed, cross = each_frame(frames, finish, (zero, zero))
    rows = stack_rows(jnp.sum(summed, axis=0, keepdims=True), root_one * jnp.sum(cross, axis=0, keepdims=True))
    if final:
        send_all(send_ref, rows, pl.ds(pl.multiple_of((tile + before) * LANES, LANES), LANES))
    else:
        send_ref[...] = rows8(rows[0:1], rows[1:2])
    gathered = fold_square(total_ref[...])
    narrow = w_ref.shape[1]
    dtaps = jnp.sum(dw_ref[...], axis=1)
    parts = (dtaps,) if half else pair_taps(dtaps)
    unused = jnp.zeros(((-taps) % 8, LANES), F32)
    values = jnp.concatenate((gathered[0:narrow],) + parts + (unused,), axis=0)
    listed = values.shape[0] // 8
    q_ref[pl.ds((tile + before) * listed, listed)] = values.reshape(listed, 8, LANES)

    if half:
        @pl.when(tile == tiles - 1)
        def tail():
            mean = nstat_ref[0:1, :]
            root_three = lax.rsqrt(nstat_ref[1:2, :] + EPSILON)

            def part(t, carry):
                flat = pl.ds(pl.multiple_of(t * 256, 256), 256)
                dx = dxpre_ref[flat, :].reshape(32, 8, LANES)
                normed = ((z3_ref[flat, :] - mean) * root_three).reshape(32, 8, LANES)
                return (carry[0] + jnp.sum(dx * normed, axis=0), carry[1] + jnp.sum(dx, axis=0))

            cross_three, summed_three = each_frame(frames, part, (zero, zero))
            rows = stack_rows(
                jnp.sum(cross_three, axis=0, keepdims=True), jnp.sum(summed_three, axis=0, keepdims=True)
            )
            width = send_ref.shape[2] - LANES
            send_all(send_ref, rows, slice(width, width + LANES))


def finish_kernel(
    counts_ref, momentum_ref, gram_ref, stat01_ref, stat02_ref, stat11_ref, stat12_ref, grad0_ref,
    grad1_ref, one_ref, zero_ref, nsum0_ref, nsum1_ref, dxpre_ref, x_ref, dx1_ref, w_ref, gain_ref, means_ref, vars_ref,
    nmeans_ref, nvars_ref,
    video_ref, less_ref, factor_ref, wgain_ref, wbias_ref, ngain_ref, nbias_ref, newm_ref, newv_ref, newnm_ref, newnv_ref,
):
    total = live_frames(counts_ref)
    full = stat01_ref[2:3, :]
    count = full[:, 0:LANES]
    width = full.shape[1]
    top_zero = row_total(zero_ref)
    top_one = row_total(one_ref, slice(0, width))
    w_zero = pad_rows(w_ref[0])
    matrix, shift = input_factors(top_zero, stat01_ref, full, gain_ref[0:1, :], w_zero)
    square = right_square(matrix)
    mean_x, cov_zero = covariance(
        gram_ref[2 * LANES : 3 * LANES, :], gram_ref[3 * LANES + 1 : 3 * LANES + 2, :], count
    )
    order = column_order()
    narrow = video_ref.shape[0]

    def frame(t, carry):
        at = pl.ds(pl.multiple_of(t * 256, 256), 256)
        centred = side_by_side(x_ref[at, :] - mean_x)
        dx = (dxpre_ref[at, :] - fold_right(plain_dot(centred, square)) - shift) * live_value(t, total) + dx1_ref[at, :]
        for part in range(2):
            own = dx[part * LANES : (part + 1) * LANES].T[0:narrow]
            pieces = pick_thirds(order, own, NN, False)
            start = pl.multiple_of(t * 256 + part * LANES, LANES)
            video_ref[:, pl.ds(start, LANES)] = pieces[0] + pieces[1] + pieces[2]
        return carry

    each_frame(x_ref.shape[0] // 256, frame, 0)
    mean_one, cov_one = covariance(gram_ref[0:LANES, :], gram_ref[3 * LANES : 3 * LANES + 1, :], count)
    plan = ((mean_x, cov_zero, stat01_ref, top_zero, w_zero), (mean_one, cov_one, stat11_ref, top_one, pad_rows(w_ref[1])))
    for block, (mean_row, cov, stat_ref, top, w) in enumerate(plan):
        root = lax.rsqrt(stat_ref[1:2, :] + EPSILON)
        factor = gain_ref[2 * block : 2 * block + 1, :] * root
        less = outer(mean_row, top[0:1]) + exact_dot(cov, w) * (root * top[1:2])
        less_ref[block] = (less * factor)[0:narrow]
        factor_ref[8 * block : 8 * block + 8, :] = rows8(factor)
    momentum = momentum_ref[0].astype(F32) / 10.0
    wgain_ref[...] = stack_rows(top_zero[1:2], grad0_ref[1:2, :], top_one[1:2], grad1_ref[1:2, :])
    wbias_ref[...] = stack_rows(top_zero[0:1], grad0_ref[0:1, :], top_one[0:1], grad1_ref[0:1, :])
    stats = (stat01_ref, stat02_ref, stat11_ref, stat12_ref)
    means = stack_rows(*(ref[0:1, :] for ref in stats))
    variances = stack_rows(*(ref[1:2, :] * (ref[2:3, :] / (ref[2:3, :] - 1.0)) for ref in stats))
    newm_ref[...] = (1.0 - momentum) * means_ref[...] + momentum * means
    newv_ref[...] = (1.0 - momentum) * vars_ref[...] + momentum * variances
    ngain_ref[...] = stack_rows(nsum0_ref[0:1, :], nsum1_ref[0:1, :])[:, 0:narrow]
    nbias_ref[...] = stack_rows(nsum0_ref[1:2, :], nsum1_ref[1:2, :])[:, 0:narrow]
    means = stack_rows(nsum0_ref[2:3, :], nsum1_ref[2:3, :])[:, 0:narrow]
    quarter = 0.25 * count
    variances = stack_rows(
        nsum0_ref[3:4, :] * (count / (count - 1.0)), nsum1_ref[3:4, :] * (quarter / (quarter - 1.0))
    )[:, 0:narrow]
    newnm_ref[...] = (1.0 - momentum) * nmeans_ref[...] + momentum * means
    newnv_ref[...] = (1.0 - momentum) * nvars_ref[...] + momentum * variances


def list_rows(core_ref, pair, at, count):
    first_core = core_ref[0] == 0
    mine, other = pair
    half = mine.shape[0]
    pieces = []
    if at < half:
        size = min(count, half - at)
        here = slice(at, at + size)
        pieces.append(jnp.where(first_core, mine[here], other[here]))
        count = count - size
        at = at + size
    if count:
        here = slice(at - half, at - half + count)
        pieces.append(jnp.where(first_core, other[here], mine[here]))
    values = pieces[0] if len(pieces) == 1 else jnp.concatenate(pieces, axis=0)
    return values.reshape(-1, LANES)


def lists_kernel(
    core_ref, pack0_ref, pack0_other_ref, pack1_ref, pack1_other_ref, less_ref, factor_ref,
    dw_ref, dtaps_ref, ddown_ref, dup_ref, dproj_ref, dupb_ref, ddownb_ref,
):
    narrow = dw_ref.shape[1]
    taps = dtaps_ref.shape[1]
    squeeze = ddown_ref.shape[1]
    tiles = dw_ref.shape[2] // LANES
    per_pack = pack_tiles(narrow, squeeze)
    per_tile = narrow // 8 + -(-taps // 8)
    packs = ((pack0_ref, pack0_other_ref), (pack1_ref, pack1_other_ref))
    for block in range(2):
        down_rows = []
        for tile in range(tiles):
            lanes = slice(tile * LANES, (tile + 1) * LANES)
            at = tile * per_pack
            dproj_ref[block, :, lanes] = list_rows(core_ref, packs[block], at, narrow // 8)
            at = at + narrow // 8
            ddown_ref[block, :, lanes] = list_rows(core_ref, packs[block], at, squeeze // 8)
            at = at + squeeze // 8
            dup_ref[block, :, lanes] = list_rows(core_ref, packs[block], at, squeeze // 8)
            biases = list_rows(core_ref, packs[block], at + squeeze // 8, 1)
            dupb_ref[block : block + 1, lanes] = biases[0:1]
            down_rows.append(biases[1:2])
        ddownb_ref[block : block + 1, :] = jnp.concatenate(down_rows, axis=1)[:, 0:squeeze]
    for tile in range(tiles):
        lanes = slice(tile * LANES, (tile + 1) * LANES)
        values = list_rows(core_ref, packs[0], per_pack * tiles + tile * per_tile, per_tile)
        dw_ref[0, :, lanes] = values[0:narrow] * factor_ref[8:9, lanes] - less_ref[0, :, lanes]
        dtaps_ref[0, :, lanes] = values[narrow : narrow + taps]


def last_kernel(core_ref, late_ref, late_other_ref, less_ref, factor_ref, _, __, dw_ref, dtaps_ref):
    narrow = dw_ref.shape[1]
    taps = dtaps_ref.shape[1]
    per_tile = narrow // 8 + -(-taps // 8)
    for tile in range(dw_ref.shape[2] // LANES):
        lanes = slice(tile * LANES, (tile + 1) * LANES)
        values = list_rows(core_ref, (late_ref, late_other_ref), tile * per_tile, per_tile)
        dw_ref[0, :, lanes] = values[0:narrow] * factor_ref[0:1, lanes] - less_ref[0, :, lanes]
        for r in range(3):
            for k in range(LAGS):
                source = narrow + r * 3 * LAGS + 3 * k
                dtaps_ref[0, k * 9 + 3 * r : k * 9 + 3 * r + 3, lanes] = values[source : source + 3]


AXES = ("dp", "z", "core")
CHIPS = ("dp", "z")


def exchange(send):
    return lax.all_to_all(send, AXES, 0, 0, tiled=True)


def together(*values):
    return lax.optimization_barrier(values)


def swap_cores(values):
    return lax.ppermute(values, "core", [(0, 1), (1, 0)])


def add_cores(tiles):
    core = lax.axis_index("core")
    pair = tiles.reshape(2, tiles.shape[0] // 2, *tiles.shape[1:])
    mine = lax.dynamic_index_in_dim(pair, core, 0, keepdims=False)
    return mine + swap_cores(lax.dynamic_index_in_dim(pair, 1 - core, 0, keepdims=False))


def share_out(tiles, names=CHIPS):
    count = 1
    for name in names:
        count = count * lax.axis_size(name)
    return lax.all_to_all(tiles.reshape(count, -1, *tiles.shape[1:]), names, 0, 0, tiled=True)


def share_back(pieces, names=CHIPS):
    own = jnp.sum(pieces, axis=0)
    everyone = lax.all_to_all(jnp.broadcast_to(own[None], pieces.shape), names, 0, 0, tiled=True)
    return everyone.reshape(-1, *pieces.shape[2:])


def shape(*dims, kind=F32):
    return jax.ShapeDtypeStruct(dims, kind)


def whole(array):
    rank = len(array.shape)
    return pl.BlockSpec(array.shape, lambda *ids: (0,) * rank)


SCALARS = pl.BlockSpec(memory_space=pltpu.SMEM)


def call(kernel, grid, in_specs, out_specs, out_shape, scratch, args, vmem=VMEM_BYTES, aliases=None):
    return pl.pallas_call(
        kernel,
        grid=grid,
        in_specs=in_specs,
        out_specs=out_specs,
        out_shape=out_shape,
        scratch_shapes=scratch,
        compiler_params=pltpu.CompilerParams(vmem_limit_bytes=vmem),
        input_output_aliases=aliases or {},
        cost_estimate=pl.CostEstimate(
            flops=1_000_000_000, bytes_accessed=1_000_000, transcendentals=0
        ),
    )(*args)


def simple_call(kernel, scalars, args, outs):
    return call(
        kernel, (1,), [SCALARS] * scalars + [whole(array) for array in args[scalars:]], [whole(item) for item in outs],
        outs, [], args,
    )


def local(
    video, frame_counts, momentum_index, expand_weight, wide_gains, wide_biases, narrow_gains, narrow_biases, depth_weight,
    squeeze_weight, squeeze_bias, excite_weight, excite_bias, project_weight, wide_means, wide_variances, narrow_means,
    narrow_variances, cotangent,
):
    devices = lax.axis_size("dp") * lax.axis_size("z") * lax.axis_size("core")
    cin, pixels = video.shape
    half_pixels = cotangent.shape[1]
    width = expand_weight.shape[1]
    squeeze = squeeze_weight.shape[1]
    frames = pixels // (SIDE * SIDE)
    tiles = width // LANES
    taps = depth_weight.shape[1]
    w_t = jnp.swapaxes(expand_weight, 1, 2)
    up_t = jnp.swapaxes(excite_weight, 1, 2)
    lanes_pad = ((0, 0), (0, LANES - cin))
    ngains = jnp.pad(narrow_gains, lanes_pad)
    nbiases = jnp.pad(narrow_biases, lanes_pad)
    full_rows = frames * FULL_ROWS
    half_rows = frames * HALF_ROWS
    low = jnp.bfloat16

    def round_up(count):
        return -(-count // devices) * devices

    def fixed(*dims):
        return pl.BlockSpec(dims, lambda *ids: (0,) * len(dims))

    def tile_rows(rows):
        return pl.BlockSpec((rows, LANES), lambda j: (0, j))

    def tile_cube(rows):
        return pl.BlockSpec((rows, 8, LANES), lambda j: (0, 0, j))

    def tile_sums(rows=2):
        return pl.BlockSpec((devices, rows, LANES), lambda j: (0, 0, j))

    def weight_tile(block, rows):
        return pl.BlockSpec((1, rows, LANES), lambda j, block=block: (block, 0, j))

    def of_block(block, rows, lanes):
        return pl.BlockSpec((1, rows, lanes), lambda *ids: (block, 0, 0))

    def early(make):
        return make(lambda p, j: j * (1 - p) + (tiles - 1) * p)

    def late(make):
        return make(lambda p, j: j * p)

    def both(make):
        return make(lambda p, j: j)

    def rows_at(rows):
        return lambda at: pl.BlockSpec((rows, LANES), lambda p, j: (0, at(p, j)))

    def cube_at(rows):
        return lambda at: pl.BlockSpec((rows, 8, LANES), lambda p, j: (0, 0, at(p, j)))

    def sums_at(rows):
        return lambda at: pl.BlockSpec((devices, rows, LANES), lambda p, j: (0, 0, at(p, j)))

    def weight_at(block, rows):
        return lambda at: pl.BlockSpec((1, rows, LANES), lambda p, j: (block, 0, at(p, j)))

    gram_zero, sums = call(
        gram_kernel, (1,), [SCALARS, whole(video), of_block(0, cin, width)],
        [fixed(LANES + 8, LANES), fixed(devices, 2, width + LANES)],
        [shape(LANES + 8, LANES), shape(devices, 2, width + LANES)],
        [], (frame_counts, video, w_t), vmem=60 * 1024 * 1024,
    )
    x, x_rows, x_columns, cot = simple_call(
        prepare_kernel, 1, (frame_counts, video, cotangent),
        [shape(pixels, LANES), shape(pixels, 2 * LANES, kind=low), shape(2 * LANES, pixels, kind=low),
         shape(half_pixels, LANES)],
    )
    sums = exchange(sums)

    def planes_shape(block, lanes, planes):
        if block:
            return (frames, planes, SIDE + 2, 8, lanes)
        return (frames, planes, 4, PAIRS, 8, lanes)

    def planes_of(block, planes, begin=0):
        dims = planes_shape(block, LANES, planes)
        zeros = (0,) * (len(dims) - 1)
        return pl.BlockSpec(dims, lambda j: zeros + (j + begin,))

    def expand(block, sums, count, count_spec, rows):
        depth_rows = half_rows if block else full_rows
        planes = 3 if block else 2
        scratch = [pltpu.VMEM((taps if block else 12 * LAGS, 8, LANES), F32)]
        if not block:
            scratch = scratch + [pltpu.VMEM(planes_shape(0, LANES, 2), F32), pltpu.VMEM((PAIRS, 4, 2, 8, LANES), F32)]
        return call(
            functools.partial(expand_kernel, block), (tiles,),
            [SCALARS, tile_sums(), count_spec, whole(rows), weight_tile(block, cin), tile_rows(4), tile_rows(4),
             weight_tile(block, taps)],
            [tile_cube(full_rows), tile_cube(depth_rows), tile_rows(8), tile_sums(), planes_of(block, planes)],
            [shape(full_rows, 8, width), shape(depth_rows, 8, width), shape(8, width), shape(devices, 2, width),
             shape(*planes_shape(block, width, planes))],
            scratch,
            (frame_counts, sums, count, rows, w_t, wide_gains, wide_biases, depth_weight),
        )

    count_spec = pl.BlockSpec((devices, 2, LANES), lambda j: (0, 0, tiles))
    e_zero, d_zero, stat01, sums, planes_zero = expand(0, sums, sums, count_spec, x_rows)
    sums = exchange(sums)

    def squeeze_forward(block, sums, stat, depth):
        rows = half_rows if block else full_rows
        kinds = 4 if block else 2
        moving = [tile_sums(), tile_rows(8), tile_cube(rows), tile_rows(4), tile_rows(4)]
        if block:
            moving = [whole(array) for array in (sums, stat, depth, wide_gains, wide_biases)]
        return call(
            functools.partial(squeeze_forward_kernel, block), (1 if block else tiles,),
            [SCALARS] + moving
            + [of_block(block, squeeze, width), whole(squeeze_bias), of_block(block, squeeze, width), whole(excite_bias),
               of_block(block, cin, width), whole(cot)],
            [fixed(rows * 8, LANES), fixed(8, width), fixed(8, width), fixed(8, squeeze),
             fixed(8, width) if block else tile_rows(8), fixed(devices, kinds, LANES)],
            [shape(rows * 8, LANES), shape(8, width), shape(8, width), shape(8, squeeze), shape(8, width),
             shape(devices, kinds, LANES)],
            [pltpu.VMEM((tiles, rows, 8, LANES), F32), pltpu.VMEM((tiles, frames, LANES), F32)],
            (frame_counts, sums, stat, depth, wide_gains, wide_biases, squeeze_weight, squeeze_bias, up_t, excite_bias,
             project_weight, cot),
        )

    z_zero, gates_zero, running_zero, pre_zero, stat02, sums = squeeze_forward(0, sums, stat01, d_zero)
    sums = exchange(sums)
    narrow_args = (frame_counts, sums, stat01, gram_zero, x, z_zero, ngains, nbiases, w_t)
    narrow_outs = [
        shape(pixels, LANES), shape(pixels, 2 * LANES, kind=low), shape(2 * LANES, pixels, kind=low),
        shape(round_up(3 * LANES // 8 + 1), 8, LANES), shape(8, LANES), shape(devices, 2, width),
    ]
    x1, x1_rows, x1_columns, gram, nstat, sums = call(
        narrow_kernel, (1,), [SCALARS] + [whole(array) for array in narrow_args[1:-1]] + [of_block(1, cin, width)],
        [whole(item) for item in narrow_outs], narrow_outs, [], narrow_args,
    )
    sums, gram = together(exchange(sums), gram)
    gram = share_out(gram, AXES)
    e_one, d_one, stat11, sums, planes_one = expand(1, sums, nstat, pl.BlockSpec((8, LANES), lambda j: (0, 0)), x1_rows)
    sums, gram = together(sums, gram)
    sums = exchange(sums)
    z_one, gates_one, running_one, pre_one, stat12, sums = squeeze_forward(1, sums, stat11, d_one)
    third, gram = together(exchange(sums), gram)
    gram = share_back(gram, AXES).reshape(-1, LANES)
    q_tiles = cin // 8 + -(-taps // 8)

    def backward_specs(block):
        rows = half_rows if block else full_rows
        ins = [fixed(8, width), fixed(rows, 8, width), fixed(4, width), fixed(4, width), of_block(block, squeeze, width),
               of_block(block, squeeze, width), of_block(block, cin, width), fixed(8, width), fixed(8, width),
               fixed(8, squeeze)]
        if not block:
            ins[0:4] = [both(rows_at(8)), both(cube_at(rows)), both(rows_at(4)), both(rows_at(4))]
            ins[6] = early(weight_at(block, cin))
        packed = round_up(tiles * (pack_tiles(cin, squeeze) + (0 if block else q_tiles)))
        wide_outs = [fixed(rows, 8, width), fixed(devices, 2, width)] if block else [late(cube_at(rows)), late(sums_at(2))]
        outs = [fixed(8, LANES)] + wide_outs + [fixed(packed, 8, LANES)]
        shapes = [shape(8, LANES), shape(rows, 8, width), shape(devices, 2, width), shape(packed, 8, LANES)]
        scratch = [pltpu.VMEM((rows * 8, 2 * LANES), low), pltpu.VMEM((2 * LANES, rows * 8), low),
                   pltpu.VMEM((2 * LANES, 2 * LANES), F32), pltpu.VMEM((tiles, rows, 8, LANES), F32),
                   pltpu.VMEM((tiles, frames, LANES), F32)]
        return (ins, outs, shapes, scratch)

    ins, outs, shapes, scratch = backward_specs(1)
    activations, nsum_one, dy2_one, sums, pack_one = call(
        squeeze_one_backward_kernel, (1,),
        [SCALARS, whole(third), whole(z_one), whole(cot), whole(ngains), whole(nbiases)] + ins,
        [fixed(cin, half_pixels)] + outs, [shape(cin, half_pixels)] + shapes, scratch,
        (frame_counts, third, z_one, cot, ngains, nbiases, stat12, d_one, wide_gains, wide_biases, squeeze_weight, up_t,
         project_weight, gates_one, running_one, pre_one),
    )
    sums, pack_one, gram = together(sums, pack_one, gram)
    sums, pack_one = together(exchange(sums), add_cores(pack_one))
    pack_one = share_out(pack_one)
    nothing = jnp.zeros((8, LANES), F32)

    def depth_backward(block, begin, end, sums, stat2, stat, dy2, depth, expanded, planes, columns, dx_in, sums_in, list_in):
        rows = half_rows if block else full_rows
        if block:
            taps_shape = (taps, 8, LANES)
            z_shape = (frames, 2, HALF_ROWS + 1, 8, LANES)
            f_shape = (full_rows, 8, LANES)
        else:
            taps_shape = (12 * LAGS, 8, LANES)
            z_shape = planes_shape(0, LANES, 4)
            f_shape = (frames, PAIRS, 4, 2, 8, LANES)
        count = end - begin
        final = end == tiles
        listed = round_up(end * q_tiles) if final and not block else end * q_tiles
        if final:
            send = (devices, 2, width + (LANES if block else 0))
            send_spec = fixed(*send)
        else:
            send = (8, count * LANES)
            send_spec = tile_rows(8)

        def wide_rows(rows):
            return pl.BlockSpec((rows, LANES), lambda j: (0, j + begin))

        def wide_cube(rows):
            return pl.BlockSpec((rows, 8, LANES), lambda j: (0, 0, j + begin))

        def wide_weight(rows):
            return pl.BlockSpec((1, rows, LANES), lambda j: (block, 0, j + begin))

        return call(
            functools.partial(depth_backward_kernel, block, begin, final), (count,),
            [SCALARS, pl.BlockSpec((devices, 2, LANES), lambda j: (0, 0, j + begin)), wide_rows(8), wide_rows(8), whole(nstat),
             wide_cube(rows), wide_cube(rows), wide_cube(full_rows), planes_of(block, 2, begin), whole(columns), wide_weight(cin), wide_rows(4),
             wide_rows(4), wide_weight(taps), whole(z_zero), whole(dx_in), whole(sums_in), whole(list_in)],
            [fixed(pixels, LANES), send_spec, fixed(listed, 8, LANES), tile_rows(8)],
            [shape(pixels, LANES), shape(*send), shape(listed, 8, LANES), shape(8, count * LANES)],
            [pltpu.VMEM(z_shape, F32), pltpu.VMEM(f_shape, F32), pltpu.VMEM(taps_shape, F32), pltpu.VMEM(taps_shape, F32),
             pltpu.VMEM((2 * LANES, 2 * LANES), F32)]
            + ([] if block else [pltpu.VMEM((frames, 4, 2, PAIRS, 8, LANES), F32)]),
            (frame_counts, sums, stat2, stat, nstat, dy2, depth, expanded, planes, columns, w_t, wide_gains, wide_biases,
             depth_weight, z_zero, dx_in, sums_in, list_in),
        )

    dxpre_one, sums, q_one, grad_one = depth_backward(
        1, 0, tiles, sums, stat12, stat11, dy2_one, d_one, e_one, planes_one, x1_columns, nothing, nothing, nothing
    )
    sums, pack_one = together(sums, pack_one)
    top_one, pack_one = together(exchange(sums), pack_one)
    pack_one = share_back(pack_one)
    ins, outs, shapes, scratch = backward_specs(0)
    dx1, nsum_zero, dy2_zero, sums, pack_zero = call(
        squeeze_zero_backward_kernel, (2, tiles),
        [SCALARS, whole(top_one), whole(stat11), whole(gram), whole(nstat), whole(dxpre_one), whole(x1), whole(z_zero),
         whole(ngains), of_block(1, cin, width), whole(wide_gains), whole(q_one)] + ins,
        [fixed(pixels, LANES)] + outs, [shape(pixels, LANES)] + shapes, scratch,
        (frame_counts, top_one, stat11, gram, nstat, dxpre_one, x1, z_zero, ngains, w_t, wide_gains, q_one, stat02, d_zero,
         wide_gains, wide_biases, squeeze_weight, up_t, project_weight, gates_zero, running_zero, pre_zero),
    )
    sums, pack_one = together(sums, pack_one)
    pack_one_other = swap_cores(pack_one)
    sums, pack_zero, pack_one_other = together(exchange(sums), add_cores(pack_zero), pack_one_other)
    pack_zero = share_out(pack_zero)
    first = tiles - tiles // 2
    dxpre_zero, sums_in, late, grad_a = depth_backward(
        0, 0, first, sums, stat02, stat01, dy2_zero, d_zero, e_zero, planes_zero, x_columns, nothing, nothing, nothing
    )
    dxpre_zero, pack_zero = together(dxpre_zero, pack_zero)
    pack_zero = share_back(pack_zero)
    dxpre_zero, sums, late, grad_b = depth_backward(
        0, first, tiles, sums, stat02, stat01, dy2_zero, d_zero, e_zero, planes_zero, x_columns, dxpre_zero, sums_in, late
    )
    grad_zero = jnp.concatenate([grad_a, grad_b], axis=1)
    sums, pack_zero = together(sums, pack_zero)
    pack_zero_other = swap_cores(pack_zero)
    top_zero, late, pack_zero_other = together(exchange(sums), add_cores(late), pack_zero_other)
    late = share_out(late)
    core = lax.axis_index("core").astype(jnp.int32).reshape(1)
    final_args = (
        frame_counts, momentum_index, gram, stat01, stat02, stat11, stat12, grad_zero, grad_one, top_one,
        top_zero, nsum_zero, nsum_one, dxpre_zero, x, dx1, w_t, wide_gains, wide_means, wide_variances, narrow_means,
        narrow_variances,
    )
    final_outs = [
        shape(cin, pixels), shape(2, cin, width), shape(16, width), shape(4, width), shape(4, width), shape(2, cin),
        shape(2, cin), shape(4, width), shape(4, width), shape(2, cin), shape(2, cin),
    ]
    video_grad, less, factor, wgain, wbias, ngain, nbias, newm, newv, newnm, newnv = simple_call(
        finish_kernel, 2, final_args, final_outs
    )
    less, late = together(less, late)
    late = share_back(late)
    list_shapes = [
        shape(2, cin, width), shape(2, taps, width), shape(2, squeeze, width), shape(2, squeeze, width),
        shape(2, cin, width), shape(2, width), shape(2, squeeze),
    ]
    list_args = (core, pack_zero, pack_zero_other, pack_one, pack_one_other, less, factor)
    dw_t, dtaps, ddown, dup, dproj, dupb, ddownb = call(
        lists_kernel, (1,), [SCALARS] + [whole(array) for array in list_args[1:5]] + [of_block(1, cin, width), whole(factor)],
        [of_block(1, cin, width), of_block(1, taps, width)] + [whole(item) for item in list_shapes[2:]], list_shapes, [],
        list_args,
    )
    dw_t, late = together(dw_t, late)
    late_other = swap_cores(late)
    stay = pl.BlockSpec(memory_space=pl.ANY)
    dw_t, dtaps = call(
        last_kernel, (1,),
        [SCALARS, whole(late), whole(late_other), of_block(0, cin, width), whole(factor), stay, stay],
        [of_block(0, cin, width), of_block(0, taps, width)], list_shapes[0:2], [],
        (core, late, late_other, less, factor, dw_t, dtaps), aliases={5: 0, 6: 1},
    )
    return (
        activations, video_grad, jnp.swapaxes(dw_t, 1, 2), wgain, wbias, ngain, nbias, dtaps, ddown, ddownb,
        jnp.swapaxes(dup, 1, 2), dupb, dproj, newm, newv, newnm, newnv,
    )


def solution(mesh):
    sizes = (mesh.shape["dp"], mesh.shape["rep"] // 2, 2)
    split_mesh = jax.sharding.Mesh(mesh.devices.reshape(sizes), AXES)
    split = P(None, AXES)
    placed = (split, P(AXES)) + (P(),) * 16 + (split,)
    return jax.shard_map(
        local, mesh=split_mesh, in_specs=placed, out_specs=(split, split) + (P(),) * 15, check_vma=False
    )
```

```python
import functools

import jax
import jax.numpy as jnp
from jax import lax
from jax.experimental import pallas as pl
from jax.experimental.pallas import tpu as pltpu
from jax.sharding import PartitionSpec as P

SIDE = 16
LANES = 128
LAGS = 5
FULL_ROWS = 2 * SIDE
HALF_ROWS = SIDE // 2
EPSILON = 1e-05
HIGHEST = lax.Precision.HIGHEST
F32 = jnp.float32
NN = (((1,), (0,)), ((), ()))
NT = (((1,), (1,)), ((), ()))
TN = (((0,), (0,)), ((), ()))
VMEM_BYTES = 52 * 1024 * 1024


def half_tanh(half_values):
    return jnp.tanh(half_values)


def sigmoid(values):
    return 0.5 * jnp.tanh(0.5 * values) + 0.5


def silu_slope(half_values, tanh):
    return 0.5 * (1.0 + tanh + half_values * (1.0 - tanh * tanh))


def exact_dot(left, right, dims=NN):
    return lax.dot_general(left, right, dims, precision=HIGHEST, preferred_element_type=F32)


def halves(values):
    high = values.astype(jnp.bfloat16)
    return (high, (values - high.astype(F32)).astype(jnp.bfloat16))


def side_by_side(values):
    return jnp.concatenate(halves(values), axis=1)


def right_square(w):
    both = side_by_side(w)
    return jnp.concatenate([both, both], axis=0)


def right_square_t(w):
    high, low = halves(w)
    return jnp.concatenate(
        [jnp.concatenate([high, high], axis=1), jnp.concatenate([low, low], axis=1)], axis=0
    )


def plain_dot(left, right, dims=NN):
    return lax.dot_general(left, right, dims, preferred_element_type=F32)


def fold_right(values):
    lanes = values.shape[1] // 2
    return values[:, :lanes] + values[:, lanes:]


def fold_square(values):
    rows = values.shape[0] // 2
    return fold_right(values[:rows] + values[rows:])


def stacked(values):
    high = values.astype(jnp.bfloat16).astype(F32)
    return jnp.concatenate([high, values - high], axis=0).astype(jnp.bfloat16)


def skinny_dot(left, right, dims=NN):
    rows = left.shape[0]
    both = stacked(left)
    high, low = halves(right)
    values = plain_dot(both, high, dims) + plain_dot(both, low, dims)
    return values[:rows] + values[rows:]


def frame_outer(left, right):
    a_high = left.astype(jnp.bfloat16).astype(F32)
    b_high = right.astype(jnp.bfloat16).astype(F32)
    a_low = left - a_high
    b_low = right - b_high
    a = jnp.concatenate([a_high, a_high, a_low, a_low], axis=0).astype(jnp.bfloat16)
    b = jnp.concatenate([b_high, b_low, b_high, b_low], axis=0).astype(jnp.bfloat16)
    return plain_dot(a, b, TN)


def pad_rows(values):
    return jnp.concatenate([values, jnp.zeros((LANES - values.shape[0], values.shape[1]), values.dtype)], axis=0)


def column_order():
    q = lax.broadcasted_iota(jnp.int32, (LANES, LANES), 0)
    n = lax.broadcasted_iota(jnp.int32, (LANES, LANES), 1)
    source = (q // 16) * 16 + (q % 8) * 2 + (q // 8) % 2
    return (source == n).astype(jnp.bfloat16)


def live_frames(counts_ref):
    total = counts_ref[0]
    for clip in range(1, counts_ref.shape[0]):
        total = total + counts_ref[clip]
    return total


def place_of(counts_ref, frame):
    begin = jnp.int32(0)
    end = jnp.int32(0)
    for clip in range(counts_ref.shape[0]):
        end = end + counts_ref[clip]
        begin = jnp.where(frame >= end, end, begin)
    return frame - begin


def running_matrix(counts_ref, frames):
    after = lax.broadcasted_iota(jnp.int32, (frames, frames), 0)
    before = lax.broadcasted_iota(jnp.int32, (frames, frames), 1)
    begin = jnp.int32(0)
    matrix = jnp.zeros((frames, frames), F32)
    for clip in range(counts_ref.shape[0]):
        end = begin + counts_ref[clip]
        inside = (before >= begin) & (before <= after) & (after < end)
        matrix = matrix + jnp.where(inside, 1.0 / (after - begin + 1).astype(F32), 0.0)
        begin = end
    return matrix


def columns_up(values):
    spot = lax.broadcasted_iota(jnp.int32, values.shape, 1)
    return jnp.where(spot == 7, 0.0, pltpu.roll(values, 7, axis=1))


def columns_down(values):
    spot = lax.broadcasted_iota(jnp.int32, values.shape, 1)
    return jnp.where(spot == 0, 0.0, pltpu.roll(values, 1, axis=1))


def tile_sum(values):
    return jnp.sum(jnp.sum(values, axis=0), axis=0, keepdims=True)


def rows8(*rows):
    lanes = rows[0].shape[1]
    spot = lax.broadcasted_iota(jnp.int32, (8, lanes), 0)
    block = jnp.zeros((8, lanes), F32)
    for index, row in enumerate(rows):
        block = jnp.where(spot == index, row, block)
    return block


def pick_row(block, index):
    spot = lax.broadcasted_iota(jnp.int32, block.shape, 0)
    return jnp.sum(jnp.where(spot == index, block, 0.0), axis=0, keepdims=True)


def outer(left, right):
    return exact_dot(rows8(left), rows8(right), TN)


def row_dot(row, matrix, dims=NN):
    return exact_dot(rows8(row), matrix, dims)[0:1]


def clear_edges(ref):
    planes = ref.shape[1]
    edge = jnp.zeros((8, LANES), F32)
    for t in range(ref.shape[0]):
        for plane in range(planes):
            ref[t, plane, 0] = edge
            ref[t, plane, ref.shape[2] - 1] = edge


def spread_taps(taps_ref, w_ref):
    for tap in range(w_ref.shape[0]):
        w_ref[tap] = jnp.broadcast_to(taps_ref[0, tap : tap + 1, :], (8, LANES))


PAIRS = SIDE // 2


def row_pairs(plane):
    pair = plane.reshape(PAIRS, 2, 8, LANES)
    d1 = pair[:, 0]
    d2 = pair[:, 1]
    edge = jnp.zeros((1, 8, LANES), F32)
    d0 = jnp.concatenate([edge, d2[:-1]], axis=0)
    d3 = jnp.concatenate([d1[1:], edge], axis=0)
    return (d0 - d2, d1 + d2, d2 - d1, d1 - d3)


def pair_rows(parts):
    upper = parts[:, 0] + parts[:, 1] + parts[:, 2]
    lower = parts[:, 1] - parts[:, 2] - parts[:, 3]
    return jnp.stack([upper, lower], axis=1).reshape(FULL_ROWS, 8, LANES)


def spread_pairs(taps_ref, w_ref):
    for k in range(LAGS):
        for c in range(3):
            g0, g1, g2 = (taps_ref[0, k * 9 + 3 * r + c : k * 9 + 3 * r + c + 1, :] for r in range(3))
            outside = 0.5 * (g0 + g2)
            combined = (g0, outside + 0.5 * g1, outside - 0.5 * g1, g2)
            for place in range(4):
                w_ref[k * 12 + 3 * place + c] = jnp.broadcast_to(combined[place], (8, LANES))


def conv_full(t, k, a_ref, b_ref, w_ref, m_ref, fresh):
    weights = [w_ref[k * 12 + tap] for tap in range(12)]
    source = t - k
    for m in range(PAIRS):
        for place in range(4):
            left, centre, right = weights[3 * place : 3 * place + 3]
            a_even, a_odd = (a_ref[source, plane, place, m] for plane in range(2))
            a_odd_down, a_even_up = (b_ref[source, plane, place, m] for plane in range(2))
            even = centre * a_even + right * a_odd + left * a_odd_down
            odd = centre * a_odd + left * a_even + right * a_even_up
            if fresh:
                m_ref[m, place, 0] = even
                m_ref[m, place, 1] = odd
            else:
                m_ref[m, place, 0] = m_ref[m, place, 0] + even
                m_ref[m, place, 1] = m_ref[m, place, 1] + odd


def conv_half(t, k, a_ref, w_ref, d_ref, fresh):
    weights = [w_ref[k * 9 + tap] for tap in range(9)]
    source = t - k
    carried = [a_ref[source, plane, 0] for plane in range(3)]
    for i in range(HALF_ROWS):
        rows = [carried]
        for need in (2 * i + 1, 2 * i + 2):
            rows.append([a_ref[source, plane, need] for plane in range(3)])
        carried = rows[2]
        total = None
        for r in range(3):
            a_even, a_odd, a_odd_down = rows[r]
            left, centre, right = weights[3 * r : 3 * r + 3]
            part = centre * a_even + right * a_odd + left * a_odd_down
            total = part if total is None else total + part
        at = t * HALF_ROWS + i
        d_ref[at] = total if fresh else d_ref[at] + total


def row_total(ref, lanes=None):
    values = ref[...] if lanes is None or lanes == slice(None) else ref[:, :, lanes]
    return jnp.sum(values, axis=0)


def send_all(send_ref, rows, lanes):
    count = rows.shape[0]

    def one(device, carry):
        send_ref[pl.ds(device, 1), 0:count, lanes] = rows[None]
        return carry

    lax.fori_loop(0, send_ref.shape[0], one, 0)


def stack_rows(*rows):
    return rows8(*rows)[0 : len(rows)]


def pick_thirds(order, values, dims, order_left):
    pieces = []
    rest = values
    for _ in range(3):
        piece = rest.astype(jnp.bfloat16)
        rest = rest - piece.astype(F32)
        args = (order, piece) if order_left else (piece, order)
        pieces.append(plain_dot(*args, dims))
    return pieces


def gram_kernel(counts_ref, video_ref, w_ref, gram_ref, send_ref):
    total = live_frames(counts_ref)
    frames = video_ref.shape[1] // 256
    ones = jnp.ones((8, 256), jnp.bfloat16)

    def frame(t, carry):
        at = pl.ds(pl.multiple_of(t * 256, 256), 256)
        both = jnp.concatenate(halves(pad_rows(video_ref[:, at] * live_value(t, total))), axis=0)
        return (carry[0] + plain_dot(both, both, NT), carry[1] + plain_dot(ones, both, NT))

    init = (jnp.zeros((2 * LANES, 2 * LANES), F32), jnp.zeros((8, 2 * LANES), F32))
    gram, summed = each_frame(frames, frame, init)
    gram = fold_square(gram)
    summed = fold_right(summed)[0:1]
    gram_ref[0:LANES, :] = gram
    gram_ref[LANES : LANES + 8, :] = rows8(summed)
    w = pad_rows(w_ref[0])
    width = w.shape[1]
    sums = stack_rows(row_dot(summed, w), jnp.sum(w * exact_dot(gram, w), axis=0, keepdims=True))
    count = jnp.full((2, LANES), 1.0, F32) * (total * (SIDE * SIDE)).astype(F32)
    send_all(send_ref, sums, slice(0, width))
    send_all(send_ref, count, slice(width, width + LANES))


def prepare_kernel(counts_ref, video_ref, cot_ref, x_ref, rows_ref, columns_ref, cot_out_ref):
    order = column_order()
    total = live_frames(counts_ref)
    for part in range(video_ref.shape[1] // LANES):
        at = slice(part * LANES, (part + 1) * LANES)
        block = pad_rows(video_ref[:, at] * live_value(part // 2, total))
        high, middle, low = pick_thirds(order, block, NT, True)
        x_ref[at, :] = high + middle + low
        rows_ref[at, :] = jnp.concatenate([high, middle], axis=1).astype(jnp.bfloat16)
        columns_ref[:, at] = jnp.concatenate([high.T, middle.T], axis=0).astype(jnp.bfloat16)
    spot = lax.broadcasted_iota(jnp.int32, (LANES, LANES), 1)
    for part in range(cot_ref.shape[1] // LANES):
        at = slice(part * LANES, (part + 1) * LANES)
        frame = (spot + part * LANES) // (HALF_ROWS * 8)
        cot_out_ref[at, :] = jnp.where(frame < total, pad_rows(cot_ref[:, at]), 0.0).T


def moments_of(sums, count):
    average = sums[0:1] / count
    return (average, sums[1:2] / count - average * average)


def narrow_kernel(
    counts_ref, sums_ref, stat_ref, gram0_ref, x_ref, z_ref, ngain_ref, nbias_ref, w_ref,
    x1_ref, rows_ref, columns_ref, gram_ref, stat_out_ref, send_ref,
):
    total = live_frames(counts_ref)
    count = stat_ref[2:3, 0:LANES]
    average, variance = moments_of(row_total(sums_ref), count)
    factor = ngain_ref[0:1, :] * lax.rsqrt(variance + EPSILON)
    shift = nbias_ref[0:1, :] - factor * average
    stat_out_ref[...] = rows8(average, variance, count)
    frames = x_ref.shape[0] // 256

    def frame(t, carry):
        gram, cross, summed = carry
        at = pl.ds(pl.multiple_of(t * 256, 256), 256)
        z = z_ref[at, :]
        rows = (x_ref[at, :] + factor * z + shift) * live_value(t, total)
        x1_ref[at, :] = rows
        both = side_by_side(rows)
        rows_ref[at, :] = both
        columns = jnp.concatenate(halves(rows.T), axis=0)
        columns_ref[:, at] = columns
        gram = gram + plain_dot(columns, both)
        cross = cross + plain_dot(columns, side_by_side(z))
        return (gram, cross, summed + jnp.sum(rows, axis=0, keepdims=True))

    zero = jnp.zeros((2 * LANES, 2 * LANES), F32)
    gram, cross, summed = each_frame(frames, frame, (zero, zero, jnp.zeros((1, LANES), F32)))

    gram = fold_square(gram)
    tiles = LANES // 8
    gram_ref[0:tiles] = gram.reshape(tiles, 8, LANES)
    gram_ref[tiles : 2 * tiles] = fold_square(cross).reshape(tiles, 8, LANES)
    gram_ref[2 * tiles : 3 * tiles] = gram0_ref[0:LANES, :].reshape(tiles, 8, LANES)
    gram_ref[3 * tiles] = rows8(summed, gram0_ref[LANES : LANES + 1, :])
    w = pad_rows(w_ref[0])
    sums = stack_rows(row_dot(summed, w), jnp.sum(w * exact_dot(gram, w), axis=0, keepdims=True))
    send_all(send_ref, sums, slice(0, w.shape[1]))


def write_first(t, total, values, scale, shift, a_ref, b_ref):
    half_pre = values * scale + shift
    first = (half_pre + half_pre * half_tanh(half_pre)) * live_value(t, total)
    first = first.reshape(SIDE, 2, 8, LANES)
    even = first[:, 0]
    odd = first[:, 1]
    if b_ref is None:
        a_ref[t, 0, 1 : SIDE + 1] = even
        a_ref[t, 1, 1 : SIDE + 1] = odd
        a_ref[t, 2, 1 : SIDE + 1] = columns_down(odd)
        return
    for ref, plane, values in ((a_ref, 0, even), (a_ref, 1, odd), (b_ref, 0, columns_down(odd)), (b_ref, 1, columns_up(even))):
        for place, part in enumerate(row_pairs(values)):
            ref[t, plane, place] = part


def expand_kernel(
    block, counts_ref, sums_ref, count_ref, rows_ref, w_ref, gain_ref, bias_ref, taps_ref,
    e_ref, d_ref, stat_ref, send_ref, a_ref, taps8_ref, *pair_refs,
):
    b_ref, m_ref = pair_refs if pair_refs else (None, None)
    if block:
        clear_edges(a_ref)
    total = live_frames(counts_ref)
    frames = a_ref.shape[0]
    count = count_ref[2:3, :] if block else row_total(count_ref)[0:1]
    average, variance = moments_of(row_total(sums_ref), count)
    stat_ref[...] = rows8(average, variance, count)
    norm_row = 2 * block
    scale = gain_ref[norm_row : norm_row + 1, :] * lax.rsqrt(variance + EPSILON)
    shift = 0.5 * (bias_ref[norm_row : norm_row + 1, :] - average * scale)
    scale = 0.5 * scale
    square = right_square(pad_rows(w_ref[0]))

    def expand(t, carry):
        at = pl.ds(pl.multiple_of(t * 256, 256), 256)
        values = fold_right(plain_dot(rows_ref[at, :], square)).reshape(FULL_ROWS, 8, LANES)
        e_ref[pl.ds(pl.multiple_of(t * FULL_ROWS, FULL_ROWS), FULL_ROWS)] = values
        write_first(t, total, values, scale, shift, a_ref, b_ref)
        return carry

    each_frame(frames, expand, 0)
    per_frame = HALF_ROWS if block else FULL_ROWS
    if block:
        spread_taps(taps_ref, taps8_ref)
        conv = functools.partial(conv_half, a_ref=a_ref, w_ref=taps8_ref, d_ref=d_ref)
    else:
        spread_pairs(taps_ref, taps8_ref)
        conv = functools.partial(conv_full, a_ref=a_ref, b_ref=b_ref, w_ref=taps8_ref, m_ref=m_ref)

    def frame(t, carry):
        conv(t, 0, fresh=True)
        last = jnp.minimum(place_of(counts_ref, t), LAGS - 1)

        def lag(k, inner):
            conv(t, k, fresh=False)
            return inner

        lax.fori_loop(1, last + 1, lag, 0)
        if not block:
            d_ref[pl.ds(t * per_frame, per_frame)] = pair_rows(m_ref[...])
        values = d_ref[pl.ds(t * per_frame, per_frame)]
        return (carry[0] + jnp.sum(values, axis=0), carry[1] + jnp.sum(values * values, axis=0))

    zero = jnp.zeros((8, LANES), F32)
    summed, squares = lax.fori_loop(0, total, frame, (zero, zero))

    def dead(t, carry):
        d_ref[pl.ds(t * per_frame, per_frame)] = jnp.zeros((per_frame, 8, LANES), F32)
        return carry

    lax.fori_loop(total, frames, dead, 0)
    sums = stack_rows(jnp.sum(summed, axis=0, keepdims=True), jnp.sum(squares, axis=0, keepdims=True))
    send_all(send_ref, sums, slice(0, LANES))


def live_value(t, total):
    return jnp.where(t < total, 1.0, 0.0).astype(F32)


def each_frame(count, body, init):
    return lax.fori_loop(0, count, body, init, unroll=min(8, count))


def lanes_of(ref, tile):
    if ref.shape[-1] == LANES:
        return slice(None)
    return pl.ds(pl.multiple_of(tile * LANES, LANES), LANES)


def squeeze_forward_kernel(
    block, counts_ref, sums_ref, stat_ref, d_ref, gain_ref, bias_ref, down_ref, downb_ref, up_ref, upb_ref, proj_ref,
    cot_ref, z_ref, gates_ref, running_ref, pre_ref, stat_out_ref, send_ref, second_ref, pooled_ref,
):
    step = pl.program_id(0)
    steps = pl.num_programs(0)
    tiles = second_ref.shape[0]
    total = live_frames(counts_ref)
    per_frame = HALF_ROWS if block else FULL_ROWS
    pixels = per_frame * 8
    frames = second_ref.shape[1] // per_frame
    group = 256 // pixels
    chunks = frames // group
    norm_row = 2 * block + 1

    def activate(tile, carry):
        lanes = lanes_of(d_ref, tile)
        count = stat_ref[2:3, lanes] * (0.25 if block else 1.0)
        average, variance = moments_of(row_total(sums_ref, lanes), count)
        stat_out_ref[:, lanes] = rows8(average, variance, count)
        scale = gain_ref[norm_row : norm_row + 1, lanes] * lax.rsqrt(variance + EPSILON)
        shift = 0.5 * (bias_ref[norm_row : norm_row + 1, lanes] - average * scale)
        scale = 0.5 * scale

        def chunk(index, inside):
            for inner in range(group):
                t = index * group + inner
                at = pl.ds(t * per_frame, per_frame)
                half_pre = d_ref[at, :, lanes] * scale + shift
                second = half_pre + half_pre * half_tanh(half_pre)
                second = second * live_value(t, total)
                second_ref[tile, at] = second
                pooled_ref[tile, pl.ds(t, 1), :] = tile_sum(second) * (1.0 / pixels)
            return inside

        each_frame(chunks, chunk, 0)
        return carry

    if block:
        lax.fori_loop(0, tiles, activate, 0)
    else:
        activate(step, 0)

    def project(tile, carry):
        lanes = lanes_of(gates_ref, tile)
        square = right_square_t(pad_rows(proj_ref[0, :, lanes]))
        gates = gates_ref[:, lanes]

        def chunk(index, inside):
            parts = []
            for inner in range(group):
                t = index * group + inner
                second = second_ref[tile, pl.ds(t * per_frame, per_frame)].reshape(pixels, LANES)
                parts.append(second * pick_row(gates, t))
            excited = parts[0] if group == 1 else jnp.concatenate(parts, axis=0)
            at = pl.ds(pl.multiple_of(index * 256, 256), 256)
            z_ref[at, :] = z_ref[at, :] + fold_right(plain_dot(side_by_side(excited), square, NT))
            return inside

        each_frame(chunks, chunk, 0)
        return carry

    @pl.when(step == steps - 1)
    def gate_and_project():
        matrix = running_matrix(counts_ref, frames)
        pooled = jnp.concatenate([pooled_ref[index] for index in range(tiles)], axis=1)
        running = exact_dot(matrix, pooled)
        running_ref[...] = running
        pre = skinny_dot(running, down_ref[0], NT) + downb_ref[block : block + 1, :]
        pre_ref[...] = pre
        gates_ref[...] = sigmoid(skinny_dot(pre * sigmoid(pre), up_ref[0]) + upb_ref[block : block + 1, :])
        z_ref[...] = jnp.zeros_like(z_ref)
        lax.fori_loop(0, tiles, project, 0)

        def chunk(index, carry):
            at = pl.ds(pl.multiple_of(index * 256, 256), 256)
            z = z_ref[at, :].reshape(32, 8, LANES)
            values = [z, z * z]
            if block:
                dy = cot_ref[at, :].reshape(32, 8, LANES)
                values = values + [dy, dy * z]
            return tuple(old + jnp.sum(new, axis=0) for old, new in zip(carry, values))

        zero = jnp.zeros((8, LANES), F32)
        sums = each_frame(chunks, chunk, (zero,) * (4 if block else 2))
        rows = stack_rows(*(jnp.sum(value, axis=0, keepdims=True) for value in sums))
        send_all(send_ref, rows, slice(0, LANES))


def pack_tiles(narrow, squeeze):
    return narrow // 8 + 2 * (squeeze // 8) + 1


def squeeze_backward_body(
    block, counts_ref, stat_ref, d_ref, gain_ref, bias_ref, down_ref, up_ref, proj_ref, gates_ref, running_ref,
    pre_ref, dy2_ref, send_ref, pack_ref, dz3_ref, dz3t_ref, total_ref, dexc_ref, dgate_ref, head,
):
    total = live_frames(counts_ref)
    per_frame = HALF_ROWS if block else FULL_ROWS
    pixels = per_frame * 8
    frames = dz3_ref.shape[0] // pixels
    group = 256 // pixels
    chunks = frames // group
    norm_row = 2 * block + 1
    tiles = dexc_ref.shape[0]
    narrow = proj_ref.shape[1]
    squeeze = down_ref.shape[1]
    per_tile = pack_tiles(narrow, squeeze)

    def norm_of(tile):
        lanes = lanes_of(d_ref, tile)
        average = stat_ref[0:1, lanes]
        root = lax.rsqrt(stat_ref[1:2, lanes] + EPSILON)
        scale = gain_ref[norm_row : norm_row + 1, lanes] * root
        shift = 0.5 * (bias_ref[norm_row : norm_row + 1, lanes] - average * scale)
        return (lanes, average, root, 0.5 * scale, shift)

    def excite(tile, carry):
        lanes, _, _, scale, shift = norm_of(tile)
        gates = gates_ref[:, lanes_of(gates_ref, tile)]
        square = right_square(pad_rows(proj_ref[0, :, lanes]))

        def chunk(index, inside):
            flat = pl.ds(pl.multiple_of(index * 256, 256), 256)
            dexc = fold_right(plain_dot(dz3_ref[flat, :], square)).reshape(32, 8, LANES)
            dexc_ref[tile, pl.ds(pl.multiple_of(index * 32, 32), 32)] = dexc
            parts = []
            for inner in range(group):
                t = index * group + inner
                half_pre = d_ref[pl.ds(t * per_frame, per_frame), :, lanes] * scale + shift
                second = half_pre + half_pre * half_tanh(half_pre)
                second = second * live_value(t, total)
                own = dexc[inner * per_frame : (inner + 1) * per_frame]
                dgate_ref[tile, pl.ds(t, 1), :] = tile_sum(own * second)
                parts.append(second.reshape(pixels, LANES) * pick_row(gates, t))
            excited = parts[0] if group == 1 else jnp.concatenate(parts, axis=0)
            total_ref[...] = total_ref[...] + plain_dot(dz3t_ref[:, flat], side_by_side(excited))
            return inside

        total_ref[...] = jnp.zeros_like(total_ref)
        each_frame(chunks, chunk, 0)
        dproj = fold_square(total_ref[...])
        pack_ref[pl.ds(tile * per_tile, narrow // 8)] = dproj[0:narrow].reshape(narrow // 8, 8, LANES)
        return carry

    def squeeze_part():
        pre = pre_ref[...]
        half_pre = 0.5 * pre
        tanh = half_tanh(half_pre)
        squeezed = half_pre + half_pre * tanh
        all_gates = gates_ref[...]
        dgate = jnp.concatenate([dgate_ref[index] for index in range(tiles)], axis=1)
        du = dgate * all_gates * (1.0 - all_gates)
        dpre = skinny_dot(du, up_ref[0], NT) * silu_slope(half_pre, tanh)
        ddown = frame_outer(dpre, running_ref[...])
        dup = frame_outer(squeezed, du)
        dpre_row = jnp.sum(dpre, axis=0, keepdims=True)
        dpre_row = jnp.concatenate([dpre_row, jnp.zeros((1, du.shape[1] - squeeze), F32)], axis=1)
        biases = rows8(jnp.sum(du, axis=0, keepdims=True), dpre_row)
        for index in range(tiles):
            own = slice(index * LANES, (index + 1) * LANES)
            at = index * per_tile + narrow // 8
            pack_ref[at : at + squeeze // 8] = ddown[:, own].reshape(squeeze // 8, 8, LANES)
            at = at + squeeze // 8
            pack_ref[at : at + squeeze // 8] = dup[:, own].reshape(squeeze // 8, 8, LANES)
            pack_ref[at + squeeze // 8] = biases[:, own]
        drunning = skinny_dot(dpre, down_ref[0])
        dpooled = exact_dot(running_matrix(counts_ref, frames), drunning, TN) * (1.0 / pixels)
        for index in range(tiles):
            dgate_ref[index] = dpooled[:, index * LANES : (index + 1) * LANES]

    def slope(tile, carry):
        lanes, average, root, scale, shift = norm_of(tile)
        gates = gates_ref[:, lanes_of(gates_ref, tile)]

        def chunk(index, inside):
            summed, cross = inside
            for inner in range(group):
                t = index * group + inner
                at = pl.ds(t * per_frame, per_frame)
                depth = d_ref[at, :, lanes]
                half_pre = depth * scale + shift
                dsecond = dexc_ref[tile, at] * pick_row(gates, t) + pick_row(dgate_ref[tile], t)
                dy = dsecond * silu_slope(half_pre, half_tanh(half_pre))
                dy = dy * live_value(t, total)
                dy2_ref[at, :, lanes] = dy
                summed = summed + jnp.sum(dy, axis=0)
                cross = cross + jnp.sum(dy * (depth - average), axis=0)
            return (summed, cross)

        zero = jnp.zeros((8, LANES), F32)
        summed, cross = each_frame(chunks, chunk, (zero, zero))
        rows = stack_rows(jnp.sum(summed, axis=0, keepdims=True), root * jnp.sum(cross, axis=0, keepdims=True))
        send_all(send_ref, rows, lanes)
        return carry

    if block:
        head()
        lax.fori_loop(0, tiles, excite, 0)
        squeeze_part()
        lax.fori_loop(0, tiles, slope, 0)
    else:
        phase = pl.program_id(0)
        tile = pl.program_id(1)

        @pl.when((phase == 0) & (tile == 0))
        def start():
            head()

        @pl.when(phase == 0)
        def first():
            excite(tile, 0)

        @pl.when((phase == 1) & (tile == 0))
        def between():
            squeeze_part()

        @pl.when(phase == 1)
        def second():
            slope(tile, 0)


def squeeze_one_backward_kernel(
    counts_ref, third_ref, z_ref, cot_ref, ngain_ref, nbias_ref, stat_ref, d_ref, gain_ref, bias_ref, down_ref,
    up_ref, proj_ref, gates_ref, running_ref, pre_ref, act_ref, nsum_ref, dy2_ref, send_ref, pack_ref,
    dz3_ref, dz3t_ref, total_ref, dexc_ref, dgate_ref,
):
    total = live_frames(counts_ref)
    pixels = HALF_ROWS * 8

    def head():
        count = stat_ref[2:3, 0:LANES]
        sums = row_total(third_ref)
        mean, variance = moments_of(sums, count)
        root = lax.rsqrt(variance + EPSILON)
        gain = ngain_ref[1:2, :]
        bias_sum = sums[2:3, :]
        gain_sum = root * (sums[3:4, :] - mean * bias_sum)
        nsum_ref[...] = rows8(gain_sum, bias_sum, mean, variance)
        row = lax.broadcasted_iota(jnp.int32, z_ref.shape, 0) // pixels
        live = row < total
        normed = (z_ref[...] - mean) * root
        act = jnp.where(live, gain * normed + nbias_ref[1:2, :], 0.0)
        act_ref[...] = act.T[0 : act_ref.shape[0]]
        dz3 = gain * root * (cot_ref[...] - bias_sum / count - normed * (gain_sum / count))
        dz3 = jnp.where(live, dz3, 0.0)
        dz3_ref[...] = side_by_side(dz3)
        dz3t_ref[...] = jnp.concatenate(halves(dz3.T), axis=0)

    squeeze_backward_body(
        1, counts_ref, stat_ref, d_ref, gain_ref, bias_ref, down_ref, up_ref, proj_ref, gates_ref, running_ref,
        pre_ref, dy2_ref, send_ref, pack_ref, dz3_ref, dz3t_ref, total_ref, dexc_ref, dgate_ref, head,
    )


def input_factors(sums, stat_ref, count, gain, w):
    root = lax.rsqrt(stat_ref[1:2, :] + EPSILON)
    factor = gain * root
    matrix = exact_dot(w * (factor * root * sums[1:2] / count), w, NT)
    return (matrix, row_dot(factor * sums[0:1] / count, w, NT))


def covariance(gram, summed, count):
    mean = summed / count
    return (mean, gram / count - outer(mean, mean))


def squeeze_zero_backward_kernel(
    counts_ref, top_ref, stat1_ref, gram_ref, nstat_ref, dxpre_ref, x1_ref, z_ref, ngain_ref, w_ref, gains_ref, q_one_ref,
    stat_ref, d_ref, gain_ref, bias_ref, down_ref, up_ref, proj_ref, gates_ref, running_ref, pre_ref,
    dx1_ref, nsum_ref, dy2_ref, send_ref, pack_ref, dz3_ref, dz3t_ref, total_ref, dexc_ref, dgate_ref,
):
    total = live_frames(counts_ref)
    width = gains_ref.shape[1]

    def head():
        start = pack_tiles(proj_ref.shape[1], down_ref.shape[1]) * (width // LANES)
        pack_ref[start : start + q_one_ref.shape[0]] = q_one_ref[...]
        count = stat_ref[2:3, :]
        wide_count = jnp.broadcast_to(count[:, 0:1], (1, width))
        sums = row_total(top_ref, slice(0, width))
        extra = row_total(top_ref, slice(width, width + LANES))
        matrix, shift = input_factors(sums, stat1_ref, wide_count, gains_ref[2:3, :], pad_rows(w_ref[0]))
        mean = nstat_ref[0:1, :]
        root = lax.rsqrt(nstat_ref[1:2, :] + EPSILON)
        mean_x1 = gram_ref[3 * LANES : 3 * LANES + 1, :] / count
        cross = (gram_ref[LANES : 2 * LANES, :] - count * outer(mean_x1, mean)) * root
        gain_sum = extra[0:1] - jnp.sum(matrix * cross, axis=0, keepdims=True)
        bias_sum = extra[1:2] - count * shift
        nsum_ref[...] = rows8(gain_sum, bias_sum, mean, nstat_ref[1:2, :])
        factor = ngain_ref[0:1, :] * root
        square = right_square(matrix)
        bias_mean = bias_sum / count
        gain_mean = gain_sum / count

        def frame(t, carry):
            at = pl.ds(pl.multiple_of(t * 256, 256), 256)
            centred = side_by_side(x1_ref[at, :] - mean_x1)
            live = live_value(t, total)
            dx1 = (dxpre_ref[at, :] - fold_right(plain_dot(centred, square)) - shift) * live
            dx1_ref[at, :] = dx1
            normed = (z_ref[at, :] - mean) * root
            dz3 = factor * (dx1 - bias_mean - normed * gain_mean) * live
            dz3_ref[at, :] = side_by_side(dz3)
            dz3t_ref[:, at] = jnp.concatenate(halves(dz3.T), axis=0)
            return carry

        each_frame(dz3_ref.shape[0] // 256, frame, 0)

    squeeze_backward_body(
        0, counts_ref, stat_ref, d_ref, gain_ref, bias_ref, down_ref, up_ref, proj_ref, gates_ref, running_ref,
        pre_ref, dy2_ref, send_ref, pack_ref, dz3_ref, dz3t_ref, total_ref, dexc_ref, dgate_ref, head,
    )

def back_full(t, k, a_ref, w_ref, z_ref, raw_ref, f_ref, dw_ref, fresh):
    weights = [w_ref[k * 12 + tap] for tap in range(12)]
    target = t - k
    sums = [None] * 12
    for m in range(PAIRS):
        for place in range(4):
            flipped = (3, 1, 2, 0)[place]
            left, centre, right = weights[3 * flipped : 3 * flipped + 3]
            b_even, b_odd, b_odd_down, b_even_up = (z_ref[t, plane, place, m] for plane in range(4))
            even = centre * b_even + right * b_odd_down + left * b_odd
            odd = centre * b_odd + right * b_even + left * b_even_up
            if fresh:
                f_ref[target, m, place, 0] = even
                f_ref[target, m, place, 1] = odd
            else:
                f_ref[target, m, place, 0] = f_ref[target, m, place, 0] + even
                f_ref[target, m, place, 1] = f_ref[target, m, place, 1] + odd
            if place in (0, 3):
                row = 0 if place == 0 else 1
                b_even, b_odd, b_odd_down, b_even_up = (raw_ref[t, plane, row, m] for plane in range(4))
            a_even, a_odd = (a_ref[target, plane, place, m] for plane in range(2))
            pieces = (
                b_even_up * a_odd + b_odd * a_even,
                b_even * a_even + b_odd * a_odd,
                b_even * a_odd + b_odd_down * a_even,
            )
            for c in range(3):
                at = 3 * place + c
                sums[at] = pieces[c] if sums[at] is None else sums[at] + pieces[c]
    for place in range(4):
        for c in range(3):
            at = place * 3 * LAGS + k * 3 + c
            dw_ref[at] = dw_ref[at] + sums[3 * place + c]


def pair_taps(totals):
    count = 3 * LAGS
    first, second, third, last = (totals[place * count : (place + 1) * count] for place in range(4))
    middle = 0.5 * (second - third)
    return (first + middle, 0.5 * (second + third), middle - last)


def back_half(t, k, a_ref, w_ref, z_ref, f_ref, dw_ref, fresh):
    weights = [w_ref[k * 9 + tap] for tap in range(9)]
    target = t - k
    sums = [None] * 9

    def put(row, parity, value):
        at = target * FULL_ROWS + 2 * row + parity
        f_ref[at] = value if fresh else f_ref[at] + value

    carried = [a_ref[target, plane, 0] for plane in range(2)]
    here = [z_ref[t, plane, 0] for plane in range(2)]
    for i in range(HALF_ROWS):
        below = [z_ref[t, plane, i + 1] for plane in range(2)]
        dz, dz_up = here
        rows = [carried]
        for need in (2 * i + 1, 2 * i + 2):
            rows.append([a_ref[target, plane, need] for plane in range(2)])
        carried = rows[2]
        put(2 * i, 0, weights[4] * dz)
        put(2 * i, 1, weights[5] * dz + weights[3] * dz_up)
        put(2 * i + 1, 0, weights[7] * dz + weights[1] * below[0])
        put(
            2 * i + 1,
            1,
            weights[8] * dz + weights[6] * dz_up + (weights[2] * below[0] + weights[0] * below[1]),
        )
        for r in range(3):
            a_even, a_odd = rows[r]
            pieces = (dz_up * a_odd, dz * a_even, dz * a_odd)
            for c in range(3):
                at = 3 * r + c
                sums[at] = pieces[c] if sums[at] is None else sums[at] + pieces[c]
        here = below
    for tap in range(9):
        dw_ref[k * 9 + tap] = dw_ref[k * 9 + tap] + sums[tap]


def depth_backward_kernel(
    block, before, final, counts_ref, grads_ref, stat2_ref, stat_ref, nstat_ref, dy2_ref, d_ref, e_ref, a_ref, columns_ref, w_ref,
    gain_ref, bias_ref, taps_ref, z3_ref, dx_in_ref, sums_in_ref, list_in_ref, dxpre_ref, send_ref, q_ref, grad_rows_ref,
    z_ref, f_ref, taps8_ref, dw_ref, total_ref, *raw_refs,
):
    tile = pl.program_id(0)
    tiles = pl.num_programs(0)
    total = live_frames(counts_ref)
    frames = a_ref.shape[0]
    norm_row = 2 * block
    half = block == 1
    per_frame = HALF_ROWS if half else FULL_ROWS
    taps = taps_ref.shape[1]

    @pl.when(tile == 0)
    def start():
        if half:
            clear_edges(z_ref)
        if before:
            dxpre_ref[...] = dx_in_ref[...]
            send_all(send_ref, sums_in_ref[0:2, :], slice(0, before * LANES))
            q_ref[0 : list_in_ref.shape[0]] = list_in_ref[...]
        else:
            dxpre_ref[...] = jnp.zeros_like(dxpre_ref)

        def dead(t, carry):
            if half:
                f_ref[pl.ds(t * FULL_ROWS, FULL_ROWS)] = jnp.zeros((FULL_ROWS, 8, LANES), F32)
            else:
                f_ref[t] = jnp.zeros(f_ref.shape[1:], F32)
            return carry

        lax.fori_loop(total, frames, dead, 0)

    count = stat2_ref[2:3, :]
    grads = row_total(grads_ref)
    grad_rows_ref[...] = rows8(grads[0:1], grads[1:2])
    average = stat2_ref[0:1, :]
    root = lax.rsqrt(stat2_ref[1:2, :] + EPSILON)
    scale_two = gain_ref[norm_row + 1 : norm_row + 2, :] * root
    slope = scale_two * root * grads[1:2] / count
    level = scale_two * grads[0:1] / count - slope * average
    average_one = stat_ref[0:1, :]
    root_one = lax.rsqrt(stat_ref[1:2, :] + EPSILON)
    scale_one = gain_ref[norm_row : norm_row + 1, :] * root_one
    shift_half = 0.5 * (bias_ref[norm_row : norm_row + 1, :] - average_one * scale_one)
    scale_half = 0.5 * scale_one

    def fill(t, carry):
        at = pl.ds(t * per_frame, per_frame)
        dz = scale_two * dy2_ref[at] - (slope * d_ref[at] + level)
        if half:
            z_ref[t, 0, 0:HALF_ROWS] = dz
            z_ref[t, 1, 0:HALF_ROWS] = columns_up(dz)
        else:
            pair = dz.reshape(SIDE, 2, 8, LANES)
            even = pair[:, 0]
            odd = pair[:, 1]
            for plane, values in enumerate((even, odd, columns_down(odd), columns_up(even))):
                for place, part in enumerate(row_pairs(values)):
                    z_ref[t, plane, place] = part
                rows = values.reshape(PAIRS, 2, 8, LANES)
                raw_refs[0][t, plane, 0] = rows[:, 0]
                raw_refs[0][t, plane, 1] = rows[:, 1]
        return carry

    each_frame(frames, fill, 0)
    dw_ref[...] = jnp.zeros_like(dw_ref)
    refs = dict(a_ref=a_ref, w_ref=taps8_ref, z_ref=z_ref, f_ref=f_ref, dw_ref=dw_ref)
    if half:
        spread_taps(taps_ref, taps8_ref)
        back = functools.partial(back_half, **refs)
    else:
        spread_pairs(taps_ref, taps8_ref)
        back = functools.partial(back_full, raw_ref=raw_refs[0], **refs)

    def frame(t, carry):
        back(t, 0, fresh=True)
        last = jnp.minimum(place_of(counts_ref, t), LAGS - 1)

        def lag(k, inner):
            back(t, k, fresh=False)
            return inner

        return lax.fori_loop(1, last + 1, lag, carry)

    lax.fori_loop(0, total, frame, 0)
    square = right_square_t(pad_rows(w_ref[0]) * scale_one)
    total_ref[...] = jnp.zeros_like(total_ref)

    def finish(t, carry):
        rows = pl.ds(pl.multiple_of(t * FULL_ROWS, FULL_ROWS), FULL_ROWS)
        flat = pl.ds(pl.multiple_of(t * 256, 256), 256)
        values = e_ref[rows]
        half_pre = values * scale_half + shift_half
        dfirst = f_ref[rows] if half else pair_rows(f_ref[t])
        dy = dfirst * silu_slope(half_pre, half_tanh(half_pre))
        summed = carry[0] + jnp.sum(dy, axis=0)
        cross = carry[1] + jnp.sum(dy * (values - average_one), axis=0)
        dy = dy.reshape(256, LANES)
        both = side_by_side(dy)
        total_ref[...] = total_ref[...] + plain_dot(columns_ref[:, flat], both)
        dxpre_ref[flat, :] = dxpre_ref[flat, :] + fold_right(plain_dot(both, square, NT))
        return (summed, cross)

    zero = jnp.zeros((8, LANES), F32)
    summed, cross = each_frame(frames, finish, (zero, zero))
    rows = stack_rows(jnp.sum(summed, axis=0, keepdims=True), root_one * jnp.sum(cross, axis=0, keepdims=True))
    if final:
        send_all(send_ref, rows, pl.ds(pl.multiple_of((tile + before) * LANES, LANES), LANES))
    else:
        send_ref[...] = rows8(rows[0:1], rows[1:2])
    gathered = fold_square(total_ref[...])
    narrow = w_ref.shape[1]
    dtaps = jnp.sum(dw_ref[...], axis=1)
    parts = (dtaps,) if half else pair_taps(dtaps)
    unused = jnp.zeros(((-taps) % 8, LANES), F32)
    values = jnp.concatenate((gathered[0:narrow],) + parts + (unused,), axis=0)
    listed = values.shape[0] // 8
    q_ref[pl.ds((tile + before) * listed, listed)] = values.reshape(listed, 8, LANES)

    if half:
        @pl.when(tile == tiles - 1)
        def tail():
            mean = nstat_ref[0:1, :]
            root_three = lax.rsqrt(nstat_ref[1:2, :] + EPSILON)

            def part(t, carry):
                flat = pl.ds(pl.multiple_of(t * 256, 256), 256)
                dx = dxpre_ref[flat, :].reshape(32, 8, LANES)
                normed = ((z3_ref[flat, :] - mean) * root_three).reshape(32, 8, LANES)
                return (carry[0] + jnp.sum(dx * normed, axis=0), carry[1] + jnp.sum(dx, axis=0))

            cross_three, summed_three = each_frame(frames, part, (zero, zero))
            rows = stack_rows(
                jnp.sum(cross_three, axis=0, keepdims=True), jnp.sum(summed_three, axis=0, keepdims=True)
            )
            width = send_ref.shape[2] - LANES
            send_all(send_ref, rows, slice(width, width + LANES))


def finish_kernel(
    counts_ref, momentum_ref, gram_ref, stat01_ref, stat02_ref, stat11_ref, stat12_ref, grad0_ref,
    grad1_ref, one_ref, zero_ref, nsum0_ref, nsum1_ref, dxpre_ref, x_ref, dx1_ref, w_ref, gain_ref, means_ref, vars_ref,
    nmeans_ref, nvars_ref,
    video_ref, less_ref, factor_ref, wgain_ref, wbias_ref, ngain_ref, nbias_ref, newm_ref, newv_ref, newnm_ref, newnv_ref,
):
    total = live_frames(counts_ref)
    full = stat01_ref[2:3, :]
    count = full[:, 0:LANES]
    width = full.shape[1]
    top_zero = row_total(zero_ref)
    top_one = row_total(one_ref, slice(0, width))
    w_zero = pad_rows(w_ref[0])
    matrix, shift = input_factors(top_zero, stat01_ref, full, gain_ref[0:1, :], w_zero)
    square = right_square(matrix)
    mean_x, cov_zero = covariance(
        gram_ref[2 * LANES : 3 * LANES, :], gram_ref[3 * LANES + 1 : 3 * LANES + 2, :], count
    )
    order = column_order()
    narrow = video_ref.shape[0]

    def frame(t, carry):
        at = pl.ds(pl.multiple_of(t * 256, 256), 256)
        centred = side_by_side(x_ref[at, :] - mean_x)
        dx = (dxpre_ref[at, :] - fold_right(plain_dot(centred, square)) - shift) * live_value(t, total) + dx1_ref[at, :]
        for part in range(2):
            own = dx[part * LANES : (part + 1) * LANES].T[0:narrow]
            pieces = pick_thirds(order, own, NN, False)
            start = pl.multiple_of(t * 256 + part * LANES, LANES)
            video_ref[:, pl.ds(start, LANES)] = pieces[0] + pieces[1] + pieces[2]
        return carry

    each_frame(x_ref.shape[0] // 256, frame, 0)
    mean_one, cov_one = covariance(gram_ref[0:LANES, :], gram_ref[3 * LANES : 3 * LANES + 1, :], count)
    plan = ((mean_x, cov_zero, stat01_ref, top_zero, w_zero), (mean_one, cov_one, stat11_ref, top_one, pad_rows(w_ref[1])))
    for block, (mean_row, cov, stat_ref, top, w) in enumerate(plan):
        root = lax.rsqrt(stat_ref[1:2, :] + EPSILON)
        factor = gain_ref[2 * block : 2 * block + 1, :] * root
        less = outer(mean_row, top[0:1]) + exact_dot(cov, w) * (root * top[1:2])
        less_ref[block] = (less * factor)[0:narrow]
        factor_ref[8 * block : 8 * block + 8, :] = rows8(factor)
    momentum = momentum_ref[0].astype(F32) / 10.0
    wgain_ref[...] = stack_rows(top_zero[1:2], grad0_ref[1:2, :], top_one[1:2], grad1_ref[1:2, :])
    wbias_ref[...] = stack_rows(top_zero[0:1], grad0_ref[0:1, :], top_one[0:1], grad1_ref[0:1, :])
    stats = (stat01_ref, stat02_ref, stat11_ref, stat12_ref)
    means = stack_rows(*(ref[0:1, :] for ref in stats))
    variances = stack_rows(*(ref[1:2, :] * (ref[2:3, :] / (ref[2:3, :] - 1.0)) for ref in stats))
    newm_ref[...] = (1.0 - momentum) * means_ref[...] + momentum * means
    newv_ref[...] = (1.0 - momentum) * vars_ref[...] + momentum * variances
    ngain_ref[...] = stack_rows(nsum0_ref[0:1, :], nsum1_ref[0:1, :])[:, 0:narrow]
    nbias_ref[...] = stack_rows(nsum0_ref[1:2, :], nsum1_ref[1:2, :])[:, 0:narrow]
    means = stack_rows(nsum0_ref[2:3, :], nsum1_ref[2:3, :])[:, 0:narrow]
    quarter = 0.25 * count
    variances = stack_rows(
        nsum0_ref[3:4, :] * (count / (count - 1.0)), nsum1_ref[3:4, :] * (quarter / (quarter - 1.0))
    )[:, 0:narrow]
    newnm_ref[...] = (1.0 - momentum) * nmeans_ref[...] + momentum * means
    newnv_ref[...] = (1.0 - momentum) * nvars_ref[...] + momentum * variances


def list_rows(core_ref, pair, at, count):
    first_core = core_ref[0] == 0
    mine, other = pair[0:2]
    if len(pair) > 2:
        share = pair[2]
        half = mine.shape[0] * share

        def run(ref, begin, size):
            pieces = []
            while size:
                length = min(size, share - begin % share)
                pieces.append(ref[begin // share, begin % share : begin % share + length])
                begin = begin + length
                size = size - length
            return pieces[0] if len(pieces) == 1 else jnp.concatenate(pieces, axis=0)
    else:
        half = mine.shape[0]

        def run(ref, begin, size):
            return ref[begin : begin + size]

    pieces = []
    if at < half:
        size = min(count, half - at)
        pieces.append(jnp.where(first_core, run(mine, at, size), run(other, at, size)))
        count = count - size
        at = at + size
    if count:
        pieces.append(jnp.where(first_core, run(other, at - half, count), run(mine, at - half, count)))
    values = pieces[0] if len(pieces) == 1 else jnp.concatenate(pieces, axis=0)
    return values.reshape(-1, LANES)


def lists_kernel(
    share, core_ref, pack0_ref, pack0_other_ref, pack1_ref, pack1_other_ref, less_ref, factor_ref,
    dw_ref, dtaps_ref, ddown_ref, dup_ref, dproj_ref, dupb_ref, ddownb_ref,
):
    narrow = dw_ref.shape[1]
    taps = dtaps_ref.shape[1]
    squeeze = ddown_ref.shape[1]
    tiles = dw_ref.shape[2] // LANES
    per_pack = pack_tiles(narrow, squeeze)
    per_tile = narrow // 8 + -(-taps // 8)
    packs = ((pack0_ref, pack0_other_ref, share), (pack1_ref, pack1_other_ref))
    for block in range(2):
        down_rows = []
        for tile in range(tiles):
            lanes = slice(tile * LANES, (tile + 1) * LANES)
            at = tile * per_pack
            dproj_ref[block, :, lanes] = list_rows(core_ref, packs[block], at, narrow // 8)
            at = at + narrow // 8
            ddown_ref[block, :, lanes] = list_rows(core_ref, packs[block], at, squeeze // 8)
            at = at + squeeze // 8
            dup_ref[block, :, lanes] = list_rows(core_ref, packs[block], at, squeeze // 8)
            biases = list_rows(core_ref, packs[block], at + squeeze // 8, 1)
            dupb_ref[block : block + 1, lanes] = biases[0:1]
            down_rows.append(biases[1:2])
        ddownb_ref[block : block + 1, :] = jnp.concatenate(down_rows, axis=1)[:, 0:squeeze]
    for tile in range(tiles):
        lanes = slice(tile * LANES, (tile + 1) * LANES)
        values = list_rows(core_ref, packs[0], per_pack * tiles + tile * per_tile, per_tile)
        dw_ref[0, :, lanes] = values[0:narrow] * factor_ref[8:9, lanes] - less_ref[0, :, lanes]
        dtaps_ref[0, :, lanes] = values[narrow : narrow + taps]


def last_kernel(core_ref, late_ref, late_other_ref, less_ref, factor_ref, _, __, dw_ref, dtaps_ref):
    narrow = dw_ref.shape[1]
    taps = dtaps_ref.shape[1]
    per_tile = narrow // 8 + -(-taps // 8)
    for tile in range(dw_ref.shape[2] // LANES):
        lanes = slice(tile * LANES, (tile + 1) * LANES)
        values = list_rows(core_ref, (late_ref, late_other_ref), tile * per_tile, per_tile)
        dw_ref[0, :, lanes] = values[0:narrow] * factor_ref[0:1, lanes] - less_ref[0, :, lanes]
        for r in range(3):
            for k in range(LAGS):
                source = narrow + r * 3 * LAGS + 3 * k
                dtaps_ref[0, k * 9 + 3 * r : k * 9 + 3 * r + 3, lanes] = values[source : source + 3]


AXES = ("dp", "z", "core")
CHIPS = ("dp", "z")


def exchange(send):
    return lax.all_to_all(send, AXES, 0, 0, tiled=True)


def together(*values):
    return lax.optimization_barrier(values)


def swap_cores(values):
    return lax.ppermute(values, "core", [(0, 1), (1, 0)])


def add_cores(tiles):
    core = lax.axis_index("core")
    pair = tiles.reshape(2, tiles.shape[0] // 2, *tiles.shape[1:])
    mine = lax.dynamic_index_in_dim(pair, core, 0, keepdims=False)
    return mine + swap_cores(lax.dynamic_index_in_dim(pair, 1 - core, 0, keepdims=False))


def share_out(tiles, names=CHIPS):
    count = 1
    for name in names:
        count = count * lax.axis_size(name)
    return lax.all_to_all(tiles.reshape(count, -1, *tiles.shape[1:]), names, 0, 0, tiled=True)


def share_back(pieces, names=CHIPS):
    own = jnp.sum(pieces, axis=0)
    everyone = lax.all_to_all(jnp.broadcast_to(own[None], pieces.shape), names, 0, 0, tiled=True)
    return everyone.reshape(-1, *pieces.shape[2:])


def shape(*dims, kind=F32):
    return jax.ShapeDtypeStruct(dims, kind)


def whole(array):
    rank = len(array.shape)
    return pl.BlockSpec(array.shape, lambda *ids: (0,) * rank)


SCALARS = pl.BlockSpec(memory_space=pltpu.SMEM)


def call(kernel, grid, in_specs, out_specs, out_shape, scratch, args, vmem=VMEM_BYTES, aliases=None):
    return pl.pallas_call(
        kernel,
        grid=grid,
        in_specs=in_specs,
        out_specs=out_specs,
        out_shape=out_shape,
        scratch_shapes=scratch,
        compiler_params=pltpu.CompilerParams(vmem_limit_bytes=vmem),
        input_output_aliases=aliases or {},
        cost_estimate=pl.CostEstimate(
            flops=1_000_000_000, bytes_accessed=1_000_000, transcendentals=0
        ),
    )(*args)


def simple_call(kernel, scalars, args, outs):
    return call(
        kernel, (1,), [SCALARS] * scalars + [whole(array) for array in args[scalars:]], [whole(item) for item in outs],
        outs, [], args,
    )


def local(
    video, frame_counts, momentum_index, expand_weight, wide_gains, wide_biases, narrow_gains, narrow_biases, depth_weight,
    squeeze_weight, squeeze_bias, excite_weight, excite_bias, project_weight, wide_means, wide_variances, narrow_means,
    narrow_variances, cotangent,
):
    devices = lax.axis_size("dp") * lax.axis_size("z") * lax.axis_size("core")
    cin, pixels = video.shape
    half_pixels = cotangent.shape[1]
    width = expand_weight.shape[1]
    squeeze = squeeze_weight.shape[1]
    frames = pixels // (SIDE * SIDE)
    tiles = width // LANES
    taps = depth_weight.shape[1]
    w_t = jnp.swapaxes(expand_weight, 1, 2)
    up_t = jnp.swapaxes(excite_weight, 1, 2)
    lanes_pad = ((0, 0), (0, LANES - cin))
    ngains = jnp.pad(narrow_gains, lanes_pad)
    nbiases = jnp.pad(narrow_biases, lanes_pad)
    full_rows = frames * FULL_ROWS
    half_rows = frames * HALF_ROWS
    low = jnp.bfloat16

    def round_up(count):
        return -(-count // devices) * devices

    def fixed(*dims):
        return pl.BlockSpec(dims, lambda *ids: (0,) * len(dims))

    def tile_rows(rows):
        return pl.BlockSpec((rows, LANES), lambda j: (0, j))

    def tile_cube(rows):
        return pl.BlockSpec((rows, 8, LANES), lambda j: (0, 0, j))

    def tile_sums(rows=2):
        return pl.BlockSpec((devices, rows, LANES), lambda j: (0, 0, j))

    def weight_tile(block, rows):
        return pl.BlockSpec((1, rows, LANES), lambda j, block=block: (block, 0, j))

    def of_block(block, rows, lanes):
        return pl.BlockSpec((1, rows, lanes), lambda *ids: (block, 0, 0))

    def early(make):
        return make(lambda p, j: j * (1 - p) + (tiles - 1) * p)

    def late(make):
        return make(lambda p, j: j * p)

    def both(make):
        return make(lambda p, j: j)

    def rows_at(rows):
        return lambda at: pl.BlockSpec((rows, LANES), lambda p, j: (0, at(p, j)))

    def cube_at(rows):
        return lambda at: pl.BlockSpec((rows, 8, LANES), lambda p, j: (0, 0, at(p, j)))

    def sums_at(rows):
        return lambda at: pl.BlockSpec((devices, rows, LANES), lambda p, j: (0, 0, at(p, j)))

    def weight_at(block, rows):
        return lambda at: pl.BlockSpec((1, rows, LANES), lambda p, j: (block, 0, at(p, j)))

    gram_zero, sums = call(
        gram_kernel, (1,), [SCALARS, whole(video), of_block(0, cin, width)],
        [fixed(LANES + 8, LANES), fixed(devices, 2, width + LANES)],
        [shape(LANES + 8, LANES), shape(devices, 2, width + LANES)],
        [], (frame_counts, video, w_t), vmem=60 * 1024 * 1024,
    )
    x, x_rows, x_columns, cot = simple_call(
        prepare_kernel, 1, (frame_counts, video, cotangent),
        [shape(pixels, LANES), shape(pixels, 2 * LANES, kind=low), shape(2 * LANES, pixels, kind=low),
         shape(half_pixels, LANES)],
    )
    sums = exchange(sums)

    def planes_shape(block, lanes, planes):
        if block:
            return (frames, planes, SIDE + 2, 8, lanes)
        return (frames, planes, 4, PAIRS, 8, lanes)

    def planes_of(block, planes, begin=0):
        dims = planes_shape(block, LANES, planes)
        zeros = (0,) * (len(dims) - 1)
        return pl.BlockSpec(dims, lambda j: zeros + (j + begin,))

    def expand(block, sums, count, count_spec, rows):
        depth_rows = half_rows if block else full_rows
        planes = 3 if block else 2
        scratch = [pltpu.VMEM((taps if block else 12 * LAGS, 8, LANES), F32)]
        if not block:
            scratch = scratch + [pltpu.VMEM(planes_shape(0, LANES, 2), F32), pltpu.VMEM((PAIRS, 4, 2, 8, LANES), F32)]
        return call(
            functools.partial(expand_kernel, block), (tiles,),
            [SCALARS, tile_sums(), count_spec, whole(rows), weight_tile(block, cin), tile_rows(4), tile_rows(4),
             weight_tile(block, taps)],
            [tile_cube(full_rows), tile_cube(depth_rows), tile_rows(8), tile_sums(), planes_of(block, planes)],
            [shape(full_rows, 8, width), shape(depth_rows, 8, width), shape(8, width), shape(devices, 2, width),
             shape(*planes_shape(block, width, planes))],
            scratch,
            (frame_counts, sums, count, rows, w_t, wide_gains, wide_biases, depth_weight),
        )

    count_spec = pl.BlockSpec((devices, 2, LANES), lambda j: (0, 0, tiles))
    e_zero, d_zero, stat01, sums, planes_zero = expand(0, sums, sums, count_spec, x_rows)
    sums = exchange(sums)

    def squeeze_forward(block, sums, stat, depth):
        rows = half_rows if block else full_rows
        kinds = 4 if block else 2
        moving = [tile_sums(), tile_rows(8), tile_cube(rows), tile_rows(4), tile_rows(4)]
        if block:
            moving = [whole(array) for array in (sums, stat, depth, wide_gains, wide_biases)]
        return call(
            functools.partial(squeeze_forward_kernel, block), (1 if block else tiles,),
            [SCALARS] + moving
            + [of_block(block, squeeze, width), whole(squeeze_bias), of_block(block, squeeze, width), whole(excite_bias),
               of_block(block, cin, width), whole(cot)],
            [fixed(rows * 8, LANES), fixed(8, width), fixed(8, width), fixed(8, squeeze),
             fixed(8, width) if block else tile_rows(8), fixed(devices, kinds, LANES)],
            [shape(rows * 8, LANES), shape(8, width), shape(8, width), shape(8, squeeze), shape(8, width),
             shape(devices, kinds, LANES)],
            [pltpu.VMEM((tiles, rows, 8, LANES), F32), pltpu.VMEM((tiles, frames, LANES), F32)],
            (frame_counts, sums, stat, depth, wide_gains, wide_biases, squeeze_weight, squeeze_bias, up_t, excite_bias,
             project_weight, cot),
        )

    z_zero, gates_zero, running_zero, pre_zero, stat02, sums = squeeze_forward(0, sums, stat01, d_zero)
    sums = exchange(sums)
    narrow_args = (frame_counts, sums, stat01, gram_zero, x, z_zero, ngains, nbiases, w_t)
    narrow_outs = [
        shape(pixels, LANES), shape(pixels, 2 * LANES, kind=low), shape(2 * LANES, pixels, kind=low),
        shape(round_up(3 * LANES // 8 + 1), 8, LANES), shape(8, LANES), shape(devices, 2, width),
    ]
    x1, x1_rows, x1_columns, gram, nstat, sums = call(
        narrow_kernel, (1,), [SCALARS] + [whole(array) for array in narrow_args[1:-1]] + [of_block(1, cin, width)],
        [whole(item) for item in narrow_outs], narrow_outs, [], narrow_args,
    )
    sums, gram = together(exchange(sums), gram)
    gram = share_out(gram, AXES)
    e_one, d_one, stat11, sums, planes_one = expand(1, sums, nstat, pl.BlockSpec((8, LANES), lambda j: (0, 0)), x1_rows)
    sums, gram = together(sums, gram)
    sums = exchange(sums)
    z_one, gates_one, running_one, pre_one, stat12, sums = squeeze_forward(1, sums, stat11, d_one)
    third, gram = together(exchange(sums), gram)
    gram = share_back(gram, AXES).reshape(-1, LANES)
    q_tiles = cin // 8 + -(-taps // 8)

    def backward_specs(block):
        rows = half_rows if block else full_rows
        ins = [fixed(8, width), fixed(rows, 8, width), fixed(4, width), fixed(4, width), of_block(block, squeeze, width),
               of_block(block, squeeze, width), of_block(block, cin, width), fixed(8, width), fixed(8, width),
               fixed(8, squeeze)]
        if not block:
            ins[0:4] = [both(rows_at(8)), both(cube_at(rows)), both(rows_at(4)), both(rows_at(4))]
            ins[6] = early(weight_at(block, cin))
        packed = round_up(tiles * (pack_tiles(cin, squeeze) + (0 if block else q_tiles)))
        wide_outs = [fixed(rows, 8, width), fixed(devices, 2, width)] if block else [late(cube_at(rows)), late(sums_at(2))]
        outs = [fixed(8, LANES)] + wide_outs + [fixed(packed, 8, LANES)]
        shapes = [shape(8, LANES), shape(rows, 8, width), shape(devices, 2, width), shape(packed, 8, LANES)]
        scratch = [pltpu.VMEM((rows * 8, 2 * LANES), low), pltpu.VMEM((2 * LANES, rows * 8), low),
                   pltpu.VMEM((2 * LANES, 2 * LANES), F32), pltpu.VMEM((tiles, rows, 8, LANES), F32),
                   pltpu.VMEM((tiles, frames, LANES), F32)]
        return (ins, outs, shapes, scratch)

    ins, outs, shapes, scratch = backward_specs(1)
    activations, nsum_one, dy2_one, sums, pack_one = call(
        squeeze_one_backward_kernel, (1,),
        [SCALARS, whole(third), whole(z_one), whole(cot), whole(ngains), whole(nbiases)] + ins,
        [fixed(cin, half_pixels)] + outs, [shape(cin, half_pixels)] + shapes, scratch,
        (frame_counts, third, z_one, cot, ngains, nbiases, stat12, d_one, wide_gains, wide_biases, squeeze_weight, up_t,
         project_weight, gates_one, running_one, pre_one),
    )
    sums, pack_one, gram = together(sums, pack_one, gram)
    sums, pack_one = together(exchange(sums), add_cores(pack_one))
    pack_one = share_out(pack_one)
    nothing = jnp.zeros((8, LANES), F32)

    def depth_backward(block, begin, end, sums, stat2, stat, dy2, depth, expanded, planes, columns, dx_in, sums_in, list_in):
        rows = half_rows if block else full_rows
        if block:
            taps_shape = (taps, 8, LANES)
            z_shape = (frames, 2, HALF_ROWS + 1, 8, LANES)
            f_shape = (full_rows, 8, LANES)
        else:
            taps_shape = (12 * LAGS, 8, LANES)
            z_shape = planes_shape(0, LANES, 4)
            f_shape = (frames, PAIRS, 4, 2, 8, LANES)
        count = end - begin
        final = end == tiles
        listed = round_up(end * q_tiles) if final and not block else end * q_tiles
        if final:
            send = (devices, 2, width + (LANES if block else 0))
            send_spec = fixed(*send)
        else:
            send = (8, count * LANES)
            send_spec = tile_rows(8)

        def wide_rows(rows):
            return pl.BlockSpec((rows, LANES), lambda j: (0, j + begin))

        def wide_cube(rows):
            return pl.BlockSpec((rows, 8, LANES), lambda j: (0, 0, j + begin))

        def wide_weight(rows):
            return pl.BlockSpec((1, rows, LANES), lambda j: (block, 0, j + begin))

        return call(
            functools.partial(depth_backward_kernel, block, begin, final), (count,),
            [SCALARS, pl.BlockSpec((devices, 2, LANES), lambda j: (0, 0, j + begin)), wide_rows(8), wide_rows(8), whole(nstat),
             wide_cube(rows), wide_cube(rows), wide_cube(full_rows), planes_of(block, 2, begin), whole(columns), wide_weight(cin), wide_rows(4),
             wide_rows(4), wide_weight(taps), whole(z_zero), whole(dx_in), whole(sums_in), whole(list_in)],
            [fixed(pixels, LANES), send_spec, fixed(listed, 8, LANES), tile_rows(8)],
            [shape(pixels, LANES), shape(*send), shape(listed, 8, LANES), shape(8, count * LANES)],
            [pltpu.VMEM(z_shape, F32), pltpu.VMEM(f_shape, F32), pltpu.VMEM(taps_shape, F32), pltpu.VMEM(taps_shape, F32),
             pltpu.VMEM((2 * LANES, 2 * LANES), F32)]
            + ([] if block else [pltpu.VMEM((frames, 4, 2, PAIRS, 8, LANES), F32)]),
            (frame_counts, sums, stat2, stat, nstat, dy2, depth, expanded, planes, columns, w_t, wide_gains, wide_biases,
             depth_weight, z_zero, dx_in, sums_in, list_in),
        )

    dxpre_one, sums, q_one, grad_one = depth_backward(
        1, 0, tiles, sums, stat12, stat11, dy2_one, d_one, e_one, planes_one, x1_columns, nothing, nothing, nothing
    )
    sums, pack_one = together(sums, pack_one)
    top_one, pack_one = together(exchange(sums), pack_one)
    pack_one = share_back(pack_one)
    ins, outs, shapes, scratch = backward_specs(0)
    dx1, nsum_zero, dy2_zero, sums, pack_zero = call(
        squeeze_zero_backward_kernel, (2, tiles),
        [SCALARS, whole(top_one), whole(stat11), whole(gram), whole(nstat), whole(dxpre_one), whole(x1), whole(z_zero),
         whole(ngains), of_block(1, cin, width), whole(wide_gains), whole(q_one)] + ins,
        [fixed(pixels, LANES)] + outs, [shape(pixels, LANES)] + shapes, scratch,
        (frame_counts, top_one, stat11, gram, nstat, dxpre_one, x1, z_zero, ngains, w_t, wide_gains, q_one, stat02, d_zero,
         wide_gains, wide_biases, squeeze_weight, up_t, project_weight, gates_zero, running_zero, pre_zero),
    )
    sums, pack_one = together(sums, pack_one)
    pack_one_other = swap_cores(pack_one)
    sums, pack_zero, pack_one_other = together(exchange(sums), add_cores(pack_zero), pack_one_other)
    pack_zero = share_out(pack_zero)
    dxpre_zero, sums, late, grad_zero = depth_backward(
        0, 0, tiles, sums, stat02, stat01, dy2_zero, d_zero, e_zero, planes_zero, x_columns, nothing, nothing, nothing
    )
    sums, pack_zero = together(sums, pack_zero)
    top_zero, late = together(exchange(sums), add_cores(late))
    own = jnp.sum(pack_zero, axis=0)
    joint = jnp.concatenate(
        [jnp.broadcast_to(own[None], pack_zero.shape), late.reshape(pack_zero.shape[0], -1, 8, LANES)], axis=1
    )
    joint = lax.all_to_all(joint, CHIPS, 0, 0, tiled=True)
    core = lax.axis_index("core").astype(jnp.int32).reshape(1)
    final_args = (
        frame_counts, momentum_index, gram, stat01, stat02, stat11, stat12, grad_zero, grad_one, top_one,
        top_zero, nsum_zero, nsum_one, dxpre_zero, x, dx1, w_t, wide_gains, wide_means, wide_variances, narrow_means,
        narrow_variances,
    )
    final_outs = [
        shape(cin, pixels), shape(2, cin, width), shape(16, width), shape(4, width), shape(4, width), shape(2, cin),
        shape(2, cin), shape(4, width), shape(4, width), shape(2, cin), shape(2, cin),
    ]
    video_grad, less, factor, wgain, wbias, ngain, nbias, newm, newv, newnm, newnv = simple_call(
        finish_kernel, 2, final_args, final_outs
    )
    less, joint = together(less, joint)
    joint_other = swap_cores(joint)
    late = share_back(joint[:, own.shape[0] :])
    list_shapes = [
        shape(2, cin, width), shape(2, taps, width), shape(2, squeeze, width), shape(2, squeeze, width),
        shape(2, cin, width), shape(2, width), shape(2, squeeze),
    ]
    list_args = (core, joint, joint_other, pack_one, pack_one_other, less, factor)
    dw_t, dtaps, ddown, dup, dproj, dupb, ddownb = call(
        functools.partial(lists_kernel, own.shape[0]), (1,), [SCALARS] + [whole(array) for array in list_args[1:5]] + [of_block(1, cin, width), whole(factor)],
        [of_block(1, cin, width), of_block(1, taps, width)] + [whole(item) for item in list_shapes[2:]], list_shapes, [],
        list_args,
    )
    dw_t, late = together(dw_t, late)
    late_other = swap_cores(late)
    stay = pl.BlockSpec(memory_space=pl.ANY)
    dw_t, dtaps = call(
        last_kernel, (1,),
        [SCALARS, whole(late), whole(late_other), of_block(0, cin, width), whole(factor), stay, stay],
        [of_block(0, cin, width), of_block(0, taps, width)], list_shapes[0:2], [],
        (core, late, late_other, less, factor, dw_t, dtaps), aliases={5: 0, 6: 1},
    )
    return (
        activations, video_grad, jnp.swapaxes(dw_t, 1, 2), wgain, wbias, ngain, nbias, dtaps, ddown, ddownb,
        jnp.swapaxes(dup, 1, 2), dupb, dproj, newm, newv, newnm, newnv,
    )


def solution(mesh):
    sizes = (mesh.shape["dp"], mesh.shape["rep"] // 2, 2)
    split_mesh = jax.sharding.Mesh(mesh.devices.reshape(sizes), AXES)
    split = P(None, AXES)
    placed = (split, P(AXES)) + (P(),) * 16 + (split,)
    return jax.shard_map(
        local, mesh=split_mesh, in_specs=placed, out_specs=(split, split) + (P(),) * 15, check_vma=False
    )
```

```python
import functools

import jax
import jax.numpy as jnp
from jax import lax
from jax.experimental import pallas as pl
from jax.experimental.pallas import tpu as pltpu
from jax.sharding import PartitionSpec as P

SIDE = 16
LANES = 128
LAGS = 5
FULL_ROWS = 2 * SIDE
HALF_ROWS = SIDE // 2
EPSILON = 1e-05
HIGHEST = lax.Precision.HIGHEST
F32 = jnp.float32
NN = (((1,), (0,)), ((), ()))
NT = (((1,), (1,)), ((), ()))
TN = (((0,), (0,)), ((), ()))
VMEM_BYTES = 52 * 1024 * 1024


def half_tanh(half_values):
    return jnp.tanh(half_values)


def sigmoid(values):
    return 0.5 * jnp.tanh(0.5 * values) + 0.5


def silu_slope(half_values, tanh):
    return 0.5 * (1.0 + tanh + half_values * (1.0 - tanh * tanh))


def exact_dot(left, right, dims=NN):
    return lax.dot_general(left, right, dims, precision=HIGHEST, preferred_element_type=F32)


def halves(values):
    high = values.astype(jnp.bfloat16)
    return (high, (values - high.astype(F32)).astype(jnp.bfloat16))


def side_by_side(values):
    return jnp.concatenate(halves(values), axis=1)


def right_square(w):
    both = side_by_side(w)
    return jnp.concatenate([both, both], axis=0)


def right_square_t(w):
    high, low = halves(w)
    return jnp.concatenate(
        [jnp.concatenate([high, high], axis=1), jnp.concatenate([low, low], axis=1)], axis=0
    )


def plain_dot(left, right, dims=NN):
    return lax.dot_general(left, right, dims, preferred_element_type=F32)


def fold_right(values):
    lanes = values.shape[1] // 2
    return values[:, :lanes] + values[:, lanes:]


def fold_square(values):
    rows = values.shape[0] // 2
    return fold_right(values[:rows] + values[rows:])


def stacked(values):
    high = values.astype(jnp.bfloat16).astype(F32)
    return jnp.concatenate([high, values - high], axis=0).astype(jnp.bfloat16)


def skinny_dot(left, right, dims=NN):
    rows = left.shape[0]
    both = stacked(left)
    high, low = halves(right)
    values = plain_dot(both, high, dims) + plain_dot(both, low, dims)
    return values[:rows] + values[rows:]


def frame_outer(left, right):
    a_high = left.astype(jnp.bfloat16).astype(F32)
    b_high = right.astype(jnp.bfloat16).astype(F32)
    a_low = left - a_high
    b_low = right - b_high
    a = jnp.concatenate([a_high, a_high, a_low, a_low], axis=0).astype(jnp.bfloat16)
    b = jnp.concatenate([b_high, b_low, b_high, b_low], axis=0).astype(jnp.bfloat16)
    return plain_dot(a, b, TN)


def pad_rows(values):
    return jnp.concatenate([values, jnp.zeros((LANES - values.shape[0], values.shape[1]), values.dtype)], axis=0)


def column_order():
    q = lax.broadcasted_iota(jnp.int32, (LANES, LANES), 0)
    n = lax.broadcasted_iota(jnp.int32, (LANES, LANES), 1)
    source = (q // 16) * 16 + (q % 8) * 2 + (q // 8) % 2
    return (source == n).astype(jnp.bfloat16)


def live_frames(counts_ref):
    total = counts_ref[0]
    for clip in range(1, counts_ref.shape[0]):
        total = total + counts_ref[clip]
    return total


def place_of(counts_ref, frame):
    begin = jnp.int32(0)
    end = jnp.int32(0)
    for clip in range(counts_ref.shape[0]):
        end = end + counts_ref[clip]
        begin = jnp.where(frame >= end, end, begin)
    return frame - begin


def running_matrix(counts_ref, frames):
    after = lax.broadcasted_iota(jnp.int32, (frames, frames), 0)
    before = lax.broadcasted_iota(jnp.int32, (frames, frames), 1)
    begin = jnp.int32(0)
    matrix = jnp.zeros((frames, frames), F32)
    for clip in range(counts_ref.shape[0]):
        end = begin + counts_ref[clip]
        inside = (before >= begin) & (before <= after) & (after < end)
        matrix = matrix + jnp.where(inside, 1.0 / (after - begin + 1).astype(F32), 0.0)
        begin = end
    return matrix


def columns_up(values):
    spot = lax.broadcasted_iota(jnp.int32, values.shape, 1)
    return jnp.where(spot == 7, 0.0, pltpu.roll(values, 7, axis=1))


def columns_down(values):
    spot = lax.broadcasted_iota(jnp.int32, values.shape, 1)
    return jnp.where(spot == 0, 0.0, pltpu.roll(values, 1, axis=1))


def tile_sum(values):
    return jnp.sum(jnp.sum(values, axis=0), axis=0, keepdims=True)


def rows8(*rows):
    lanes = rows[0].shape[1]
    spot = lax.broadcasted_iota(jnp.int32, (8, lanes), 0)
    block = jnp.zeros((8, lanes), F32)
    for index, row in enumerate(rows):
        block = jnp.where(spot == index, row, block)
    return block


def pick_row(block, index):
    spot = lax.broadcasted_iota(jnp.int32, block.shape, 0)
    return jnp.sum(jnp.where(spot == index, block, 0.0), axis=0, keepdims=True)


def outer(left, right):
    return exact_dot(rows8(left), rows8(right), TN)


def row_dot(row, matrix, dims=NN):
    return exact_dot(rows8(row), matrix, dims)[0:1]


def clear_edges(ref):
    planes = ref.shape[1]
    edge = jnp.zeros((8, LANES), F32)
    for t in range(ref.shape[0]):
        for plane in range(planes):
            ref[t, plane, 0] = edge
            ref[t, plane, ref.shape[2] - 1] = edge


def spread_taps(taps_ref, w_ref):
    for tap in range(w_ref.shape[0]):
        w_ref[tap] = jnp.broadcast_to(taps_ref[0, tap : tap + 1, :], (8, LANES))


PAIRS = SIDE // 2


def row_pairs(plane):
    pair = plane.reshape(PAIRS, 2, 8, LANES)
    d1 = pair[:, 0]
    d2 = pair[:, 1]
    edge = jnp.zeros((1, 8, LANES), F32)
    d0 = jnp.concatenate([edge, d2[:-1]], axis=0)
    d3 = jnp.concatenate([d1[1:], edge], axis=0)
    return (d0 - d2, d1 + d2, d2 - d1, d1 - d3)


def pair_rows(parts):
    upper = parts[:, 0] + parts[:, 1] + parts[:, 2]
    lower = parts[:, 1] - parts[:, 2] - parts[:, 3]
    return jnp.stack([upper, lower], axis=1).reshape(FULL_ROWS, 8, LANES)


def spread_pairs(taps_ref, w_ref):
    for k in range(LAGS):
        for c in range(3):
            g0, g1, g2 = (taps_ref[0, k * 9 + 3 * r + c : k * 9 + 3 * r + c + 1, :] for r in range(3))
            outside = 0.5 * (g0 + g2)
            combined = (g0, outside + 0.5 * g1, outside - 0.5 * g1, g2)
            for place in range(4):
                w_ref[k * 12 + 3 * place + c] = jnp.broadcast_to(combined[place], (8, LANES))


def conv_full(t, k, a_ref, b_ref, w_ref, m_ref, fresh):
    weights = [w_ref[k * 12 + tap] for tap in range(12)]
    source = t - k
    for m in range(PAIRS):
        for place in range(4):
            left, centre, right = weights[3 * place : 3 * place + 3]
            a_even, a_odd = (a_ref[source, plane, place, m] for plane in range(2))
            a_odd_down, a_even_up = (b_ref[source, plane, place, m] for plane in range(2))
            even = centre * a_even + right * a_odd + left * a_odd_down
            odd = centre * a_odd + left * a_even + right * a_even_up
            if fresh:
                m_ref[m, place, 0] = even
                m_ref[m, place, 1] = odd
            else:
                m_ref[m, place, 0] = m_ref[m, place, 0] + even
                m_ref[m, place, 1] = m_ref[m, place, 1] + odd


def conv_half(t, k, a_ref, w_ref, d_ref, fresh):
    weights = [w_ref[k * 9 + tap] for tap in range(9)]
    source = t - k
    carried = [a_ref[source, plane, 0] for plane in range(3)]
    for i in range(HALF_ROWS):
        rows = [carried]
        for need in (2 * i + 1, 2 * i + 2):
            rows.append([a_ref[source, plane, need] for plane in range(3)])
        carried = rows[2]
        total = None
        for r in range(3):
            a_even, a_odd, a_odd_down = rows[r]
            left, centre, right = weights[3 * r : 3 * r + 3]
            part = centre * a_even + right * a_odd + left * a_odd_down
            total = part if total is None else total + part
        at = t * HALF_ROWS + i
        d_ref[at] = total if fresh else d_ref[at] + total


def row_total(ref, lanes=None):
    values = ref[...] if lanes is None or lanes == slice(None) else ref[:, :, lanes]
    return jnp.sum(values, axis=0)


def send_all(send_ref, rows, lanes):
    count = rows.shape[0]

    def one(device, carry):
        send_ref[pl.ds(device, 1), 0:count, lanes] = rows[None]
        return carry

    lax.fori_loop(0, send_ref.shape[0], one, 0)


def stack_rows(*rows):
    return rows8(*rows)[0 : len(rows)]


def pick_thirds(order, values, dims, order_left):
    pieces = []
    rest = values
    for _ in range(3):
        piece = rest.astype(jnp.bfloat16)
        rest = rest - piece.astype(F32)
        args = (order, piece) if order_left else (piece, order)
        pieces.append(plain_dot(*args, dims))
    return pieces


def gram_kernel(counts_ref, video_ref, w_ref, gram_ref, send_ref):
    total = live_frames(counts_ref)
    frames = video_ref.shape[1] // 256
    ones = jnp.ones((8, 256), jnp.bfloat16)

    def frame(t, carry):
        at = pl.ds(pl.multiple_of(t * 256, 256), 256)
        both = jnp.concatenate(halves(pad_rows(video_ref[:, at] * live_value(t, total))), axis=0)
        return (carry[0] + plain_dot(both, both, NT), carry[1] + plain_dot(ones, both, NT))

    init = (jnp.zeros((2 * LANES, 2 * LANES), F32), jnp.zeros((8, 2 * LANES), F32))
    gram, summed = each_frame(frames, frame, init)
    gram = fold_square(gram)
    summed = fold_right(summed)[0:1]
    gram_ref[0:LANES, :] = gram
    gram_ref[LANES : LANES + 8, :] = rows8(summed)
    w = pad_rows(w_ref[0])
    width = w.shape[1]
    sums = stack_rows(row_dot(summed, w), jnp.sum(w * exact_dot(gram, w), axis=0, keepdims=True))
    count = jnp.full((2, LANES), 1.0, F32) * (total * (SIDE * SIDE)).astype(F32)
    send_all(send_ref, sums, slice(0, width))
    send_all(send_ref, count, slice(width, width + LANES))


def prepare_kernel(counts_ref, video_ref, cot_ref, x_ref, rows_ref, columns_ref, cot_out_ref):
    order = column_order()
    total = live_frames(counts_ref)
    for part in range(video_ref.shape[1] // LANES):
        at = slice(part * LANES, (part + 1) * LANES)
        block = pad_rows(video_ref[:, at] * live_value(part // 2, total))
        high, middle, low = pick_thirds(order, block, NT, True)
        x_ref[at, :] = high + middle + low
        rows_ref[at, :] = jnp.concatenate([high, middle], axis=1).astype(jnp.bfloat16)
        columns_ref[:, at] = jnp.concatenate([high.T, middle.T], axis=0).astype(jnp.bfloat16)
    spot = lax.broadcasted_iota(jnp.int32, (LANES, LANES), 1)
    for part in range(cot_ref.shape[1] // LANES):
        at = slice(part * LANES, (part + 1) * LANES)
        frame = (spot + part * LANES) // (HALF_ROWS * 8)
        cot_out_ref[at, :] = jnp.where(frame < total, pad_rows(cot_ref[:, at]), 0.0).T


def moments_of(sums, count):
    average = sums[0:1] / count
    return (average, sums[1:2] / count - average * average)


def narrow_kernel(
    counts_ref, sums_ref, stat_ref, gram0_ref, x_ref, z_ref, ngain_ref, nbias_ref, w_ref,
    x1_ref, rows_ref, columns_ref, gram_ref, stat_out_ref, send_ref,
):
    total = live_frames(counts_ref)
    count = stat_ref[2:3, 0:LANES]
    average, variance = moments_of(row_total(sums_ref), count)
    factor = ngain_ref[0:1, :] * lax.rsqrt(variance + EPSILON)
    shift = nbias_ref[0:1, :] - factor * average
    stat_out_ref[...] = rows8(average, variance, count)
    frames = x_ref.shape[0] // 256

    def frame(t, carry):
        gram, cross, summed = carry
        at = pl.ds(pl.multiple_of(t * 256, 256), 256)
        z = z_ref[at, :]
        rows = (x_ref[at, :] + factor * z + shift) * live_value(t, total)
        x1_ref[at, :] = rows
        both = side_by_side(rows)
        rows_ref[at, :] = both
        columns = jnp.concatenate(halves(rows.T), axis=0)
        columns_ref[:, at] = columns
        gram = gram + plain_dot(columns, both)
        cross = cross + plain_dot(columns, side_by_side(z))
        return (gram, cross, summed + jnp.sum(rows, axis=0, keepdims=True))

    zero = jnp.zeros((2 * LANES, 2 * LANES), F32)
    gram, cross, summed = each_frame(frames, frame, (zero, zero, jnp.zeros((1, LANES), F32)))

    gram = fold_square(gram)
    tiles = LANES // 8
    gram_ref[0:tiles] = gram.reshape(tiles, 8, LANES)
    gram_ref[tiles : 2 * tiles] = fold_square(cross).reshape(tiles, 8, LANES)
    gram_ref[2 * tiles : 3 * tiles] = gram0_ref[0:LANES, :].reshape(tiles, 8, LANES)
    gram_ref[3 * tiles] = rows8(summed, gram0_ref[LANES : LANES + 1, :])
    w = pad_rows(w_ref[0])
    sums = stack_rows(row_dot(summed, w), jnp.sum(w * exact_dot(gram, w), axis=0, keepdims=True))
    send_all(send_ref, sums, slice(0, w.shape[1]))


def write_first(t, total, values, scale, shift, a_ref, b_ref):
    half_pre = values * scale + shift
    first = (half_pre + half_pre * half_tanh(half_pre)) * live_value(t, total)
    first = first.reshape(SIDE, 2, 8, LANES)
    even = first[:, 0]
    odd = first[:, 1]
    if b_ref is None:
        a_ref[t, 0, 1 : SIDE + 1] = even
        a_ref[t, 1, 1 : SIDE + 1] = odd
        a_ref[t, 2, 1 : SIDE + 1] = columns_down(odd)
        return
    for ref, plane, values in ((a_ref, 0, even), (a_ref, 1, odd), (b_ref, 0, columns_down(odd)), (b_ref, 1, columns_up(even))):
        for place, part in enumerate(row_pairs(values)):
            ref[t, plane, place] = part


def expand_kernel(
    block, counts_ref, sums_ref, count_ref, rows_ref, w_ref, gain_ref, bias_ref, taps_ref,
    e_ref, d_ref, stat_ref, send_ref, a_ref, taps8_ref, *pair_refs,
):
    b_ref, m_ref = pair_refs if pair_refs else (None, None)
    if block:
        clear_edges(a_ref)
    total = live_frames(counts_ref)
    frames = a_ref.shape[0]
    count = count_ref[2:3, :] if block else row_total(count_ref)[0:1]
    average, variance = moments_of(row_total(sums_ref), count)
    stat_ref[...] = rows8(average, variance, count)
    norm_row = 2 * block
    scale = gain_ref[norm_row : norm_row + 1, :] * lax.rsqrt(variance + EPSILON)
    shift = 0.5 * (bias_ref[norm_row : norm_row + 1, :] - average * scale)
    scale = 0.5 * scale
    square = right_square(pad_rows(w_ref[0]))

    def expand(t, carry):
        at = pl.ds(pl.multiple_of(t * 256, 256), 256)
        values = fold_right(plain_dot(rows_ref[at, :], square)).reshape(FULL_ROWS, 8, LANES)
        e_ref[pl.ds(pl.multiple_of(t * FULL_ROWS, FULL_ROWS), FULL_ROWS)] = values
        write_first(t, total, values, scale, shift, a_ref, b_ref)
        return carry

    each_frame(frames, expand, 0)
    per_frame = HALF_ROWS if block else FULL_ROWS
    if block:
        spread_taps(taps_ref, taps8_ref)
        conv = functools.partial(conv_half, a_ref=a_ref, w_ref=taps8_ref, d_ref=d_ref)
    else:
        spread_pairs(taps_ref, taps8_ref)
        conv = functools.partial(conv_full, a_ref=a_ref, b_ref=b_ref, w_ref=taps8_ref, m_ref=m_ref)

    def frame(t, carry):
        conv(t, 0, fresh=True)
        last = jnp.minimum(place_of(counts_ref, t), LAGS - 1)

        def lag(k, inner):
            conv(t, k, fresh=False)
            return inner

        lax.fori_loop(1, last + 1, lag, 0)
        if not block:
            d_ref[pl.ds(t * per_frame, per_frame)] = pair_rows(m_ref[...])
        values = d_ref[pl.ds(t * per_frame, per_frame)]
        return (carry[0] + jnp.sum(values, axis=0), carry[1] + jnp.sum(values * values, axis=0))

    zero = jnp.zeros((8, LANES), F32)
    summed, squares = lax.fori_loop(0, total, frame, (zero, zero))

    def dead(t, carry):
        d_ref[pl.ds(t * per_frame, per_frame)] = jnp.zeros((per_frame, 8, LANES), F32)
        return carry

    lax.fori_loop(total, frames, dead, 0)
    sums = stack_rows(jnp.sum(summed, axis=0, keepdims=True), jnp.sum(squares, axis=0, keepdims=True))
    send_all(send_ref, sums, slice(0, LANES))


def live_value(t, total):
    return jnp.where(t < total, 1.0, 0.0).astype(F32)


def each_frame(count, body, init):
    return lax.fori_loop(0, count, body, init, unroll=min(8, count))


def lanes_of(ref, tile):
    if ref.shape[-1] == LANES:
        return slice(None)
    return pl.ds(pl.multiple_of(tile * LANES, LANES), LANES)


def squeeze_forward_kernel(
    block, counts_ref, sums_ref, stat_ref, d_ref, gain_ref, bias_ref, down_ref, downb_ref, up_ref, upb_ref, proj_ref,
    cot_ref, z_ref, gates_ref, running_ref, pre_ref, stat_out_ref, send_ref, second_ref, pooled_ref,
):
    step = pl.program_id(0)
    steps = pl.num_programs(0)
    tiles = second_ref.shape[0]
    total = live_frames(counts_ref)
    per_frame = HALF_ROWS if block else FULL_ROWS
    pixels = per_frame * 8
    frames = second_ref.shape[1] // per_frame
    group = 256 // pixels
    chunks = frames // group
    norm_row = 2 * block + 1

    def activate(tile, carry):
        lanes = lanes_of(d_ref, tile)
        count = stat_ref[2:3, lanes] * (0.25 if block else 1.0)
        average, variance = moments_of(row_total(sums_ref, lanes), count)
        stat_out_ref[:, lanes] = rows8(average, variance, count)
        scale = gain_ref[norm_row : norm_row + 1, lanes] * lax.rsqrt(variance + EPSILON)
        shift = 0.5 * (bias_ref[norm_row : norm_row + 1, lanes] - average * scale)
        scale = 0.5 * scale

        def chunk(index, inside):
            for inner in range(group):
                t = index * group + inner
                at = pl.ds(t * per_frame, per_frame)
                half_pre = d_ref[at, :, lanes] * scale + shift
                second = half_pre + half_pre * half_tanh(half_pre)
                second = second * live_value(t, total)
                second_ref[tile, at] = second
                pooled_ref[tile, pl.ds(t, 1), :] = tile_sum(second) * (1.0 / pixels)
            return inside

        each_frame(chunks, chunk, 0)
        return carry

    if block:
        lax.fori_loop(0, tiles, activate, 0, unroll=tiles)
    else:
        activate(step, 0)

    def project(tile, carry):
        lanes = lanes_of(gates_ref, tile)
        square = right_square_t(pad_rows(proj_ref[0, :, lanes]))
        gates = gates_ref[:, lanes]

        def chunk(index, inside):
            parts = []
            for inner in range(group):
                t = index * group + inner
                second = second_ref[tile, pl.ds(t * per_frame, per_frame)].reshape(pixels, LANES)
                parts.append(second * pick_row(gates, t))
            excited = parts[0] if group == 1 else jnp.concatenate(parts, axis=0)
            at = pl.ds(pl.multiple_of(index * 256, 256), 256)
            z_ref[at, :] = z_ref[at, :] + fold_right(plain_dot(side_by_side(excited), square, NT))
            return inside

        each_frame(chunks, chunk, 0)
        return carry

    @pl.when(step == steps - 1)
    def gate_and_project():
        matrix = running_matrix(counts_ref, frames)
        pooled = jnp.concatenate([pooled_ref[index] for index in range(tiles)], axis=1)
        running = exact_dot(matrix, pooled)
        running_ref[...] = running
        pre = skinny_dot(running, down_ref[0], NT) + downb_ref[block : block + 1, :]
        pre_ref[...] = pre
        gates_ref[...] = sigmoid(skinny_dot(pre * sigmoid(pre), up_ref[0]) + upb_ref[block : block + 1, :])
        z_ref[...] = jnp.zeros_like(z_ref)
        lax.fori_loop(0, tiles, project, 0, unroll=tiles if block else 1)

        def chunk(index, carry):
            at = pl.ds(pl.multiple_of(index * 256, 256), 256)
            z = z_ref[at, :].reshape(32, 8, LANES)
            values = [z, z * z]
            if block:
                dy = cot_ref[at, :].reshape(32, 8, LANES)
                values = values + [dy, dy * z]
            return tuple(old + jnp.sum(new, axis=0) for old, new in zip(carry, values))

        zero = jnp.zeros((8, LANES), F32)
        sums = each_frame(chunks, chunk, (zero,) * (4 if block else 2))
        rows = stack_rows(*(jnp.sum(value, axis=0, keepdims=True) for value in sums))
        send_all(send_ref, rows, slice(0, LANES))


def put_lists(core_ref, refs, writes):
    size = refs[0].shape[0]

    for core in range(2):
        @pl.when(core_ref[0] == core)
        def write(core=core):
            for at, values in writes:
                for half in range(2):
                    begin = max(at, half * size)
                    end = min(at + values.shape[0], (half + 1) * size)
                    if begin < end:
                        refs[half ^ core][begin - half * size : end - half * size] = values[begin - at : end - at]


def put_tile_list(core_ref, refs, at, values):
    size = refs[0].shape[0]
    half = jnp.where(at >= size, 1, 0)
    place = pl.ds(at - half * size, values.shape[0])
    for other in range(2):
        @pl.when((core_ref[0] == half) == (other == 0))
        def write(other=other):
            refs[other][place] = values


def pack_tiles(narrow, squeeze):
    return narrow // 8 + 2 * (squeeze // 8) + 1


def squeeze_backward_body(
    block, counts_ref, stat_ref, d_ref, gain_ref, bias_ref, down_ref, up_ref, proj_ref, gates_ref, running_ref,
    pre_ref, dy2_ref, send_ref, core_ref, list_refs, dz3_ref, dz3t_ref, total_ref, dexc_ref, dgate_ref, head,
):
    total = live_frames(counts_ref)
    per_frame = HALF_ROWS if block else FULL_ROWS
    pixels = per_frame * 8
    frames = dz3_ref.shape[0] // pixels
    group = 256 // pixels
    chunks = frames // group
    norm_row = 2 * block + 1
    tiles = dexc_ref.shape[0]
    narrow = proj_ref.shape[1]
    squeeze = down_ref.shape[1]
    per_tile = pack_tiles(narrow, squeeze)

    def norm_of(tile):
        lanes = lanes_of(d_ref, tile)
        average = stat_ref[0:1, lanes]
        root = lax.rsqrt(stat_ref[1:2, lanes] + EPSILON)
        scale = gain_ref[norm_row : norm_row + 1, lanes] * root
        shift = 0.5 * (bias_ref[norm_row : norm_row + 1, lanes] - average * scale)
        return (lanes, average, root, 0.5 * scale, shift)

    def excite(tile, carry):
        lanes, _, _, scale, shift = norm_of(tile)
        gates = gates_ref[:, lanes_of(gates_ref, tile)]
        square = right_square(pad_rows(proj_ref[0, :, lanes]))

        def chunk(index, inside):
            flat = pl.ds(pl.multiple_of(index * 256, 256), 256)
            dexc = fold_right(plain_dot(dz3_ref[flat, :], square)).reshape(32, 8, LANES)
            dexc_ref[tile, pl.ds(pl.multiple_of(index * 32, 32), 32)] = dexc
            parts = []
            for inner in range(group):
                t = index * group + inner
                half_pre = d_ref[pl.ds(t * per_frame, per_frame), :, lanes] * scale + shift
                second = half_pre + half_pre * half_tanh(half_pre)
                second = second * live_value(t, total)
                own = dexc[inner * per_frame : (inner + 1) * per_frame]
                dgate_ref[tile, pl.ds(t, 1), :] = tile_sum(own * second)
                parts.append(second.reshape(pixels, LANES) * pick_row(gates, t))
            excited = parts[0] if group == 1 else jnp.concatenate(parts, axis=0)
            total_ref[...] = total_ref[...] + plain_dot(dz3t_ref[:, flat], side_by_side(excited))
            return inside

        total_ref[...] = jnp.zeros_like(total_ref)
        each_frame(chunks, chunk, 0)
        dproj = fold_square(total_ref[...])
        put_tile_list(core_ref, list_refs, tile * per_tile, dproj[0:narrow].reshape(narrow // 8, 8, LANES))
        return carry

    def squeeze_part():
        pre = pre_ref[...]
        half_pre = 0.5 * pre
        tanh = half_tanh(half_pre)
        squeezed = half_pre + half_pre * tanh
        all_gates = gates_ref[...]
        dgate = jnp.concatenate([dgate_ref[index] for index in range(tiles)], axis=1)
        du = dgate * all_gates * (1.0 - all_gates)
        dpre = skinny_dot(du, up_ref[0], NT) * silu_slope(half_pre, tanh)
        ddown = frame_outer(dpre, running_ref[...])
        dup = frame_outer(squeezed, du)
        dpre_row = jnp.sum(dpre, axis=0, keepdims=True)
        dpre_row = jnp.concatenate([dpre_row, jnp.zeros((1, du.shape[1] - squeeze), F32)], axis=1)
        biases = rows8(jnp.sum(du, axis=0, keepdims=True), dpre_row)
        writes = []
        for index in range(tiles):
            own = slice(index * LANES, (index + 1) * LANES)
            at = index * per_tile + narrow // 8
            writes.append((at, ddown[:, own].reshape(squeeze // 8, 8, LANES)))
            at = at + squeeze // 8
            writes.append((at, dup[:, own].reshape(squeeze // 8, 8, LANES)))
            writes.append((at + squeeze // 8, biases[:, own].reshape(1, 8, LANES)))
        put_lists(core_ref, list_refs, writes)
        drunning = skinny_dot(dpre, down_ref[0])
        dpooled = exact_dot(running_matrix(counts_ref, frames), drunning, TN) * (1.0 / pixels)
        for index in range(tiles):
            dgate_ref[index] = dpooled[:, index * LANES : (index + 1) * LANES]

    def slope(tile, carry):
        lanes, average, root, scale, shift = norm_of(tile)
        gates = gates_ref[:, lanes_of(gates_ref, tile)]

        def chunk(index, inside):
            summed, cross = inside
            for inner in range(group):
                t = index * group + inner
                at = pl.ds(t * per_frame, per_frame)
                depth = d_ref[at, :, lanes]
                half_pre = depth * scale + shift
                dsecond = dexc_ref[tile, at] * pick_row(gates, t) + pick_row(dgate_ref[tile], t)
                dy = dsecond * silu_slope(half_pre, half_tanh(half_pre))
                dy = dy * live_value(t, total)
                dy2_ref[at, :, lanes] = dy
                summed = summed + jnp.sum(dy, axis=0)
                cross = cross + jnp.sum(dy * (depth - average), axis=0)
            return (summed, cross)

        zero = jnp.zeros((8, LANES), F32)
        summed, cross = each_frame(chunks, chunk, (zero, zero))
        rows = stack_rows(jnp.sum(summed, axis=0, keepdims=True), root * jnp.sum(cross, axis=0, keepdims=True))
        send_all(send_ref, rows, lanes)
        return carry

    if block:
        head()
        lax.fori_loop(0, tiles, excite, 0, unroll=tiles)
        squeeze_part()
        lax.fori_loop(0, tiles, slope, 0, unroll=tiles)
    else:
        phase = pl.program_id(0)
        tile = pl.program_id(1)

        @pl.when((phase == 0) & (tile == 0))
        def start():
            head()

        @pl.when(phase == 0)
        def first():
            excite(tile, 0)

        @pl.when((phase == 1) & (tile == 0))
        def between():
            squeeze_part()

        @pl.when(phase == 1)
        def second():
            slope(tile, 0)


def squeeze_one_backward_kernel(
    counts_ref, core_ref, third_ref, z_ref, cot_ref, ngain_ref, nbias_ref, stat_ref, d_ref, gain_ref, bias_ref, down_ref,
    up_ref, proj_ref, gates_ref, running_ref, pre_ref, act_ref, nsum_ref, dy2_ref, send_ref, mine_ref, theirs_ref,
    dz3_ref, dz3t_ref, total_ref, dexc_ref, dgate_ref,
):
    total = live_frames(counts_ref)
    pixels = HALF_ROWS * 8

    def head():
        count = stat_ref[2:3, 0:LANES]
        sums = row_total(third_ref)
        mean, variance = moments_of(sums, count)
        root = lax.rsqrt(variance + EPSILON)
        gain = ngain_ref[1:2, :]
        bias_sum = sums[2:3, :]
        gain_sum = root * (sums[3:4, :] - mean * bias_sum)
        nsum_ref[...] = rows8(gain_sum, bias_sum, mean, variance)
        row = lax.broadcasted_iota(jnp.int32, z_ref.shape, 0) // pixels
        live = row < total
        normed = (z_ref[...] - mean) * root
        act = jnp.where(live, gain * normed + nbias_ref[1:2, :], 0.0)
        act_ref[...] = act.T[0 : act_ref.shape[0]]
        dz3 = gain * root * (cot_ref[...] - bias_sum / count - normed * (gain_sum / count))
        dz3 = jnp.where(live, dz3, 0.0)
        dz3_ref[...] = side_by_side(dz3)
        dz3t_ref[...] = jnp.concatenate(halves(dz3.T), axis=0)

    squeeze_backward_body(
        1, counts_ref, stat_ref, d_ref, gain_ref, bias_ref, down_ref, up_ref, proj_ref, gates_ref, running_ref,
        pre_ref, dy2_ref, send_ref, core_ref, (mine_ref, theirs_ref), dz3_ref, dz3t_ref, total_ref, dexc_ref, dgate_ref, head,
    )


def input_factors(sums, stat_ref, count, gain, w):
    root = lax.rsqrt(stat_ref[1:2, :] + EPSILON)
    factor = gain * root
    matrix = exact_dot(w * (factor * root * sums[1:2] / count), w, NT)
    return (matrix, row_dot(factor * sums[0:1] / count, w, NT))


def covariance(gram, summed, count):
    mean = summed / count
    return (mean, gram / count - outer(mean, mean))


def squeeze_zero_backward_kernel(
    counts_ref, core_ref, top_ref, stat1_ref, gram_ref, nstat_ref, dxpre_ref, x1_ref, z_ref, ngain_ref, w_ref, gains_ref, q_one_ref,
    stat_ref, d_ref, gain_ref, bias_ref, down_ref, up_ref, proj_ref, gates_ref, running_ref, pre_ref,
    dx1_ref, nsum_ref, dy2_ref, send_ref, mine_ref, theirs_ref, dz3_ref, dz3t_ref, total_ref, dexc_ref, dgate_ref,
):
    total = live_frames(counts_ref)
    width = gains_ref.shape[1]

    def head():
        start = pack_tiles(proj_ref.shape[1], down_ref.shape[1]) * (width // LANES)
        put_lists(core_ref, (mine_ref, theirs_ref), [(start, q_one_ref)])
        count = stat_ref[2:3, :]
        wide_count = jnp.broadcast_to(count[:, 0:1], (1, width))
        sums = row_total(top_ref, slice(0, width))
        extra = row_total(top_ref, slice(width, width + LANES))
        matrix, shift = input_factors(sums, stat1_ref, wide_count, gains_ref[2:3, :], pad_rows(w_ref[0]))
        mean = nstat_ref[0:1, :]
        root = lax.rsqrt(nstat_ref[1:2, :] + EPSILON)
        mean_x1 = gram_ref[3 * LANES : 3 * LANES + 1, :] / count
        cross = (gram_ref[LANES : 2 * LANES, :] - count * outer(mean_x1, mean)) * root
        gain_sum = extra[0:1] - jnp.sum(matrix * cross, axis=0, keepdims=True)
        bias_sum = extra[1:2] - count * shift
        nsum_ref[...] = rows8(gain_sum, bias_sum, mean, nstat_ref[1:2, :])
        factor = ngain_ref[0:1, :] * root
        square = right_square(matrix)
        bias_mean = bias_sum / count
        gain_mean = gain_sum / count

        def frame(t, carry):
            at = pl.ds(pl.multiple_of(t * 256, 256), 256)
            centred = side_by_side(x1_ref[at, :] - mean_x1)
            live = live_value(t, total)
            dx1 = (dxpre_ref[at, :] - fold_right(plain_dot(centred, square)) - shift) * live
            dx1_ref[at, :] = dx1
            normed = (z_ref[at, :] - mean) * root
            dz3 = factor * (dx1 - bias_mean - normed * gain_mean) * live
            dz3_ref[at, :] = side_by_side(dz3)
            dz3t_ref[:, at] = jnp.concatenate(halves(dz3.T), axis=0)
            return carry

        each_frame(dz3_ref.shape[0] // 256, frame, 0)

    squeeze_backward_body(
        0, counts_ref, stat_ref, d_ref, gain_ref, bias_ref, down_ref, up_ref, proj_ref, gates_ref, running_ref,
        pre_ref, dy2_ref, send_ref, core_ref, (mine_ref, theirs_ref), dz3_ref, dz3t_ref, total_ref, dexc_ref, dgate_ref, head,
    )

def back_full(t, k, a_ref, w_ref, z_ref, raw_ref, f_ref, dw_ref, fresh):
    weights = [w_ref[k * 12 + tap] for tap in range(12)]
    target = t - k
    sums = [None] * 12
    for m in range(PAIRS):
        for place in range(4):
            flipped = (3, 1, 2, 0)[place]
            left, centre, right = weights[3 * flipped : 3 * flipped + 3]
            b_even, b_odd, b_odd_down, b_even_up = (z_ref[t, plane, place, m] for plane in range(4))
            even = centre * b_even + right * b_odd_down + left * b_odd
            odd = centre * b_odd + right * b_even + left * b_even_up
            if fresh:
                f_ref[target, m, place, 0] = even
                f_ref[target, m, place, 1] = odd
            else:
                f_ref[target, m, place, 0] = f_ref[target, m, place, 0] + even
                f_ref[target, m, place, 1] = f_ref[target, m, place, 1] + odd
            if place in (0, 3):
                row = 0 if place == 0 else 1
                b_even, b_odd, b_odd_down, b_even_up = (raw_ref[t, plane, row, m] for plane in range(4))
            a_even, a_odd = (a_ref[target, plane, place, m] for plane in range(2))
            pieces = (
                b_even_up * a_odd + b_odd * a_even,
                b_even * a_even + b_odd * a_odd,
                b_even * a_odd + b_odd_down * a_even,
            )
            for c in range(3):
                at = 3 * place + c
                sums[at] = pieces[c] if sums[at] is None else sums[at] + pieces[c]
    for place in range(4):
        for c in range(3):
            at = place * 3 * LAGS + k * 3 + c
            dw_ref[at] = dw_ref[at] + sums[3 * place + c]


def pair_taps(totals):
    count = 3 * LAGS
    first, second, third, last = (totals[place * count : (place + 1) * count] for place in range(4))
    middle = 0.5 * (second - third)
    return (first + middle, 0.5 * (second + third), middle - last)


def back_half(t, k, a_ref, w_ref, z_ref, f_ref, dw_ref, fresh):
    weights = [w_ref[k * 9 + tap] for tap in range(9)]
    target = t - k
    sums = [None] * 9

    def put(row, parity, value):
        at = target * FULL_ROWS + 2 * row + parity
        f_ref[at] = value if fresh else f_ref[at] + value

    carried = [a_ref[target, plane, 0] for plane in range(2)]
    here = [z_ref[t, plane, 0] for plane in range(2)]
    for i in range(HALF_ROWS):
        below = [z_ref[t, plane, i + 1] for plane in range(2)]
        dz, dz_up = here
        rows = [carried]
        for need in (2 * i + 1, 2 * i + 2):
            rows.append([a_ref[target, plane, need] for plane in range(2)])
        carried = rows[2]
        put(2 * i, 0, weights[4] * dz)
        put(2 * i, 1, weights[5] * dz + weights[3] * dz_up)
        put(2 * i + 1, 0, weights[7] * dz + weights[1] * below[0])
        put(
            2 * i + 1,
            1,
            weights[8] * dz + weights[6] * dz_up + (weights[2] * below[0] + weights[0] * below[1]),
        )
        for r in range(3):
            a_even, a_odd = rows[r]
            pieces = (dz_up * a_odd, dz * a_even, dz * a_odd)
            for c in range(3):
                at = 3 * r + c
                sums[at] = pieces[c] if sums[at] is None else sums[at] + pieces[c]
        here = below
    for tap in range(9):
        dw_ref[k * 9 + tap] = dw_ref[k * 9 + tap] + sums[tap]


def depth_backward_kernel(
    block, before, final, counts_ref, grads_ref, stat2_ref, stat_ref, nstat_ref, dy2_ref, d_ref, e_ref, a_ref, columns_ref, w_ref,
    gain_ref, bias_ref, taps_ref, z3_ref, dx_in_ref, sums_in_ref, list_in_ref, dxpre_ref, send_ref, q_ref, grad_rows_ref,
    z_ref, f_ref, taps8_ref, dw_ref, total_ref, *raw_refs,
):
    tile = pl.program_id(0)
    tiles = pl.num_programs(0)
    total = live_frames(counts_ref)
    frames = a_ref.shape[0]
    norm_row = 2 * block
    half = block == 1
    per_frame = HALF_ROWS if half else FULL_ROWS
    taps = taps_ref.shape[1]

    @pl.when(tile == 0)
    def start():
        if half:
            clear_edges(z_ref)
        if before:
            dxpre_ref[...] = dx_in_ref[...]
            send_all(send_ref, sums_in_ref[0:2, :], slice(0, before * LANES))
            q_ref[0 : list_in_ref.shape[0]] = list_in_ref[...]
        else:
            dxpre_ref[...] = jnp.zeros_like(dxpre_ref)

        def dead(t, carry):
            if half:
                f_ref[pl.ds(t * FULL_ROWS, FULL_ROWS)] = jnp.zeros((FULL_ROWS, 8, LANES), F32)
            else:
                f_ref[t] = jnp.zeros(f_ref.shape[1:], F32)
            return carry

        lax.fori_loop(total, frames, dead, 0)

    count = stat2_ref[2:3, :]
    grads = row_total(grads_ref)
    grad_rows_ref[...] = rows8(grads[0:1], grads[1:2])
    average = stat2_ref[0:1, :]
    root = lax.rsqrt(stat2_ref[1:2, :] + EPSILON)
    scale_two = gain_ref[norm_row + 1 : norm_row + 2, :] * root
    slope = scale_two * root * grads[1:2] / count
    level = scale_two * grads[0:1] / count - slope * average
    average_one = stat_ref[0:1, :]
    root_one = lax.rsqrt(stat_ref[1:2, :] + EPSILON)
    scale_one = gain_ref[norm_row : norm_row + 1, :] * root_one
    shift_half = 0.5 * (bias_ref[norm_row : norm_row + 1, :] - average_one * scale_one)
    scale_half = 0.5 * scale_one

    def fill(t, carry):
        at = pl.ds(t * per_frame, per_frame)
        dz = scale_two * dy2_ref[at] - (slope * d_ref[at] + level)
        if half:
            z_ref[t, 0, 0:HALF_ROWS] = dz
            z_ref[t, 1, 0:HALF_ROWS] = columns_up(dz)
        else:
            pair = dz.reshape(SIDE, 2, 8, LANES)
            even = pair[:, 0]
            odd = pair[:, 1]
            for plane, values in enumerate((even, odd, columns_down(odd), columns_up(even))):
                for place, part in enumerate(row_pairs(values)):
                    z_ref[t, plane, place] = part
                rows = values.reshape(PAIRS, 2, 8, LANES)
                raw_refs[0][t, plane, 0] = rows[:, 0]
                raw_refs[0][t, plane, 1] = rows[:, 1]
        return carry

    each_frame(frames, fill, 0)
    dw_ref[...] = jnp.zeros_like(dw_ref)
    refs = dict(a_ref=a_ref, w_ref=taps8_ref, z_ref=z_ref, f_ref=f_ref, dw_ref=dw_ref)
    if half:
        spread_taps(taps_ref, taps8_ref)
        back = functools.partial(back_half, **refs)
    else:
        spread_pairs(taps_ref, taps8_ref)
        back = functools.partial(back_full, raw_ref=raw_refs[0], **refs)

    def frame(t, carry):
        back(t, 0, fresh=True)
        last = jnp.minimum(place_of(counts_ref, t), LAGS - 1)

        def lag(k, inner):
            back(t, k, fresh=False)
            return inner

        return lax.fori_loop(1, last + 1, lag, carry)

    lax.fori_loop(0, total, frame, 0)
    square = right_square_t(pad_rows(w_ref[0]) * scale_one)
    total_ref[...] = jnp.zeros_like(total_ref)

    def finish(t, carry):
        rows = pl.ds(pl.multiple_of(t * FULL_ROWS, FULL_ROWS), FULL_ROWS)
        flat = pl.ds(pl.multiple_of(t * 256, 256), 256)
        values = e_ref[rows]
        half_pre = values * scale_half + shift_half
        dfirst = f_ref[rows] if half else pair_rows(f_ref[t])
        dy = dfirst * silu_slope(half_pre, half_tanh(half_pre))
        summed = carry[0] + jnp.sum(dy, axis=0)
        cross = carry[1] + jnp.sum(dy * (values - average_one), axis=0)
        dy = dy.reshape(256, LANES)
        both = side_by_side(dy)
        total_ref[...] = total_ref[...] + plain_dot(columns_ref[:, flat], both)
        dxpre_ref[flat, :] = dxpre_ref[flat, :] + fold_right(plain_dot(both, square, NT))
        return (summed, cross)

    zero = jnp.zeros((8, LANES), F32)
    summed, cross = each_frame(frames, finish, (zero, zero))
    rows = stack_rows(jnp.sum(summed, axis=0, keepdims=True), root_one * jnp.sum(cross, axis=0, keepdims=True))
    if final:
        send_all(send_ref, rows, pl.ds(pl.multiple_of((tile + before) * LANES, LANES), LANES))
    else:
        send_ref[...] = rows8(rows[0:1], rows[1:2])
    gathered = fold_square(total_ref[...])
    narrow = w_ref.shape[1]
    dtaps = jnp.sum(dw_ref[...], axis=1)
    parts = (dtaps,) if half else pair_taps(dtaps)
    unused = jnp.zeros(((-taps) % 8, LANES), F32)
    values = jnp.concatenate((gathered[0:narrow],) + parts + (unused,), axis=0)
    listed = values.shape[0] // 8
    q_ref[pl.ds((tile + before) * listed, listed)] = values.reshape(listed, 8, LANES)

    if half:
        @pl.when(tile == tiles - 1)
        def tail():
            mean = nstat_ref[0:1, :]
            root_three = lax.rsqrt(nstat_ref[1:2, :] + EPSILON)

            def part(t, carry):
                flat = pl.ds(pl.multiple_of(t * 256, 256), 256)
                dx = dxpre_ref[flat, :].reshape(32, 8, LANES)
                normed = ((z3_ref[flat, :] - mean) * root_three).reshape(32, 8, LANES)
                return (carry[0] + jnp.sum(dx * normed, axis=0), carry[1] + jnp.sum(dx, axis=0))

            cross_three, summed_three = each_frame(frames, part, (zero, zero))
            rows = stack_rows(
                jnp.sum(cross_three, axis=0, keepdims=True), jnp.sum(summed_three, axis=0, keepdims=True)
            )
            width = send_ref.shape[2] - LANES
            send_all(send_ref, rows, slice(width, width + LANES))


def finish_kernel(
    counts_ref, momentum_ref, gram_ref, stat01_ref, stat02_ref, stat11_ref, stat12_ref, grad0_ref,
    grad1_ref, one_ref, zero_ref, nsum0_ref, nsum1_ref, dxpre_ref, x_ref, dx1_ref, w_ref, gain_ref, means_ref, vars_ref,
    nmeans_ref, nvars_ref,
    video_ref, less_ref, factor_ref, wgain_ref, wbias_ref, ngain_ref, nbias_ref, newm_ref, newv_ref, newnm_ref, newnv_ref,
):
    total = live_frames(counts_ref)
    full = stat01_ref[2:3, :]
    count = full[:, 0:LANES]
    width = full.shape[1]
    top_zero = row_total(zero_ref)
    top_one = row_total(one_ref, slice(0, width))
    w_zero = pad_rows(w_ref[0])
    matrix, shift = input_factors(top_zero, stat01_ref, full, gain_ref[0:1, :], w_zero)
    square = right_square(matrix)
    mean_x, cov_zero = covariance(
        gram_ref[2 * LANES : 3 * LANES, :], gram_ref[3 * LANES + 1 : 3 * LANES + 2, :], count
    )
    order = column_order()
    narrow = video_ref.shape[0]

    def frame(t, carry):
        at = pl.ds(pl.multiple_of(t * 256, 256), 256)
        centred = side_by_side(x_ref[at, :] - mean_x)
        dx = (dxpre_ref[at, :] - fold_right(plain_dot(centred, square)) - shift) * live_value(t, total) + dx1_ref[at, :]
        for part in range(2):
            own = dx[part * LANES : (part + 1) * LANES].T[0:narrow]
            pieces = pick_thirds(order, own, NN, False)
            start = pl.multiple_of(t * 256 + part * LANES, LANES)
            video_ref[:, pl.ds(start, LANES)] = pieces[0] + pieces[1] + pieces[2]
        return carry

    each_frame(x_ref.shape[0] // 256, frame, 0)
    mean_one, cov_one = covariance(gram_ref[0:LANES, :], gram_ref[3 * LANES : 3 * LANES + 1, :], count)
    plan = ((mean_x, cov_zero, stat01_ref, top_zero, w_zero), (mean_one, cov_one, stat11_ref, top_one, pad_rows(w_ref[1])))
    for block, (mean_row, cov, stat_ref, top, w) in enumerate(plan):
        root = lax.rsqrt(stat_ref[1:2, :] + EPSILON)
        factor = gain_ref[2 * block : 2 * block + 1, :] * root
        less = outer(mean_row, top[0:1]) + exact_dot(cov, w) * (root * top[1:2])
        less_ref[block] = (less * factor)[0:narrow]
        factor_ref[8 * block : 8 * block + 8, :] = rows8(factor)
    momentum = momentum_ref[0].astype(F32) / 10.0
    wgain_ref[...] = stack_rows(top_zero[1:2], grad0_ref[1:2, :], top_one[1:2], grad1_ref[1:2, :])
    wbias_ref[...] = stack_rows(top_zero[0:1], grad0_ref[0:1, :], top_one[0:1], grad1_ref[0:1, :])
    stats = (stat01_ref, stat02_ref, stat11_ref, stat12_ref)
    means = stack_rows(*(ref[0:1, :] for ref in stats))
    variances = stack_rows(*(ref[1:2, :] * (ref[2:3, :] / (ref[2:3, :] - 1.0)) for ref in stats))
    newm_ref[...] = (1.0 - momentum) * means_ref[...] + momentum * means
    newv_ref[...] = (1.0 - momentum) * vars_ref[...] + momentum * variances
    ngain_ref[...] = stack_rows(nsum0_ref[0:1, :], nsum1_ref[0:1, :])[:, 0:narrow]
    nbias_ref[...] = stack_rows(nsum0_ref[1:2, :], nsum1_ref[1:2, :])[:, 0:narrow]
    means = stack_rows(nsum0_ref[2:3, :], nsum1_ref[2:3, :])[:, 0:narrow]
    quarter = 0.25 * count
    variances = stack_rows(
        nsum0_ref[3:4, :] * (count / (count - 1.0)), nsum1_ref[3:4, :] * (quarter / (quarter - 1.0))
    )[:, 0:narrow]
    newnm_ref[...] = (1.0 - momentum) * nmeans_ref[...] + momentum * means
    newnv_ref[...] = (1.0 - momentum) * nvars_ref[...] + momentum * variances


def list_rows(core_ref, pair, at, count):
    first_core = core_ref[0] == 0
    mine, other = pair[0:2]
    if len(pair) > 2:
        share = pair[2]
        half = mine.shape[0] * share

        def run(ref, begin, size):
            pieces = []
            while size:
                length = min(size, share - begin % share)
                pieces.append(ref[begin // share, begin % share : begin % share + length])
                begin = begin + length
                size = size - length
            return pieces[0] if len(pieces) == 1 else jnp.concatenate(pieces, axis=0)
    else:
        half = mine.shape[0]

        def run(ref, begin, size):
            return ref[begin : begin + size]

    pieces = []
    if at < half:
        size = min(count, half - at)
        pieces.append(jnp.where(first_core, run(mine, at, size), run(other, at, size)))
        count = count - size
        at = at + size
    if count:
        pieces.append(jnp.where(first_core, run(other, at - half, count), run(mine, at - half, count)))
    values = pieces[0] if len(pieces) == 1 else jnp.concatenate(pieces, axis=0)
    return values.reshape(-1, LANES)


def lists_kernel(
    share, core_ref, pack0_ref, pack0_other_ref, pack1_ref, pack1_other_ref, less_ref, factor_ref,
    dw_ref, dtaps_ref, ddown_ref, dup_ref, dproj_ref, dupb_ref, ddownb_ref,
):
    narrow = dw_ref.shape[1]
    taps = dtaps_ref.shape[1]
    squeeze = ddown_ref.shape[1]
    tiles = dw_ref.shape[2] // LANES
    per_pack = pack_tiles(narrow, squeeze)
    per_tile = narrow // 8 + -(-taps // 8)
    packs = ((pack0_ref, pack0_other_ref, share), (pack1_ref, pack1_other_ref))
    for block in range(2):
        down_rows = []
        for tile in range(tiles):
            lanes = slice(tile * LANES, (tile + 1) * LANES)
            at = tile * per_pack
            dproj_ref[block, :, lanes] = list_rows(core_ref, packs[block], at, narrow // 8)
            at = at + narrow // 8
            ddown_ref[block, :, lanes] = list_rows(core_ref, packs[block], at, squeeze // 8)
            at = at + squeeze // 8
            dup_ref[block, :, lanes] = list_rows(core_ref, packs[block], at, squeeze // 8)
            biases = list_rows(core_ref, packs[block], at + squeeze // 8, 1)
            dupb_ref[block : block + 1, lanes] = biases[0:1]
            down_rows.append(biases[1:2])
        ddownb_ref[block : block + 1, :] = jnp.concatenate(down_rows, axis=1)[:, 0:squeeze]
    for tile in range(tiles):
        lanes = slice(tile * LANES, (tile + 1) * LANES)
        values = list_rows(core_ref, packs[0], per_pack * tiles + tile * per_tile, per_tile)
        dw_ref[0, :, lanes] = values[0:narrow] * factor_ref[8:9, lanes] - less_ref[0, :, lanes]
        dtaps_ref[0, :, lanes] = values[narrow : narrow + taps]


def last_kernel(core_ref, late_ref, late_other_ref, less_ref, factor_ref, _, __, dw_ref, dtaps_ref):
    narrow = dw_ref.shape[1]
    taps = dtaps_ref.shape[1]
    per_tile = narrow // 8 + -(-taps // 8)
    for tile in range(dw_ref.shape[2] // LANES):
        lanes = slice(tile * LANES, (tile + 1) * LANES)
        values = list_rows(core_ref, (late_ref, late_other_ref), tile * per_tile, per_tile)
        dw_ref[0, :, lanes] = values[0:narrow] * factor_ref[0:1, lanes] - less_ref[0, :, lanes]
        for r in range(3):
            for k in range(LAGS):
                source = narrow + r * 3 * LAGS + 3 * k
                dtaps_ref[0, k * 9 + 3 * r : k * 9 + 3 * r + 3, lanes] = values[source : source + 3]


AXES = ("dp", "z", "core")
CHIPS = ("dp", "z")


def exchange(send):
    return lax.all_to_all(send, AXES, 0, 0, tiled=True)


def together(*values):
    return lax.optimization_barrier(values)


def swap_cores(values):
    return lax.ppermute(values, "core", [(0, 1), (1, 0)])


def add_cores(tiles):
    core = lax.axis_index("core")
    pair = tiles.reshape(2, tiles.shape[0] // 2, *tiles.shape[1:])
    mine = lax.dynamic_index_in_dim(pair, core, 0, keepdims=False)
    return mine + swap_cores(lax.dynamic_index_in_dim(pair, 1 - core, 0, keepdims=False))


def share_out(tiles, names=CHIPS):
    count = 1
    for name in names:
        count = count * lax.axis_size(name)
    return lax.all_to_all(tiles.reshape(count, -1, *tiles.shape[1:]), names, 0, 0, tiled=True)


def share_back(pieces, names=CHIPS):
    own = jnp.sum(pieces, axis=0)
    everyone = lax.all_to_all(jnp.broadcast_to(own[None], pieces.shape), names, 0, 0, tiled=True)
    return everyone.reshape(-1, *pieces.shape[2:])


def shape(*dims, kind=F32):
    return jax.ShapeDtypeStruct(dims, kind)


def whole(array):
    rank = len(array.shape)
    return pl.BlockSpec(array.shape, lambda *ids: (0,) * rank)


SCALARS = pl.BlockSpec(memory_space=pltpu.SMEM)


def call(kernel, grid, in_specs, out_specs, out_shape, scratch, args, vmem=VMEM_BYTES, aliases=None):
    return pl.pallas_call(
        kernel,
        grid=grid,
        in_specs=in_specs,
        out_specs=out_specs,
        out_shape=out_shape,
        scratch_shapes=scratch,
        compiler_params=pltpu.CompilerParams(vmem_limit_bytes=vmem),
        input_output_aliases=aliases or {},
        cost_estimate=pl.CostEstimate(
            flops=1_000_000_000, bytes_accessed=1_000_000, transcendentals=0
        ),
    )(*args)


def simple_call(kernel, scalars, args, outs):
    return call(
        kernel, (1,), [SCALARS] * scalars + [whole(array) for array in args[scalars:]], [whole(item) for item in outs],
        outs, [], args,
    )


def local(
    video, frame_counts, momentum_index, expand_weight, wide_gains, wide_biases, narrow_gains, narrow_biases, depth_weight,
    squeeze_weight, squeeze_bias, excite_weight, excite_bias, project_weight, wide_means, wide_variances, narrow_means,
    narrow_variances, cotangent,
):
    devices = lax.axis_size("dp") * lax.axis_size("z") * lax.axis_size("core")
    cin, pixels = video.shape
    half_pixels = cotangent.shape[1]
    width = expand_weight.shape[1]
    squeeze = squeeze_weight.shape[1]
    frames = pixels // (SIDE * SIDE)
    tiles = width // LANES
    taps = depth_weight.shape[1]
    w_t = jnp.swapaxes(expand_weight, 1, 2)
    up_t = jnp.swapaxes(excite_weight, 1, 2)
    lanes_pad = ((0, 0), (0, LANES - cin))
    ngains = jnp.pad(narrow_gains, lanes_pad)
    nbiases = jnp.pad(narrow_biases, lanes_pad)
    full_rows = frames * FULL_ROWS
    half_rows = frames * HALF_ROWS
    low = jnp.bfloat16
    core = lax.axis_index("core").astype(jnp.int32).reshape(1)

    def round_up(count):
        return -(-count // devices) * devices

    def fixed(*dims):
        return pl.BlockSpec(dims, lambda *ids: (0,) * len(dims))

    def tile_rows(rows):
        return pl.BlockSpec((rows, LANES), lambda j: (0, j))

    def tile_cube(rows):
        return pl.BlockSpec((rows, 8, LANES), lambda j: (0, 0, j))

    def tile_sums(rows=2):
        return pl.BlockSpec((devices, rows, LANES), lambda j: (0, 0, j))

    def weight_tile(block, rows):
        return pl.BlockSpec((1, rows, LANES), lambda j, block=block: (block, 0, j))

    def of_block(block, rows, lanes):
        return pl.BlockSpec((1, rows, lanes), lambda *ids: (block, 0, 0))

    def early(make):
        return make(lambda p, j: j * (1 - p) + (tiles - 1) * p)

    def late(make):
        return make(lambda p, j: j * p)

    def both(make):
        return make(lambda p, j: j)

    def rows_at(rows):
        return lambda at: pl.BlockSpec((rows, LANES), lambda p, j: (0, at(p, j)))

    def cube_at(rows):
        return lambda at: pl.BlockSpec((rows, 8, LANES), lambda p, j: (0, 0, at(p, j)))

    def sums_at(rows):
        return lambda at: pl.BlockSpec((devices, rows, LANES), lambda p, j: (0, 0, at(p, j)))

    def weight_at(block, rows):
        return lambda at: pl.BlockSpec((1, rows, LANES), lambda p, j: (block, 0, at(p, j)))

    gram_zero, sums = call(
        gram_kernel, (1,), [SCALARS, whole(video), of_block(0, cin, width)],
        [fixed(LANES + 8, LANES), fixed(devices, 2, width + LANES)],
        [shape(LANES + 8, LANES), shape(devices, 2, width + LANES)],
        [], (frame_counts, video, w_t), vmem=60 * 1024 * 1024,
    )
    x, x_rows, x_columns, cot = simple_call(
        prepare_kernel, 1, (frame_counts, video, cotangent),
        [shape(pixels, LANES), shape(pixels, 2 * LANES, kind=low), shape(2 * LANES, pixels, kind=low),
         shape(half_pixels, LANES)],
    )
    sums = exchange(sums)

    def planes_shape(block, lanes, planes):
        if block:
            return (frames, planes, SIDE + 2, 8, lanes)
        return (frames, planes, 4, PAIRS, 8, lanes)

    def planes_of(block, planes, begin=0):
        dims = planes_shape(block, LANES, planes)
        zeros = (0,) * (len(dims) - 1)
        return pl.BlockSpec(dims, lambda j: zeros + (j + begin,))

    def expand(block, sums, count, count_spec, rows):
        depth_rows = half_rows if block else full_rows
        planes = 3 if block else 2
        scratch = [pltpu.VMEM((taps if block else 12 * LAGS, 8, LANES), F32)]
        if not block:
            scratch = scratch + [pltpu.VMEM(planes_shape(0, LANES, 2), F32), pltpu.VMEM((PAIRS, 4, 2, 8, LANES), F32)]
        return call(
            functools.partial(expand_kernel, block), (tiles,),
            [SCALARS, tile_sums(), count_spec, whole(rows), weight_tile(block, cin), tile_rows(4), tile_rows(4),
             weight_tile(block, taps)],
            [tile_cube(full_rows), tile_cube(depth_rows), tile_rows(8), tile_sums(), planes_of(block, planes)],
            [shape(full_rows, 8, width), shape(depth_rows, 8, width), shape(8, width), shape(devices, 2, width),
             shape(*planes_shape(block, width, planes))],
            scratch,
            (frame_counts, sums, count, rows, w_t, wide_gains, wide_biases, depth_weight),
        )

    count_spec = pl.BlockSpec((devices, 2, LANES), lambda j: (0, 0, tiles))
    e_zero, d_zero, stat01, sums, planes_zero = expand(0, sums, sums, count_spec, x_rows)
    sums = exchange(sums)

    def squeeze_forward(block, sums, stat, depth):
        rows = half_rows if block else full_rows
        kinds = 4 if block else 2
        moving = [tile_sums(), tile_rows(8), tile_cube(rows), tile_rows(4), tile_rows(4)]
        if block:
            moving = [whole(array) for array in (sums, stat, depth, wide_gains, wide_biases)]
        return call(
            functools.partial(squeeze_forward_kernel, block), (1 if block else tiles,),
            [SCALARS] + moving
            + [of_block(block, squeeze, width), whole(squeeze_bias), of_block(block, squeeze, width), whole(excite_bias),
               of_block(block, cin, width), whole(cot)],
            [fixed(rows * 8, LANES), fixed(8, width), fixed(8, width), fixed(8, squeeze),
             fixed(8, width) if block else tile_rows(8), fixed(devices, kinds, LANES)],
            [shape(rows * 8, LANES), shape(8, width), shape(8, width), shape(8, squeeze), shape(8, width),
             shape(devices, kinds, LANES)],
            [pltpu.VMEM((tiles, rows, 8, LANES), F32), pltpu.VMEM((tiles, frames, LANES), F32)],
            (frame_counts, sums, stat, depth, wide_gains, wide_biases, squeeze_weight, squeeze_bias, up_t, excite_bias,
             project_weight, cot),
        )

    z_zero, gates_zero, running_zero, pre_zero, stat02, sums = squeeze_forward(0, sums, stat01, d_zero)
    sums = exchange(sums)
    narrow_args = (frame_counts, sums, stat01, gram_zero, x, z_zero, ngains, nbiases, w_t)
    narrow_outs = [
        shape(pixels, LANES), shape(pixels, 2 * LANES, kind=low), shape(2 * LANES, pixels, kind=low),
        shape(round_up(3 * LANES // 8 + 1), 8, LANES), shape(8, LANES), shape(devices, 2, width),
    ]
    x1, x1_rows, x1_columns, gram, nstat, sums = call(
        narrow_kernel, (1,), [SCALARS] + [whole(array) for array in narrow_args[1:-1]] + [of_block(1, cin, width)],
        [whole(item) for item in narrow_outs], narrow_outs, [], narrow_args,
    )
    sums, gram = together(exchange(sums), gram)
    gram = share_out(gram, AXES)
    e_one, d_one, stat11, sums, planes_one = expand(1, sums, nstat, pl.BlockSpec((8, LANES), lambda j: (0, 0)), x1_rows)
    sums, gram = together(sums, gram)
    sums = exchange(sums)
    z_one, gates_one, running_one, pre_one, stat12, sums = squeeze_forward(1, sums, stat11, d_one)
    third, gram = together(exchange(sums), gram)
    gram = share_back(gram, AXES).reshape(-1, LANES)
    q_tiles = cin // 8 + -(-taps // 8)

    def backward_specs(block):
        rows = half_rows if block else full_rows
        ins = [fixed(8, width), fixed(rows, 8, width), fixed(4, width), fixed(4, width), of_block(block, squeeze, width),
               of_block(block, squeeze, width), of_block(block, cin, width), fixed(8, width), fixed(8, width),
               fixed(8, squeeze)]
        if not block:
            ins[0:4] = [both(rows_at(8)), both(cube_at(rows)), both(rows_at(4)), both(rows_at(4))]
            ins[6] = early(weight_at(block, cin))
        packed = round_up(tiles * (pack_tiles(cin, squeeze) + (0 if block else q_tiles)))
        wide_outs = [fixed(rows, 8, width), fixed(devices, 2, width)] if block else [late(cube_at(rows)), late(sums_at(2))]
        outs = [fixed(8, LANES)] + wide_outs + [fixed(packed // 2, 8, LANES)] * 2
        shapes = [shape(8, LANES), shape(rows, 8, width), shape(devices, 2, width)] + [shape(packed // 2, 8, LANES)] * 2
        scratch = [pltpu.VMEM((rows * 8, 2 * LANES), low), pltpu.VMEM((2 * LANES, rows * 8), low),
                   pltpu.VMEM((2 * LANES, 2 * LANES), F32), pltpu.VMEM((tiles, rows, 8, LANES), F32),
                   pltpu.VMEM((tiles, frames, LANES), F32)]
        return (ins, outs, shapes, scratch)

    ins, outs, shapes, scratch = backward_specs(1)
    activations, nsum_one, dy2_one, sums, pack_one, theirs = call(
        squeeze_one_backward_kernel, (1,),
        [SCALARS, SCALARS, whole(third), whole(z_one), whole(cot), whole(ngains), whole(nbiases)] + ins,
        [fixed(cin, half_pixels)] + outs, [shape(cin, half_pixels)] + shapes, scratch,
        (frame_counts, core, third, z_one, cot, ngains, nbiases, stat12, d_one, wide_gains, wide_biases, squeeze_weight, up_t,
         project_weight, gates_one, running_one, pre_one),
    )
    sums, theirs, gram = together(sums, theirs, gram)
    sums, pack_one = together(exchange(sums), pack_one + swap_cores(theirs))
    pack_one = share_out(pack_one)
    nothing = jnp.zeros((8, LANES), F32)

    def depth_backward(block, begin, end, sums, stat2, stat, dy2, depth, expanded, planes, columns, dx_in, sums_in, list_in):
        rows = half_rows if block else full_rows
        if block:
            taps_shape = (taps, 8, LANES)
            z_shape = (frames, 2, HALF_ROWS + 1, 8, LANES)
            f_shape = (full_rows, 8, LANES)
        else:
            taps_shape = (12 * LAGS, 8, LANES)
            z_shape = planes_shape(0, LANES, 4)
            f_shape = (frames, PAIRS, 4, 2, 8, LANES)
        count = end - begin
        final = end == tiles
        listed = round_up(end * q_tiles) if final and not block else end * q_tiles
        if final:
            send = (devices, 2, width + (LANES if block else 0))
            send_spec = fixed(*send)
        else:
            send = (8, count * LANES)
            send_spec = tile_rows(8)

        def wide_rows(rows):
            return pl.BlockSpec((rows, LANES), lambda j: (0, j + begin))

        def wide_cube(rows):
            return pl.BlockSpec((rows, 8, LANES), lambda j: (0, 0, j + begin))

        def wide_weight(rows):
            return pl.BlockSpec((1, rows, LANES), lambda j: (block, 0, j + begin))

        return call(
            functools.partial(depth_backward_kernel, block, begin, final), (count,),
            [SCALARS, pl.BlockSpec((devices, 2, LANES), lambda j: (0, 0, j + begin)), wide_rows(8), wide_rows(8), whole(nstat),
             wide_cube(rows), wide_cube(rows), wide_cube(full_rows), planes_of(block, 2, begin), whole(columns), wide_weight(cin), wide_rows(4),
             wide_rows(4), wide_weight(taps), whole(z_zero), whole(dx_in), whole(sums_in), whole(list_in)],
            [fixed(pixels, LANES), send_spec, fixed(listed, 8, LANES), tile_rows(8)],
            [shape(pixels, LANES), shape(*send), shape(listed, 8, LANES), shape(8, count * LANES)],
            [pltpu.VMEM(z_shape, F32), pltpu.VMEM(f_shape, F32), pltpu.VMEM(taps_shape, F32), pltpu.VMEM(taps_shape, F32),
             pltpu.VMEM((2 * LANES, 2 * LANES), F32)]
            + ([] if block else [pltpu.VMEM((frames, 4, 2, PAIRS, 8, LANES), F32)]),
            (frame_counts, sums, stat2, stat, nstat, dy2, depth, expanded, planes, columns, w_t, wide_gains, wide_biases,
             depth_weight, z_zero, dx_in, sums_in, list_in),
        )

    dxpre_one, sums, q_one, grad_one = depth_backward(
        1, 0, tiles, sums, stat12, stat11, dy2_one, d_one, e_one, planes_one, x1_columns, nothing, nothing, nothing
    )
    sums, pack_one = together(sums, pack_one)
    top_one, pack_one = together(exchange(sums), pack_one)
    pack_one = share_back(pack_one)
    ins, outs, shapes, scratch = backward_specs(0)
    dx1, nsum_zero, dy2_zero, sums, pack_zero, theirs = call(
        squeeze_zero_backward_kernel, (2, tiles),
        [SCALARS, SCALARS, whole(top_one), whole(stat11), whole(gram), whole(nstat), whole(dxpre_one), whole(x1), whole(z_zero),
         whole(ngains), of_block(1, cin, width), whole(wide_gains), whole(q_one)] + ins,
        [fixed(pixels, LANES)] + outs, [shape(pixels, LANES)] + shapes, scratch,
        (frame_counts, core, top_one, stat11, gram, nstat, dxpre_one, x1, z_zero, ngains, w_t, wide_gains, q_one, stat02, d_zero,
         wide_gains, wide_biases, squeeze_weight, up_t, project_weight, gates_zero, running_zero, pre_zero),
    )
    sums, pack_one = together(sums, pack_one)
    pack_one_other = swap_cores(pack_one)
    sums, pack_zero, pack_one_other = together(
        exchange(sums), pack_zero + swap_cores(theirs), pack_one_other
    )
    pack_zero = share_out(pack_zero)
    dxpre_zero, sums, late, grad_zero = depth_backward(
        0, 0, tiles, sums, stat02, stat01, dy2_zero, d_zero, e_zero, planes_zero, x_columns, nothing, nothing, nothing
    )
    sums, pack_zero = together(sums, pack_zero)
    top_zero, late = together(exchange(sums), add_cores(late))
    own = jnp.sum(pack_zero, axis=0)
    joint = jnp.concatenate(
        [jnp.broadcast_to(own[None], pack_zero.shape), late.reshape(pack_zero.shape[0], -1, 8, LANES)], axis=1
    )
    joint = lax.all_to_all(joint, CHIPS, 0, 0, tiled=True)
    final_args = (
        frame_counts, momentum_index, gram, stat01, stat02, stat11, stat12, grad_zero, grad_one, top_one,
        top_zero, nsum_zero, nsum_one, dxpre_zero, x, dx1, w_t, wide_gains, wide_means, wide_variances, narrow_means,
        narrow_variances,
    )
    final_outs = [
        shape(cin, pixels), shape(2, cin, width), shape(16, width), shape(4, width), shape(4, width), shape(2, cin),
        shape(2, cin), shape(4, width), shape(4, width), shape(2, cin), shape(2, cin),
    ]
    video_grad, less, factor, wgain, wbias, ngain, nbias, newm, newv, newnm, newnv = simple_call(
        finish_kernel, 2, final_args, final_outs
    )
    less, joint = together(less, joint)
    joint_other = swap_cores(joint)
    late = share_back(joint[:, own.shape[0] :])
    list_shapes = [
        shape(2, cin, width), shape(2, taps, width), shape(2, squeeze, width), shape(2, squeeze, width),
        shape(2, cin, width), shape(2, width), shape(2, squeeze),
    ]
    list_args = (core, joint, joint_other, pack_one, pack_one_other, less, factor)
    dw_t, dtaps, ddown, dup, dproj, dupb, ddownb = call(
        functools.partial(lists_kernel, own.shape[0]), (1,), [SCALARS] + [whole(array) for array in list_args[1:5]] + [of_block(1, cin, width), whole(factor)],
        [of_block(1, cin, width), of_block(1, taps, width)] + [whole(item) for item in list_shapes[2:]], list_shapes, [],
        list_args,
    )
    dw_t, late = together(dw_t, late)
    late_other = swap_cores(late)
    stay = pl.BlockSpec(memory_space=pl.ANY)
    dw_t, dtaps = call(
        last_kernel, (1,),
        [SCALARS, whole(late), whole(late_other), of_block(0, cin, width), whole(factor), stay, stay],
        [of_block(0, cin, width), of_block(0, taps, width)], list_shapes[0:2], [],
        (core, late, late_other, less, factor, dw_t, dtaps), aliases={5: 0, 6: 1},
    )
    return (
        activations, video_grad, jnp.swapaxes(dw_t, 1, 2), wgain, wbias, ngain, nbias, dtaps, ddown, ddownb,
        jnp.swapaxes(dup, 1, 2), dupb, dproj, newm, newv, newnm, newnv,
    )


def solution(mesh):
    sizes = (mesh.shape["dp"], mesh.shape["rep"] // 2, 2)
    split_mesh = jax.sharding.Mesh(mesh.devices.reshape(sizes), AXES)
    split = P(None, AXES)
    placed = (split, P(AXES)) + (P(),) * 16 + (split,)
    return jax.shard_map(
        local, mesh=split_mesh, in_specs=placed, out_specs=(split, split) + (P(),) * 15, check_vma=False
    )
```

```python
import functools

import jax
import jax.numpy as jnp
from jax import lax
from jax.experimental import pallas as pl
from jax.experimental.pallas import tpu as pltpu
from jax.sharding import PartitionSpec as P

SIDE = 16
LANES = 128
LAGS = 5
FULL_ROWS = 2 * SIDE
HALF_ROWS = SIDE // 2
EPSILON = 1e-05
HIGHEST = lax.Precision.HIGHEST
F32 = jnp.float32
NN = (((1,), (0,)), ((), ()))
NT = (((1,), (1,)), ((), ()))
TN = (((0,), (0,)), ((), ()))
VMEM_BYTES = 52 * 1024 * 1024


def half_tanh(half_values):
    return jnp.tanh(half_values)


def sigmoid(values):
    return 0.5 * jnp.tanh(0.5 * values) + 0.5


def silu_slope(half_values, tanh):
    return 0.5 * (1.0 + tanh + half_values * (1.0 - tanh * tanh))


def exact_dot(left, right, dims=NN):
    return lax.dot_general(left, right, dims, precision=HIGHEST, preferred_element_type=F32)


def halves(values):
    high = values.astype(jnp.bfloat16)
    return (high, (values - high.astype(F32)).astype(jnp.bfloat16))


def side_by_side(values):
    return jnp.concatenate(halves(values), axis=1)


def right_square(w):
    both = side_by_side(w)
    return jnp.concatenate([both, both], axis=0)


def right_square_t(w):
    high, low = halves(w)
    return jnp.concatenate(
        [jnp.concatenate([high, high], axis=1), jnp.concatenate([low, low], axis=1)], axis=0
    )


def plain_dot(left, right, dims=NN):
    return lax.dot_general(left, right, dims, preferred_element_type=F32)


def fold_right(values):
    lanes = values.shape[1] // 2
    return values[:, :lanes] + values[:, lanes:]


def fold_square(values):
    rows = values.shape[0] // 2
    return fold_right(values[:rows] + values[rows:])


def stacked(values):
    high = values.astype(jnp.bfloat16).astype(F32)
    return jnp.concatenate([high, values - high], axis=0).astype(jnp.bfloat16)


def skinny_dot(left, right, dims=NN):
    rows = left.shape[0]
    both = stacked(left)
    high, low = halves(right)
    values = plain_dot(both, high, dims) + plain_dot(both, low, dims)
    return values[:rows] + values[rows:]


def frame_outer(left, right):
    a_high = left.astype(jnp.bfloat16).astype(F32)
    b_high = right.astype(jnp.bfloat16).astype(F32)
    a_low = left - a_high
    b_low = right - b_high
    a = jnp.concatenate([a_high, a_high, a_low, a_low], axis=0).astype(jnp.bfloat16)
    b = jnp.concatenate([b_high, b_low, b_high, b_low], axis=0).astype(jnp.bfloat16)
    return plain_dot(a, b, TN)


def pad_rows(values):
    return jnp.concatenate([values, jnp.zeros((LANES - values.shape[0], values.shape[1]), values.dtype)], axis=0)


def column_order():
    q = lax.broadcasted_iota(jnp.int32, (LANES, LANES), 0)
    n = lax.broadcasted_iota(jnp.int32, (LANES, LANES), 1)
    source = (q // 16) * 16 + (q % 8) * 2 + (q // 8) % 2
    return (source == n).astype(jnp.bfloat16)


def live_frames(counts_ref):
    total = counts_ref[0]
    for clip in range(1, counts_ref.shape[0]):
        total = total + counts_ref[clip]
    return total


def place_of(counts_ref, frame):
    begin = jnp.int32(0)
    end = jnp.int32(0)
    for clip in range(counts_ref.shape[0]):
        end = end + counts_ref[clip]
        begin = jnp.where(frame >= end, end, begin)
    return frame - begin


def running_matrix(counts_ref, frames):
    after = lax.broadcasted_iota(jnp.int32, (frames, frames), 0)
    before = lax.broadcasted_iota(jnp.int32, (frames, frames), 1)
    begin = jnp.int32(0)
    matrix = jnp.zeros((frames, frames), F32)
    for clip in range(counts_ref.shape[0]):
        end = begin + counts_ref[clip]
        inside = (before >= begin) & (before <= after) & (after < end)
        matrix = matrix + jnp.where(inside, 1.0 / (after - begin + 1).astype(F32), 0.0)
        begin = end
    return matrix


def columns_up(values):
    spot = lax.broadcasted_iota(jnp.int32, values.shape, 1)
    return jnp.where(spot == 7, 0.0, pltpu.roll(values, 7, axis=1))


def columns_down(values):
    spot = lax.broadcasted_iota(jnp.int32, values.shape, 1)
    return jnp.where(spot == 0, 0.0, pltpu.roll(values, 1, axis=1))


def tile_sum(values):
    return jnp.sum(jnp.sum(values, axis=0), axis=0, keepdims=True)


def rows8(*rows):
    lanes = rows[0].shape[1]
    spot = lax.broadcasted_iota(jnp.int32, (8, lanes), 0)
    block = jnp.zeros((8, lanes), F32)
    for index, row in enumerate(rows):
        block = jnp.where(spot == index, row, block)
    return block


def pick_row(block, index):
    spot = lax.broadcasted_iota(jnp.int32, block.shape, 0)
    return jnp.sum(jnp.where(spot == index, block, 0.0), axis=0, keepdims=True)


def outer(left, right):
    return exact_dot(rows8(left), rows8(right), TN)


def row_dot(row, matrix, dims=NN):
    return exact_dot(rows8(row), matrix, dims)[0:1]


def clear_edges(ref):
    planes = ref.shape[1]
    edge = jnp.zeros((8, LANES), F32)
    for t in range(ref.shape[0]):
        for plane in range(planes):
            ref[t, plane, 0] = edge
            ref[t, plane, ref.shape[2] - 1] = edge


def spread_taps(taps_ref, w_ref):
    for tap in range(w_ref.shape[0]):
        w_ref[tap] = jnp.broadcast_to(taps_ref[0, tap : tap + 1, :], (8, LANES))


PAIRS = SIDE // 2


def row_pairs(plane):
    pair = plane.reshape(PAIRS, 2, 8, LANES)
    d1 = pair[:, 0]
    d2 = pair[:, 1]
    edge = jnp.zeros((1, 8, LANES), F32)
    d0 = jnp.concatenate([edge, d2[:-1]], axis=0)
    d3 = jnp.concatenate([d1[1:], edge], axis=0)
    return (d0 - d2, d1 + d2, d2 - d1, d1 - d3)


def pair_rows(parts):
    upper = parts[:, 0] + parts[:, 1] + parts[:, 2]
    lower = parts[:, 1] - parts[:, 2] - parts[:, 3]
    return jnp.stack([upper, lower], axis=1).reshape(FULL_ROWS, 8, LANES)


def spread_pairs(taps_ref, w_ref):
    for k in range(LAGS):
        for c in range(3):
            g0, g1, g2 = (taps_ref[0, k * 9 + 3 * r + c : k * 9 + 3 * r + c + 1, :] for r in range(3))
            outside = 0.5 * (g0 + g2)
            combined = (g0, outside + 0.5 * g1, outside - 0.5 * g1, g2)
            for place in range(4):
                w_ref[k * 12 + 3 * place + c] = jnp.broadcast_to(combined[place], (8, LANES))


def conv_full(t, k, a_ref, b_ref, w_ref, m_ref, fresh):
    weights = [w_ref[k * 12 + tap] for tap in range(12)]
    source = t - k
    for m in range(PAIRS):
        for place in range(4):
            left, centre, right = weights[3 * place : 3 * place + 3]
            a_even, a_odd = (a_ref[source, plane, place, m] for plane in range(2))
            a_odd_down, a_even_up = (b_ref[source, plane, place, m] for plane in range(2))
            even = centre * a_even + right * a_odd + left * a_odd_down
            odd = centre * a_odd + left * a_even + right * a_even_up
            if fresh:
                m_ref[m, place, 0] = even
                m_ref[m, place, 1] = odd
            else:
                m_ref[m, place, 0] = m_ref[m, place, 0] + even
                m_ref[m, place, 1] = m_ref[m, place, 1] + odd


def conv_half(t, k, a_ref, w_ref, d_ref, fresh):
    weights = [w_ref[k * 9 + tap] for tap in range(9)]
    source = t - k
    carried = [a_ref[source, plane, 0] for plane in range(3)]
    for i in range(HALF_ROWS):
        rows = [carried]
        for need in (2 * i + 1, 2 * i + 2):
            rows.append([a_ref[source, plane, need] for plane in range(3)])
        carried = rows[2]
        total = None
        for r in range(3):
            a_even, a_odd, a_odd_down = rows[r]
            left, centre, right = weights[3 * r : 3 * r + 3]
            part = centre * a_even + right * a_odd + left * a_odd_down
            total = part if total is None else total + part
        at = t * HALF_ROWS + i
        d_ref[at] = total if fresh else d_ref[at] + total


def row_total(ref, lanes=None):
    values = ref[...] if lanes is None or lanes == slice(None) else ref[:, :, lanes]
    return jnp.sum(values, axis=0)


def send_all(send_ref, rows, lanes):
    count = rows.shape[0]

    def one(device, carry):
        send_ref[pl.ds(device, 1), 0:count, lanes] = rows[None]
        return carry

    lax.fori_loop(0, send_ref.shape[0], one, 0)


def stack_rows(*rows):
    return rows8(*rows)[0 : len(rows)]


def pick_thirds(order, values, dims, order_left):
    pieces = []
    rest = values
    for _ in range(3):
        piece = rest.astype(jnp.bfloat16)
        rest = rest - piece.astype(F32)
        args = (order, piece) if order_left else (piece, order)
        pieces.append(plain_dot(*args, dims))
    return pieces


def gram_kernel(counts_ref, video_ref, w_ref, gram_ref, send_ref):
    total = live_frames(counts_ref)
    frames = video_ref.shape[1] // 256
    ones = jnp.ones((8, 256), jnp.bfloat16)

    def frame(t, carry):
        at = pl.ds(pl.multiple_of(t * 256, 256), 256)
        both = jnp.concatenate(halves(pad_rows(video_ref[:, at] * live_value(t, total))), axis=0)
        return (carry[0] + plain_dot(both, both, NT), carry[1] + plain_dot(ones, both, NT))

    init = (jnp.zeros((2 * LANES, 2 * LANES), F32), jnp.zeros((8, 2 * LANES), F32))
    gram, summed = each_frame(frames, frame, init)
    gram = fold_square(gram)
    summed = fold_right(summed)[0:1]
    gram_ref[0:LANES, :] = gram
    gram_ref[LANES : LANES + 8, :] = rows8(summed)
    w = pad_rows(w_ref[0])
    width = w.shape[1]
    sums = stack_rows(row_dot(summed, w), jnp.sum(w * exact_dot(gram, w), axis=0, keepdims=True))
    count = jnp.full((2, LANES), 1.0, F32) * (total * (SIDE * SIDE)).astype(F32)
    send_all(send_ref, sums, slice(0, width))
    send_all(send_ref, count, slice(width, width + LANES))


def prepare_kernel(counts_ref, video_ref, cot_ref, x_ref, rows_ref, columns_ref, cot_out_ref):
    order = column_order()
    total = live_frames(counts_ref)
    for part in range(video_ref.shape[1] // LANES):
        at = slice(part * LANES, (part + 1) * LANES)
        block = pad_rows(video_ref[:, at] * live_value(part // 2, total))
        high, middle, low = pick_thirds(order, block, NT, True)
        x_ref[at, :] = high + middle + low
        rows_ref[at, :] = jnp.concatenate([high, middle], axis=1).astype(jnp.bfloat16)
        columns_ref[:, at] = jnp.concatenate([high.T, middle.T], axis=0).astype(jnp.bfloat16)
    spot = lax.broadcasted_iota(jnp.int32, (LANES, LANES), 1)
    for part in range(cot_ref.shape[1] // LANES):
        at = slice(part * LANES, (part + 1) * LANES)
        frame = (spot + part * LANES) // (HALF_ROWS * 8)
        cot_out_ref[at, :] = jnp.where(frame < total, pad_rows(cot_ref[:, at]), 0.0).T


def moments_of(sums, count):
    average = sums[0:1] / count
    return (average, sums[1:2] / count - average * average)


def narrow_kernel(
    counts_ref, sums_ref, stat_ref, gram0_ref, x_ref, z_ref, ngain_ref, nbias_ref, w_ref,
    x1_ref, rows_ref, columns_ref, gram_ref, stat_out_ref, send_ref,
):
    total = live_frames(counts_ref)
    count = stat_ref[2:3, 0:LANES]
    average, variance = moments_of(row_total(sums_ref), count)
    factor = ngain_ref[0:1, :] * lax.rsqrt(variance + EPSILON)
    shift = nbias_ref[0:1, :] - factor * average
    stat_out_ref[...] = rows8(average, variance, count)
    frames = x_ref.shape[0] // 256

    def frame(t, carry):
        gram, cross, summed = carry
        at = pl.ds(pl.multiple_of(t * 256, 256), 256)
        z = z_ref[at, :]
        rows = (x_ref[at, :] + factor * z + shift) * live_value(t, total)
        x1_ref[at, :] = rows
        both = side_by_side(rows)
        rows_ref[at, :] = both
        columns = jnp.concatenate(halves(rows.T), axis=0)
        columns_ref[:, at] = columns
        gram = gram + plain_dot(columns, both)
        cross = cross + plain_dot(columns, side_by_side(z))
        return (gram, cross, summed + jnp.sum(rows, axis=0, keepdims=True))

    zero = jnp.zeros((2 * LANES, 2 * LANES), F32)
    gram, cross, summed = each_frame(frames, frame, (zero, zero, jnp.zeros((1, LANES), F32)))

    gram = fold_square(gram)
    tiles = LANES // 8
    gram_ref[0:tiles] = gram.reshape(tiles, 8, LANES)
    gram_ref[tiles : 2 * tiles] = fold_square(cross).reshape(tiles, 8, LANES)
    gram_ref[2 * tiles : 3 * tiles] = gram0_ref[0:LANES, :].reshape(tiles, 8, LANES)
    gram_ref[3 * tiles] = rows8(summed, gram0_ref[LANES : LANES + 1, :])
    w = pad_rows(w_ref[0])
    sums = stack_rows(row_dot(summed, w), jnp.sum(w * exact_dot(gram, w), axis=0, keepdims=True))
    send_all(send_ref, sums, slice(0, w.shape[1]))


def write_first(t, total, values, scale, shift, a_ref, b_ref):
    half_pre = values * scale + shift
    first = (half_pre + half_pre * half_tanh(half_pre)) * live_value(t, total)
    first = first.reshape(SIDE, 2, 8, LANES)
    even = first[:, 0]
    odd = first[:, 1]
    if b_ref is None:
        a_ref[t, 0, 1 : SIDE + 1] = even
        a_ref[t, 1, 1 : SIDE + 1] = odd
        a_ref[t, 2, 1 : SIDE + 1] = columns_down(odd)
        return
    for ref, plane, values in ((a_ref, 0, even), (a_ref, 1, odd), (b_ref, 0, columns_down(odd)), (b_ref, 1, columns_up(even))):
        for place, part in enumerate(row_pairs(values)):
            ref[t, plane, place] = part


def expand_kernel(
    block, counts_ref, sums_ref, count_ref, rows_ref, w_ref, gain_ref, bias_ref, taps_ref,
    e_ref, d_ref, stat_ref, send_ref, a_ref, taps8_ref, *pair_refs,
):
    b_ref, m_ref = pair_refs if pair_refs else (None, None)
    if block:
        clear_edges(a_ref)
    total = live_frames(counts_ref)
    frames = a_ref.shape[0]
    count = count_ref[2:3, :] if block else row_total(count_ref)[0:1]
    average, variance = moments_of(row_total(sums_ref), count)
    stat_ref[...] = rows8(average, variance, count)
    norm_row = 2 * block
    scale = gain_ref[norm_row : norm_row + 1, :] * lax.rsqrt(variance + EPSILON)
    shift = 0.5 * (bias_ref[norm_row : norm_row + 1, :] - average * scale)
    scale = 0.5 * scale
    square = right_square(pad_rows(w_ref[0]))

    def expand(t, carry):
        at = pl.ds(pl.multiple_of(t * 256, 256), 256)
        values = fold_right(plain_dot(rows_ref[at, :], square)).reshape(FULL_ROWS, 8, LANES)
        e_ref[pl.ds(pl.multiple_of(t * FULL_ROWS, FULL_ROWS), FULL_ROWS)] = values
        write_first(t, total, values, scale, shift, a_ref, b_ref)
        return carry

    each_frame(frames, expand, 0)
    per_frame = HALF_ROWS if block else FULL_ROWS
    if block:
        spread_taps(taps_ref, taps8_ref)
        conv = functools.partial(conv_half, a_ref=a_ref, w_ref=taps8_ref, d_ref=d_ref)
    else:
        spread_pairs(taps_ref, taps8_ref)
        conv = functools.partial(conv_full, a_ref=a_ref, b_ref=b_ref, w_ref=taps8_ref, m_ref=m_ref)

    def frame(t, carry):
        conv(t, 0, fresh=True)
        last = jnp.minimum(place_of(counts_ref, t), LAGS - 1)

        def lag(k, inner):
            conv(t, k, fresh=False)
            return inner

        lax.fori_loop(1, last + 1, lag, 0)
        if not block:
            d_ref[pl.ds(t * per_frame, per_frame)] = pair_rows(m_ref[...])
        values = d_ref[pl.ds(t * per_frame, per_frame)]
        return (carry[0] + jnp.sum(values, axis=0), carry[1] + jnp.sum(values * values, axis=0))

    zero = jnp.zeros((8, LANES), F32)
    summed, squares = lax.fori_loop(0, total, frame, (zero, zero))

    def dead(t, carry):
        d_ref[pl.ds(t * per_frame, per_frame)] = jnp.zeros((per_frame, 8, LANES), F32)
        return carry

    lax.fori_loop(total, frames, dead, 0)
    sums = stack_rows(jnp.sum(summed, axis=0, keepdims=True), jnp.sum(squares, axis=0, keepdims=True))
    send_all(send_ref, sums, slice(0, LANES))


def live_value(t, total):
    return jnp.where(t < total, 1.0, 0.0).astype(F32)


def each_frame(count, body, init):
    return lax.fori_loop(0, count, body, init, unroll=min(8, count))


def lanes_of(ref, tile):
    if ref.shape[-1] == LANES:
        return slice(None)
    return pl.ds(pl.multiple_of(tile * LANES, LANES), LANES)


def squeeze_forward_kernel(
    block, counts_ref, sums_ref, stat_ref, d_ref, gain_ref, bias_ref, down_ref, downb_ref, up_ref, upb_ref, proj_ref,
    cot_ref, z_ref, gates_ref, running_ref, pre_ref, stat_out_ref, send_ref, second_ref, pooled_ref,
):
    step = pl.program_id(0)
    steps = pl.num_programs(0)
    tiles = second_ref.shape[0]
    total = live_frames(counts_ref)
    per_frame = HALF_ROWS if block else FULL_ROWS
    pixels = per_frame * 8
    frames = second_ref.shape[1] // per_frame
    group = 256 // pixels
    chunks = frames // group
    norm_row = 2 * block + 1

    def activate(tile, carry):
        lanes = lanes_of(d_ref, tile)
        count = stat_ref[2:3, lanes] * (0.25 if block else 1.0)
        average, variance = moments_of(row_total(sums_ref, lanes), count)
        stat_out_ref[:, lanes] = rows8(average, variance, count)
        scale = gain_ref[norm_row : norm_row + 1, lanes] * lax.rsqrt(variance + EPSILON)
        shift = 0.5 * (bias_ref[norm_row : norm_row + 1, lanes] - average * scale)
        scale = 0.5 * scale

        def chunk(index, inside):
            for inner in range(group):
                t = index * group + inner
                at = pl.ds(t * per_frame, per_frame)
                half_pre = d_ref[at, :, lanes] * scale + shift
                second = half_pre + half_pre * half_tanh(half_pre)
                second = second * live_value(t, total)
                second_ref[tile, at] = second
                pooled_ref[tile, pl.ds(t, 1), :] = tile_sum(second) * (1.0 / pixels)
            return inside

        each_frame(chunks, chunk, 0)
        return carry

    if block:
        lax.fori_loop(0, tiles, activate, 0, unroll=tiles)
    else:
        activate(step, 0)

    def project(tile, carry):
        lanes = lanes_of(gates_ref, tile)
        square = right_square_t(pad_rows(proj_ref[0, :, lanes]))
        gates = gates_ref[:, lanes]

        def chunk(index, inside):
            parts = []
            for inner in range(group):
                t = index * group + inner
                second = second_ref[tile, pl.ds(t * per_frame, per_frame)].reshape(pixels, LANES)
                parts.append(second * pick_row(gates, t))
            excited = parts[0] if group == 1 else jnp.concatenate(parts, axis=0)
            at = pl.ds(pl.multiple_of(index * 256, 256), 256)
            z_ref[at, :] = z_ref[at, :] + fold_right(plain_dot(side_by_side(excited), square, NT))
            return inside

        each_frame(chunks, chunk, 0)
        return carry

    @pl.when(step == steps - 1)
    def gate_and_project():
        matrix = running_matrix(counts_ref, frames)
        pooled = jnp.concatenate([pooled_ref[index] for index in range(tiles)], axis=1)
        running = exact_dot(matrix, pooled)
        running_ref[...] = running
        pre = skinny_dot(running, down_ref[0], NT) + downb_ref[block : block + 1, :]
        pre_ref[...] = pre
        gates_ref[...] = sigmoid(skinny_dot(pre * sigmoid(pre), up_ref[0]) + upb_ref[block : block + 1, :])
        z_ref[...] = jnp.zeros_like(z_ref)
        lax.fori_loop(0, tiles, project, 0, unroll=tiles if block else 1)

        def chunk(index, carry):
            at = pl.ds(pl.multiple_of(index * 256, 256), 256)
            z = z_ref[at, :].reshape(32, 8, LANES)
            values = [z, z * z]
            if block:
                dy = cot_ref[at, :].reshape(32, 8, LANES)
                values = values + [dy, dy * z]
            return tuple(old + jnp.sum(new, axis=0) for old, new in zip(carry, values))

        zero = jnp.zeros((8, LANES), F32)
        sums = each_frame(chunks, chunk, (zero,) * (4 if block else 2))
        rows = stack_rows(*(jnp.sum(value, axis=0, keepdims=True) for value in sums))
        send_all(send_ref, rows, slice(0, LANES))


def put_lists(core_ref, refs, writes):
    size = refs[0].shape[0]

    for core in range(2):
        @pl.when(core_ref[0] == core)
        def write(core=core):
            for at, values in writes:
                for half in range(2):
                    begin = max(at, half * size)
                    end = min(at + values.shape[0], (half + 1) * size)
                    if begin < end:
                        refs[half ^ core][begin - half * size : end - half * size] = values[begin - at : end - at]


def put_tile_list(core_ref, refs, at, values):
    size = refs[0].shape[0]
    half = jnp.where(at >= size, 1, 0)
    place = pl.ds(at - half * size, values.shape[0])
    for other in range(2):
        @pl.when((core_ref[0] == half) == (other == 0))
        def write(other=other):
            refs[other][place] = values


def pack_tiles(narrow, squeeze):
    return narrow // 8 + 2 * (squeeze // 8) + 1


def squeeze_backward_body(
    block, counts_ref, stat_ref, d_ref, gain_ref, bias_ref, down_ref, up_ref, proj_ref, gates_ref, running_ref,
    pre_ref, dy2_ref, send_ref, core_ref, list_refs, dz3_ref, dz3t_ref, total_ref, dexc_ref, dgate_ref, head,
):
    total = live_frames(counts_ref)
    per_frame = HALF_ROWS if block else FULL_ROWS
    pixels = per_frame * 8
    frames = dz3_ref.shape[0] // pixels
    group = 256 // pixels
    chunks = frames // group
    norm_row = 2 * block + 1
    tiles = dexc_ref.shape[0]
    narrow = proj_ref.shape[1]
    squeeze = down_ref.shape[1]
    per_tile = pack_tiles(narrow, squeeze)

    def norm_of(tile):
        lanes = lanes_of(d_ref, tile)
        average = stat_ref[0:1, lanes]
        root = lax.rsqrt(stat_ref[1:2, lanes] + EPSILON)
        scale = gain_ref[norm_row : norm_row + 1, lanes] * root
        shift = 0.5 * (bias_ref[norm_row : norm_row + 1, lanes] - average * scale)
        return (lanes, average, root, 0.5 * scale, shift)

    def excite(tile, carry):
        lanes, _, _, scale, shift = norm_of(tile)
        gates = gates_ref[:, lanes_of(gates_ref, tile)]
        square = right_square(pad_rows(proj_ref[0, :, lanes]))

        def chunk(index, inside):
            flat = pl.ds(pl.multiple_of(index * 256, 256), 256)
            dexc = fold_right(plain_dot(dz3_ref[flat, :], square)).reshape(32, 8, LANES)
            dexc_ref[tile, pl.ds(pl.multiple_of(index * 32, 32), 32)] = dexc
            parts = []
            for inner in range(group):
                t = index * group + inner
                half_pre = d_ref[pl.ds(t * per_frame, per_frame), :, lanes] * scale + shift
                second = half_pre + half_pre * half_tanh(half_pre)
                second = second * live_value(t, total)
                own = dexc[inner * per_frame : (inner + 1) * per_frame]
                dgate_ref[tile, pl.ds(t, 1), :] = tile_sum(own * second)
                parts.append(second.reshape(pixels, LANES) * pick_row(gates, t))
            excited = parts[0] if group == 1 else jnp.concatenate(parts, axis=0)
            total_ref[...] = total_ref[...] + plain_dot(dz3t_ref[:, flat], side_by_side(excited))
            return inside

        total_ref[...] = jnp.zeros_like(total_ref)
        each_frame(chunks, chunk, 0)
        dproj = fold_square(total_ref[...])
        put_tile_list(core_ref, list_refs, tile * per_tile, dproj[0:narrow].reshape(narrow // 8, 8, LANES))
        return carry

    def squeeze_part():
        pre = pre_ref[...]
        half_pre = 0.5 * pre
        tanh = half_tanh(half_pre)
        squeezed = half_pre + half_pre * tanh
        all_gates = gates_ref[...]
        dgate = jnp.concatenate([dgate_ref[index] for index in range(tiles)], axis=1)
        du = dgate * all_gates * (1.0 - all_gates)
        dpre = skinny_dot(du, up_ref[0], NT) * silu_slope(half_pre, tanh)
        ddown = frame_outer(dpre, running_ref[...])
        dup = frame_outer(squeezed, du)
        dpre_row = jnp.sum(dpre, axis=0, keepdims=True)
        dpre_row = jnp.concatenate([dpre_row, jnp.zeros((1, du.shape[1] - squeeze), F32)], axis=1)
        biases = rows8(jnp.sum(du, axis=0, keepdims=True), dpre_row)
        writes = []
        for index in range(tiles):
            own = slice(index * LANES, (index + 1) * LANES)
            at = index * per_tile + narrow // 8
            writes.append((at, ddown[:, own].reshape(squeeze // 8, 8, LANES)))
            at = at + squeeze // 8
            writes.append((at, dup[:, own].reshape(squeeze // 8, 8, LANES)))
            writes.append((at + squeeze // 8, biases[:, own].reshape(1, 8, LANES)))
        put_lists(core_ref, list_refs, writes)
        drunning = skinny_dot(dpre, down_ref[0])
        dpooled = exact_dot(running_matrix(counts_ref, frames), drunning, TN) * (1.0 / pixels)
        for index in range(tiles):
            dgate_ref[index] = dpooled[:, index * LANES : (index + 1) * LANES]

    def slope(tile, carry):
        lanes, average, root, scale, shift = norm_of(tile)
        gates = gates_ref[:, lanes_of(gates_ref, tile)]

        def chunk(index, inside):
            summed, cross = inside
            for inner in range(group):
                t = index * group + inner
                at = pl.ds(t * per_frame, per_frame)
                depth = d_ref[at, :, lanes]
                half_pre = depth * scale + shift
                dsecond = dexc_ref[tile, at] * pick_row(gates, t) + pick_row(dgate_ref[tile], t)
                dy = dsecond * silu_slope(half_pre, half_tanh(half_pre))
                dy = dy * live_value(t, total)
                dy2_ref[at, :, lanes] = dy
                summed = summed + jnp.sum(dy, axis=0)
                cross = cross + jnp.sum(dy * (depth - average), axis=0)
            return (summed, cross)

        zero = jnp.zeros((8, LANES), F32)
        summed, cross = each_frame(chunks, chunk, (zero, zero))
        rows = stack_rows(jnp.sum(summed, axis=0, keepdims=True), root * jnp.sum(cross, axis=0, keepdims=True))
        send_all(send_ref, rows, lanes)
        return carry

    if block:
        head()
        lax.fori_loop(0, tiles, excite, 0, unroll=tiles)
        squeeze_part()
        lax.fori_loop(0, tiles, slope, 0, unroll=tiles)
    else:
        phase = pl.program_id(0)
        tile = pl.program_id(1)

        @pl.when((phase == 0) & (tile == 0))
        def start():
            head()

        @pl.when(phase == 0)
        def first():
            excite(tile, 0)

        @pl.when((phase == 1) & (tile == 0))
        def between():
            squeeze_part()

        @pl.when(phase == 1)
        def second():
            slope(tile, 0)


def squeeze_one_backward_kernel(
    counts_ref, core_ref, third_ref, z_ref, cot_ref, ngain_ref, nbias_ref, stat_ref, d_ref, gain_ref, bias_ref, down_ref,
    up_ref, proj_ref, gates_ref, running_ref, pre_ref, act_ref, nsum_ref, dy2_ref, send_ref, mine_ref, theirs_ref,
    dz3_ref, dz3t_ref, total_ref, dexc_ref, dgate_ref,
):
    total = live_frames(counts_ref)
    pixels = HALF_ROWS * 8

    def head():
        count = stat_ref[2:3, 0:LANES]
        sums = row_total(third_ref)
        mean, variance = moments_of(sums, count)
        root = lax.rsqrt(variance + EPSILON)
        gain = ngain_ref[1:2, :]
        bias_sum = sums[2:3, :]
        gain_sum = root * (sums[3:4, :] - mean * bias_sum)
        nsum_ref[...] = rows8(gain_sum, bias_sum, mean, variance)
        row = lax.broadcasted_iota(jnp.int32, z_ref.shape, 0) // pixels
        live = row < total
        normed = (z_ref[...] - mean) * root
        act = jnp.where(live, gain * normed + nbias_ref[1:2, :], 0.0)
        act_ref[...] = act.T[0 : act_ref.shape[0]]
        dz3 = gain * root * (cot_ref[...] - bias_sum / count - normed * (gain_sum / count))
        dz3 = jnp.where(live, dz3, 0.0)
        dz3_ref[...] = side_by_side(dz3)
        dz3t_ref[...] = jnp.concatenate(halves(dz3.T), axis=0)

    squeeze_backward_body(
        1, counts_ref, stat_ref, d_ref, gain_ref, bias_ref, down_ref, up_ref, proj_ref, gates_ref, running_ref,
        pre_ref, dy2_ref, send_ref, core_ref, (mine_ref, theirs_ref), dz3_ref, dz3t_ref, total_ref, dexc_ref, dgate_ref, head,
    )


def input_factors(sums, stat_ref, count, gain, w):
    root = lax.rsqrt(stat_ref[1:2, :] + EPSILON)
    factor = gain * root
    matrix = exact_dot(w * (factor * root * sums[1:2] / count), w, NT)
    return (matrix, row_dot(factor * sums[0:1] / count, w, NT))


def covariance(gram, summed, count):
    mean = summed / count
    return (mean, gram / count - outer(mean, mean))


def squeeze_zero_backward_kernel(
    counts_ref, core_ref, top_ref, stat1_ref, gram_ref, nstat_ref, dxpre_ref, x1_ref, z_ref, ngain_ref, w_ref, gains_ref, q_one_ref,
    stat_ref, d_ref, gain_ref, bias_ref, down_ref, up_ref, proj_ref, gates_ref, running_ref, pre_ref,
    dx1_ref, nsum_ref, dy2_ref, send_ref, mine_ref, theirs_ref, dz3_ref, dz3t_ref, total_ref, dexc_ref, dgate_ref,
):
    total = live_frames(counts_ref)
    width = gains_ref.shape[1]

    def head():
        start = pack_tiles(proj_ref.shape[1], down_ref.shape[1]) * (width // LANES)
        put_lists(core_ref, (mine_ref, theirs_ref), [(start, q_one_ref)])
        count = stat_ref[2:3, :]
        wide_count = jnp.broadcast_to(count[:, 0:1], (1, width))
        sums = row_total(top_ref, slice(0, width))
        extra = row_total(top_ref, slice(width, width + LANES))
        matrix, shift = input_factors(sums, stat1_ref, wide_count, gains_ref[2:3, :], pad_rows(w_ref[0]))
        mean = nstat_ref[0:1, :]
        root = lax.rsqrt(nstat_ref[1:2, :] + EPSILON)
        mean_x1 = gram_ref[3 * LANES : 3 * LANES + 1, :] / count
        cross = (gram_ref[LANES : 2 * LANES, :] - count * outer(mean_x1, mean)) * root
        gain_sum = extra[0:1] - jnp.sum(matrix * cross, axis=0, keepdims=True)
        bias_sum = extra[1:2] - count * shift
        nsum_ref[...] = rows8(gain_sum, bias_sum, mean, nstat_ref[1:2, :])
        factor = ngain_ref[0:1, :] * root
        square = right_square(matrix)
        bias_mean = bias_sum / count
        gain_mean = gain_sum / count

        def frame(t, carry):
            at = pl.ds(pl.multiple_of(t * 256, 256), 256)
            centred = side_by_side(x1_ref[at, :] - mean_x1)
            live = live_value(t, total)
            dx1 = (dxpre_ref[at, :] - fold_right(plain_dot(centred, square)) - shift) * live
            dx1_ref[at, :] = dx1
            normed = (z_ref[at, :] - mean) * root
            dz3 = factor * (dx1 - bias_mean - normed * gain_mean) * live
            dz3_ref[at, :] = side_by_side(dz3)
            dz3t_ref[:, at] = jnp.concatenate(halves(dz3.T), axis=0)
            return carry

        each_frame(dz3_ref.shape[0] // 256, frame, 0)

    squeeze_backward_body(
        0, counts_ref, stat_ref, d_ref, gain_ref, bias_ref, down_ref, up_ref, proj_ref, gates_ref, running_ref,
        pre_ref, dy2_ref, send_ref, core_ref, (mine_ref, theirs_ref), dz3_ref, dz3t_ref, total_ref, dexc_ref, dgate_ref, head,
    )

def back_full(t, k, a_ref, w_ref, z_ref, raw_ref, f_ref, dw_ref, fresh):
    weights = [w_ref[k * 12 + tap] for tap in range(12)]
    target = t - k
    sums = [None] * 12
    for m in range(PAIRS):
        for place in range(4):
            flipped = (3, 1, 2, 0)[place]
            left, centre, right = weights[3 * flipped : 3 * flipped + 3]
            b_even, b_odd, b_odd_down, b_even_up = (z_ref[t, plane, place, m] for plane in range(4))
            even = centre * b_even + right * b_odd_down + left * b_odd
            odd = centre * b_odd + right * b_even + left * b_even_up
            if fresh:
                f_ref[target, m, place, 0] = even
                f_ref[target, m, place, 1] = odd
            else:
                f_ref[target, m, place, 0] = f_ref[target, m, place, 0] + even
                f_ref[target, m, place, 1] = f_ref[target, m, place, 1] + odd
            if place in (0, 3):
                row = 0 if place == 0 else 1
                b_even, b_odd, b_odd_down, b_even_up = (raw_ref[t, plane, row, m] for plane in range(4))
            a_even, a_odd = (a_ref[target, plane, place, m] for plane in range(2))
            pieces = (
                b_even_up * a_odd + b_odd * a_even,
                b_even * a_even + b_odd * a_odd,
                b_even * a_odd + b_odd_down * a_even,
            )
            for c in range(3):
                at = 3 * place + c
                sums[at] = pieces[c] if sums[at] is None else sums[at] + pieces[c]
    for place in range(4):
        for c in range(3):
            at = place * 3 * LAGS + k * 3 + c
            dw_ref[at] = dw_ref[at] + sums[3 * place + c]


def pair_taps(totals):
    count = 3 * LAGS
    first, second, third, last = (totals[place * count : (place + 1) * count] for place in range(4))
    middle = 0.5 * (second - third)
    return (first + middle, 0.5 * (second + third), middle - last)


def back_half(t, k, a_ref, w_ref, z_ref, f_ref, dw_ref, fresh):
    weights = [w_ref[k * 9 + tap] for tap in range(9)]
    target = t - k
    sums = [None] * 9

    def put(row, parity, value):
        at = target * FULL_ROWS + 2 * row + parity
        f_ref[at] = value if fresh else f_ref[at] + value

    carried = [a_ref[target, plane, 0] for plane in range(2)]
    here = [z_ref[t, plane, 0] for plane in range(2)]
    for i in range(HALF_ROWS):
        below = [z_ref[t, plane, i + 1] for plane in range(2)]
        dz, dz_up = here
        rows = [carried]
        for need in (2 * i + 1, 2 * i + 2):
            rows.append([a_ref[target, plane, need] for plane in range(2)])
        carried = rows[2]
        put(2 * i, 0, weights[4] * dz)
        put(2 * i, 1, weights[5] * dz + weights[3] * dz_up)
        put(2 * i + 1, 0, weights[7] * dz + weights[1] * below[0])
        put(
            2 * i + 1,
            1,
            weights[8] * dz + weights[6] * dz_up + (weights[2] * below[0] + weights[0] * below[1]),
        )
        for r in range(3):
            a_even, a_odd = rows[r]
            pieces = (dz_up * a_odd, dz * a_even, dz * a_odd)
            for c in range(3):
                at = 3 * r + c
                sums[at] = pieces[c] if sums[at] is None else sums[at] + pieces[c]
        here = below
    for tap in range(9):
        dw_ref[k * 9 + tap] = dw_ref[k * 9 + tap] + sums[tap]


def depth_backward_kernel(
    block, counts_ref, grads_ref, stat2_ref, stat_ref, nstat_ref, dy2_ref, d_ref, e_ref, a_ref, columns_ref, w_ref,
    gain_ref, bias_ref, taps_ref, z3_ref, dxpre_ref, send_ref, q_ref, grad_rows_ref,
    z_ref, f_ref, taps8_ref, dw_ref, total_ref, *raw_refs,
):
    tile = pl.program_id(0)
    tiles = pl.num_programs(0)
    total = live_frames(counts_ref)
    frames = a_ref.shape[0]
    norm_row = 2 * block
    half = block == 1
    per_frame = HALF_ROWS if half else FULL_ROWS
    taps = taps_ref.shape[1]

    @pl.when(tile == 0)
    def start():
        if half:
            clear_edges(z_ref)
        dxpre_ref[...] = jnp.zeros_like(dxpre_ref)
        if not half:
            send_ref[...] = jnp.zeros_like(send_ref)

        def dead(t, carry):
            if half:
                f_ref[pl.ds(t * FULL_ROWS, FULL_ROWS)] = jnp.zeros((FULL_ROWS, 8, LANES), F32)
            else:
                f_ref[t] = jnp.zeros(f_ref.shape[1:], F32)
            return carry

        lax.fori_loop(total, frames, dead, 0)

    count = stat2_ref[2:3, :]
    grads = row_total(grads_ref)
    grad_rows_ref[...] = rows8(grads[0:1], grads[1:2])
    average = stat2_ref[0:1, :]
    root = lax.rsqrt(stat2_ref[1:2, :] + EPSILON)
    scale_two = gain_ref[norm_row + 1 : norm_row + 2, :] * root
    slope = scale_two * root * grads[1:2] / count
    level = scale_two * grads[0:1] / count - slope * average
    average_one = stat_ref[0:1, :]
    root_one = lax.rsqrt(stat_ref[1:2, :] + EPSILON)
    scale_one = gain_ref[norm_row : norm_row + 1, :] * root_one
    shift_half = 0.5 * (bias_ref[norm_row : norm_row + 1, :] - average_one * scale_one)
    scale_half = 0.5 * scale_one

    def fill(t, carry):
        at = pl.ds(t * per_frame, per_frame)
        dz = scale_two * dy2_ref[at] - (slope * d_ref[at] + level)
        if half:
            z_ref[t, 0, 0:HALF_ROWS] = dz
            z_ref[t, 1, 0:HALF_ROWS] = columns_up(dz)
        else:
            pair = dz.reshape(SIDE, 2, 8, LANES)
            even = pair[:, 0]
            odd = pair[:, 1]
            for plane, values in enumerate((even, odd, columns_down(odd), columns_up(even))):
                for place, part in enumerate(row_pairs(values)):
                    z_ref[t, plane, place] = part
                rows = values.reshape(PAIRS, 2, 8, LANES)
                raw_refs[0][t, plane, 0] = rows[:, 0]
                raw_refs[0][t, plane, 1] = rows[:, 1]
        return carry

    each_frame(frames, fill, 0)
    dw_ref[...] = jnp.zeros_like(dw_ref)
    refs = dict(a_ref=a_ref, w_ref=taps8_ref, z_ref=z_ref, f_ref=f_ref, dw_ref=dw_ref)
    if half:
        spread_taps(taps_ref, taps8_ref)
        back = functools.partial(back_half, **refs)
    else:
        spread_pairs(taps_ref, taps8_ref)
        back = functools.partial(back_full, raw_ref=raw_refs[0], **refs)

    def frame(t, carry):
        back(t, 0, fresh=True)
        last = jnp.minimum(place_of(counts_ref, t), LAGS - 1)

        def lag(k, inner):
            back(t, k, fresh=False)
            return inner

        return lax.fori_loop(1, last + 1, lag, carry)

    lax.fori_loop(0, total, frame, 0)
    square = right_square_t(pad_rows(w_ref[0]) * scale_one)
    total_ref[...] = jnp.zeros_like(total_ref)

    def finish(t, carry):
        rows = pl.ds(pl.multiple_of(t * FULL_ROWS, FULL_ROWS), FULL_ROWS)
        flat = pl.ds(pl.multiple_of(t * 256, 256), 256)
        values = e_ref[rows]
        half_pre = values * scale_half + shift_half
        dfirst = f_ref[rows] if half else pair_rows(f_ref[t])
        dy = dfirst * silu_slope(half_pre, half_tanh(half_pre))
        summed = carry[0] + jnp.sum(dy, axis=0)
        cross = carry[1] + jnp.sum(dy * (values - average_one), axis=0)
        dy = dy.reshape(256, LANES)
        both = side_by_side(dy)
        total_ref[...] = total_ref[...] + plain_dot(columns_ref[:, flat], both)
        dxpre_ref[flat, :] = dxpre_ref[flat, :] + fold_right(plain_dot(both, square, NT))
        return (summed, cross)

    zero = jnp.zeros((8, LANES), F32)
    summed, cross = each_frame(frames, finish, (zero, zero))
    rows = stack_rows(jnp.sum(summed, axis=0, keepdims=True), root_one * jnp.sum(cross, axis=0, keepdims=True))
    if half:
        send_all(send_ref, rows, pl.ds(pl.multiple_of(tile * LANES, LANES), LANES))
    else:
        spot = lax.broadcasted_iota(jnp.int32, (8, LANES), 0)
        for index in range(2):
            send_ref[index] = jnp.where(spot == tile, rows[index : index + 1], send_ref[index])
    gathered = fold_square(total_ref[...])
    narrow = w_ref.shape[1]
    dtaps = jnp.sum(dw_ref[...], axis=1)
    parts = (dtaps,) if half else pair_taps(dtaps)
    unused = jnp.zeros(((-taps) % 8, LANES), F32)
    values = jnp.concatenate((gathered[0:narrow],) + parts + (unused,), axis=0)
    listed = values.shape[0] // 8
    q_ref[pl.ds(tile * listed, listed)] = values.reshape(listed, 8, LANES)

    if half:
        @pl.when(tile == tiles - 1)
        def tail():
            mean = nstat_ref[0:1, :]
            root_three = lax.rsqrt(nstat_ref[1:2, :] + EPSILON)

            def part(t, carry):
                flat = pl.ds(pl.multiple_of(t * 256, 256), 256)
                dx = dxpre_ref[flat, :].reshape(32, 8, LANES)
                normed = ((z3_ref[flat, :] - mean) * root_three).reshape(32, 8, LANES)
                return (carry[0] + jnp.sum(dx * normed, axis=0), carry[1] + jnp.sum(dx, axis=0))

            cross_three, summed_three = each_frame(frames, part, (zero, zero))
            rows = stack_rows(
                jnp.sum(cross_three, axis=0, keepdims=True), jnp.sum(summed_three, axis=0, keepdims=True)
            )
            width = send_ref.shape[2] - LANES
            send_all(send_ref, rows, slice(width, width + LANES))


def finish_kernel(
    counts_ref, momentum_ref, gram_ref, stat01_ref, stat02_ref, stat11_ref, stat12_ref, grad0_ref,
    grad1_ref, one_ref, zero_ref, nsum0_ref, nsum1_ref, dxpre_ref, x_ref, dx1_ref, w_ref, gain_ref, means_ref, vars_ref,
    nmeans_ref, nvars_ref,
    video_ref, less_ref, factor_ref, wgain_ref, wbias_ref, ngain_ref, nbias_ref, newm_ref, newv_ref, newnm_ref, newnv_ref,
):
    total = live_frames(counts_ref)
    full = stat01_ref[2:3, :]
    count = full[:, 0:LANES]
    width = full.shape[1]
    tiles = width // LANES
    top_zero = stack_rows(
        *(jnp.concatenate([zero_ref[index, tile : tile + 1, :] for tile in range(tiles)], axis=1) for index in range(2))
    )
    top_one = row_total(one_ref, slice(0, width))
    w_zero = pad_rows(w_ref[0])
    matrix, shift = input_factors(top_zero, stat01_ref, full, gain_ref[0:1, :], w_zero)
    square = right_square(matrix)
    mean_x, cov_zero = covariance(
        gram_ref[2 * LANES : 3 * LANES, :], gram_ref[3 * LANES + 1 : 3 * LANES + 2, :], count
    )
    order = column_order()
    narrow = video_ref.shape[0]

    def frame(t, carry):
        at = pl.ds(pl.multiple_of(t * 256, 256), 256)
        centred = side_by_side(x_ref[at, :] - mean_x)
        dx = (dxpre_ref[at, :] - fold_right(plain_dot(centred, square)) - shift) * live_value(t, total) + dx1_ref[at, :]
        for part in range(2):
            own = dx[part * LANES : (part + 1) * LANES].T[0:narrow]
            pieces = pick_thirds(order, own, NN, False)
            start = pl.multiple_of(t * 256 + part * LANES, LANES)
            video_ref[:, pl.ds(start, LANES)] = pieces[0] + pieces[1] + pieces[2]
        return carry

    each_frame(x_ref.shape[0] // 256, frame, 0)
    mean_one, cov_one = covariance(gram_ref[0:LANES, :], gram_ref[3 * LANES : 3 * LANES + 1, :], count)
    plan = ((mean_x, cov_zero, stat01_ref, top_zero, w_zero), (mean_one, cov_one, stat11_ref, top_one, pad_rows(w_ref[1])))
    for block, (mean_row, cov, stat_ref, top, w) in enumerate(plan):
        root = lax.rsqrt(stat_ref[1:2, :] + EPSILON)
        factor = gain_ref[2 * block : 2 * block + 1, :] * root
        less = outer(mean_row, top[0:1]) + exact_dot(cov, w) * (root * top[1:2])
        less_ref[block] = (less * factor)[0:narrow]
        factor_ref[8 * block : 8 * block + 8, :] = rows8(factor)
    momentum = momentum_ref[0].astype(F32) / 10.0
    wgain_ref[...] = stack_rows(top_zero[1:2], grad0_ref[1:2, :], top_one[1:2], grad1_ref[1:2, :])
    wbias_ref[...] = stack_rows(top_zero[0:1], grad0_ref[0:1, :], top_one[0:1], grad1_ref[0:1, :])
    stats = (stat01_ref, stat02_ref, stat11_ref, stat12_ref)
    means = stack_rows(*(ref[0:1, :] for ref in stats))
    variances = stack_rows(*(ref[1:2, :] * (ref[2:3, :] / (ref[2:3, :] - 1.0)) for ref in stats))
    newm_ref[...] = (1.0 - momentum) * means_ref[...] + momentum * means
    newv_ref[...] = (1.0 - momentum) * vars_ref[...] + momentum * variances
    ngain_ref[...] = stack_rows(nsum0_ref[0:1, :], nsum1_ref[0:1, :])[:, 0:narrow]
    nbias_ref[...] = stack_rows(nsum0_ref[1:2, :], nsum1_ref[1:2, :])[:, 0:narrow]
    means = stack_rows(nsum0_ref[2:3, :], nsum1_ref[2:3, :])[:, 0:narrow]
    quarter = 0.25 * count
    variances = stack_rows(
        nsum0_ref[3:4, :] * (count / (count - 1.0)), nsum1_ref[3:4, :] * (quarter / (quarter - 1.0))
    )[:, 0:narrow]
    newnm_ref[...] = (1.0 - momentum) * nmeans_ref[...] + momentum * means
    newnv_ref[...] = (1.0 - momentum) * nvars_ref[...] + momentum * variances


def list_rows(core_ref, pair, at, count):
    first_core = core_ref[0] == 0
    mine, other = pair[0:2]
    if len(pair) > 2:
        share = pair[2]
        half = mine.shape[0] * share

        def run(ref, begin, size):
            pieces = []
            while size:
                length = min(size, share - begin % share)
                pieces.append(ref[begin // share, begin % share : begin % share + length])
                begin = begin + length
                size = size - length
            return pieces[0] if len(pieces) == 1 else jnp.concatenate(pieces, axis=0)
    else:
        half = mine.shape[0]

        def run(ref, begin, size):
            return ref[begin : begin + size]

    pieces = []
    if at < half:
        size = min(count, half - at)
        pieces.append(jnp.where(first_core, run(mine, at, size), run(other, at, size)))
        count = count - size
        at = at + size
    if count:
        pieces.append(jnp.where(first_core, run(other, at - half, count), run(mine, at - half, count)))
    values = pieces[0] if len(pieces) == 1 else jnp.concatenate(pieces, axis=0)
    return values.reshape(-1, LANES)


def lists_kernel(
    share, core_ref, pack0_ref, pack0_other_ref, pack1_ref, pack1_other_ref, less_ref, factor_ref,
    dw_ref, dtaps_ref, ddown_ref, dup_ref, dproj_ref, dupb_ref, ddownb_ref,
):
    narrow = dw_ref.shape[1]
    taps = dtaps_ref.shape[1]
    squeeze = ddown_ref.shape[1]
    tiles = dw_ref.shape[2] // LANES
    per_pack = pack_tiles(narrow, squeeze)
    per_tile = narrow // 8 + -(-taps // 8)
    packs = ((pack0_ref, pack0_other_ref, share), (pack1_ref, pack1_other_ref))
    for block in range(2):
        down_rows = []
        for tile in range(tiles):
            lanes = slice(tile * LANES, (tile + 1) * LANES)
            at = tile * per_pack
            dproj_ref[block, :, lanes] = list_rows(core_ref, packs[block], at, narrow // 8)
            at = at + narrow // 8
            ddown_ref[block, :, lanes] = list_rows(core_ref, packs[block], at, squeeze // 8)
            at = at + squeeze // 8
            dup_ref[block, :, lanes] = list_rows(core_ref, packs[block], at, squeeze // 8)
            biases = list_rows(core_ref, packs[block], at + squeeze // 8, 1)
            dupb_ref[block : block + 1, lanes] = biases[0:1]
            down_rows.append(biases[1:2])
        ddownb_ref[block : block + 1, :] = jnp.concatenate(down_rows, axis=1)[:, 0:squeeze]
    for tile in range(tiles):
        lanes = slice(tile * LANES, (tile + 1) * LANES)
        values = list_rows(core_ref, packs[0], per_pack * tiles + tile * per_tile, per_tile)
        dw_ref[0, :, lanes] = values[0:narrow] * factor_ref[8:9, lanes] - less_ref[0, :, lanes]
        dtaps_ref[0, :, lanes] = values[narrow : narrow + taps]


def last_kernel(core_ref, late_ref, late_other_ref, less_ref, factor_ref, _, __, dw_ref, dtaps_ref):
    narrow = dw_ref.shape[1]
    taps = dtaps_ref.shape[1]
    per_tile = narrow // 8 + -(-taps // 8)
    for tile in range(dw_ref.shape[2] // LANES):
        lanes = slice(tile * LANES, (tile + 1) * LANES)
        values = list_rows(core_ref, (late_ref, late_other_ref), tile * per_tile, per_tile)
        dw_ref[0, :, lanes] = values[0:narrow] * factor_ref[0:1, lanes] - less_ref[0, :, lanes]
        for r in range(3):
            for k in range(LAGS):
                source = narrow + r * 3 * LAGS + 3 * k
                dtaps_ref[0, k * 9 + 3 * r : k * 9 + 3 * r + 3, lanes] = values[source : source + 3]


AXES = ("dp", "z", "core")
CHIPS = ("dp", "z")


def exchange(send):
    return lax.all_to_all(send, AXES, 0, 0, tiled=True)


def together(*values):
    return lax.optimization_barrier(values)


def swap_cores(values):
    return lax.ppermute(values, "core", [(0, 1), (1, 0)])


def add_cores(tiles):
    core = lax.axis_index("core")
    pair = tiles.reshape(2, tiles.shape[0] // 2, *tiles.shape[1:])
    mine = lax.dynamic_index_in_dim(pair, core, 0, keepdims=False)
    return mine + swap_cores(lax.dynamic_index_in_dim(pair, 1 - core, 0, keepdims=False))


def share_out(tiles, names=CHIPS):
    count = 1
    for name in names:
        count = count * lax.axis_size(name)
    return lax.all_to_all(tiles.reshape(count, -1, *tiles.shape[1:]), names, 0, 0, tiled=True)


def share_back(pieces, names=CHIPS):
    own = jnp.sum(pieces, axis=0)
    everyone = lax.all_to_all(jnp.broadcast_to(own[None], pieces.shape), names, 0, 0, tiled=True)
    return everyone.reshape(-1, *pieces.shape[2:])


def shape(*dims, kind=F32):
    return jax.ShapeDtypeStruct(dims, kind)


def whole(array):
    rank = len(array.shape)
    return pl.BlockSpec(array.shape, lambda *ids: (0,) * rank)


SCALARS = pl.BlockSpec(memory_space=pltpu.SMEM)


def call(kernel, grid, in_specs, out_specs, out_shape, scratch, args, vmem=VMEM_BYTES, aliases=None):
    return pl.pallas_call(
        kernel,
        grid=grid,
        in_specs=in_specs,
        out_specs=out_specs,
        out_shape=out_shape,
        scratch_shapes=scratch,
        compiler_params=pltpu.CompilerParams(vmem_limit_bytes=vmem),
        input_output_aliases=aliases or {},
        cost_estimate=pl.CostEstimate(
            flops=1_000_000_000, bytes_accessed=1_000_000, transcendentals=0
        ),
    )(*args)


def simple_call(kernel, scalars, args, outs):
    return call(
        kernel, (1,), [SCALARS] * scalars + [whole(array) for array in args[scalars:]], [whole(item) for item in outs],
        outs, [], args,
    )


def local(
    video, frame_counts, momentum_index, expand_weight, wide_gains, wide_biases, narrow_gains, narrow_biases, depth_weight,
    squeeze_weight, squeeze_bias, excite_weight, excite_bias, project_weight, wide_means, wide_variances, narrow_means,
    narrow_variances, cotangent,
):
    devices = lax.axis_size("dp") * lax.axis_size("z") * lax.axis_size("core")
    cin, pixels = video.shape
    half_pixels = cotangent.shape[1]
    width = expand_weight.shape[1]
    squeeze = squeeze_weight.shape[1]
    frames = pixels // (SIDE * SIDE)
    tiles = width // LANES
    taps = depth_weight.shape[1]
    w_t = jnp.swapaxes(expand_weight, 1, 2)
    up_t = jnp.swapaxes(excite_weight, 1, 2)
    lanes_pad = ((0, 0), (0, LANES - cin))
    ngains = jnp.pad(narrow_gains, lanes_pad)
    nbiases = jnp.pad(narrow_biases, lanes_pad)
    full_rows = frames * FULL_ROWS
    half_rows = frames * HALF_ROWS
    low = jnp.bfloat16
    core = lax.axis_index("core").astype(jnp.int32).reshape(1)

    def round_up(count):
        return -(-count // devices) * devices

    def fixed(*dims):
        return pl.BlockSpec(dims, lambda *ids: (0,) * len(dims))

    def tile_rows(rows):
        return pl.BlockSpec((rows, LANES), lambda j: (0, j))

    def tile_cube(rows):
        return pl.BlockSpec((rows, 8, LANES), lambda j: (0, 0, j))

    def tile_sums(rows=2):
        return pl.BlockSpec((devices, rows, LANES), lambda j: (0, 0, j))

    def weight_tile(block, rows):
        return pl.BlockSpec((1, rows, LANES), lambda j, block=block: (block, 0, j))

    def of_block(block, rows, lanes):
        return pl.BlockSpec((1, rows, lanes), lambda *ids: (block, 0, 0))

    def early(make):
        return make(lambda p, j: j * (1 - p) + (tiles - 1) * p)

    def late(make):
        return make(lambda p, j: j * p)

    def both(make):
        return make(lambda p, j: j)

    def rows_at(rows):
        return lambda at: pl.BlockSpec((rows, LANES), lambda p, j: (0, at(p, j)))

    def cube_at(rows):
        return lambda at: pl.BlockSpec((rows, 8, LANES), lambda p, j: (0, 0, at(p, j)))

    def sums_at(rows):
        return lambda at: pl.BlockSpec((devices, rows, LANES), lambda p, j: (0, 0, at(p, j)))

    def weight_at(block, rows):
        return lambda at: pl.BlockSpec((1, rows, LANES), lambda p, j: (block, 0, at(p, j)))

    gram_zero, sums = call(
        gram_kernel, (1,), [SCALARS, whole(video), of_block(0, cin, width)],
        [fixed(LANES + 8, LANES), fixed(devices, 2, width + LANES)],
        [shape(LANES + 8, LANES), shape(devices, 2, width + LANES)],
        [], (frame_counts, video, w_t), vmem=60 * 1024 * 1024,
    )
    x, x_rows, x_columns, cot = simple_call(
        prepare_kernel, 1, (frame_counts, video, cotangent),
        [shape(pixels, LANES), shape(pixels, 2 * LANES, kind=low), shape(2 * LANES, pixels, kind=low),
         shape(half_pixels, LANES)],
    )
    sums = exchange(sums)

    def planes_shape(block, lanes, planes):
        if block:
            return (frames, planes, SIDE + 2, 8, lanes)
        return (frames, planes, 4, PAIRS, 8, lanes)

    def planes_of(block, planes, begin=0):
        dims = planes_shape(block, LANES, planes)
        zeros = (0,) * (len(dims) - 1)
        return pl.BlockSpec(dims, lambda j: zeros + (j + begin,))

    def expand(block, sums, count, count_spec, rows):
        depth_rows = half_rows if block else full_rows
        planes = 3 if block else 2
        scratch = [pltpu.VMEM((taps if block else 12 * LAGS, 8, LANES), F32)]
        if not block:
            scratch = scratch + [pltpu.VMEM(planes_shape(0, LANES, 2), F32), pltpu.VMEM((PAIRS, 4, 2, 8, LANES), F32)]
        return call(
            functools.partial(expand_kernel, block), (tiles,),
            [SCALARS, tile_sums(), count_spec, whole(rows), weight_tile(block, cin), tile_rows(4), tile_rows(4),
             weight_tile(block, taps)],
            [tile_cube(full_rows), tile_cube(depth_rows), tile_rows(8), tile_sums(), planes_of(block, planes)],
            [shape(full_rows, 8, width), shape(depth_rows, 8, width), shape(8, width), shape(devices, 2, width),
             shape(*planes_shape(block, width, planes))],
            scratch,
            (frame_counts, sums, count, rows, w_t, wide_gains, wide_biases, depth_weight),
        )

    count_spec = pl.BlockSpec((devices, 2, LANES), lambda j: (0, 0, tiles))
    e_zero, d_zero, stat01, sums, planes_zero = expand(0, sums, sums, count_spec, x_rows)
    sums = exchange(sums)

    def squeeze_forward(block, sums, stat, depth):
        rows = half_rows if block else full_rows
        kinds = 4 if block else 2
        moving = [tile_sums(), tile_rows(8), tile_cube(rows), tile_rows(4), tile_rows(4)]
        if block:
            moving = [whole(array) for array in (sums, stat, depth, wide_gains, wide_biases)]
        return call(
            functools.partial(squeeze_forward_kernel, block), (1 if block else tiles,),
            [SCALARS] + moving
            + [of_block(block, squeeze, width), whole(squeeze_bias), of_block(block, squeeze, width), whole(excite_bias),
               of_block(block, cin, width), whole(cot)],
            [fixed(rows * 8, LANES), fixed(8, width), fixed(8, width), fixed(8, squeeze),
             fixed(8, width) if block else tile_rows(8), fixed(devices, kinds, LANES)],
            [shape(rows * 8, LANES), shape(8, width), shape(8, width), shape(8, squeeze), shape(8, width),
             shape(devices, kinds, LANES)],
            [pltpu.VMEM((tiles, rows, 8, LANES), F32), pltpu.VMEM((tiles, frames, LANES), F32)],
            (frame_counts, sums, stat, depth, wide_gains, wide_biases, squeeze_weight, squeeze_bias, up_t, excite_bias,
             project_weight, cot),
        )

    z_zero, gates_zero, running_zero, pre_zero, stat02, sums = squeeze_forward(0, sums, stat01, d_zero)
    sums = exchange(sums)
    narrow_args = (frame_counts, sums, stat01, gram_zero, x, z_zero, ngains, nbiases, w_t)
    narrow_outs = [
        shape(pixels, LANES), shape(pixels, 2 * LANES, kind=low), shape(2 * LANES, pixels, kind=low),
        shape(round_up(3 * LANES // 8 + 1), 8, LANES), shape(8, LANES), shape(devices, 2, width),
    ]
    x1, x1_rows, x1_columns, gram, nstat, sums = call(
        narrow_kernel, (1,), [SCALARS] + [whole(array) for array in narrow_args[1:-1]] + [of_block(1, cin, width)],
        [whole(item) for item in narrow_outs], narrow_outs, [], narrow_args,
    )
    sums, gram = together(exchange(sums), gram)
    gram = share_out(gram, AXES)
    e_one, d_one, stat11, sums, planes_one = expand(1, sums, nstat, pl.BlockSpec((8, LANES), lambda j: (0, 0)), x1_rows)
    sums, gram = together(sums, gram)
    sums = exchange(sums)
    z_one, gates_one, running_one, pre_one, stat12, sums = squeeze_forward(1, sums, stat11, d_one)
    third, gram = together(exchange(sums), gram)
    gram = share_back(gram, AXES).reshape(-1, LANES)
    q_tiles = cin // 8 + -(-taps // 8)

    def backward_specs(block):
        rows = half_rows if block else full_rows
        ins = [fixed(8, width), fixed(rows, 8, width), fixed(4, width), fixed(4, width), of_block(block, squeeze, width),
               of_block(block, squeeze, width), of_block(block, cin, width), fixed(8, width), fixed(8, width),
               fixed(8, squeeze)]
        if not block:
            ins[0:4] = [both(rows_at(8)), both(cube_at(rows)), both(rows_at(4)), both(rows_at(4))]
            ins[6] = early(weight_at(block, cin))
        packed = round_up(tiles * (pack_tiles(cin, squeeze) + (0 if block else q_tiles)))
        wide_outs = [fixed(rows, 8, width), fixed(devices, 2, width)] if block else [late(cube_at(rows)), late(sums_at(2))]
        outs = [fixed(8, LANES)] + wide_outs + [fixed(packed // 2, 8, LANES)] * 2
        shapes = [shape(8, LANES), shape(rows, 8, width), shape(devices, 2, width)] + [shape(packed // 2, 8, LANES)] * 2
        scratch = [pltpu.VMEM((rows * 8, 2 * LANES), low), pltpu.VMEM((2 * LANES, rows * 8), low),
                   pltpu.VMEM((2 * LANES, 2 * LANES), F32), pltpu.VMEM((tiles, rows, 8, LANES), F32),
                   pltpu.VMEM((tiles, frames, LANES), F32)]
        return (ins, outs, shapes, scratch)

    ins, outs, shapes, scratch = backward_specs(1)
    activations, nsum_one, dy2_one, sums, pack_one, theirs = call(
        squeeze_one_backward_kernel, (1,),
        [SCALARS, SCALARS, whole(third), whole(z_one), whole(cot), whole(ngains), whole(nbiases)] + ins,
        [fixed(cin, half_pixels)] + outs, [shape(cin, half_pixels)] + shapes, scratch,
        (frame_counts, core, third, z_one, cot, ngains, nbiases, stat12, d_one, wide_gains, wide_biases, squeeze_weight, up_t,
         project_weight, gates_one, running_one, pre_one),
    )
    sums, theirs, gram = together(sums, theirs, gram)
    sums, pack_one = together(exchange(sums), pack_one + swap_cores(theirs))
    pack_one = share_out(pack_one)

    def depth_backward(block, sums, stat2, stat, dy2, depth, expanded, planes, columns):
        rows = half_rows if block else full_rows
        listed = tiles * q_tiles if block else round_up(tiles * q_tiles)
        send = (devices, 2, width + LANES) if block else (2, 8, LANES)
        if block:
            taps_shape = (taps, 8, LANES)
            z_shape = (frames, 2, HALF_ROWS + 1, 8, LANES)
            f_shape = (full_rows, 8, LANES)
        else:
            taps_shape = (12 * LAGS, 8, LANES)
            z_shape = planes_shape(0, LANES, 4)
            f_shape = (frames, PAIRS, 4, 2, 8, LANES)
        return call(
            functools.partial(depth_backward_kernel, block), (tiles,),
            [SCALARS, tile_sums(), tile_rows(8), tile_rows(8), whole(nstat),
             tile_cube(rows), tile_cube(rows), tile_cube(full_rows), planes_of(block, 2), whole(columns), weight_tile(block, cin), tile_rows(4),
             tile_rows(4), weight_tile(block, taps), whole(z_zero)],
            [fixed(pixels, LANES), fixed(*send), fixed(listed, 8, LANES), tile_rows(8)],
            [shape(pixels, LANES), shape(*send), shape(listed, 8, LANES), shape(8, width)],
            [pltpu.VMEM(z_shape, F32), pltpu.VMEM(f_shape, F32), pltpu.VMEM(taps_shape, F32), pltpu.VMEM(taps_shape, F32),
             pltpu.VMEM((2 * LANES, 2 * LANES), F32)]
            + ([] if block else [pltpu.VMEM((frames, 4, 2, PAIRS, 8, LANES), F32)]),
            (frame_counts, sums, stat2, stat, nstat, dy2, depth, expanded, planes, columns, w_t, wide_gains, wide_biases,
             depth_weight, z_zero),
        )

    dxpre_one, sums, q_one, grad_one = depth_backward(
        1, sums, stat12, stat11, dy2_one, d_one, e_one, planes_one, x1_columns
    )
    sums, pack_one = together(sums, pack_one)
    top_one, pack_one = together(exchange(sums), pack_one)
    pack_one = share_back(pack_one)
    ins, outs, shapes, scratch = backward_specs(0)
    dx1, nsum_zero, dy2_zero, sums, pack_zero, theirs = call(
        squeeze_zero_backward_kernel, (2, tiles),
        [SCALARS, SCALARS, whole(top_one), whole(stat11), whole(gram), whole(nstat), whole(dxpre_one), whole(x1), whole(z_zero),
         whole(ngains), of_block(1, cin, width), whole(wide_gains), whole(q_one)] + ins,
        [fixed(pixels, LANES)] + outs, [shape(pixels, LANES)] + shapes, scratch,
        (frame_counts, core, top_one, stat11, gram, nstat, dxpre_one, x1, z_zero, ngains, w_t, wide_gains, q_one, stat02, d_zero,
         wide_gains, wide_biases, squeeze_weight, up_t, project_weight, gates_zero, running_zero, pre_zero),
    )
    sums, pack_one = together(sums, pack_one)
    pack_one_other = swap_cores(pack_one)
    sums, pack_zero, pack_one_other = together(
        exchange(sums), pack_zero + swap_cores(theirs), pack_one_other
    )
    pack_zero = share_out(pack_zero)
    dxpre_zero, top, late, grad_zero = depth_backward(
        0, sums, stat02, stat01, dy2_zero, d_zero, e_zero, planes_zero, x_columns
    )
    top, pack_zero = together(top, pack_zero)
    top = top + swap_cores(top)
    late = add_cores(late)
    own = jnp.sum(pack_zero, axis=0)
    chips = pack_zero.shape[0]
    joint = jnp.concatenate(
        [jnp.broadcast_to(own[None], pack_zero.shape), late.reshape(chips, -1, 8, LANES),
         jnp.broadcast_to(top[None], (chips,) + top.shape)], axis=1,
    )
    joint = lax.all_to_all(joint, CHIPS, 0, 0, tiled=True)
    added = jnp.sum(joint[:, own.shape[0] :], axis=0)
    top_zero = added[-2:]
    late = lax.all_to_all(
        jnp.broadcast_to(added[None, :-2], (chips, added.shape[0] - 2, 8, LANES)), CHIPS, 0, 0, tiled=True
    ).reshape(-1, 8, LANES)
    joint_other = swap_cores(joint)
    final_args = (
        frame_counts, momentum_index, gram, stat01, stat02, stat11, stat12, grad_zero, grad_one, top_one,
        top_zero, nsum_zero, nsum_one, dxpre_zero, x, dx1, w_t, wide_gains, wide_means, wide_variances, narrow_means,
        narrow_variances,
    )
    final_outs = [
        shape(cin, pixels), shape(2, cin, width), shape(16, width), shape(4, width), shape(4, width), shape(2, cin),
        shape(2, cin), shape(4, width), shape(4, width), shape(2, cin), shape(2, cin),
    ]
    video_grad, less, factor, wgain, wbias, ngain, nbias, newm, newv, newnm, newnv = simple_call(
        finish_kernel, 2, final_args, final_outs
    )
    list_shapes = [
        shape(2, cin, width), shape(2, taps, width), shape(2, squeeze, width), shape(2, squeeze, width),
        shape(2, cin, width), shape(2, width), shape(2, squeeze),
    ]
    list_args = (core, joint, joint_other, pack_one, pack_one_other, less, factor)
    dw_t, dtaps, ddown, dup, dproj, dupb, ddownb = call(
        functools.partial(lists_kernel, own.shape[0]), (1,), [SCALARS] + [whole(array) for array in list_args[1:5]] + [of_block(1, cin, width), whole(factor)],
        [of_block(1, cin, width), of_block(1, taps, width)] + [whole(item) for item in list_shapes[2:]], list_shapes, [],
        list_args,
    )
    dw_t, late = together(dw_t, late)
    late_other = swap_cores(late)
    stay = pl.BlockSpec(memory_space=pl.ANY)
    dw_t, dtaps = call(
        last_kernel, (1,),
        [SCALARS, whole(late), whole(late_other), of_block(0, cin, width), whole(factor), stay, stay],
        [of_block(0, cin, width), of_block(0, taps, width)], list_shapes[0:2], [],
        (core, late, late_other, less, factor, dw_t, dtaps), aliases={5: 0, 6: 1},
    )
    return (
        activations, video_grad, jnp.swapaxes(dw_t, 1, 2), wgain, wbias, ngain, nbias, dtaps, ddown, ddownb,
        jnp.swapaxes(dup, 1, 2), dupb, dproj, newm, newv, newnm, newnv,
    )


def solution(mesh):
    sizes = (mesh.shape["dp"], mesh.shape["rep"] // 2, 2)
    split_mesh = jax.sharding.Mesh(mesh.devices.reshape(sizes), AXES)
    split = P(None, AXES)
    placed = (split, P(AXES)) + (P(),) * 16 + (split,)
    return jax.shard_map(
        local, mesh=split_mesh, in_specs=placed, out_specs=(split, split) + (P(),) * 15, check_vma=False
    )
```
